32 devices in a mesh: dp: 4 (over y, x), blk: 8 (over z, core).
Axes of the slice: x: 2, y: 2, z: 4, core: 2. Of those that a mesh axis runs over, the one named last changes fastest.
Arguments:
- tokens: bfloat16 [16, 2048, 512], P('dp', 'blk'), may hold values from -6 to 6
- teacher_tokens: bfloat16 [16, 2048, 512], P('dp', 'blk'), may hold values from -6 to 6
- segment_ids: int32 [16, 2048], P('dp', 'blk'), may hold values from 0 to 510, as said below
- cotangent: bfloat16 [16, 2048, 512], P('dp', 'blk'), may hold values from -6 to 6
- latent_qkv: bfloat16 [3, 512, 512], replicated, may hold values from -0.375 to 0.375
- latent_out: bfloat16 [512, 512], replicated, may hold values from -1.5 to 1.5
- latent_up: bfloat16 [512, 2048], replicated, may hold values from -0.25 to 0.25
- latent_down: bfloat16 [2048, 512], replicated, may hold values from -0.125 to 0.125
- student_gain: float32 [2, 512], replicated, may hold values from 0.25 to 1.75
- student_bias: float32 [6, 512], replicated, may hold values from -3 to 3
- student_up_bias: float32 [2048], replicated, may hold values from -3 to 3
- teacher_qkv: bfloat16 [3, 512, 512], P(None, 'dp'), may hold values from -0.375 to 0.375
- teacher_out: bfloat16 [512, 512], P('dp'), may hold values from -1.5 to 1.5
- teacher_up: bfloat16 [512, 2048], P('dp'), may hold values from -0.25 to 0.25
- teacher_down: bfloat16 [2048, 512], P('dp'), may hold values from -0.125 to 0.125
- teacher_gain: float32 [2, 512], replicated, may hold values from 0.25 to 1.75
- teacher_bias: float32 [6, 512], replicated, may hold values from -3 to 3
- teacher_up_bias: float32 [2048], replicated, may hold values from -3 to 3
Outputs:
- output: bfloat16 [16, 2048, 512], P('dp', 'blk')
- grad_tokens: bfloat16 [16, 2048, 512], P('dp', 'blk')
- grad_latent_qkv: float32 [3, 512, 512], replicated
- grad_latent_out: float32 [512, 512], replicated
- grad_latent_up: float32 [512, 2048], replicated
- grad_latent_down: float32 [2048, 512], replicated
- grad_student_gain: float32 [2, 512], replicated
- grad_student_bias: float32 [6, 512], replicated
- grad_student_up_bias: float32 [2048], replicated
The draws below stay inside these ranges and needn't reach their ends.
Inputs may be any that keep to these rules, and one draw needn't show every extreme that they name: `segment_ids`: in each stream the ids start at 0 and never fall; one document of every stream begins within its first 256 tokens and ends within its last 256 tokens.
All inputs are finite; a program needn't handle non-finite values.
Results may differ from the reference program's by a relative error of at most 0.014.
Values may be sent and summed in bfloat16 or wider, within the bound.
A program may use at most 384 MiB of HBM per device.

```python
import jax
import jax.numpy as jnp
from jax import lax

D = 512
HEADS = 8
FF = 2048
SEQ = 2048
SHARD = 256
STREAMS = 16


def draw_segment_ids(key, part):
    key = jax.random.fold_in(key, 11)
    head_key, tail_key, cut_key, pick_key = jax.random.split(key, 4)
    chosen = jax.random.randint(pick_key, (), 0, STREAMS)
    stream_rows = jnp.arange(STREAMS, dtype=jnp.int32)[:, None]
    forced = stream_rows == chosen
    head_len = jnp.where(forced, SHARD - 1, jax.random.randint(head_key, (STREAMS, 1), 1, SHARD))
    tail_len = jnp.where(forced, SHARD - 1, jax.random.randint(tail_key, (STREAMS, 1), 1, SHARD))
    places = jnp.arange(SEQ, dtype=jnp.int32)[None, :]
    cut_draw = jax.random.randint(cut_key, (STREAMS, SEQ), 0, 6)
    cut_here = (cut_draw == 0) | forced
    border = (places < head_len) | (places >= SEQ - tail_len)
    starts = (places == head_len) | (places == SEQ - tail_len) | cut_here & border & (places > 0)
    return jnp.cumsum(starts.astype(jnp.int32), axis=1).astype(jnp.int32)


def steps_of(stream_key, dims, cuts, smallest, high):
    def one(axis_at, shards_of):
        heights = jax.random.uniform(jax.random.fold_in(jax.random.fold_in(stream_key, 6), axis_at), (shards_of,), jnp.float32, smallest / len(cuts), high / len(cuts))
        return jnp.repeat(jnp.exp(heights), dims[axis_at] // shards_of).reshape((-1,) + (1,) * (len(dims) - axis_at - 1))

    factor_of = one(*cuts[0])
    for cut in cuts[1:]:
        factor_of = factor_of * one(*cut)
    return factor_of


def centred(key, shape, deviation, reach, cuts=(), kind=jnp.bfloat16):
    level = steps_of(key, shape, cuts, -0.22, 0.18) if cuts else 1.0
    result = jax.random.normal(key, shape, jnp.float32) * deviation * level
    return jnp.minimum(jnp.maximum(result, -reach), reach).astype(kind)


def setup_inputs(seed: int = 0) -> dict:
    seeds = jax.random.split(jax.random.key(seed), 19)
    return {
        "tokens": centred(seeds[0], (STREAMS, SEQ, D), 1.0, 6.0, ((0, 4), (1, 8))),
        "teacher_tokens": centred(seeds[1], (STREAMS, SEQ, D), 1.0, 6.0, ((0, 4), (1, 8))),
        "segment_ids": draw_segment_ids(jax.random.fold_in(seeds[18], 71), 0),
        "cotangent": centred(seeds[3], (STREAMS, SEQ, D), 1.0, 6.0, ((0, 4), (1, 8))),
        "latent_qkv": centred(seeds[4], (3, D, D), (D // 2) ** -0.5, 0.375),
        "latent_out": centred(seeds[5], (D, D), (D // 32) ** -0.5, 1.5),
        "latent_up": centred(seeds[6], (D, FF), D ** -0.5, 0.25),
        "latent_down": centred(seeds[7], (FF, D), FF ** -0.5, 0.125),
        "student_gain": jnp.clip(1.0 + 0.15 * jax.random.normal(seeds[8], (2, D), jnp.float32), 0.25, 1.75),
        "student_bias": centred(seeds[9], (6, D), 0.5, 3.0, (), jnp.float32),
        "student_up_bias": centred(seeds[10], (FF,), 0.5, 3.0, (), jnp.float32),
        "teacher_qkv": centred(seeds[11], (3, D, D), (D // 2) ** -0.5, 0.375, ((1, 4),)),
        "teacher_out": centred(seeds[12], (D, D), (D // 32) ** -0.5, 1.5, ((0, 4),)),
        "teacher_up": centred(seeds[13], (D, FF), D ** -0.5, 0.25, ((0, 4),)),
        "teacher_down": centred(seeds[14], (FF, D), FF ** -0.5, 0.125, ((0, 4),)),
        "teacher_gain": jnp.clip(1.0 + 0.15 * jax.random.normal(seeds[15], (2, D), jnp.float32), 0.25, 1.75),
        "teacher_bias": centred(seeds[16], (6, D), 0.5, 3.0, (), jnp.float32),
        "teacher_up_bias": centred(seeds[17], (FF,), 0.5, 3.0, (), jnp.float32),
    }


@jax.custom_vjp
def low(v):
    return lax.optimization_barrier(v.astype(jnp.bfloat16)).astype(jnp.float32)

@jax.custom_vjp
def low_back(v):
    return v

def low_keep(v):
    return (low(v), None)

def low_pass(kept, grad):
    return (grad,)

def back_keep(v):
    return (v, None)

def back_low(kept, grad):
    return (low(grad),)
low.defvjp(low_keep, low_pass)
low_back.defvjp(back_keep, back_low)
highest = lax.Precision.HIGHEST
clip_level = 2.5
masked_score = -1e+30

def squash(tensor):
    return clip_level * jnp.tanh(tensor / clip_level)

def binarize(matrix):
    column_scale = jnp.sqrt(lax.optimization_barrier(jnp.mean(matrix * matrix, axis=-2, keepdims=True)) + 1e-06)
    return column_scale * jnp.tanh(2.0 * matrix / column_scale)

def gelu(tensor):
    return 0.5 * tensor * (1.0 + lax.erf(tensor * 0.7071067811865476))

def layer_norm(tensor, gain_row, shift_row):
    centre = tensor - lax.optimization_barrier(jnp.mean(tensor, axis=-1, keepdims=True))
    inverse_std = lax.rsqrt(lax.optimization_barrier(jnp.mean(centre * centre, axis=-1, keepdims=True)) + 1e-05)
    return centre * inverse_std * gain_row + shift_row

def both_ways(tensor):
    return low(low_back(tensor))

def split_heads(tensor):
    return tensor.reshape(tensor.shape[0], HEADS, D // HEADS)

def masked_softmax(scores, same_doc):
    masked = jnp.where(same_doc, scores, masked_score)
    row_max = lax.optimization_barrier(jnp.max(masked, axis=-1, keepdims=True))
    numerators = jnp.where(same_doc, jnp.exp(masked - row_max), 0.0)
    return numerators / lax.optimization_barrier(jnp.sum(numerators, axis=-1, keepdims=True))

def teacher_stream(stream_tokens, stream_docs, qkv_matrix, out_matrix, up_matrix, down_matrix, gain_rows, bias_rows, up_shift):
    projected = jnp.einsum('sd,kde->kse', stream_tokens, qkv_matrix, precision=highest)
    queries = low(projected[0] + bias_rows[0])
    key_rows = low(projected[1])
    values = low(projected[2] + bias_rows[1])
    same_doc = (stream_docs[:, None] == stream_docs[None, :])[None]
    scores = jnp.einsum('qhd,khd->hqk', split_heads(queries), split_heads(key_rows), precision=highest) * 0.125
    attn_probs = masked_softmax(scores, same_doc)
    context = jnp.einsum('hqk,khd->qhd', low(attn_probs), split_heads(values), precision=highest).reshape(-1, D)
    hidden = layer_norm(stream_tokens + jnp.dot(low(context), out_matrix, precision=highest) + bias_rows[2], gain_rows[0], bias_rows[3])
    inner_act = gelu(jnp.dot(low(hidden), up_matrix, precision=highest) + up_shift)
    output = layer_norm(hidden + jnp.dot(low(inner_act), down_matrix, precision=highest) + bias_rows[4], gain_rows[1], bias_rows[5])
    return (queries, key_rows, output)

def student_stream(stream_tokens, stream_docs, teacher_queries, teacher_keys, binary_set):
    qkv_bin, out_bin, up_bin, down_bin, gain_rows, bias_rows, up_shift = binary_set
    active = low(squash(stream_tokens))
    projected = jnp.einsum('sd,kde->kse', active, qkv_bin, precision=highest)
    queries = both_ways(projected[0] + bias_rows[0])
    key_rows = both_ways(projected[1])
    values = both_ways(projected[2] + bias_rows[1])
    same_doc = (stream_docs[:, None] == stream_docs[None, :])[None]
    scores = low_back(jnp.einsum('qhd,khd->hqk', split_heads(queries), split_heads(key_rows), precision=highest) * 0.125)
    teacher_scores = jnp.einsum('qhd,khd->hqk', split_heads(teacher_queries), split_heads(teacher_keys), precision=highest) * 0.125
    attn_probs = masked_softmax(scores, same_doc)
    context = low_back(jnp.einsum('hqk,khd->qhd', low(attn_probs), split_heads(values), precision=highest)).reshape(-1, D)
    mismatch = scores - teacher_scores
    distill = jnp.sum(jnp.where(same_doc, mismatch * mismatch, 0.0)) / (2.0 * SEQ)
    attended = low_back(jnp.dot(low(squash(context)), out_bin, precision=highest) + bias_rows[2])
    hidden = layer_norm(stream_tokens + attended, gain_rows[0], bias_rows[3])
    inner_pre = low_back(jnp.dot(low(squash(hidden)), up_bin, precision=highest) + up_shift)
    branch = low_back(jnp.dot(low(squash(gelu(inner_pre))), down_bin, precision=highest) + bias_rows[4])
    output = layer_norm(hidden + branch, gain_rows[1], bias_rows[5])
    return (output, distill)

def reference(tokens, teacher_tokens, segment_ids, cotangent, latent_qkv, latent_out, latent_up, latent_down, student_gain, student_bias, student_up_bias, teacher_qkv, teacher_out, teacher_up, teacher_down, teacher_gain, teacher_bias, teacher_up_bias):
    teacher_args = (teacher_qkv.astype(jnp.float32), teacher_out.astype(jnp.float32), teacher_up.astype(jnp.float32), teacher_down.astype(jnp.float32), teacher_gain.astype(jnp.float32), teacher_bias.astype(jnp.float32), teacher_up_bias.astype(jnp.float32))

    def teacher_step(inputs):
        return teacher_stream(inputs[0], inputs[1], teacher_args[0], teacher_args[1], teacher_args[2], teacher_args[3], teacher_args[4], teacher_args[5], teacher_args[6])
    teacher_queries, teacher_keys, teacher_output = lax.map(teacher_step, (teacher_tokens.astype(jnp.float32), segment_ids))
    cotangent_float = cotangent.astype(jnp.float32)

    def objective(inputs, qkv_latent, out_latent, up_latent, down_latent, gain_rows, bias_rows, up_shift):
        binary_set = (low(binarize(qkv_latent)), low(binarize(out_latent)), low(binarize(up_latent)), low(binarize(down_latent)), gain_rows, bias_rows, up_shift)

        def stream_step(running, stream_inputs):
            stream_tokens, stream_docs, stream_tq, stream_tk, stream_target, stream_cot = stream_inputs
            output, distill = student_stream(stream_tokens, stream_docs, stream_tq, stream_tk, binary_set)
            mismatch = output - stream_target
            running = running + jnp.sum(stream_cot * output) + 0.25 * jnp.sum(mismatch * mismatch) + distill
            return (running, output)
        running, outputs = lax.scan(jax.checkpoint(stream_step), jnp.zeros((), jnp.float32), (inputs, segment_ids, teacher_queries, teacher_keys, teacher_output, cotangent_float))
        return (running, outputs)
    running, pullback, outputs = jax.vjp(objective, tokens.astype(jnp.float32), latent_qkv.astype(jnp.float32), latent_out.astype(jnp.float32), latent_up.astype(jnp.float32), latent_down.astype(jnp.float32), student_gain.astype(jnp.float32), student_bias.astype(jnp.float32), student_up_bias.astype(jnp.float32), has_aux=True)
    gradients = pullback(jnp.ones_like(running))
    return (outputs.astype(jnp.bfloat16), gradients[0].astype(jnp.bfloat16), gradients[1], gradients[2], gradients[3], gradients[4], gradients[5], gradients[6], gradients[7])
```

```python
import functools

import jax
import jax.numpy as jnp
from jax import lax
from jax.experimental import pallas as pl
from jax.experimental.pallas import tpu as pltpu
from jax.sharding import PartitionSpec as P

HEADS = 8
BF = jnp.bfloat16
F32 = jnp.float32
LOG2E = 1.4426950408889634
clip_level = 2.5
masked_score = -1e30
VMEM_BYTES = 56 << 20
MESH = pl.DeviceIdType.MESH
NT = (((1,), (1,)), ((), ()))
TN = (((0,), (0,)), ((), ()))


def squash(tensor):
    return clip_level * jnp.tanh(tensor * (1.0 / clip_level))


def gelu_parts(tensor):
    phi = 0.5 * (1.0 + lax.erf(tensor * 0.7071067811865476))
    return tensor * phi, phi


def binarize(matrix):
    column_scale = jnp.sqrt(jnp.mean(matrix * matrix, axis=-2, keepdims=True) + 1e-06)
    return column_scale * jnp.tanh(2.0 * matrix / column_scale)


def layer_norm(tensor, gain_row, shift_row):
    centre = tensor - jnp.mean(tensor, axis=-1, keepdims=True)
    inverse_std = lax.rsqrt(jnp.mean(centre * centre, axis=-1, keepdims=True) + 1e-05)
    normed = centre * inverse_std
    return (normed * gain_row + shift_row, normed, inverse_std)


def norm_back(upstream, gain_row, normed, inverse_std):
    scaled = upstream * gain_row
    return inverse_std * (
        scaled
        - jnp.mean(scaled, axis=-1, keepdims=True)
        - normed * jnp.mean(scaled * normed, axis=-1, keepdims=True)
    )


def dot(a, b, dims=(((1,), (0,)), ((), ()))):
    return lax.dot_general(a, b, dims, preferred_element_type=F32)


def latent_grad(latent, binary_grad):
    matrix = latent.astype(F32)
    unused, pullback = jax.vjp(binarize, matrix)
    return pullback(binary_grad)[0]


def place(groups):
    here = lax.axis_index("blk")
    return here // groups, lax.rem(here, groups)


def greet(peers):
    barrier = pltpu.get_barrier_semaphore()
    for peer in peers:
        pl.semaphore_signal(barrier, inc=1, device_id={"blk": peer}, device_id_type=MESH)
    pl.semaphore_wait(barrier, len(peers))


def stream_peers(streams, groups):
    s, r = place(groups)
    return [lax.rem(s + d, streams) * groups + r for d in range(1, streams)]


def core_peers(groups):
    s, r = place(groups)
    return [s * groups + lax.rem(r + j, groups) for j in range(1, groups)]


def swap_copies(streams, groups, source, target, base, send, recv):
    s, r = place(groups)
    return [
        pltpu.make_async_remote_copy(
            src_ref=source.at[lax.rem(s + d, streams)],
            dst_ref=target.at[base + s],
            send_sem=send.at[d],
            recv_sem=recv.at[d],
            device_id={"blk": lax.rem(s + d, streams) * groups + r},
            device_id_type=MESH,
        )
        for d in range(1, streams)
    ]


def share_copy(streams, groups, source, slot, target, d, j, send, recv):
    s, r = place(groups)
    return pltpu.make_async_remote_copy(
        src_ref=source,
        dst_ref=target.at[slot],
        send_sem=send.at[j * streams + d],
        recv_sem=recv.at[j * streams + d],
        device_id={"blk": s * groups + lax.rem(r + j, groups)},
        device_id_type=MESH,
    )


class Gather:
    def __init__(self, streams, groups):
        self.streams, self.groups = streams, groups

    def scratch(self):
        b, g = self.streams, self.groups
        return [
            pltpu.SemaphoreType.DMA((b,)),
            pltpu.SemaphoreType.DMA((b,)),
            pltpu.SemaphoreType.DMA((b * g,)),
            pltpu.SemaphoreType.DMA((b * g,)),
        ]

    def peers(self):
        return stream_peers(self.streams, self.groups) + core_peers(self.groups)

    def first(self, source, target, send, recv, share_send, share_recv):
        b, g = self.streams, self.groups
        s, r = place(g)
        for copy in swap_copies(b, g, source, target, r * b, send, recv):
            copy.start()
        pltpu.make_async_copy(source.at[s], target.at[r * b + s], send.at[0]).start()
        for j in range(1, g):
            share_copy(
                b, g, source.at[s], r * b + s, target, 0, j, share_send, share_recv
            ).start()

    def last(self, source, target, send, recv, share_send, share_recv):
        b, g = self.streams, self.groups
        s, r = place(g)
        swaps = swap_copies(b, g, source, target, r * b, send, recv)
        shares = []
        for d in (1, 3, 2) if b == 4 else range(1, b):
            swaps[d - 1].wait_recv()
            slot = r * b + lax.rem(s + b - d, b)
            for j in range(1, g):
                copy = share_copy(b, g, target.at[slot], slot, target, d, j, share_send, share_recv)
                copy.start()
                shares.append(copy)
        pltpu.make_async_copy(source.at[s], target.at[r * b + s], send.at[0]).wait()
        for j in range(1, g):
            shares.append(
                share_copy(b, g, source.at[s], r * b + s, target, 0, j, share_send, share_recv)
            )
        for copy in shares:
            copy.wait()
        for copy in swaps:
            copy.wait_send()


class Swap:
    def __init__(self, streams, groups):
        self.streams, self.groups = streams, groups

    def scratch(self):
        return [
            pltpu.SemaphoreType.DMA((self.streams,)),
            pltpu.SemaphoreType.DMA((self.streams,)),
        ]

    def peers(self):
        return stream_peers(self.streams, self.groups)

    def first(self, source, target, send, recv):
        s, r = place(self.groups)
        for copy in swap_copies(self.streams, self.groups, source, target, 0, send, recv):
            copy.start()
        pltpu.make_async_copy(source.at[s], target.at[s], send.at[0]).start()

    def last(self, source, target, send, recv):
        s, r = place(self.groups)
        for copy in swap_copies(self.streams, self.groups, source, target, 0, send, recv):
            copy.wait()
        pltpu.make_async_copy(source.at[s], target.at[s], send.at[0]).wait()


class Rows:
    def __init__(self, groups):
        self.groups = groups

    def scratch(self):
        return [
            pltpu.SemaphoreType.DMA((self.groups,)),
            pltpu.SemaphoreType.DMA((self.groups,)),
        ]

    def peers(self):
        return core_peers(self.groups)

    def copies(self, source, target, send, recv):
        s, r = place(self.groups)
        g = self.groups
        return [
            pltpu.make_async_remote_copy(
                src_ref=source.at[lax.rem(r + j, g)],
                dst_ref=target.at[r],
                send_sem=send.at[j],
                recv_sem=recv.at[j],
                device_id={"blk": s * g + lax.rem(r + j, g)},
                device_id_type=MESH,
            )
            for j in range(1, g)
        ]

    def first(self, source, target, send, recv):
        s, r = place(self.groups)
        for copy in self.copies(source, target, send, recv):
            copy.start()
        pltpu.make_async_copy(source.at[r], target.at[r], send.at[0]).start()

    def last(self, source, target, send, recv):
        s, r = place(self.groups)
        for copy in self.copies(source, target, send, recv):
            copy.wait()
        pltpu.make_async_copy(source.at[r], target.at[r], send.at[0]).wait()


def move(job, arrays, out_shapes, collective_id, name):
    count = len(arrays)
    n_sems = len(job.scratch())

    def kernel(*refs):
        sources, targets = refs[:count], refs[count : 2 * count]
        sems = refs[2 * count :]
        greet(job.peers())
        for i in range(count):
            job.first(sources[i], targets[i], *sems[i * n_sems : (i + 1) * n_sems])
        for i in range(count):
            job.last(sources[i], targets[i], *sems[i * n_sems : (i + 1) * n_sems])

    return pl.pallas_call(
        kernel,
        out_shape=out_shapes,
        in_specs=[pl.BlockSpec(memory_space=pl.ANY)] * count,
        out_specs=[pl.BlockSpec(memory_space=pl.ANY)] * count,
        scratch_shapes=job.scratch() * count,
        compiler_params=pltpu.CompilerParams(collective_id=collective_id, has_side_effects=True),
        name=name,
    )(*arrays)


def lanes_of(shape):
    return lax.broadcasted_iota(jnp.int32, shape, 1)


def forward_kernel(job, keep, tile, edge, q_ref, k_ref, v_ref, col_ref, row_ref, src_ref, *rest):
    if keep:
        e_ref, ctx_ref, inv_ref, dst_ref, k_aug, v_aug, *sems = rest
    else:
        ctx_ref, dst_ref, k_aug, v_aug, *sems = rest
    pair, step = pl.program_id(0), pl.program_id(1)
    steps = pl.num_programs(1)
    seq = k_ref.shape[0]

    @pl.when((pair == 0) & (step == 0))
    def _():
        greet(job.peers())
        job.first(src_ref, dst_ref, *sems)

    @pl.when(step == 0)
    def _():
        low = lanes_of((seq, 128)) < 64
        lane = lanes_of((seq, 128))
        keys = k_ref[...].astype(F32)
        turned = pltpu.roll(keys, 64, 1)
        k_aug[0] = jnp.where(low, keys, turned).astype(BF)
        k_aug[1] = jnp.where(low, turned, keys).astype(BF)
        values = v_ref[...].astype(F32)
        v_aug[0] = jnp.where(low, values, jnp.where(lane < 66, 1.0, 0.0)).astype(BF)
        v_aug[1] = jnp.where(low, jnp.where(lane < 2, 1.0, 0.0), values).astype(BF)

    def body(whole):
        low = lanes_of((tile, 128)) < 64
        scaled = q_ref[...].astype(F32) * LOG2E
        upper = scaled.astype(BF).astype(F32)
        rest_part = scaled - upper
        results = []
        for h in range(2):
            if h == 0:
                q_aug = jnp.where(low, upper, pltpu.roll(rest_part, 64, 1)).astype(BF)
            else:
                q_aug = jnp.where(low, pltpu.roll(upper, 64, 1), rest_part).astype(BF)
            scores = dot(q_aug, k_aug[h], NT)
            if whole:
                scores = jnp.where(col_ref[...] == row_ref[...], scores, masked_score)
            else:
                left = jnp.where(
                    col_ref[...] == row_ref[:, :edge], scores[:, :edge], masked_score
                )
                right = jnp.where(
                    col_ref[...] == row_ref[:, seq - edge :], scores[:, seq - edge :], masked_score
                )
                scores = jnp.concatenate([left, scores[:, edge : seq - edge], right], axis=1)
            peak = jnp.max(scores, axis=1, keepdims=True)
            numerators = jnp.exp2(scores - peak).astype(BF)
            if keep:
                e_ref[h] = numerators
            total = dot(numerators, v_aug[h])
            where_sum = 64 if h == 0 else 0
            inverse = 1.0 / total[:, where_sum : where_sum + 1]
            results.append((total * inverse, inverse))
        ctx_ref[...] = jnp.where(low, results[0][0], results[1][0]).astype(BF)
        if keep:
            inv_ref[...] = jnp.where(low, results[0][1], results[1][1])

    at_edge = (step == 0) | (step == steps - 1)

    @pl.when(at_edge)
    def _():
        body(True)

    @pl.when(jnp.logical_not(at_edge))
    def _():
        body(False)

    @pl.when((pair == pl.num_programs(0) - 1) & (step == steps - 1))
    def _():
        job.last(src_ref, dst_ref, *sems)


def attention(qkv, docs, job, moved, moved_shape, keep, collective_id, name):
    seq, width3 = qkv.shape
    width = width3 // 3
    pairs = width // 128
    tile = 256
    edge = 256
    col = docs.reshape(seq, 1)
    row = docs.reshape(1, seq)
    blocks = [
        pl.BlockSpec((tile, 128), lambda p, i: (i, p)),
        pl.BlockSpec((seq, 128), lambda p, i: (0, pairs + p)),
        pl.BlockSpec((seq, 128), lambda p, i: (0, 2 * pairs + p)),
        pl.BlockSpec((tile, 1), lambda p, i: (i, 0)),
        pl.BlockSpec((1, seq), lambda p, i: (0, 0)),
        pl.BlockSpec(memory_space=pl.ANY),
    ]
    outs = [pl.BlockSpec((tile, 128), lambda p, i: (i, p))]
    shapes = [jax.ShapeDtypeStruct((seq, width), BF)]
    if keep:
        outs = [pl.BlockSpec((2, tile, seq), lambda p, i: (p, i, 0))] + outs
        shapes = [jax.ShapeDtypeStruct((2 * pairs, seq, seq), BF)] + shapes
        outs = outs + [pl.BlockSpec((tile, 128), lambda p, i: (i, p))]
        shapes = shapes + [jax.ShapeDtypeStruct((seq, width), F32)]
    outs.append(pl.BlockSpec(memory_space=pl.ANY))
    shapes.append(jax.ShapeDtypeStruct(moved_shape, moved.dtype))
    return pl.pallas_call(
        functools.partial(forward_kernel, job, keep, tile, edge),
        grid=(pairs, seq // tile),
        in_specs=blocks,
        out_specs=outs,
        out_shape=shapes,
        scratch_shapes=[pltpu.VMEM((2, seq, 128), BF), pltpu.VMEM((2, seq, 128), BF)]
        + job.scratch(),
        compiler_params=pltpu.CompilerParams(
            collective_id=collective_id, has_side_effects=True, vmem_limit_bytes=VMEM_BYTES
        ),
        name=name,
    )(qkv, qkv, qkv, col, row, moved)


def split(matrix):
    upper = matrix.astype(BF)
    return upper, (matrix - upper.astype(F32)).astype(BF)


def backward_kernel(
    job,
    tile,
    e_ref,
    q_ref,
    k_ref,
    v_ref,
    tq_ref,
    tk_ref,
    dc_ref,
    ctx_ref,
    inv_ref,
    col_ref,
    row_ref,
    bigc_ref,
    src_ref,
    dq_ref,
    dk_ref,
    dv_ref,
    dst_ref,
    v_aug,
    dk_acc,
    dv_acc,
    grams,
    *sems,
):
    pair, step = pl.program_id(0), pl.program_id(1)
    steps = pl.num_programs(1)
    seq = k_ref.shape[0]
    share = 1.0 / seq

    @pl.when((pair == 0) & (step == 0))
    def _():
        greet(job.peers())
        job.first(src_ref, dst_ref, *sems)

    @pl.when(step == 0)
    def _():
        lane = lanes_of((seq, 128))
        low = lane < 64
        values = v_ref[...].astype(F32)
        v_aug[0] = jnp.where(low, values, jnp.where(lane < 66, 1.0, 0.0)).astype(BF)
        v_aug[1] = jnp.where(low, jnp.where(lane < 2, 1.0, 0.0), values).astype(BF)
        dk_acc[...] = jnp.zeros_like(dk_acc)
        dv_acc[...] = jnp.zeros_like(dv_acc)
        in_big = bigc_ref[...] > 0.0
        kb = jnp.where(in_big, k_ref[...].astype(F32), 0.0).astype(BF)
        tkb = jnp.where(in_big, tk_ref[...].astype(F32), 0.0).astype(BF)
        qb = jnp.where(in_big, q_ref[...].astype(F32), 0.0).astype(BF)
        tqb = jnp.where(in_big, tq_ref[...].astype(F32), 0.0).astype(BF)
        same_head = (lax.broadcasted_iota(jnp.int32, (128, 128), 0) < 64) == (
            lanes_of((128, 128)) < 64
        )
        for i, (a, b) in enumerate(((kb, kb), (tkb, kb), (qb, qb), (tqb, qb))):
            gram = jnp.where(same_head, dot(a, b, TN) * share, 0.0)
            grams[2 * i], grams[2 * i + 1] = split(gram)

    start = pl.multiple_of(step * tile, tile)
    rows = pl.ds(start, tile)
    lane = lanes_of((tile, 128))
    low = lane < 64

    def body(whole, columns):
        in_big = bigc_ref[rows, :] > 0.0
        q8 = q_ref[rows, :]
        tq8 = tq_ref[rows, :]
        dc = dc_ref[...].astype(F32)
        inv = inv_ref[...]
        scaled = dc * inv
        product = scaled * ctx_ref[...].astype(F32)
        scaled_low = scaled.astype(BF)
        q_turned = q8.astype(F32).T.astype(BF)
        dc_turned = scaled_low.astype(F32).T.astype(BF)
        d_queries = []
        for h in range(2):
            mine = low if h == 0 else jnp.logical_not(low)
            delta = -jnp.sum(jnp.where(mine, product, 0.0), axis=1, keepdims=True)
            upper = delta.astype(BF).astype(F32)
            first = 64 if h == 0 else 0
            extra = jnp.where(
                lane == first, upper, jnp.where(lane == first + 1, delta - upper, 0.0)
            )
            dc_aug = jnp.where(mine, scaled, extra).astype(BF)
            numerators = e_ref[h]
            d_probs = dot(dc_aug, v_aug[h], NT)
            d_scores = numerators.astype(F32) * d_probs
            if whole:
                q_mine = jnp.where(mine, q8, 0.0).astype(BF)
                tq_mine = jnp.where(mine, tq8, 0.0).astype(BF)
                gap = dot(q_mine, k_ref[columns, :], NT) - dot(tq_mine, tk_ref[columns, :], NT)
                small = (col_ref[...] == row_ref[:, columns]) & jnp.logical_not(in_big)
                gap = jnp.where(small, gap * share, 0.0)
                if columns.start == 0:
                    d_scores = jnp.concatenate(
                        [d_scores[:, :tile] + gap, d_scores[:, tile:]], axis=1
                    )
                else:
                    d_scores = jnp.concatenate(
                        [d_scores[:, : seq - tile], d_scores[:, seq - tile :] + gap], axis=1
                    )
            d_scores = d_scores.astype(BF)
            d_queries.append(dot(d_scores, k_ref[...]))
            half = slice(64 * h, 64 * h + 64)
            dk_acc[half, :] += dot(q_turned[half, :], d_scores)
            dv_acc[half, :] += dot(dc_turned[half, :], numerators)
        d_query = jnp.where(low, d_queries[0], d_queries[1])
        qb = jnp.where(in_big, q8.astype(F32), 0.0).astype(BF)
        tqb = jnp.where(in_big, tq8.astype(F32), 0.0).astype(BF)
        d_query += dot(qb, grams[0]) + dot(qb, grams[1]) - dot(tqb, grams[2]) - dot(tqb, grams[3])
        dq_ref[...] = (d_query * 0.125).astype(BF)

    @pl.when(step == 0)
    def _():
        body(True, slice(0, tile))

    @pl.when(step == steps - 1)
    def _():
        body(True, slice(seq - tile, seq))

    @pl.when((step > 0) & (step < steps - 1))
    def _():
        body(False, None)

    @pl.when(step == steps - 1)
    def _():
        in_big = bigc_ref[...] > 0.0
        kb = jnp.where(in_big, k_ref[...].astype(F32), 0.0).astype(BF)
        tkb = jnp.where(in_big, tk_ref[...].astype(F32), 0.0).astype(BF)
        d_key = dk_acc[...].T
        d_key += dot(kb, grams[4]) + dot(kb, grams[5]) - dot(tkb, grams[6]) - dot(tkb, grams[7])
        dk_ref[...] = d_key.astype(BF)
        dv_ref[...] = dv_acc[...].T.astype(BF)

    @pl.when((pair == pl.num_programs(0) - 1) & (step == steps - 1))
    def _():
        job.last(src_ref, dst_ref, *sems)


def attention_back(numerators, qkv, teacher_qkv, d_context, context, inverse, docs, in_big, job, moved, collective_id):
    seq, width3 = qkv.shape
    width = width3 // 3
    pairs = width // 128
    tile = 256
    part = pl.BlockSpec((tile, 128), lambda p, i: (i, p))

    def whole(which):
        return pl.BlockSpec((seq, 128), lambda p, i: (0, which * pairs + p))

    any_space = pl.BlockSpec(memory_space=pl.ANY)
    return pl.pallas_call(
        functools.partial(backward_kernel, job, tile),
        grid=(pairs, seq // tile),
        in_specs=[
            pl.BlockSpec((2, tile, seq), lambda p, i: (p, i, 0)),
            whole(0),
            whole(1),
            whole(2),
            whole(0),
            whole(1),
            part,
            part,
            part,
            pl.BlockSpec((tile, 1), lambda p, i: (i, 0)),
            pl.BlockSpec((1, seq), lambda p, i: (0, 0)),
            pl.BlockSpec((seq, 1), lambda p, i: (0, 0)),
            any_space,
        ],
        out_specs=[part, whole(0), whole(0), any_space],
        out_shape=[
            jax.ShapeDtypeStruct((seq, width), BF),
            jax.ShapeDtypeStruct((seq, width), BF),
            jax.ShapeDtypeStruct((seq, width), BF),
            jax.ShapeDtypeStruct(moved.shape, moved.dtype),
        ],
        scratch_shapes=[
            pltpu.VMEM((2, seq, 128), BF),
            pltpu.VMEM((128, seq), F32),
            pltpu.VMEM((128, seq), F32),
            pltpu.VMEM((8, 128, 128), BF),
        ]
        + job.scratch(),
        compiler_params=pltpu.CompilerParams(
            collective_id=collective_id, has_side_effects=True, vmem_limit_bytes=VMEM_BYTES
        ),
        name="attention_back",
    )(
        numerators,
        qkv,
        qkv,
        qkv,
        teacher_qkv,
        teacher_qkv,
        d_context,
        context,
        inverse,
        docs.reshape(seq, 1),
        docs.reshape(1, seq),
        in_big.astype(F32).reshape(seq, 1),
        moved,
    )


def middle_kernel(
    x_ref,
    tx_ref,
    cot_ref,
    ctx_ref,
    tctx_ref,
    bo_ref,
    bup_ref,
    bdown_ref,
    to_ref,
    tup_ref,
    tdown_ref,
    sg_ref,
    sb_ref,
    sub_ref,
    tg_ref,
    tb_ref,
    tub_ref,
    out_ref,
    d1_ref,
    dctx_ref,
    gout_ref,
    gup_ref,
    gdown_ref,
    ggain_ref,
    gbias_ref,
    gub_ref,
):
    step = pl.program_id(0)
    groups = ctx_ref.shape[0]
    width = ctx_ref.shape[2]

    @pl.when(step == 0)
    def _():
        for ref in (gout_ref, gup_ref, gdown_ref, ggain_ref, gbias_ref, gub_ref):
            ref[...] = jnp.zeros_like(ref)

    def row(ref, i):
        return ref[i : i + 1, :]

    tctx = jnp.concatenate([tctx_ref[j] for j in range(groups)], axis=1)
    t_att = dot(tctx, to_ref[...]) + row(tb_ref, 2)
    t_hidden = layer_norm(tx_ref[...].astype(F32) + t_att, row(tg_ref, 0), row(tb_ref, 3))[0]
    t_inner = gelu_parts(dot(t_hidden.astype(BF), tup_ref[...]) + tub_ref[...])[0]
    t_out = layer_norm(
        t_hidden + dot(t_inner.astype(BF), tdown_ref[...]) + row(tb_ref, 4),
        row(tg_ref, 1),
        row(tb_ref, 5),
    )[0]

    context = jnp.concatenate([ctx_ref[j] for j in range(groups)], axis=1).astype(F32)
    bent = jnp.tanh(context * (1.0 / clip_level))
    ctx_active = (clip_level * bent).astype(BF)
    ctx_slope = 1.0 - bent * bent
    attended = dot(ctx_active, bo_ref[...]) + row(sb_ref, 2)
    hidden, normed_one, inverse_one = layer_norm(
        x_ref[...].astype(F32) + attended, row(sg_ref, 0), row(sb_ref, 3)
    )
    bent = jnp.tanh(hidden * (1.0 / clip_level))
    hidden_active = (clip_level * bent).astype(BF)
    hidden_slope = 1.0 - bent * bent
    inner_pre = dot(hidden_active, bup_ref[...]) + sub_ref[...]
    inner_act, phi = gelu_parts(inner_pre)
    bent = jnp.tanh(inner_act * (1.0 / clip_level))
    inner_active = (clip_level * bent).astype(BF)
    slope = (1.0 - bent * bent) * (
        phi + inner_pre * jnp.exp(-0.5 * inner_pre * inner_pre) * 0.3989422804014327
    )
    branch = dot(inner_active, bdown_ref[...]) + row(sb_ref, 4)
    output, normed_two, inverse_two = layer_norm(hidden + branch, row(sg_ref, 1), row(sb_ref, 5))
    out_ref[...] = output.astype(BF)
    upstream = cot_ref[...].astype(F32) + 0.5 * (output - t_out)
    d_two = norm_back(upstream, row(sg_ref, 1), normed_two, inverse_two)
    d_branch = d_two.astype(BF)
    gdown_ref[...] += dot(inner_active, d_branch, TN)
    d_inner = (dot(d_branch, bdown_ref[...], NT) * slope).astype(BF)
    gup_ref[...] += dot(hidden_active, d_inner, TN)
    d_hidden = d_two + dot(d_inner, bup_ref[...], NT) * hidden_slope
    d_one = norm_back(d_hidden, row(sg_ref, 0), normed_one, inverse_one)
    d1_ref[...] = d_one
    d_attended = d_one.astype(BF)
    gout_ref[...] += dot(ctx_active, d_attended, TN)
    d_context = (dot(d_attended, bo_ref[...], NT) * ctx_slope).astype(BF)
    for j in range(groups):
        dctx_ref[j] = d_context[:, j * width : (j + 1) * width]

    def total(value):
        return jnp.sum(value, axis=0, keepdims=True)

    ggain_ref[0:1, :] += total(d_hidden * normed_one)
    ggain_ref[1:2, :] += total(upstream * normed_two)
    gbias_ref[2:3, :] += total(d_attended.astype(F32))
    gbias_ref[3:4, :] += total(d_hidden)
    gbias_ref[4:5, :] += total(d_branch.astype(F32))
    gbias_ref[5:6, :] += total(upstream)
    gub_ref[...] += total(d_inner.astype(F32))


def middle(x, tx, cot, ctx, tctx, weights, teacher_weights, vectors):
    rows, depth = x.shape
    ff = weights[1].shape[1]
    tile = min(256, rows)
    groups, unused, width = ctx.shape
    tall = pl.BlockSpec((tile, depth), lambda i: (i, 0))
    split_rows = pl.BlockSpec((groups, tile, width), lambda i: (0, i, 0))

    def full(shape):
        return pl.BlockSpec(shape, lambda i: (0,) * len(shape))

    def full_of(array):
        return full(array.shape)

    out_full = [(depth, depth), (depth, ff), (ff, depth), (2, depth), (6, depth), (1, ff)]
    return pl.pallas_call(
        middle_kernel,
        grid=(rows // tile,),
        in_specs=[tall, tall, tall, split_rows, split_rows]
        + [full_of(a) for a in weights + teacher_weights + vectors],
        out_specs=[tall, tall, split_rows] + [full(s) for s in out_full],
        out_shape=[
            jax.ShapeDtypeStruct((rows, depth), BF),
            jax.ShapeDtypeStruct((rows, depth), F32),
            jax.ShapeDtypeStruct((groups, rows, width), BF),
        ]
        + [jax.ShapeDtypeStruct(s, F32) for s in out_full],
        compiler_params=pltpu.CompilerParams(vmem_limit_bytes=VMEM_BYTES),
        name="middle",
    )(x, tx, cot, ctx, tctx, *weights, *teacher_weights, *vectors)


def shards(
    tokens,
    teacher_tokens,
    segment_ids,
    cotangent,
    latent_qkv,
    latent_out,
    latent_up,
    latent_down,
    student_gain,
    student_bias,
    student_up_bias,
    teacher_qkv,
    teacher_out,
    teacher_up,
    teacher_down,
    teacher_gain,
    teacher_bias,
    teacher_up_bias,
):
    streams, shard_len, depth = tokens.shape
    blocks = lax.axis_size("blk")
    groups = blocks // streams
    seq = shard_len * blocks
    rows = seq // groups
    width = depth // groups
    s, r = place(groups)

    gather, swap, by_rows = Gather(streams, groups), Swap(streams, groups), Rows(groups)
    whole_shape = (blocks, shard_len, depth)

    docs_all = lax.all_gather(segment_ids, "blk", axis=0, tiled=False)
    docs = lax.dynamic_index_in_dim(docs_all, s, axis=1, keepdims=False)
    big = docs[1, 0]
    docs = docs.reshape(streams, groups, shard_len).transpose(1, 0, 2).reshape(seq)
    in_big = docs == big

    (token_blocks,) = move(
        gather, [tokens], [jax.ShapeDtypeStruct(whole_shape, BF)], 1, "gather_tokens"
    )
    stream_tokens = token_blocks.reshape(seq, depth)

    def own_columns(matrices):
        mine = lax.dynamic_slice_in_dim(matrices, r * width, width, axis=2)
        return mine.transpose(1, 0, 2).reshape(depth, 3 * width)

    def own_bias(bias):
        q_part = lax.dynamic_slice_in_dim(bias[0], r * width, width, axis=0)
        v_part = lax.dynamic_slice_in_dim(bias[1], r * width, width, axis=0)
        return jnp.concatenate([q_part, jnp.zeros_like(q_part), v_part])

    scale = jnp.concatenate([jnp.full((width,), 0.125, F32), jnp.ones((2 * width,), F32)])

    bin_own = binarize(own_columns(latent_qkv).astype(F32)).astype(BF)
    bin_out = binarize(latent_out.astype(F32)).astype(BF)
    bin_up = binarize(latent_up.astype(F32)).astype(BF)
    bin_down = binarize(latent_down.astype(F32)).astype(BF)

    full_qkv = lax.all_gather(teacher_qkv, "dp", axis=1, tiled=True)
    full_out = lax.all_gather(teacher_out, "dp", axis=0, tiled=True)
    full_up = lax.all_gather(teacher_up, "dp", axis=0, tiled=True)
    full_down = lax.all_gather(teacher_down, "dp", axis=0, tiled=True)

    active = squash(stream_tokens.astype(F32)).astype(BF)
    qkv = ((dot(active, bin_own) + own_bias(student_bias)).astype(BF).astype(F32) * scale).astype(
        BF
    )
    numerators, context, inverse, teacher_blocks = attention(
        qkv, docs, gather, teacher_tokens, whole_shape, True, 2, "attention_student"
    )
    teacher_stream = teacher_blocks.reshape(seq, depth)
    teacher_own = (
        (dot(teacher_stream, own_columns(full_qkv)) + own_bias(teacher_bias))
        .astype(BF)
        .astype(F32)
        * scale
    ).astype(BF)
    teacher_context, cot_blocks = attention(
        teacher_own, docs, swap, cotangent, cotangent.shape, False, 3, "attention_teacher"
    )
    row_shape = (groups, rows, width)
    ctx_rows, tctx_rows = move(
        by_rows,
        [context.reshape(row_shape), teacher_context.reshape(row_shape)],
        [jax.ShapeDtypeStruct(row_shape, BF)] * 2,
        4,
        "context_rows",
    )
    own_rows = lax.dynamic_slice_in_dim(stream_tokens, r * rows, rows, axis=0)
    own_teacher = lax.dynamic_slice_in_dim(teacher_stream, r * rows, rows, axis=0)
    output, d_one, d_context, g_out, g_up, g_down, g_gain, g_bias, g_ub = middle(
        own_rows,
        own_teacher,
        cot_blocks.reshape(rows, depth),
        ctx_rows,
        tctx_rows,
        [bin_out, bin_up, bin_down],
        [full_out, full_up, full_down],
        [
            student_gain,
            student_bias,
            student_up_bias.reshape(1, -1),
            teacher_gain,
            teacher_bias,
            teacher_up_bias.reshape(1, -1),
        ],
    )
    early = lax.psum(
        (g_out.astype(BF), g_up.astype(BF), g_down.astype(BF)), ("dp", "blk")
    )
    (d_ctx_rows,) = move(
        by_rows, [d_context], [jax.ShapeDtypeStruct(row_shape, BF)], 5, "d_context_rows"
    )
    d_queries, d_keys, d_values, output_blocks = attention_back(
        numerators,
        qkv,
        teacher_own,
        d_ctx_rows.reshape(seq, width),
        context,
        inverse,
        docs,
        in_big,
        swap,
        output.reshape(streams, shard_len, depth),
        6,
    )
    d_qkv = jnp.concatenate([d_queries, d_keys, d_values], axis=1)
    g_own = dot(active, d_qkv, TN)
    d_active = dot(d_qkv, bin_own, NT).astype(BF)
    (d_active_parts,) = move(
        by_rows,
        [d_active.reshape(groups, rows, depth)],
        [jax.ShapeDtypeStruct((groups, rows, depth), BF)],
        7,
        "d_active_rows",
    )
    bent = jnp.tanh(own_rows.astype(F32) * (1.0 / clip_level))
    grad_rows = d_one + jnp.sum(d_active_parts.astype(F32), axis=0) * (1.0 - bent * bent)
    (grad_tokens,) = move(
        swap,
        [grad_rows.astype(BF).reshape(streams, shard_len, depth)],
        [jax.ShapeDtypeStruct((streams, shard_len, depth), BF)],
        8,
        "grad_tokens_back",
    )
    zero_at = jnp.zeros((3, depth, depth), BF)
    g_qkv = lax.dynamic_update_slice_in_dim(
        zero_at, g_own.reshape(depth, 3, width).transpose(1, 0, 2).astype(BF), r * width, axis=2
    )

    def columns_back(vector):
        return lax.dynamic_update_slice_in_dim(jnp.zeros((depth,), F32), vector, r * width, axis=0)

    g_bias = g_bias.at[0].set(columns_back(jnp.sum(d_queries.astype(F32), axis=0)))
    g_bias = g_bias.at[1].set(columns_back(jnp.sum(d_values.astype(F32), axis=0)))
    late, small = lax.psum(g_qkv, ("dp", "blk")), lax.psum((g_gain, g_bias, g_ub), ("dp", "blk"))
    return (
        output_blocks,
        grad_tokens,
        latent_grad(latent_qkv, late.astype(F32)),
        latent_grad(latent_out, early[0].astype(F32)),
        latent_grad(latent_up, early[1].astype(F32)),
        latent_grad(latent_down, early[2].astype(F32)),
        small[0],
        small[1],
        small[2].reshape(-1),
    )


def solution(mesh):
    return jax.shard_map(
        shards,
        mesh=mesh,
        in_specs=(
            P("dp", "blk", None),
            P("dp", "blk", None),
            P("dp", "blk"),
            P("dp", "blk", None),
            P(),
            P(),
            P(),
            P(),
            P(),
            P(),
            P(),
            P(None, "dp", None),
            P("dp", None),
            P("dp", None),
            P("dp", None),
            P(),
            P(),
            P(),
        ),
        out_specs=(P("dp", "blk", None), P("dp", "blk", None), P(), P(), P(), P(), P(), P(), P()),
        check_vma=False,
    )
```

```python
import functools

import jax
import jax.numpy as jnp
from jax import lax
from jax.experimental import pallas as pl
from jax.experimental.pallas import tpu as pltpu
from jax.sharding import PartitionSpec as P

HEADS = 8
BF = jnp.bfloat16
F32 = jnp.float32
LOG2E = 1.4426950408889634
clip_level = 2.5
masked_score = -1e30
VMEM_BYTES = 56 << 20
MESH = pl.DeviceIdType.MESH
NT = (((1,), (1,)), ((), ()))
TN = (((0,), (0,)), ((), ()))


def squash(tensor):
    return clip_level * jnp.tanh(tensor * (1.0 / clip_level))


def gelu_parts(tensor):
    phi = 0.5 * (1.0 + lax.erf(tensor * 0.7071067811865476))
    return tensor * phi, phi


def binarize(matrix):
    column_scale = jnp.sqrt(jnp.mean(matrix * matrix, axis=-2, keepdims=True) + 1e-06)
    return column_scale * jnp.tanh(2.0 * matrix / column_scale)


def layer_norm(tensor, gain_row, shift_row):
    centre = tensor - jnp.mean(tensor, axis=-1, keepdims=True)
    inverse_std = lax.rsqrt(jnp.mean(centre * centre, axis=-1, keepdims=True) + 1e-05)
    normed = centre * inverse_std
    return (normed * gain_row + shift_row, normed, inverse_std)


def norm_back(upstream, gain_row, normed, inverse_std):
    scaled = upstream * gain_row
    return inverse_std * (
        scaled
        - jnp.mean(scaled, axis=-1, keepdims=True)
        - normed * jnp.mean(scaled * normed, axis=-1, keepdims=True)
    )


def dot(a, b, dims=(((1,), (0,)), ((), ()))):
    return lax.dot_general(a, b, dims, preferred_element_type=F32)


def latent_grad(latent, binary_grad):
    matrix = latent.astype(F32)
    unused, pullback = jax.vjp(binarize, matrix)
    return pullback(binary_grad)[0]


def place(groups):
    here = lax.axis_index("blk")
    return here // groups, lax.rem(here, groups)


def greet(peers):
    barrier = pltpu.get_barrier_semaphore()
    for peer in peers:
        pl.semaphore_signal(barrier, inc=1, device_id=peer, device_id_type=MESH)
    pl.semaphore_wait(barrier, len(peers))


def stream_peers(streams, groups):
    s, r = place(groups)
    return [{"blk": lax.rem(s + d, streams) * groups + r} for d in range(1, streams)]


def core_peers(groups):
    s, r = place(groups)
    return [{"blk": s * groups + lax.rem(r + j, groups)} for j in range(1, groups)]


def dp_peers():
    size = lax.axis_size("dp")
    here = lax.axis_index("dp")
    return [{"dp": lax.rem(here + d, size)} for d in range(1, size)]


def unique(jobs):
    peers, kinds = [], []
    for job in jobs:
        for kind, found in job.peers():
            if kind not in kinds:
                kinds.append(kind)
                peers += found
    return peers


def remote(source, target, send, recv, peer):
    return pltpu.make_async_remote_copy(
        src_ref=source,
        dst_ref=target,
        send_sem=send,
        recv_sem=recv,
        device_id=peer,
        device_id_type=MESH,
    )


def dma(count):
    return pltpu.SemaphoreType.DMA((count,))


class Staged:
    def __init__(self, source, target, stage, sems):
        self.load = pltpu.make_async_copy(source, stage, sems.at[0])
        self.store = pltpu.make_async_copy(stage, target, sems.at[1])

    def first(self):
        self.load.start()

    def last(self):
        self.load.wait()
        self.store.start()
        self.store.wait()


class Gather:
    def __init__(self, streams, groups, block, dtype):
        self.streams, self.groups, self.block, self.dtype = streams, groups, block, dtype

    def scratch(self):
        b, g = self.streams, self.groups
        return [dma(b), dma(b), dma(b * g), dma(b * g), pltpu.VMEM(self.block, self.dtype), dma(2)]

    def out_shape(self):
        return jax.ShapeDtypeStruct((self.streams * self.groups,) + self.block, self.dtype)

    def peers(self):
        return [
            ("stream", stream_peers(self.streams, self.groups)),
            ("core", core_peers(self.groups)),
        ]

    def parts(self, source, target, send, recv, share_send, share_recv, stage, sems):
        b, g = self.streams, self.groups
        s, r = place(g)
        peers, cores = stream_peers(b, g), core_peers(g)
        swaps = [
            remote(
                source.at[lax.rem(s + d, b)],
                target.at[r * b + s],
                send.at[d],
                recv.at[d],
                peers[d - 1],
            )
            for d in range(1, b)
        ]
        shares = [
            [
                remote(
                    source.at[s] if d == 0 else target.at[r * b + lax.rem(s + b - d, b)],
                    target.at[r * b + lax.rem(s + b - d, b)],
                    share_send.at[j * b + d],
                    share_recv.at[j * b + d],
                    cores[j - 1],
                )
                for j in range(1, g)
            ]
            for d in range(b)
        ]
        own = Staged(source.at[s], target.at[r * b + s], stage, sems)
        return swaps, shares, own

    def first(self, *refs):
        swaps, shares, own = self.parts(*refs)
        for copy in swaps:
            copy.start()
        own.first()
        for copy in shares[0]:
            copy.start()

    def last(self, *refs):
        swaps, shares, own = self.parts(*refs)
        own.last()
        for d in [1, 3, 2] if self.streams == 4 else range(1, self.streams):
            swaps[d - 1].wait_recv()
            for copy in shares[d]:
                copy.start()
        for row in shares:
            for copy in row:
                copy.wait()
        for copy in swaps:
            copy.wait_send()


class Swap:
    def __init__(self, streams, groups, block, dtype):
        self.streams, self.groups, self.block, self.dtype = streams, groups, block, dtype

    def scratch(self):
        return [dma(self.streams), dma(self.streams), pltpu.VMEM(self.block, self.dtype), dma(2)]

    def out_shape(self):
        return jax.ShapeDtypeStruct((self.streams,) + self.block, self.dtype)

    def peers(self):
        return [("stream", stream_peers(self.streams, self.groups))]

    def parts(self, source, target, send, recv, stage, sems):
        b, g = self.streams, self.groups
        s, r = place(g)
        peers = stream_peers(b, g)
        swaps = [
            remote(source.at[lax.rem(s + d, b)], target.at[s], send.at[d], recv.at[d], peers[d - 1])
            for d in range(1, b)
        ]
        return swaps, Staged(source.at[s], target.at[s], stage, sems)

    def first(self, *refs):
        swaps, own = self.parts(*refs)
        for copy in swaps:
            copy.start()
        own.first()

    def last(self, *refs):
        swaps, own = self.parts(*refs)
        own.last()
        for copy in swaps:
            copy.wait()


class Rows:
    def __init__(self, streams, groups, block, dtype):
        self.groups, self.block, self.dtype = groups, block, dtype

    def scratch(self):
        return [dma(self.groups), dma(self.groups), pltpu.VMEM(self.block, self.dtype), dma(2)]

    def out_shape(self):
        return jax.ShapeDtypeStruct((self.groups,) + self.block, self.dtype)

    def peers(self):
        return [("core", core_peers(self.groups))]

    def parts(self, source, target, send, recv, stage, sems):
        g = self.groups
        s, r = place(g)
        cores = core_peers(g)
        copies = [
            remote(source.at[lax.rem(r + j, g)], target.at[r], send.at[j], recv.at[j], cores[j - 1])
            for j in range(1, g)
        ]
        return copies, Staged(source.at[r], target.at[r], stage, sems)

    first = Swap.first
    last = Swap.last


class Spread:
    def __init__(self, block, dtype):
        self.block, self.dtype = block, dtype

    def scratch(self):
        size = lax.axis_size("dp")
        return [dma(size), dma(size), pltpu.VMEM(self.block, self.dtype), dma(2)]

    def out_shape(self):
        return jax.ShapeDtypeStruct((lax.axis_size("dp"),) + self.block, self.dtype)

    def peers(self):
        return [("dp", dp_peers())]

    def parts(self, source, target, send, recv, stage, sems):
        here = lax.axis_index("dp")
        copies = [
            remote(source, target.at[here], send.at[d], recv.at[d], peer)
            for d, peer in enumerate(dp_peers(), 1)
        ]
        return copies, Staged(source, target.at[here], stage, sems)

    first = Swap.first
    last = Swap.last


class Moves:
    def __init__(self, *jobs):
        self.jobs = jobs
        self.counts = [len(job.scratch()) for job in jobs]

    def scratch(self):
        return [item for job in self.jobs for item in job.scratch()]

    def out_shapes(self):
        return [job.out_shape() for job in self.jobs]

    def spaces(self):
        return [pl.BlockSpec(memory_space=pl.ANY)] * len(self.jobs)

    def each(self, sources, targets, scratch):
        at = 0
        for job, count, source, target in zip(self.jobs, self.counts, sources, targets):
            yield job, (source, target, *scratch[at : at + count])
            at += count

    def first(self, sources, targets, scratch):
        greet(unique(self.jobs))
        for job, refs in self.each(sources, targets, scratch):
            job.first(*refs)

    def last(self, sources, targets, scratch):
        for job, refs in self.each(sources, targets, scratch):
            job.last(*refs)


def remote_params(collective_id):
    return pltpu.CompilerParams(
        collective_id=collective_id, has_side_effects=True, vmem_limit_bytes=VMEM_BYTES
    )


def move(moves, arrays, collective_id, name):
    count = len(arrays)

    def kernel(*refs):
        sources, targets, scratch = refs[:count], refs[count : 2 * count], refs[2 * count :]
        moves.first(sources, targets, scratch)
        moves.last(sources, targets, scratch)

    return pl.pallas_call(
        kernel,
        out_shape=moves.out_shapes(),
        in_specs=moves.spaces(),
        out_specs=moves.spaces(),
        scratch_shapes=moves.scratch(),
        compiler_params=remote_params(collective_id),
        name=name,
    )(*arrays)


def binary_columns(latent):
    matrix = latent.astype(F32)
    scale = jnp.sqrt(jnp.mean(matrix * matrix, axis=0, keepdims=True) + 1e-06)
    return (scale * jnp.tanh(matrix * (2.0 / scale))).astype(BF)


def intake_kernel(moves, qkv_ref, out_ref, up_ref, down_ref, *refs):
    count = len(moves.jobs)
    sources = refs[:count]
    own_bin, out_bin, up_bin, down_bin = refs[count : count + 4]
    targets = refs[count + 4 : 2 * count + 4]
    scratch = refs[2 * count + 4 :]
    moves.first(sources, targets, scratch)
    for i in range(3):
        own_bin[i] = binary_columns(qkv_ref[i])
    out_bin[...] = binary_columns(out_ref[...])
    for i in range(0, up_ref.shape[1], 512):
        up_bin[:, i : i + 512] = binary_columns(up_ref[:, i : i + 512])
    for i in range(0, down_ref.shape[1], 128):
        down_bin[:, i : i + 128] = binary_columns(down_ref[:, i : i + 128])
    moves.last(sources, targets, scratch)


def intake(moves, latents, arrays, collective_id):
    vmem = pl.BlockSpec(memory_space=pltpu.VMEM)
    return pl.pallas_call(
        functools.partial(intake_kernel, moves),
        out_shape=[jax.ShapeDtypeStruct(a.shape, BF) for a in latents] + moves.out_shapes(),
        in_specs=[vmem] * 4 + moves.spaces(),
        out_specs=[vmem] * 4 + moves.spaces(),
        scratch_shapes=moves.scratch(),
        compiler_params=remote_params(collective_id),
        name="intake",
    )(*latents, *arrays)


def lanes_of(shape):
    return lax.broadcasted_iota(jnp.int32, shape, 1)


def forward_kernel(moves, keep, tile, edge, q_ref, k_ref, v_ref, col_ref, row_ref, *rest):
    count = len(moves.jobs)
    sources, rest = rest[:count], rest[count:]
    if keep:
        e_ref, ctx_ref, inv_ref, *rest = rest
    else:
        ctx_ref, *rest = rest
    targets, (k_aug, v_aug, *scratch) = rest[:count], rest[count:]
    pair, step = pl.program_id(0), pl.program_id(1)
    steps = pl.num_programs(1)
    seq = k_ref.shape[0]

    @pl.when((pair == 0) & (step == 0))
    def _():
        moves.first(sources, targets, scratch)

    @pl.when(step == 0)
    def _():
        low = lanes_of((seq, 128)) < 64
        lane = lanes_of((seq, 128))
        keys = k_ref[...].astype(F32)
        turned = pltpu.roll(keys, 64, 1)
        k_aug[0] = jnp.where(low, keys, turned).astype(BF)
        k_aug[1] = jnp.where(low, turned, keys).astype(BF)
        values = v_ref[...].astype(F32)
        v_aug[0] = jnp.where(low, values, jnp.where(lane < 66, 1.0, 0.0)).astype(BF)
        v_aug[1] = jnp.where(low, jnp.where(lane < 2, 1.0, 0.0), values).astype(BF)

    def body(whole):
        low = lanes_of((tile, 128)) < 64
        scaled = q_ref[...].astype(F32) * LOG2E
        upper = scaled.astype(BF).astype(F32)
        rest_part = scaled - upper
        results = []
        for h in range(2):
            if h == 0:
                q_aug = jnp.where(low, upper, pltpu.roll(rest_part, 64, 1)).astype(BF)
            else:
                q_aug = jnp.where(low, pltpu.roll(upper, 64, 1), rest_part).astype(BF)
            scores = dot(q_aug, k_aug[h], NT)
            if whole:
                scores = jnp.where(col_ref[...] == row_ref[...], scores, masked_score)
            else:
                left = jnp.where(
                    col_ref[...] == row_ref[:, :edge], scores[:, :edge], masked_score
                )
                right = jnp.where(
                    col_ref[...] == row_ref[:, seq - edge :], scores[:, seq - edge :], masked_score
                )
                scores = jnp.concatenate([left, scores[:, edge : seq - edge], right], axis=1)
            peak = jnp.max(scores, axis=1, keepdims=True)
            numerators = jnp.exp2(scores - peak).astype(BF)
            if keep:
                e_ref[h] = numerators
            total = dot(numerators, v_aug[h])
            where_sum = 64 if h == 0 else 0
            inverse = 1.0 / total[:, where_sum : where_sum + 1]
            results.append((total * inverse, inverse))
        ctx_ref[...] = jnp.where(low, results[0][0], results[1][0]).astype(BF)
        if keep:
            inv_ref[...] = jnp.where(low, results[0][1], results[1][1])

    at_edge = (step == 0) | (step == steps - 1)

    @pl.when(at_edge)
    def _():
        body(True)

    @pl.when(jnp.logical_not(at_edge))
    def _():
        body(False)

    @pl.when((pair == pl.num_programs(0) - 1) & (step == steps - 1))
    def _():
        moves.last(sources, targets, scratch)


def attention(qkv, docs, moves, moved, keep, collective_id, name):
    seq, width3 = qkv.shape
    width = width3 // 3
    pairs = width // 128
    tile = 256
    edge = 256
    col = docs.reshape(seq, 1)
    row = docs.reshape(1, seq)
    blocks = [
        pl.BlockSpec((tile, 128), lambda p, i: (i, p)),
        pl.BlockSpec((seq, 128), lambda p, i: (0, pairs + p)),
        pl.BlockSpec((seq, 128), lambda p, i: (0, 2 * pairs + p)),
        pl.BlockSpec((tile, 1), lambda p, i: (i, 0)),
        pl.BlockSpec((1, seq), lambda p, i: (0, 0)),
    ] + moves.spaces()
    outs = [pl.BlockSpec((tile, 128), lambda p, i: (i, p))]
    shapes = [jax.ShapeDtypeStruct((seq, width), BF)]
    if keep:
        outs = [pl.BlockSpec((2, tile, seq), lambda p, i: (p, i, 0))] + outs
        shapes = [jax.ShapeDtypeStruct((2 * pairs, seq, seq), BF)] + shapes
        outs = outs + [pl.BlockSpec((tile, 128), lambda p, i: (i, p))]
        shapes = shapes + [jax.ShapeDtypeStruct((seq, width), F32)]
    return pl.pallas_call(
        functools.partial(forward_kernel, moves, keep, tile, edge),
        grid=(pairs, seq // tile),
        in_specs=blocks,
        out_specs=outs + moves.spaces(),
        out_shape=shapes + moves.out_shapes(),
        scratch_shapes=[pltpu.VMEM((2, seq, 128), BF), pltpu.VMEM((2, seq, 128), BF)]
        + moves.scratch(),
        compiler_params=remote_params(collective_id),
        name=name,
    )(qkv, qkv, qkv, col, row, *moved)


def split(matrix):
    upper = matrix.astype(BF)
    return upper, (matrix - upper.astype(F32)).astype(BF)


def backward_kernel(
    moves,
    tile,
    e_ref,
    q_ref,
    k_ref,
    v_ref,
    tq_ref,
    tk_ref,
    dc_ref,
    ctx_ref,
    inv_ref,
    col_ref,
    row_ref,
    bigc_ref,
    *rest,
):
    count = len(moves.jobs)
    sources, (dq_ref, dk_ref, dv_ref, *rest) = rest[:count], rest[count:]
    targets, (v_aug, dk_acc, dv_acc, grams, *scratch) = rest[:count], rest[count:]
    pair, step = pl.program_id(0), pl.program_id(1)
    steps = pl.num_programs(1)
    seq = k_ref.shape[0]
    share = 1.0 / seq

    @pl.when((pair == 0) & (step == 0))
    def _():
        moves.first(sources, targets, scratch)

    @pl.when(step == 0)
    def _():
        lane = lanes_of((seq, 128))
        low = lane < 64
        values = v_ref[...].astype(F32)
        v_aug[0] = jnp.where(low, values, jnp.where(lane < 66, 1.0, 0.0)).astype(BF)
        v_aug[1] = jnp.where(low, jnp.where(lane < 2, 1.0, 0.0), values).astype(BF)
        dk_acc[...] = jnp.zeros_like(dk_acc)
        dv_acc[...] = jnp.zeros_like(dv_acc)
        in_big = bigc_ref[...] > 0.0
        kb = jnp.where(in_big, k_ref[...].astype(F32), 0.0).astype(BF)
        tkb = jnp.where(in_big, tk_ref[...].astype(F32), 0.0).astype(BF)
        qb = jnp.where(in_big, q_ref[...].astype(F32), 0.0).astype(BF)
        tqb = jnp.where(in_big, tq_ref[...].astype(F32), 0.0).astype(BF)
        same_head = (lax.broadcasted_iota(jnp.int32, (128, 128), 0) < 64) == (
            lanes_of((128, 128)) < 64
        )
        for i, (a, b) in enumerate(((kb, kb), (tkb, kb), (qb, qb), (tqb, qb))):
            gram = jnp.where(same_head, dot(a, b, TN) * share, 0.0)
            grams[2 * i], grams[2 * i + 1] = split(gram)

    start = pl.multiple_of(step * tile, tile)
    rows = pl.ds(start, tile)
    lane = lanes_of((tile, 128))
    low = lane < 64

    def body(whole, columns):
        in_big = bigc_ref[rows, :] > 0.0
        q8 = q_ref[rows, :]
        tq8 = tq_ref[rows, :]
        dc = dc_ref[...].astype(F32)
        inv = inv_ref[...]
        scaled = dc * inv
        product = scaled * ctx_ref[...].astype(F32)
        scaled_low = scaled.astype(BF)
        q_turned = q8.astype(F32).T.astype(BF)
        dc_turned = scaled_low.astype(F32).T.astype(BF)
        d_queries = []
        for h in range(2):
            mine = low if h == 0 else jnp.logical_not(low)
            delta = -jnp.sum(jnp.where(mine, product, 0.0), axis=1, keepdims=True)
            upper = delta.astype(BF).astype(F32)
            first = 64 if h == 0 else 0
            extra = jnp.where(
                lane == first, upper, jnp.where(lane == first + 1, delta - upper, 0.0)
            )
            dc_aug = jnp.where(mine, scaled, extra).astype(BF)
            numerators = e_ref[h]
            d_probs = dot(dc_aug, v_aug[h], NT)
            d_scores = numerators.astype(F32) * d_probs
            if whole:
                q_mine = jnp.where(mine, q8, 0.0).astype(BF)
                tq_mine = jnp.where(mine, tq8, 0.0).astype(BF)
                gap = dot(q_mine, k_ref[columns, :], NT) - dot(tq_mine, tk_ref[columns, :], NT)
                small = (col_ref[...] == row_ref[:, columns]) & jnp.logical_not(in_big)
                gap = jnp.where(small, gap * share, 0.0)
                if columns.start == 0:
                    d_scores = jnp.concatenate(
                        [d_scores[:, :tile] + gap, d_scores[:, tile:]], axis=1
                    )
                else:
                    d_scores = jnp.concatenate(
                        [d_scores[:, : seq - tile], d_scores[:, seq - tile :] + gap], axis=1
                    )
            d_scores = d_scores.astype(BF)
            d_queries.append(dot(d_scores, k_ref[...]))
            half = slice(64 * h, 64 * h + 64)
            dk_acc[half, :] += dot(q_turned[half, :], d_scores)
            dv_acc[half, :] += dot(dc_turned[half, :], numerators)
        d_query = jnp.where(low, d_queries[0], d_queries[1])
        qb = jnp.where(in_big, q8.astype(F32), 0.0).astype(BF)
        tqb = jnp.where(in_big, tq8.astype(F32), 0.0).astype(BF)
        d_query += dot(qb, grams[0]) + dot(qb, grams[1]) - dot(tqb, grams[2]) - dot(tqb, grams[3])
        dq_ref[...] = (d_query * 0.125).astype(BF)

    @pl.when(step == 0)
    def _():
        body(True, slice(0, tile))

    @pl.when(step == steps - 1)
    def _():
        body(True, slice(seq - tile, seq))

    @pl.when((step > 0) & (step < steps - 1))
    def _():
        body(False, None)

    @pl.when(step == steps - 1)
    def _():
        in_big = bigc_ref[...] > 0.0
        kb = jnp.where(in_big, k_ref[...].astype(F32), 0.0).astype(BF)
        tkb = jnp.where(in_big, tk_ref[...].astype(F32), 0.0).astype(BF)
        d_key = dk_acc[...].T
        d_key += dot(kb, grams[4]) + dot(kb, grams[5]) - dot(tkb, grams[6]) - dot(tkb, grams[7])
        dk_ref[...] = d_key.astype(BF)
        dv_ref[...] = dv_acc[...].T.astype(BF)

    @pl.when((pair == pl.num_programs(0) - 1) & (step == steps - 1))
    def _():
        moves.last(sources, targets, scratch)


def attention_back(
    numerators, qkv, teacher_qkv, d_context, context, inverse, docs, in_big, moves, moved, collective_id
):
    seq, width3 = qkv.shape
    width = width3 // 3
    pairs = width // 128
    tile = 256
    part = pl.BlockSpec((tile, 128), lambda p, i: (i, p))

    def whole(which):
        return pl.BlockSpec((seq, 128), lambda p, i: (0, which * pairs + p))

    return pl.pallas_call(
        functools.partial(backward_kernel, moves, tile),
        grid=(pairs, seq // tile),
        in_specs=[
            pl.BlockSpec((2, tile, seq), lambda p, i: (p, i, 0)),
            whole(0),
            whole(1),
            whole(2),
            whole(0),
            whole(1),
            part,
            part,
            part,
            pl.BlockSpec((tile, 1), lambda p, i: (i, 0)),
            pl.BlockSpec((1, seq), lambda p, i: (0, 0)),
            pl.BlockSpec((seq, 1), lambda p, i: (0, 0)),
        ]
        + moves.spaces(),
        out_specs=[part, whole(0), whole(0)] + moves.spaces(),
        out_shape=[
            jax.ShapeDtypeStruct((seq, width), BF),
            jax.ShapeDtypeStruct((seq, width), BF),
            jax.ShapeDtypeStruct((seq, width), BF),
        ]
        + moves.out_shapes(),
        scratch_shapes=[
            pltpu.VMEM((2, seq, 128), BF),
            pltpu.VMEM((128, seq), F32),
            pltpu.VMEM((128, seq), F32),
            pltpu.VMEM((8, 128, 128), BF),
        ]
        + moves.scratch(),
        compiler_params=remote_params(collective_id),
        name="attention_back",
    )(
        numerators,
        qkv,
        qkv,
        qkv,
        teacher_qkv,
        teacher_qkv,
        d_context,
        context,
        inverse,
        docs.reshape(seq, 1),
        docs.reshape(1, seq),
        in_big.astype(F32).reshape(seq, 1),
        *moved,
    )


def middle_kernel(
    unused_place,
    x_ref,
    tx_ref,
    cot_ref,
    ctx_ref,
    tctx_ref,
    bo_ref,
    bup_ref,
    bdown_ref,
    to_ref,
    tup_ref,
    tdown_ref,
    sg_ref,
    sb_ref,
    sub_ref,
    tg_ref,
    tb_ref,
    tub_ref,
    out_ref,
    d1_ref,
    dctx_ref,
    gout_ref,
    gup_ref,
    gdown_ref,
    ggain_ref,
    gbias_ref,
    gub_ref,
):
    step = pl.program_id(0)
    groups = ctx_ref.shape[0]
    width = ctx_ref.shape[2]

    @pl.when(step == 0)
    def _():
        for ref in (gout_ref, gup_ref, gdown_ref, ggain_ref, gbias_ref, gub_ref):
            ref[...] = jnp.zeros_like(ref)

    def row(ref, i):
        return ref[i : i + 1, :]

    tctx = jnp.concatenate([tctx_ref[j] for j in range(groups)], axis=1)
    t_att = dot(tctx, to_ref[...]) + row(tb_ref, 2)
    t_hidden = layer_norm(tx_ref[...].astype(F32) + t_att, row(tg_ref, 0), row(tb_ref, 3))[0]
    t_inner = gelu_parts(dot(t_hidden.astype(BF), tup_ref[...]) + tub_ref[...])[0]
    t_out = layer_norm(
        t_hidden + dot(t_inner.astype(BF), tdown_ref[...]) + row(tb_ref, 4),
        row(tg_ref, 1),
        row(tb_ref, 5),
    )[0]

    context = jnp.concatenate([ctx_ref[j] for j in range(groups)], axis=1).astype(F32)
    bent = jnp.tanh(context * (1.0 / clip_level))
    ctx_active = (clip_level * bent).astype(BF)
    ctx_slope = 1.0 - bent * bent
    attended = dot(ctx_active, bo_ref[...]) + row(sb_ref, 2)
    hidden, normed_one, inverse_one = layer_norm(
        x_ref[...].astype(F32) + attended, row(sg_ref, 0), row(sb_ref, 3)
    )
    bent = jnp.tanh(hidden * (1.0 / clip_level))
    hidden_active = (clip_level * bent).astype(BF)
    hidden_slope = 1.0 - bent * bent
    inner_pre = dot(hidden_active, bup_ref[...]) + sub_ref[...]
    inner_act, phi = gelu_parts(inner_pre)
    bent = jnp.tanh(inner_act * (1.0 / clip_level))
    inner_active = (clip_level * bent).astype(BF)
    slope = (1.0 - bent * bent) * (
        phi + inner_pre * jnp.exp(-0.5 * inner_pre * inner_pre) * 0.3989422804014327
    )
    branch = dot(inner_active, bdown_ref[...]) + row(sb_ref, 4)
    output, normed_two, inverse_two = layer_norm(hidden + branch, row(sg_ref, 1), row(sb_ref, 5))
    out_ref[...] = output.astype(BF)
    upstream = cot_ref[...].astype(F32) + 0.5 * (output - t_out)
    d_two = norm_back(upstream, row(sg_ref, 1), normed_two, inverse_two)
    d_branch = d_two.astype(BF)
    gdown_ref[...] += dot(inner_active, d_branch, TN)
    d_inner = (dot(d_branch, bdown_ref[...], NT) * slope).astype(BF)
    gup_ref[...] += dot(hidden_active, d_inner, TN)
    d_hidden = d_two + dot(d_inner, bup_ref[...], NT) * hidden_slope
    d_one = norm_back(d_hidden, row(sg_ref, 0), normed_one, inverse_one)
    d1_ref[...] = d_one
    d_attended = d_one.astype(BF)
    gout_ref[...] += dot(ctx_active, d_attended, TN)
    d_context = (dot(d_attended, bo_ref[...], NT) * ctx_slope).astype(BF)
    for j in range(groups):
        dctx_ref[j] = d_context[:, j * width : (j + 1) * width]

    def total(value):
        return jnp.sum(value, axis=0, keepdims=True)

    ggain_ref[0:1, :] += total(d_hidden * normed_one)
    ggain_ref[1:2, :] += total(upstream * normed_two)
    gbias_ref[2:3, :] += total(d_attended.astype(F32))
    gbias_ref[3:4, :] += total(d_hidden)
    gbias_ref[4:5, :] += total(d_branch.astype(F32))
    gbias_ref[5:6, :] += total(upstream)
    gub_ref[...] += total(d_inner.astype(F32))


def middle(r, x, tx, cot, ctx, tctx, weights, teacher_weights, vectors):
    rows, depth = cot.shape
    ff = weights[1].shape[1]
    tile = min(256, rows)
    groups, unused, width = ctx.shape
    steps = rows // tile
    tall = pl.BlockSpec((tile, depth), lambda i, r: (i, 0))
    of_stream = pl.BlockSpec((tile, depth), lambda i, r: (r[0] * steps + i, 0))
    split_rows = pl.BlockSpec((groups, tile, width), lambda i, r: (0, i, 0))

    def full(shape):
        return pl.BlockSpec(shape, lambda i, r: (0,) * len(shape))

    def full_of(array):
        return full(array.shape)

    out_full = [(depth, depth), (depth, ff), (ff, depth), (2, depth), (6, depth), (1, ff)]
    return pl.pallas_call(
        middle_kernel,
        grid_spec=pltpu.PrefetchScalarGridSpec(
            num_scalar_prefetch=1,
            grid=(steps,),
            in_specs=[of_stream, of_stream, tall, split_rows, split_rows]
            + [full_of(a) for a in weights + teacher_weights + vectors],
            out_specs=[tall, tall, split_rows] + [full(s) for s in out_full],
        ),
        out_shape=[
            jax.ShapeDtypeStruct((rows, depth), BF),
            jax.ShapeDtypeStruct((rows, depth), F32),
            jax.ShapeDtypeStruct((groups, rows, width), BF),
        ]
        + [jax.ShapeDtypeStruct(s, F32) for s in out_full],
        compiler_params=pltpu.CompilerParams(vmem_limit_bytes=VMEM_BYTES),
        name="middle",
    )(r.reshape(1), x, tx, cot, ctx, tctx, *weights, *teacher_weights, *vectors)


def finish_kernel(
    streams,
    groups,
    wire,
    dq_ref,
    dk_ref,
    dv_ref,
    active_ref,
    bin_ref,
    d1_ref,
    tokens_ref,
    small_ref,
    grad_ref,
    late_ref,
    sum_ref,
    mine,
    outbox,
    inbox,
    x_rows,
    blocks,
    partial,
    partial_wire,
    dp_box,
    chunk_wire,
    z_box,
    piece,
    small_send,
    small_dp,
    small_z,
    small_core,
    x_sem,
    core_send,
    core_recv,
    back_send,
    back_recv,
    dp_send,
    dp_recv,
    z_send,
    z_recv,
    zg_send,
    zg_recv,
    dpg_send,
    dpg_recv,
    cg_send,
    cg_recv,
    ss,
    sr,
    local_sems,
):
    size = lax.axis_size("dp")
    here = lax.axis_index("dp")
    s, r = place(groups)
    rows, depth = mine.shape
    width = dq_ref.shape[1]
    parts = (dq_ref, dk_ref, dv_ref)
    along_z, cores, along_dp = stream_peers(streams, groups), core_peers(groups), dp_peers()
    greet(along_z + cores + along_dp)
    load = pltpu.make_async_copy(tokens_ref.at[pl.ds(r * streams, streams)], x_rows, x_sem)
    load.start()

    def d_active(start):
        total = None
        for i, ref in enumerate(parts):
            term = dot(ref[pl.ds(start, rows), :], bin_ref[i], NT)
            total = term if total is None else total + term
        return total

    core_copies = []
    for j in range(1, groups):
        other = lax.rem(r + j, groups)
        outbox[j - 1] = d_active(pl.multiple_of(other * rows, rows)).astype(BF)
        copy = remote(
            outbox.at[j - 1], inbox.at[j - 1], core_send.at[j], core_recv.at[j], cores[j - 1]
        )
        copy.start()
        core_copies.append(copy)

    chunk = depth // size
    for i, ref in enumerate(parts):
        partial[:, i * width : (i + 1) * width] = dot(active_ref[...], ref[...], TN)
    for p in range(size):
        partial_wire[p] = partial[p * chunk : (p + 1) * chunk, :].astype(wire)
    dp_copies = []
    for d, peer in enumerate(along_dp, 1):
        copy = remote(
            partial_wire.at[lax.rem(here + d, size)],
            dp_box.at[d - 1],
            dp_send.at[d],
            dp_recv.at[d],
            peer,
        )
        copy.start()
        dp_copies.append(copy)

    def own_columns(vector):
        return jnp.concatenate(
            [jnp.where(r == j, vector, 0.0) for j in range(groups)], axis=1
        )

    small_send[0] = small_ref[...]
    small_send[0, 2:3, :] = own_columns(jnp.sum(dq_ref[...].astype(F32), axis=0, keepdims=True))
    small_send[0, 3:4, :] = own_columns(jnp.sum(dv_ref[...].astype(F32), axis=0, keepdims=True))
    small_copies = []
    for d, peer in enumerate(along_dp, 1):
        copy = remote(small_send.at[0], small_dp.at[d - 1], ss.at[d], sr.at[d], peer)
        copy.start()
        small_copies.append(copy)

    mine[...] = d_active(pl.multiple_of(r * rows, rows))
    load.wait()
    for copy in core_copies:
        copy.wait_recv()
    shard = rows // streams
    back_copies = []
    order = [2, 1, 3] if streams == 4 else list(range(1, streams))
    for d in order + [0]:
        target = lax.rem(s + d, streams)
        at = pl.ds(pl.multiple_of(target * shard, shard), shard)
        bent = jnp.tanh(x_rows[target].astype(F32) * (1.0 / clip_level))
        total = mine[at, :]
        for j in range(groups - 1):
            total = total + inbox[j, at, :].astype(F32)
        blocks[target] = (d1_ref[at, :] + total * (1.0 - bent * bent)).astype(BF)
        if d:
            copy = remote(
                blocks.at[target], grad_ref.at[s], back_send.at[d], back_recv.at[d], along_z[d - 1]
            )
        else:
            copy = pltpu.make_async_copy(blocks.at[s], grad_ref.at[s], local_sems.at[0])
        copy.start()
        back_copies.append(copy)

    for copy in dp_copies:
        copy.wait_recv()
    total = partial[pl.ds(pl.multiple_of(here * chunk, chunk), chunk), :]
    for d in range(size - 1):
        total = total + dp_box[d].astype(F32)
    slim = chunk // streams
    for z in range(streams):
        chunk_wire[z] = total[z * slim : (z + 1) * slim, :].astype(wire)
    z_copies = []
    for d, peer in enumerate(along_z, 1):
        copy = remote(
            chunk_wire.at[lax.rem(s + d, streams)], z_box.at[d - 1], z_send.at[d], z_recv.at[d], peer
        )
        copy.start()
        z_copies.append(copy)
    for copy in small_copies:
        copy.wait_recv()
    small_total = small_send[0]
    for d in range(size - 1):
        small_total = small_total + small_dp[d]
    small_send[1] = small_total
    small_z_copies = []
    for d, peer in enumerate(along_z, 1):
        at = size + d
        copy = remote(small_send.at[1], small_z.at[d - 1], ss.at[at], sr.at[at], peer)
        copy.start()
        small_z_copies.append(copy)

    for copy in z_copies:
        copy.wait_recv()
    total = chunk_wire[s].astype(F32)
    for d in range(streams - 1):
        total = total + z_box[d].astype(F32)
    piece[...] = total.astype(wire)
    zg_copies = []
    keep = pltpu.make_async_copy(piece, late_ref.at[r, here, s], local_sems.at[1])
    keep.start()
    for d, peer in enumerate(along_z, 1):
        copy = remote(piece, late_ref.at[r, here, s], zg_send.at[d], zg_recv.at[d], peer)
        copy.start()
        zg_copies.append(copy)
    for copy in small_z_copies:
        copy.wait_recv()
    small_total = small_send[1]
    for d in range(streams - 1):
        small_total = small_total + small_z[d]
    small_send[2] = small_total
    small_c_copies = []
    for j, peer in enumerate(cores, 1):
        at = size + streams + j
        copy = remote(small_send.at[2], small_core.at[j - 1], ss.at[at], sr.at[at], peer)
        copy.start()
        small_c_copies.append(copy)

    keep.wait()
    for copy in zg_copies:
        copy.wait_recv()
    dpg_copies = []
    for d, peer in enumerate(along_dp, 1):
        copy = remote(
            late_ref.at[r, here], late_ref.at[r, here], dpg_send.at[d], dpg_recv.at[d], peer
        )
        copy.start()
        dpg_copies.append(copy)
    for copy in small_c_copies:
        copy.wait_recv()
    small_total = small_send[2]
    for j in range(groups - 1):
        small_total = small_total + small_core[j]
    sum_ref[...] = small_total
    for copy in dpg_copies:
        copy.wait_recv()
    cg_copies = []
    for j, peer in enumerate(cores, 1):
        copy = remote(late_ref.at[r], late_ref.at[r], cg_send.at[j], cg_recv.at[j], peer)
        copy.start()
        cg_copies.append(copy)
    for copy in cg_copies:
        copy.wait()
    for copy in back_copies:
        copy.wait()
    for copy in (
        core_copies
        + dp_copies
        + z_copies
        + zg_copies
        + dpg_copies
        + small_copies
        + small_z_copies
        + small_c_copies
    ):
        copy.wait_send()


def finish(streams, groups, d_queries, d_keys, d_values, active, bin_own, d_one, tokens, small, cid):
    seq, width = d_queries.shape
    rows, depth = d_one.shape
    size = lax.axis_size("dp")
    chunk = depth // size
    slim = chunk // streams
    wire = BF if slim % 16 == 0 else F32
    wide = 3 * width
    vmem = pl.BlockSpec(memory_space=pltpu.VMEM)
    any_space = pl.BlockSpec(memory_space=pl.ANY)
    small_shape = small.shape
    return pl.pallas_call(
        functools.partial(finish_kernel, streams, groups, wire),
        in_specs=[vmem] * 6 + [any_space, vmem],
        out_specs=[any_space, any_space, vmem],
        out_shape=[
            jax.ShapeDtypeStruct((streams, rows // streams, depth), BF),
            jax.ShapeDtypeStruct((groups, size, streams, slim, wide), wire),
            jax.ShapeDtypeStruct(small_shape, F32),
        ],
        scratch_shapes=[
            pltpu.VMEM((rows, depth), F32),
            pltpu.VMEM((groups - 1, rows, depth), BF),
            pltpu.VMEM((groups - 1, rows, depth), BF),
            pltpu.VMEM((streams, rows // streams, depth), BF),
            pltpu.VMEM((streams, rows // streams, depth), BF),
            pltpu.VMEM((depth, wide), F32),
            pltpu.VMEM((size, chunk, wide), wire),
            pltpu.VMEM((size - 1, chunk, wide), wire),
            pltpu.VMEM((streams, slim, wide), wire),
            pltpu.VMEM((streams - 1, slim, wide), wire),
            pltpu.VMEM((slim, wide), wire),
            pltpu.VMEM((3,) + small_shape, F32),
            pltpu.VMEM((size - 1,) + small_shape, F32),
            pltpu.VMEM((streams - 1,) + small_shape, F32),
            pltpu.VMEM((groups - 1,) + small_shape, F32),
            pltpu.SemaphoreType.DMA,
            dma(groups),
            dma(groups),
            dma(streams),
            dma(streams),
            dma(size),
            dma(size),
            dma(streams),
            dma(streams),
            dma(streams),
            dma(streams),
            dma(size),
            dma(size),
            dma(groups),
            dma(groups),
            dma(size + streams + groups),
            dma(size + streams + groups),
            dma(2),
        ],
        compiler_params=remote_params(cid),
        name="finish",
    )(d_queries, d_keys, d_values, active, bin_own, d_one, tokens, small)


def latent_columns(latent, binary_grad):
    matrix = latent.astype(F32)
    grad = binary_grad.astype(F32)
    scale = jnp.sqrt(jnp.mean(matrix * matrix, axis=0, keepdims=True) + 1e-06)
    inner = matrix * (2.0 / scale)
    bent = jnp.tanh(inner)
    slope = 1.0 - bent * bent
    through_scale = jnp.sum(grad * (bent - inner * slope), axis=0, keepdims=True)
    factor = through_scale / (matrix.shape[0] * scale)
    return 2.0 * grad * slope + matrix * factor


def early_latents_kernel(lo, lu, ld, go, gu, gd, oo, ou, od):
    oo[...] = latent_columns(lo[...], go[...])
    ou[...] = latent_columns(lu[...], gu[...])
    od[...] = latent_columns(ld[...], gd[...])


def early_latents(latents, grads):
    steps = 4
    specs = [
        pl.BlockSpec((a.shape[0], a.shape[1] // steps), lambda i: (0, i)) for a in latents
    ]
    return pl.pallas_call(
        early_latents_kernel,
        grid=(steps,),
        in_specs=specs * 2,
        out_specs=specs,
        out_shape=[jax.ShapeDtypeStruct(a.shape, F32) for a in latents],
        compiler_params=pltpu.CompilerParams(vmem_limit_bytes=VMEM_BYTES),
        name="early_latents",
    )(*latents, *grads)


def late_latents_kernel(latent, grad, out):
    out[0] = latent_columns(latent[0], grad[0])


def late_latents(latent, grads):
    groups, depth, wide = grads.shape
    width = wide // 3
    spec = pl.BlockSpec((1, depth, width), lambda m, j: (m, 0, j))
    return pl.pallas_call(
        late_latents_kernel,
        grid=(3, groups),
        in_specs=[spec, pl.BlockSpec((1, depth, width), lambda m, j: (j, 0, m))],
        out_specs=spec,
        out_shape=jax.ShapeDtypeStruct(latent.shape, F32),
        compiler_params=pltpu.CompilerParams(vmem_limit_bytes=VMEM_BYTES),
        name="late_latents",
    )(latent, grads)


def shards(
    tokens,
    teacher_tokens,
    segment_ids,
    cotangent,
    latent_qkv,
    latent_out,
    latent_up,
    latent_down,
    student_gain,
    student_bias,
    student_up_bias,
    teacher_qkv,
    teacher_out,
    teacher_up,
    teacher_down,
    teacher_gain,
    teacher_bias,
    teacher_up_bias,
):
    streams, shard_len, depth = tokens.shape
    blocks = lax.axis_size("blk")
    groups = blocks // streams
    seq = shard_len * blocks
    rows = seq // groups
    width = depth // groups
    s, r = place(groups)
    block = (shard_len, depth)
    gather, swap = Gather(streams, groups, block, BF), Swap(streams, groups, block, BF)
    row_block = (rows, width)
    by_rows = Rows(streams, groups, row_block, BF)
    doc_block = (shard_len // 128, 128)

    def own_columns(matrices):
        return lax.dynamic_slice_in_dim(matrices, r * width, width, axis=2)

    def own_bias(bias):
        return lax.dynamic_slice_in_dim(bias, r * width, width, axis=1)

    latents = [own_columns(latent_qkv), latent_out, latent_up, latent_down]
    taken = [
        tokens,
        segment_ids.reshape((streams,) + doc_block),
        teacher_qkv,
        teacher_out,
    ]
    bin_own, bin_out, bin_up, bin_down, token_blocks, docs, qkv_parts, out_parts = intake(
        Moves(
            gather,
            Gather(streams, groups, doc_block, jnp.int32),
            Spread(teacher_qkv.shape, BF),
            Spread(teacher_out.shape, BF),
        ),
        latents,
        taken,
        1,
    )
    docs = docs.reshape(seq)
    big = docs[streams * shard_len] if groups > 1 else docs[shard_len]
    in_big = docs == big
    stream_tokens = token_blocks.reshape(seq, depth)

    def project(rows_in, matrices, bias):
        q = dot(rows_in, matrices[0]) + own_bias(bias)[0]
        k = dot(rows_in, matrices[1])
        v = dot(rows_in, matrices[2]) + own_bias(bias)[1]
        return jnp.concatenate(
            [(q.astype(BF).astype(F32) * 0.125).astype(BF), k.astype(BF), v.astype(BF)], axis=1
        )

    active = squash(stream_tokens.astype(F32)).astype(BF)
    qkv = project(active, bin_own, student_bias)
    numerators, context, inverse, teacher_blocks, up_parts = attention(
        qkv,
        docs,
        Moves(gather, Spread(teacher_up.shape, BF)),
        [teacher_tokens, teacher_up],
        True,
        2,
        "attention_student",
    )
    teacher_stream = teacher_blocks.reshape(seq, depth)
    full_qkv = own_columns(qkv_parts.transpose(1, 0, 2, 3).reshape(3, depth, depth))
    teacher_own = project(teacher_stream, full_qkv, teacher_bias)
    row_shape = (groups,) + row_block
    teacher_context, cot_blocks, down_parts, ctx_rows = attention(
        teacher_own,
        docs,
        Moves(swap, Spread(teacher_down.shape, BF), by_rows),
        [cotangent, teacher_down, context.reshape(row_shape)],
        False,
        3,
        "attention_teacher",
    )
    (tctx_rows,) = move(
        Moves(by_rows), [teacher_context.reshape(row_shape)], 4, "teacher_context_rows"
    )
    output, d_one, d_context, g_out, g_up, g_down, g_gain, g_bias, g_ub = middle(
        r,
        stream_tokens,
        teacher_stream,
        cot_blocks.reshape(rows, depth),
        ctx_rows,
        tctx_rows,
        [bin_out, bin_up, bin_down],
        [
            out_parts.reshape(-1, depth),
            up_parts.reshape(depth, -1),
            down_parts.reshape(-1, depth),
        ],
        [
            student_gain,
            student_bias,
            student_up_bias.reshape(1, -1),
            teacher_gain,
            teacher_bias,
            teacher_up_bias.reshape(1, -1),
        ],
    )
    early = lax.psum((g_out.astype(BF), g_up.astype(BF), g_down.astype(BF)), ("dp", "blk"))
    small = jnp.concatenate(
        [g_gain, g_bias, g_ub.reshape(-1, depth), jnp.zeros((4, depth), F32)], axis=0
    )
    (d_ctx_rows,) = move(Moves(by_rows), [d_context], 5, "d_context_rows")
    d_queries, d_keys, d_values, output_blocks = attention_back(
        numerators,
        qkv,
        teacher_own,
        d_ctx_rows.reshape(seq, width),
        context,
        inverse,
        docs,
        in_big,
        Moves(swap),
        [output.reshape(streams, shard_len, depth)],
        6,
    )
    grad_tokens, late, small = finish(
        streams, groups, d_queries, d_keys, d_values, active, bin_own, d_one, token_blocks, small, 7
    )
    up_rows = latent_up.shape[1] // depth
    grad_out, grad_up, grad_down = early_latents([latent_out, latent_up, latent_down], early)
    return (
        output_blocks,
        grad_tokens,
        late_latents(latent_qkv, late.reshape(groups, depth, 3 * width)),
        grad_out,
        grad_up,
        grad_down,
        small[0:2],
        small[2:8],
        small[8 : 8 + up_rows].reshape(-1),
    )


def solution(mesh):
    return jax.shard_map(
        shards,
        mesh=mesh,
        in_specs=(
            P("dp", "blk", None),
            P("dp", "blk", None),
            P("dp", "blk"),
            P("dp", "blk", None),
            P(),
            P(),
            P(),
            P(),
            P(),
            P(),
            P(),
            P(None, "dp", None),
            P("dp", None),
            P("dp", None),
            P("dp", None),
            P(),
            P(),
            P(),
        ),
        out_specs=(P("dp", "blk", None), P("dp", "blk", None), P(), P(), P(), P(), P(), P(), P()),
        check_vma=False,
    )
```

```python
import functools

import jax
import jax.numpy as jnp
from jax import lax
from jax.experimental import pallas as pl
from jax.experimental.pallas import tpu as pltpu
from jax.sharding import PartitionSpec as P

HEADS = 8
BF = jnp.bfloat16
F32 = jnp.float32
LOG2E = 1.4426950408889634
clip_level = 2.5
masked_score = -1e30
VMEM_BYTES = 56 << 20
MESH = pl.DeviceIdType.MESH
NT = (((1,), (1,)), ((), ()))
TN = (((0,), (0,)), ((), ()))


def squash(tensor):
    return clip_level * jnp.tanh(tensor * (1.0 / clip_level))


def gelu_parts(tensor):
    phi = 0.5 * (1.0 + lax.erf(tensor * 0.7071067811865476))
    return tensor * phi, phi


def binarize(matrix):
    column_scale = jnp.sqrt(jnp.mean(matrix * matrix, axis=-2, keepdims=True) + 1e-06)
    return column_scale * jnp.tanh(2.0 * matrix / column_scale)


def layer_norm(tensor, gain_row, shift_row):
    centre = tensor - jnp.mean(tensor, axis=-1, keepdims=True)
    inverse_std = lax.rsqrt(jnp.mean(centre * centre, axis=-1, keepdims=True) + 1e-05)
    normed = centre * inverse_std
    return (normed * gain_row + shift_row, normed, inverse_std)


def norm_back(upstream, gain_row, normed, inverse_std):
    scaled = upstream * gain_row
    return inverse_std * (
        scaled
        - jnp.mean(scaled, axis=-1, keepdims=True)
        - normed * jnp.mean(scaled * normed, axis=-1, keepdims=True)
    )


def dot(a, b, dims=(((1,), (0,)), ((), ()))):
    return lax.dot_general(a, b, dims, preferred_element_type=F32)


def latent_grad(latent, binary_grad):
    matrix = latent.astype(F32)
    unused, pullback = jax.vjp(binarize, matrix)
    return pullback(binary_grad)[0]


def place(groups):
    here = lax.axis_index("blk")
    return here // groups, lax.rem(here, groups)


def greet(peers):
    barrier = pltpu.get_barrier_semaphore()
    for peer in peers:
        pl.semaphore_signal(barrier, inc=1, device_id=peer, device_id_type=MESH)
    pl.semaphore_wait(barrier, len(peers))


def stream_peers(streams, groups):
    s, r = place(groups)
    return [{"blk": lax.rem(s + d, streams) * groups + r} for d in range(1, streams)]


def core_peers(groups):
    s, r = place(groups)
    return [{"blk": s * groups + lax.rem(r + j, groups)} for j in range(1, groups)]


def dp_peers():
    size = lax.axis_size("dp")
    here = lax.axis_index("dp")
    return [{"dp": lax.rem(here + d, size)} for d in range(1, size)]


def unique(jobs):
    peers, kinds = [], []
    for job in jobs:
        for kind, found in job.peers():
            if kind not in kinds:
                kinds.append(kind)
                peers += found
    return peers


def remote(source, target, send, recv, peer):
    return pltpu.make_async_remote_copy(
        src_ref=source,
        dst_ref=target,
        send_sem=send,
        recv_sem=recv,
        device_id=peer,
        device_id_type=MESH,
    )


def dma(count):
    return pltpu.SemaphoreType.DMA((count,))


class Staged:
    def __init__(self, source, target, stage, sems):
        self.load = pltpu.make_async_copy(source, stage, sems.at[0])
        self.store = pltpu.make_async_copy(stage, target, sems.at[1])

    def first(self):
        self.load.start()

    def last(self):
        self.load.wait()
        self.store.start()
        self.store.wait()


class Gather:
    def __init__(self, streams, groups, block, dtype):
        self.streams, self.groups, self.block, self.dtype = streams, groups, block, dtype

    def scratch(self):
        b, g = self.streams, self.groups
        return [dma(b), dma(b), dma(b * g), dma(b * g), pltpu.VMEM(self.block, self.dtype), dma(2)]

    def out_shape(self):
        return jax.ShapeDtypeStruct((self.streams * self.groups,) + self.block, self.dtype)

    def peers(self):
        return [
            ("stream", stream_peers(self.streams, self.groups)),
            ("core", core_peers(self.groups)),
        ]

    def parts(self, source, target, send, recv, share_send, share_recv, stage, sems):
        b, g = self.streams, self.groups
        s, r = place(g)
        peers, cores = stream_peers(b, g), core_peers(g)
        swaps = [
            remote(
                source.at[lax.rem(s + d, b)],
                target.at[r * b + s],
                send.at[d],
                recv.at[d],
                peers[d - 1],
            )
            for d in range(1, b)
        ]
        shares = [
            [
                remote(
                    source.at[s] if d == 0 else target.at[r * b + lax.rem(s + b - d, b)],
                    target.at[r * b + lax.rem(s + b - d, b)],
                    share_send.at[j * b + d],
                    share_recv.at[j * b + d],
                    cores[j - 1],
                )
                for j in range(1, g)
            ]
            for d in range(b)
        ]
        own = Staged(source.at[s], target.at[r * b + s], stage, sems)
        return swaps, shares, own

    def first(self, *refs):
        swaps, shares, own = self.parts(*refs)
        for copy in swaps:
            copy.start()
        own.first()
        for copy in shares[0]:
            copy.start()

    def last(self, *refs):
        swaps, shares, own = self.parts(*refs)
        own.last()
        for d in [1, 3, 2] if self.streams == 4 else range(1, self.streams):
            swaps[d - 1].wait_recv()
            for copy in shares[d]:
                copy.start()
        for row in shares:
            for copy in row:
                copy.wait()
        for copy in swaps:
            copy.wait_send()


class Swap:
    def __init__(self, streams, groups, block, dtype):
        self.streams, self.groups, self.block, self.dtype = streams, groups, block, dtype

    def scratch(self):
        return [dma(self.streams), dma(self.streams), pltpu.VMEM(self.block, self.dtype), dma(2)]

    def out_shape(self):
        return jax.ShapeDtypeStruct((self.streams,) + self.block, self.dtype)

    def peers(self):
        return [("stream", stream_peers(self.streams, self.groups))]

    def parts(self, source, target, send, recv, stage, sems):
        b, g = self.streams, self.groups
        s, r = place(g)
        peers = stream_peers(b, g)
        swaps = [
            remote(source.at[lax.rem(s + d, b)], target.at[s], send.at[d], recv.at[d], peers[d - 1])
            for d in range(1, b)
        ]
        return swaps, Staged(source.at[s], target.at[s], stage, sems)

    def first(self, *refs):
        swaps, own = self.parts(*refs)
        for copy in swaps:
            copy.start()
        own.first()

    def last(self, *refs):
        swaps, own = self.parts(*refs)
        own.last()
        for copy in swaps:
            copy.wait()


class Rows:
    def __init__(self, streams, groups, block, dtype):
        self.groups, self.block, self.dtype = groups, block, dtype

    def scratch(self):
        return [dma(self.groups), dma(self.groups), pltpu.VMEM(self.block, self.dtype), dma(2)]

    def out_shape(self):
        return jax.ShapeDtypeStruct((self.groups,) + self.block, self.dtype)

    def peers(self):
        return [("core", core_peers(self.groups))]

    def parts(self, source, target, send, recv, stage, sems):
        g = self.groups
        s, r = place(g)
        cores = core_peers(g)
        copies = [
            remote(source.at[lax.rem(r + j, g)], target.at[r], send.at[j], recv.at[j], cores[j - 1])
            for j in range(1, g)
        ]
        return copies, Staged(source.at[r], target.at[r], stage, sems)

    first = Swap.first
    last = Swap.last


class Spread:
    def __init__(self, block, dtype):
        self.block, self.dtype = block, dtype

    def scratch(self):
        size = lax.axis_size("dp")
        return [dma(size), dma(size), pltpu.VMEM(self.block, self.dtype), dma(2)]

    def out_shape(self):
        return jax.ShapeDtypeStruct((lax.axis_size("dp"),) + self.block, self.dtype)

    def peers(self):
        return [("dp", dp_peers())]

    def parts(self, source, target, send, recv, stage, sems):
        here = lax.axis_index("dp")
        copies = [
            remote(source, target.at[here], send.at[d], recv.at[d], peer)
            for d, peer in enumerate(dp_peers(), 1)
        ]
        return copies, Staged(source, target.at[here], stage, sems)

    first = Swap.first
    last = Swap.last


class Bag:
    def __init__(self):
        self.items = {}

    def add(self, name, item):
        self.items[name] = item

    def bind(self, refs):
        return dict(zip(self.items, refs))


class Reduce:
    def __init__(self, bag, name, streams, groups, shapes, over_cores):
        self.name, self.streams, self.groups = name, streams, groups
        self.size = lax.axis_size("dp")
        self.over_cores = over_cores
        self.count = len(shapes)
        share = self.size * (groups if over_cores else 1)
        self.shapes = [(rows // share, cols) for rows, cols in shapes]
        self.wires = [BF if (c // streams) % 16 == 0 else F32 for c, cols in self.shapes]
        for i, (chunk, cols) in enumerate(self.shapes):
            wire, slim = self.wires[i], chunk // streams
            bag.add(f"{name}half{i}", pltpu.VMEM((self.size, chunk, cols), wire))
            if over_cores:
                bag.add(f"{name}core{i}", pltpu.VMEM((groups - 1, self.size, chunk, cols), wire))
            bag.add(f"{name}dp{i}", pltpu.VMEM((self.size - 1, chunk, cols), wire))
            bag.add(f"{name}cut{i}", pltpu.VMEM((streams, slim, cols), wire))
            bag.add(f"{name}z{i}", pltpu.VMEM((streams - 1, slim, cols), wire))
            bag.add(f"{name}fin{i}", pltpu.VMEM((slim, cols), wire))
            for kind, n in self.sem_counts().items():
                bag.add(f"{name}{kind}s{i}", dma(n))
                bag.add(f"{name}{kind}r{i}", dma(n))
            bag.add(f"{name}local{i}", dma(2))

    def sem_counts(self):
        b, g, d = self.streams, self.groups, self.size
        return {"a": g, "b": d, "c": b, "d": b, "e": d, "f": g}

    def out_shapes(self):
        return [
            jax.ShapeDtypeStruct(
                (self.groups, self.size, self.streams, chunk // self.streams, cols), wire
            )
            for (chunk, cols), wire in zip(self.shapes, self.wires)
        ]

    def bind(self, sources, targets, scratch):
        self.sources, self.targets, self.scratch = sources, targets, scratch

    def get(self, what, i):
        return self.scratch[f"{self.name}{what}{i}"]

    def copies(self, kind, i):
        s, r = place(self.groups)
        here = lax.axis_index("dp")
        b, g, size = self.streams, self.groups, self.size
        send, recv = self.get(kind + "s", i), self.get(kind + "r", i)
        if kind in "af":
            peers = core_peers(g)
        elif kind in "be":
            peers = dp_peers()
        else:
            peers = stream_peers(b, g)
        order = list(enumerate(peers, 1))
        if kind in "cd" and b == 4:
            order = [order[1], order[0], order[2]]
        for d, peer in order:
            if kind == "a":
                pair = self.sources[i].at[lax.rem(r + d, g)], self.get("core", i).at[d - 1]
            elif kind == "b":
                pair = self.get("half", i).at[lax.rem(here + d, size)], self.get("dp", i).at[d - 1]
            elif kind == "c":
                pair = self.get("cut", i).at[lax.rem(s + d, b)], self.get("z", i).at[d - 1]
            elif kind == "d":
                pair = self.get("fin", i), self.targets[i].at[r, here, s]
            elif kind == "e":
                pair = self.targets[i].at[r, here], self.targets[i].at[r, here]
            else:
                pair = self.targets[i].at[r], self.targets[i].at[r]
            yield remote(*pair, send.at[d], recv.at[d], peer)

    def start(self, kind, i):
        for copy in self.copies(kind, i):
            copy.start()

    def arrive(self, kind, i):
        for copy in self.copies(kind, i):
            copy.wait_recv()

    def load(self, i):
        s, r = place(self.groups)
        return pltpu.make_async_copy(
            self.sources[i].at[r], self.get("half", i), self.get("local", i).at[0]
        )

    def keep(self, i):
        s, r = place(self.groups)
        return pltpu.make_async_copy(
            self.get("fin", i),
            self.targets[i].at[r, lax.axis_index("dp"), s],
            self.get("local", i).at[1],
        )

    def core_start(self):
        for i in range(self.count):
            self.start("a", i)
            self.load(i).start()

    def dp_start(self):
        for i in range(self.count):
            if self.over_cores:
                self.load(i).wait()
                self.arrive("a", i)
                half, box, wire = self.get("half", i), self.get("core", i), self.wires[i]
                for p in range(self.size):
                    total = half[p].astype(F32)
                    for j in range(self.groups - 1):
                        total = total + box[j, p].astype(F32)
                    half[p] = total.astype(wire)
            self.start("b", i)

    def z_start(self):
        here = lax.axis_index("dp")
        for i in range(self.count):
            self.arrive("b", i)
            half, box, cut, wire = (
                self.get("half", i),
                self.get("dp", i),
                self.get("cut", i),
                self.wires[i],
            )
            slim = self.shapes[i][0] // self.streams
            for z in range(self.streams):
                at = slice(z * slim, (z + 1) * slim)
                total = half[here, at, :].astype(F32)
                for d in range(self.size - 1):
                    total = total + box[d, at, :].astype(F32)
                cut[z] = total.astype(wire)
            self.start("c", i)

    def z_back(self):
        s, r = place(self.groups)
        for i in range(self.count):
            self.arrive("c", i)
            box = self.get("z", i)
            total = self.get("cut", i)[s].astype(F32)
            for d in range(self.streams - 1):
                total = total + box[d].astype(F32)
            self.get("fin", i)[...] = total.astype(self.wires[i])
            self.keep(i).start()
            self.start("d", i)

    def dp_back(self):
        for i in range(self.count):
            self.keep(i).wait()
            self.arrive("d", i)
            self.start("e", i)

    def core_back(self):
        for i in range(self.count):
            self.arrive("e", i)
            self.start("f", i)

    def end(self):
        for i in range(self.count):
            self.arrive("f", i)
            for kind in "abcdef" if self.over_cores else "bcdef":
                for copy in self.copies(kind, i):
                    copy.wait_send()


class Moves:
    def __init__(self, *jobs):
        self.jobs = jobs
        self.counts = [len(job.scratch()) for job in jobs]

    def scratch(self):
        return [item for job in self.jobs for item in job.scratch()]

    def out_shapes(self):
        return [job.out_shape() for job in self.jobs]

    def spaces(self):
        return [pl.BlockSpec(memory_space=pl.ANY)] * len(self.jobs)

    def each(self, sources, targets, scratch):
        at = 0
        for job, count, source, target in zip(self.jobs, self.counts, sources, targets):
            yield job, (source, target, *scratch[at : at + count])
            at += count

    def first(self, sources, targets, scratch):
        greet(unique(self.jobs))
        for job, refs in self.each(sources, targets, scratch):
            job.first(*refs)

    def last(self, sources, targets, scratch):
        for job, refs in self.each(sources, targets, scratch):
            job.last(*refs)


def remote_params(collective_id):
    return pltpu.CompilerParams(
        collective_id=collective_id, has_side_effects=True, vmem_limit_bytes=VMEM_BYTES
    )


def move(moves, arrays, collective_id, name):
    count = len(arrays)

    def kernel(*refs):
        sources, targets, scratch = refs[:count], refs[count : 2 * count], refs[2 * count :]
        moves.first(sources, targets, scratch)
        moves.last(sources, targets, scratch)

    return pl.pallas_call(
        kernel,
        out_shape=moves.out_shapes(),
        in_specs=moves.spaces(),
        out_specs=moves.spaces(),
        scratch_shapes=moves.scratch(),
        compiler_params=remote_params(collective_id),
        name=name,
    )(*arrays)


def binary_columns(latent):
    matrix = latent.astype(F32)
    scale = jnp.sqrt(jnp.mean(matrix * matrix, axis=0, keepdims=True) + 1e-06)
    return (scale * jnp.tanh(matrix * (2.0 / scale))).astype(BF)


def intake_kernel(moves, qkv_ref, out_ref, up_ref, down_ref, *refs):
    count = len(moves.jobs)
    sources = refs[:count]
    own_bin, out_bin, up_bin, down_bin = refs[count : count + 4]
    targets = refs[count + 4 : 2 * count + 4]
    scratch = refs[2 * count + 4 :]
    moves.first(sources, targets, scratch)
    for i in range(3):
        own_bin[i] = binary_columns(qkv_ref[i])
    out_bin[...] = binary_columns(out_ref[...])
    for i in range(0, up_ref.shape[1], 512):
        up_bin[:, i : i + 512] = binary_columns(up_ref[:, i : i + 512])
    for i in range(0, down_ref.shape[1], 128):
        down_bin[:, i : i + 128] = binary_columns(down_ref[:, i : i + 128])
    moves.last(sources, targets, scratch)


def intake(moves, latents, arrays, collective_id):
    vmem = pl.BlockSpec(memory_space=pltpu.VMEM)
    return pl.pallas_call(
        functools.partial(intake_kernel, moves),
        out_shape=[jax.ShapeDtypeStruct(a.shape, BF) for a in latents] + moves.out_shapes(),
        in_specs=[vmem] * 4 + moves.spaces(),
        out_specs=[vmem] * 4 + moves.spaces(),
        scratch_shapes=moves.scratch(),
        compiler_params=remote_params(collective_id),
        name="intake",
    )(*latents, *arrays)


def lanes_of(shape):
    return lax.broadcasted_iota(jnp.int32, shape, 1)


def forward_kernel(moves, keep, tile, edge, q_ref, k_ref, v_ref, col_ref, row_ref, *rest):
    count = len(moves.jobs)
    sources, rest = rest[:count], rest[count:]
    if keep:
        e_ref, ctx_ref, inv_ref, *rest = rest
    else:
        ctx_ref, *rest = rest
    targets, (k_aug, v_aug, *scratch) = rest[:count], rest[count:]
    pair, step = pl.program_id(0), pl.program_id(1)
    steps = pl.num_programs(1)
    seq = k_ref.shape[0]

    @pl.when((pair == 0) & (step == 0))
    def _():
        moves.first(sources, targets, scratch)

    @pl.when(step == 0)
    def _():
        low = lanes_of((seq, 128)) < 64
        lane = lanes_of((seq, 128))
        keys = k_ref[...].astype(F32)
        turned = pltpu.roll(keys, 64, 1)
        k_aug[0] = jnp.where(low, keys, turned).astype(BF)
        k_aug[1] = jnp.where(low, turned, keys).astype(BF)
        values = v_ref[...].astype(F32)
        v_aug[0] = jnp.where(low, values, jnp.where(lane < 66, 1.0, 0.0)).astype(BF)
        v_aug[1] = jnp.where(low, jnp.where(lane < 2, 1.0, 0.0), values).astype(BF)

    def body(whole):
        low = lanes_of((tile, 128)) < 64
        scaled = q_ref[...].astype(F32) * LOG2E
        upper = scaled.astype(BF).astype(F32)
        rest_part = scaled - upper
        results = []
        for h in range(2):
            if h == 0:
                q_aug = jnp.where(low, upper, pltpu.roll(rest_part, 64, 1)).astype(BF)
            else:
                q_aug = jnp.where(low, pltpu.roll(upper, 64, 1), rest_part).astype(BF)
            scores = dot(q_aug, k_aug[h], NT)
            if whole:
                scores = jnp.where(col_ref[...] == row_ref[...], scores, masked_score)
            else:
                left = jnp.where(
                    col_ref[...] == row_ref[:, :edge], scores[:, :edge], masked_score
                )
                right = jnp.where(
                    col_ref[...] == row_ref[:, seq - edge :], scores[:, seq - edge :], masked_score
                )
                scores = jnp.concatenate([left, scores[:, edge : seq - edge], right], axis=1)
            peak = jnp.max(scores, axis=1, keepdims=True)
            numerators = jnp.exp2(scores - peak).astype(BF)
            if keep:
                e_ref[h] = numerators
            total = dot(numerators, v_aug[h])
            where_sum = 64 if h == 0 else 0
            inverse = 1.0 / total[:, where_sum : where_sum + 1]
            results.append((total * inverse, inverse))
        ctx_ref[...] = jnp.where(low, results[0][0], results[1][0]).astype(BF)
        if keep:
            inv_ref[...] = jnp.where(low, results[0][1], results[1][1])

    at_edge = (step == 0) | (step == steps - 1)

    @pl.when(at_edge)
    def _():
        body(True)

    @pl.when(jnp.logical_not(at_edge))
    def _():
        body(False)

    @pl.when((pair == pl.num_programs(0) - 1) & (step == steps - 1))
    def _():
        moves.last(sources, targets, scratch)


def attention(qkv, docs, moves, moved, keep, collective_id, name):
    seq, width3 = qkv.shape
    width = width3 // 3
    pairs = width // 128
    tile = 256
    edge = 256
    col = docs.reshape(seq, 1)
    row = docs.reshape(1, seq)
    blocks = [
        pl.BlockSpec((tile, 128), lambda p, i: (i, p)),
        pl.BlockSpec((seq, 128), lambda p, i: (0, pairs + p)),
        pl.BlockSpec((seq, 128), lambda p, i: (0, 2 * pairs + p)),
        pl.BlockSpec((tile, 1), lambda p, i: (i, 0)),
        pl.BlockSpec((1, seq), lambda p, i: (0, 0)),
    ] + moves.spaces()
    outs = [pl.BlockSpec((tile, 128), lambda p, i: (i, p))]
    shapes = [jax.ShapeDtypeStruct((seq, width), BF)]
    if keep:
        outs = [pl.BlockSpec((2, tile, seq), lambda p, i: (p, i, 0))] + outs
        shapes = [jax.ShapeDtypeStruct((2 * pairs, seq, seq), BF)] + shapes
        outs = outs + [pl.BlockSpec((tile, 128), lambda p, i: (i, p))]
        shapes = shapes + [jax.ShapeDtypeStruct((seq, width), F32)]
    return pl.pallas_call(
        functools.partial(forward_kernel, moves, keep, tile, edge),
        grid=(pairs, seq // tile),
        in_specs=blocks,
        out_specs=outs + moves.spaces(),
        out_shape=shapes + moves.out_shapes(),
        scratch_shapes=[pltpu.VMEM((2, seq, 128), BF), pltpu.VMEM((2, seq, 128), BF)]
        + moves.scratch(),
        compiler_params=remote_params(collective_id),
        name=name,
    )(qkv, qkv, qkv, col, row, *moved)


def split(matrix):
    upper = matrix.astype(BF)
    return upper, (matrix - upper.astype(F32)).astype(BF)


def backward_kernel(
    streams,
    groups,
    tile,
    bag,
    back,
    early,
    late,
    e_ref,
    q_ref,
    k_ref,
    v_ref,
    tq_ref,
    tk_ref,
    dc_ref,
    ctx_ref,
    inv_ref,
    col_ref,
    row_ref,
    bigc_ref,
    small_ref,
    active_hbm,
    bin_hbm,
    d1_hbm,
    tokens_hbm,
    output_ref,
    *rest,
):
    n_early = sum(job.count for job in early)
    sources, rest = rest[:n_early], rest[n_early:]
    output_back, grad_ref, *rest = rest
    early_out, rest = rest[:n_early], rest[n_early:]
    late_out, (sum_ref, *rest) = rest[: len(late)], rest[len(late) :]
    have = bag.bind(rest)
    at = 0
    for job in early:
        job.bind(sources[at : at + job.count], early_out[at : at + job.count], have)
        at += job.count
    for job, target in zip(late, late_out):
        job.bind(None, [target], have)
    back_refs = (output_ref, output_back) + tuple(have[f"back{i}"] for i in range(4))

    pair, step = pl.program_id(0), pl.program_id(1)
    pairs, steps = len(late), q_ref.shape[0] // tile
    seq = k_ref.shape[0]
    share = 1.0 / seq
    time = pair * steps + step
    total_time = pairs * steps
    size = lax.axis_size("dp")
    here = lax.axis_index("dp")
    s, r = place(groups)
    rows, depth = d1_hbm.shape
    width = pairs * 128
    v_aug, dk_acc, dv_acc, grams = have["v_aug"], have["dk_acc"], have["dv_acc"], have["grams"]
    dq_all, d_act, active, weights = have["dq_all"], have["d_act"], have["active"], have["weights"]
    d_one, x_rows = have["d_one"], have["x_rows"]
    along_z, cores, along_dp = stream_peers(streams, groups), core_peers(groups), dp_peers()

    def loads():
        sems = have["load"]
        return [
            pltpu.make_async_copy(active_hbm, active, sems.at[0]),
            pltpu.make_async_copy(bin_hbm, weights, sems.at[1]),
            pltpu.make_async_copy(d1_hbm, d_one, sems.at[2]),
            pltpu.make_async_copy(tokens_hbm.at[pl.ds(r * streams, streams)], x_rows, sems.at[3]),
        ]

    def at_time(when, *work):
        @pl.when(time == when)
        def _():
            for item in work:
                item()

    def begin():
        greet(along_z + cores + along_dp)
        back.first(*back_refs)
        for job in early:
            job.core_start()
        for copy in loads():
            copy.start()

    at_time(0, begin)
    unit = total_time / 16
    for n, job in enumerate(early):
        for when, work in zip(EARLY_TIMES[n], (job.dp_start, job.z_start, job.z_back, job.dp_back)):
            at_time(int(when * unit), work)
    for p, job in enumerate(late[:-1]):
        first = (p + 1) * steps
        for when, work in zip(LATE_TIMES, (job.dp_start, job.z_start, job.z_back, job.dp_back)):
            at_time(first + when, work)

    @pl.when(step == 0)
    def _():
        lane = lanes_of((seq, 128))
        low = lane < 64
        values = v_ref[...].astype(F32)
        v_aug[0] = jnp.where(low, values, jnp.where(lane < 66, 1.0, 0.0)).astype(BF)
        v_aug[1] = jnp.where(low, jnp.where(lane < 2, 1.0, 0.0), values).astype(BF)
        dk_acc[...] = jnp.zeros_like(dk_acc)
        dv_acc[...] = jnp.zeros_like(dv_acc)
        in_big = bigc_ref[...] > 0.0
        kb = jnp.where(in_big, k_ref[...].astype(F32), 0.0).astype(BF)
        tkb = jnp.where(in_big, tk_ref[...].astype(F32), 0.0).astype(BF)
        qb = jnp.where(in_big, q_ref[...].astype(F32), 0.0).astype(BF)
        tqb = jnp.where(in_big, tq_ref[...].astype(F32), 0.0).astype(BF)
        same_head = (lax.broadcasted_iota(jnp.int32, (128, 128), 0) < 64) == (
            lanes_of((128, 128)) < 64
        )
        for i, (a, b) in enumerate(((kb, kb), (tkb, kb), (qb, qb), (tqb, qb))):
            gram = jnp.where(same_head, dot(a, b, TN) * share, 0.0)
            grams[2 * i], grams[2 * i + 1] = split(gram)

    start = pl.multiple_of(step * tile, tile)
    rows_here = pl.ds(start, tile)
    lane = lanes_of((tile, 128))
    low = lane < 64

    def body(whole, columns):
        in_big = bigc_ref[rows_here, :] > 0.0
        q8 = q_ref[rows_here, :]
        tq8 = tq_ref[rows_here, :]
        dc = dc_ref[...].astype(F32)
        inv = inv_ref[...]
        scaled = dc * inv
        product = scaled * ctx_ref[...].astype(F32)
        scaled_low = scaled.astype(BF)
        q_turned = q8.astype(F32).T.astype(BF)
        dc_turned = scaled_low.astype(F32).T.astype(BF)
        d_queries = []
        for h in range(2):
            mine = low if h == 0 else jnp.logical_not(low)
            delta = -jnp.sum(jnp.where(mine, product, 0.0), axis=1, keepdims=True)
            upper = delta.astype(BF).astype(F32)
            first = 64 if h == 0 else 0
            extra = jnp.where(
                lane == first, upper, jnp.where(lane == first + 1, delta - upper, 0.0)
            )
            dc_aug = jnp.where(mine, scaled, extra).astype(BF)
            numerators = e_ref[h]
            d_probs = dot(dc_aug, v_aug[h], NT)
            d_scores = numerators.astype(F32) * d_probs
            if whole:
                q_mine = jnp.where(mine, q8, 0.0).astype(BF)
                tq_mine = jnp.where(mine, tq8, 0.0).astype(BF)
                gap = dot(q_mine, k_ref[columns, :], NT) - dot(tq_mine, tk_ref[columns, :], NT)
                small = (col_ref[...] == row_ref[:, columns]) & jnp.logical_not(in_big)
                gap = jnp.where(small, gap * share, 0.0)
                if columns.start == 0:
                    d_scores = jnp.concatenate(
                        [d_scores[:, :tile] + gap, d_scores[:, tile:]], axis=1
                    )
                else:
                    d_scores = jnp.concatenate(
                        [d_scores[:, : seq - tile], d_scores[:, seq - tile :] + gap], axis=1
                    )
            d_scores = d_scores.astype(BF)
            d_queries.append(dot(d_scores, k_ref[...]))
            half = slice(64 * h, 64 * h + 64)
            dk_acc[half, :] += dot(q_turned[half, :], d_scores)
            dv_acc[half, :] += dot(dc_turned[half, :], numerators)
        d_query = jnp.where(low, d_queries[0], d_queries[1])
        qb = jnp.where(in_big, q8.astype(F32), 0.0).astype(BF)
        tqb = jnp.where(in_big, tq8.astype(F32), 0.0).astype(BF)
        d_query += dot(qb, grams[0]) + dot(qb, grams[1]) - dot(tqb, grams[2]) - dot(tqb, grams[3])
        dq_all[rows_here, :] = (d_query * 0.125).astype(BF)

    @pl.when(step == 0)
    def _():
        body(True, slice(0, tile))

    @pl.when(step == steps - 1)
    def _():
        body(True, slice(seq - tile, seq))

    @pl.when((step > 0) & (step < steps - 1))
    def _():
        body(False, None)

    def pair_end(p):
        job = late[p]
        in_big = bigc_ref[...] > 0.0
        kb = jnp.where(in_big, k_ref[...].astype(F32), 0.0).astype(BF)
        tkb = jnp.where(in_big, tk_ref[...].astype(F32), 0.0).astype(BF)
        d_key = dk_acc[...].T
        d_key += dot(kb, grams[4]) + dot(kb, grams[5]) - dot(tkb, grams[6]) - dot(tkb, grams[7])
        d_value = dv_acc[...].T.astype(BF)
        d_query = dq_all[...]
        d_pair = jnp.concatenate([d_query, d_key.astype(BF), d_value], axis=1)
        if p == 0:
            for copy in loads():
                copy.wait()
        columns = slice(p * 128, (p + 1) * 128)
        bins = jnp.concatenate([weights[i, :, columns] for i in range(3)], axis=1)
        if p == 0:
            d_act[...] = dot(d_pair, bins, NT)
        else:
            d_act[...] += dot(d_pair, bins, NT)
        if p == pairs - 1:
            for j in range(1, groups):
                other = pl.multiple_of(lax.rem(r + j, groups) * rows, rows)
                have["outbox"][j - 1] = d_act[pl.ds(other, rows), :].astype(BF)
            for copy in core_copies():
                copy.start()
        partial = dot(active[...], d_pair, TN)
        chunk = depth // size
        half = job.get("half", 0)
        for d in range(size):
            half[d] = partial[d * chunk : (d + 1) * chunk, :].astype(job.wires[0])
        sums = have["sums"]
        sums[0:1, columns] = jnp.sum(d_query.astype(F32), axis=0, keepdims=True)
        sums[1:2, columns] = jnp.sum(d_value.astype(F32), axis=0, keepdims=True)

    def core_copies():
        return [
            remote(
                have["outbox"].at[j - 1],
                have["inbox"].at[j - 1],
                have["core_s"].at[j],
                have["core_r"].at[j],
                cores[j - 1],
            )
            for j in range(1, groups)
        ]

    def small_copies(stage, peers, base):
        return [
            remote(
                have["small"].at[stage],
                have["small_box"].at[base + d],
                have["small_s"].at[base + d],
                have["small_r"].at[base + d],
                peer,
            )
            for d, peer in enumerate(peers)
        ]

    def small_start(stage, peers, base):
        for copy in small_copies(stage, peers, base):
            copy.start()

    def small_sum(stage, peers, base):
        for copy in small_copies(stage, peers, base):
            copy.wait_recv()
        total = have["small"][stage]
        for d in range(len(peers)):
            total = total + have["small_box"][base + d]
        return total

    for p in range(pairs - 1):

        @pl.when((pair == p) & (step == steps - 1))
        def _():
            pair_end(p)

    @pl.when(time == total_time - 1)
    def _():
        pair_end(pairs - 1)
        last = late[-1]
        last.dp_start()
        small = have["small"]
        small[0] = small_ref[...]
        for i in range(2):
            vector = have["sums"][i : i + 1, :]
            small[0, 2 + i : 3 + i, :] = jnp.concatenate(
                [jnp.where(r == j, vector, 0.0) for j in range(groups)], axis=1
            )
        small_start(0, along_dp, 0)
        for copy in core_copies():
            copy.wait_recv()
        shard = rows // streams
        back_copies = []
        blocks = have["blocks"]
        order = [2, 1, 3] if streams == 4 else list(range(1, streams))
        for d in order + [0]:
            target = lax.rem(s + d, streams)
            here_rows = pl.ds(pl.multiple_of(target * shard, shard), shard)
            bent = jnp.tanh(x_rows[target].astype(F32) * (1.0 / clip_level))
            total = d_act[pl.ds(pl.multiple_of(r * rows + target * shard, shard), shard), :]
            for j in range(groups - 1):
                total = total + have["inbox"][j, here_rows, :].astype(F32)
            blocks[target] = (d_one[here_rows, :] + total * (1.0 - bent * bent)).astype(BF)
            if d:
                copy = remote(
                    blocks.at[target],
                    grad_ref.at[s],
                    have["grad_s"].at[d],
                    have["grad_r"].at[d],
                    along_z[d - 1],
                )
            else:
                copy = pltpu.make_async_copy(blocks.at[s], grad_ref.at[s], have["grad_s"].at[0])
            copy.start()
            back_copies.append(copy)
        for job in early[:1]:
            job.core_back()
        last.z_start()
        small[1] = small_sum(0, along_dp, 0)
        small_start(1, along_z, size)
        for job in late[:-1]:
            job.core_back()
        last.z_back()
        for job in early[1:]:
            job.core_back()
        small[2] = small_sum(1, along_z, size)
        small_start(2, cores, size + streams)
        last.dp_back()
        sum_ref[...] = small_sum(2, cores, size + streams)
        last.core_back()
        back.last(*back_refs)
        for copy in back_copies:
            copy.wait()
        for job in early + late:
            job.end()
        for copy in (
            core_copies()
            + small_copies(0, along_dp, 0)
            + small_copies(1, along_z, size)
            + small_copies(2, cores, size + streams)
        ):
            copy.wait_send()


EARLY_TIMES = ((1, 7, 10, 12), (2, 11, 13, 15))
LATE_TIMES = (0, 3, 5, 7)


def attention_back(
    streams,
    groups,
    numerators,
    qkv,
    teacher_qkv,
    d_context,
    context,
    inverse,
    docs,
    in_big,
    small,
    active,
    bin_own,
    d_one,
    tokens,
    output,
    early_arrays,
    collective_id,
):
    seq, width3 = qkv.shape
    width = width3 // 3
    pairs = width // 128
    tile = 256
    rows, depth = d_one.shape
    size = lax.axis_size("dp")
    shard = rows // streams
    bag = Bag()
    bag.add("v_aug", pltpu.VMEM((2, seq, 128), BF))
    bag.add("dk_acc", pltpu.VMEM((128, seq), F32))
    bag.add("dv_acc", pltpu.VMEM((128, seq), F32))
    bag.add("grams", pltpu.VMEM((8, 128, 128), BF))
    bag.add("dq_all", pltpu.VMEM((seq, 128), BF))
    bag.add("d_act", pltpu.VMEM((seq, depth), F32))
    bag.add("active", pltpu.VMEM((seq, depth), BF))
    bag.add("weights", pltpu.VMEM((3, depth, width), BF))
    bag.add("d_one", pltpu.VMEM((rows, depth), F32))
    bag.add("x_rows", pltpu.VMEM((streams, shard, depth), BF))
    bag.add("load", dma(4))
    bag.add("sums", pltpu.VMEM((8, width), F32))
    bag.add("outbox", pltpu.VMEM((groups - 1, rows, depth), BF))
    bag.add("inbox", pltpu.VMEM((groups - 1, rows, depth), BF))
    bag.add("core_s", dma(groups))
    bag.add("core_r", dma(groups))
    bag.add("blocks", pltpu.VMEM((streams, shard, depth), BF))
    bag.add("grad_s", dma(streams))
    bag.add("grad_r", dma(streams))
    count = size + streams + groups
    bag.add("small", pltpu.VMEM((3,) + small.shape, F32))
    bag.add("small_box", pltpu.VMEM((count,) + small.shape, F32))
    bag.add("small_s", dma(count))
    bag.add("small_r", dma(count))
    back = Swap(streams, groups, (shard, depth), BF)
    for i, item in enumerate(back.scratch()):
        bag.add(f"back{i}", item)
    early, flat = [], []
    for n, arrays in enumerate(early_arrays):
        job = Reduce(bag, f"early{n}", streams, groups, [a.shape for a in arrays], True)
        early.append(job)
        flat += [
            a.reshape(groups, size, chunk, cols) for a, (chunk, cols) in zip(arrays, job.shapes)
        ]
    late = [
        Reduce(bag, f"late{p}", streams, groups, [(depth, 3 * 128)], False) for p in range(pairs)
    ]
    part = pl.BlockSpec((tile, 128), lambda p, i: (i, p))
    any_space = pl.BlockSpec(memory_space=pl.ANY)

    def whole(which):
        return pl.BlockSpec((seq, 128), lambda p, i: (0, which * pairs + p))

    def constant(shape):
        return pl.BlockSpec(shape, lambda p, i: (0,) * len(shape))

    early_shapes = [shape for job in early for shape in job.out_shapes()]
    late_shapes = [shape for job in late for shape in job.out_shapes()]
    results = pl.pallas_call(
        functools.partial(backward_kernel, streams, groups, tile, bag, back, early, late),
        grid=(pairs, seq // tile),
        in_specs=[
            pl.BlockSpec((2, tile, seq), lambda p, i: (p, i, 0)),
            whole(0),
            whole(1),
            whole(2),
            whole(0),
            whole(1),
            part,
            part,
            part,
            pl.BlockSpec((tile, 1), lambda p, i: (i, 0)),
            constant((1, seq)),
            constant((seq, 1)),
            constant(small.shape),
        ]
        + [any_space] * (5 + len(flat)),
        out_specs=[any_space] * (2 + len(early_shapes) + len(late_shapes))
        + [constant(small.shape)],
        out_shape=[back.out_shape(), jax.ShapeDtypeStruct((streams, shard, depth), BF)]
        + early_shapes
        + late_shapes
        + [jax.ShapeDtypeStruct(small.shape, F32)],
        scratch_shapes=list(bag.items.values()),
        compiler_params=remote_params(collective_id),
        name="attention_back",
    )(
        numerators,
        qkv,
        qkv,
        qkv,
        teacher_qkv,
        teacher_qkv,
        d_context,
        context,
        inverse,
        docs.reshape(seq, 1),
        docs.reshape(1, seq),
        in_big.astype(F32).reshape(seq, 1),
        small,
        active,
        bin_own,
        d_one,
        tokens,
        output,
        *flat,
    )
    output_back, grad_tokens, *rest = results
    early_sums = rest[: len(flat)]
    late_sums = rest[len(flat) : -1]
    shapes = [a.shape for arrays in early_arrays for a in arrays]
    return (
        output_back,
        grad_tokens,
        [e.reshape(shape) for e, shape in zip(early_sums, shapes)],
        [l.reshape(groups, depth, 3 * 128) for l in late_sums],
        rest[-1],
    )


def middle_kernel(
    unused_place,
    x_ref,
    tx_ref,
    cot_ref,
    ctx_ref,
    tctx_ref,
    bo_ref,
    bup_ref,
    bdown_ref,
    to_ref,
    tup_ref,
    tdown_ref,
    sg_ref,
    sb_ref,
    sub_ref,
    tg_ref,
    tb_ref,
    tub_ref,
    out_ref,
    d1_ref,
    dctx_ref,
    gout_ref,
    gup_ref,
    gdown_ref,
    ggain_ref,
    gbias_ref,
    gub_ref,
    gout_acc,
    gup_acc,
    gdown_acc,
):
    step = pl.program_id(0)
    groups = ctx_ref.shape[0]
    width = ctx_ref.shape[2]

    @pl.when(step == 0)
    def _():
        for ref in (gout_acc, gup_acc, gdown_acc, ggain_ref, gbias_ref, gub_ref):
            ref[...] = jnp.zeros_like(ref)

    def row(ref, i):
        return ref[i : i + 1, :]

    tctx = jnp.concatenate([tctx_ref[j] for j in range(groups)], axis=1)
    t_att = dot(tctx, to_ref[...]) + row(tb_ref, 2)
    t_hidden = layer_norm(tx_ref[...].astype(F32) + t_att, row(tg_ref, 0), row(tb_ref, 3))[0]
    t_inner = gelu_parts(dot(t_hidden.astype(BF), tup_ref[...]) + tub_ref[...])[0]
    t_out = layer_norm(
        t_hidden + dot(t_inner.astype(BF), tdown_ref[...]) + row(tb_ref, 4),
        row(tg_ref, 1),
        row(tb_ref, 5),
    )[0]

    context = jnp.concatenate([ctx_ref[j] for j in range(groups)], axis=1).astype(F32)
    bent = jnp.tanh(context * (1.0 / clip_level))
    ctx_active = (clip_level * bent).astype(BF)
    ctx_slope = 1.0 - bent * bent
    attended = dot(ctx_active, bo_ref[...]) + row(sb_ref, 2)
    hidden, normed_one, inverse_one = layer_norm(
        x_ref[...].astype(F32) + attended, row(sg_ref, 0), row(sb_ref, 3)
    )
    bent = jnp.tanh(hidden * (1.0 / clip_level))
    hidden_active = (clip_level * bent).astype(BF)
    hidden_slope = 1.0 - bent * bent
    inner_pre = dot(hidden_active, bup_ref[...]) + sub_ref[...]
    inner_act, phi = gelu_parts(inner_pre)
    bent = jnp.tanh(inner_act * (1.0 / clip_level))
    inner_active = (clip_level * bent).astype(BF)
    slope = (1.0 - bent * bent) * (
        phi + inner_pre * jnp.exp(-0.5 * inner_pre * inner_pre) * 0.3989422804014327
    )
    branch = dot(inner_active, bdown_ref[...]) + row(sb_ref, 4)
    output, normed_two, inverse_two = layer_norm(hidden + branch, row(sg_ref, 1), row(sb_ref, 5))
    out_ref[...] = output.astype(BF)
    upstream = cot_ref[...].astype(F32) + 0.5 * (output - t_out)
    d_two = norm_back(upstream, row(sg_ref, 1), normed_two, inverse_two)
    d_branch = d_two.astype(BF)
    gdown_acc[...] += dot(inner_active, d_branch, TN)
    d_inner = (dot(d_branch, bdown_ref[...], NT) * slope).astype(BF)
    gup_acc[...] += dot(hidden_active, d_inner, TN)
    d_hidden = d_two + dot(d_inner, bup_ref[...], NT) * hidden_slope
    d_one = norm_back(d_hidden, row(sg_ref, 0), normed_one, inverse_one)
    d1_ref[...] = d_one
    d_attended = d_one.astype(BF)
    gout_acc[...] += dot(ctx_active, d_attended, TN)
    d_context = (dot(d_attended, bo_ref[...], NT) * ctx_slope).astype(BF)
    for j in range(groups):
        dctx_ref[j] = d_context[:, j * width : (j + 1) * width]

    def total(value):
        return jnp.sum(value, axis=0, keepdims=True)

    ggain_ref[0:1, :] += total(d_hidden * normed_one)
    ggain_ref[1:2, :] += total(upstream * normed_two)
    gbias_ref[2:3, :] += total(d_attended.astype(F32))
    gbias_ref[3:4, :] += total(d_hidden)
    gbias_ref[4:5, :] += total(d_branch.astype(F32))
    gbias_ref[5:6, :] += total(upstream)
    gub_ref[...] += total(d_inner.astype(F32))

    @pl.when(step == pl.num_programs(0) - 1)
    def _():
        gout_ref[...] = gout_acc[...].astype(BF)
        gup_ref[...] = gup_acc[...].astype(BF)
        gdown_ref[...] = gdown_acc[...].astype(BF)


def middle(r, x, tx, cot, ctx, tctx, weights, teacher_weights, vectors):
    rows, depth = cot.shape
    ff = weights[1].shape[1]
    tile = min(256, rows)
    groups, unused, width = ctx.shape
    steps = rows // tile
    tall = pl.BlockSpec((tile, depth), lambda i, r: (i, 0))
    of_stream = pl.BlockSpec((tile, depth), lambda i, r: (r[0] * steps + i, 0))
    split_rows = pl.BlockSpec((groups, tile, width), lambda i, r: (0, i, 0))

    def full(shape):
        return pl.BlockSpec(shape, lambda i, r: (0,) * len(shape))

    def full_of(array):
        return full(array.shape)

    out_full = [(depth, depth), (depth, ff), (ff, depth), (2, depth), (6, depth), (1, ff)]
    return pl.pallas_call(
        middle_kernel,
        grid_spec=pltpu.PrefetchScalarGridSpec(
            num_scalar_prefetch=1,
            grid=(steps,),
            in_specs=[of_stream, of_stream, tall, split_rows, split_rows]
            + [full_of(a) for a in weights + teacher_weights + vectors],
            out_specs=[tall, tall, split_rows] + [full(s) for s in out_full],
            scratch_shapes=[pltpu.VMEM(s, F32) for s in out_full[:3]],
        ),
        out_shape=[
            jax.ShapeDtypeStruct((rows, depth), BF),
            jax.ShapeDtypeStruct((rows, depth), F32),
            jax.ShapeDtypeStruct((groups, rows, width), BF),
        ]
        + [jax.ShapeDtypeStruct(s, BF if i < 3 else F32) for i, s in enumerate(out_full)],
        compiler_params=pltpu.CompilerParams(vmem_limit_bytes=VMEM_BYTES),
        name="middle",
    )(r.reshape(1), x, tx, cot, ctx, tctx, *weights, *teacher_weights, *vectors)


def latent_columns(latent, binary_grad):
    matrix = latent.astype(F32)
    grad = binary_grad.astype(F32)
    scale = jnp.sqrt(jnp.mean(matrix * matrix, axis=0, keepdims=True) + 1e-06)
    inner = matrix * (2.0 / scale)
    bent = jnp.tanh(inner)
    slope = 1.0 - bent * bent
    through_scale = jnp.sum(grad * (bent - inner * slope), axis=0, keepdims=True)
    factor = through_scale / (matrix.shape[0] * scale)
    return 2.0 * grad * slope + matrix * factor


def early_latents_kernel(lo, lu, ld, go, gu, gd, oo, ou, od):
    oo[...] = latent_columns(lo[...], go[...])
    ou[...] = latent_columns(lu[...], gu[...])
    od[...] = latent_columns(ld[...], gd[...])


def early_latents(latents, grads):
    steps = 4
    specs = [
        pl.BlockSpec((a.shape[0], a.shape[1] // steps), lambda i: (0, i)) for a in latents
    ]
    return pl.pallas_call(
        early_latents_kernel,
        grid=(steps,),
        in_specs=specs * 2,
        out_specs=specs,
        out_shape=[jax.ShapeDtypeStruct(a.shape, F32) for a in latents],
        compiler_params=pltpu.CompilerParams(vmem_limit_bytes=VMEM_BYTES),
        name="early_latents",
    )(*latents, *grads)


def late_latents_kernel(pairs, latent, *refs):
    grads, out = refs[:pairs], refs[pairs]
    for p in range(pairs):
        columns = slice(p * 128, (p + 1) * 128)
        out[0, :, columns] = latent_columns(latent[0, :, columns], grads[p][0])


def late_latents(latent, grads):
    pairs = len(grads)
    groups, depth, wide = grads[0].shape
    spec = pl.BlockSpec((1, depth, pairs * 128), lambda m, j: (m, 0, j))
    return pl.pallas_call(
        functools.partial(late_latents_kernel, pairs),
        grid=(3, groups),
        in_specs=[spec] + [pl.BlockSpec((1, depth, 128), lambda m, j: (j, 0, m))] * pairs,
        out_specs=spec,
        out_shape=jax.ShapeDtypeStruct(latent.shape, F32),
        compiler_params=pltpu.CompilerParams(vmem_limit_bytes=VMEM_BYTES),
        name="late_latents",
    )(latent, *grads)


def shards(
    tokens,
    teacher_tokens,
    segment_ids,
    cotangent,
    latent_qkv,
    latent_out,
    latent_up,
    latent_down,
    student_gain,
    student_bias,
    student_up_bias,
    teacher_qkv,
    teacher_out,
    teacher_up,
    teacher_down,
    teacher_gain,
    teacher_bias,
    teacher_up_bias,
):
    streams, shard_len, depth = tokens.shape
    blocks = lax.axis_size("blk")
    groups = blocks // streams
    seq = shard_len * blocks
    rows = seq // groups
    width = depth // groups
    s, r = place(groups)
    block = (shard_len, depth)
    gather, swap = Gather(streams, groups, block, BF), Swap(streams, groups, block, BF)
    row_block = (rows, width)
    by_rows = Rows(streams, groups, row_block, BF)
    doc_block = (shard_len // 128, 128)

    def own_columns(matrices):
        return lax.dynamic_slice_in_dim(matrices, r * width, width, axis=2)

    def own_bias(bias):
        return lax.dynamic_slice_in_dim(bias, r * width, width, axis=1)

    latents = [own_columns(latent_qkv), latent_out, latent_up, latent_down]
    taken = [
        tokens,
        segment_ids.reshape((streams,) + doc_block),
        teacher_qkv,
        teacher_out,
    ]
    bin_own, bin_out, bin_up, bin_down, token_blocks, docs, qkv_parts, out_parts = intake(
        Moves(
            gather,
            Gather(streams, groups, doc_block, jnp.int32),
            Spread(teacher_qkv.shape, BF),
            Spread(teacher_out.shape, BF),
        ),
        latents,
        taken,
        1,
    )
    docs = docs.reshape(seq)
    big = docs[streams * shard_len] if groups > 1 else docs[shard_len]
    in_big = docs == big
    stream_tokens = token_blocks.reshape(seq, depth)

    def project(rows_in, matrices, bias):
        q = dot(rows_in, matrices[0]) + own_bias(bias)[0]
        k = dot(rows_in, matrices[1])
        v = dot(rows_in, matrices[2]) + own_bias(bias)[1]
        return jnp.concatenate(
            [(q.astype(BF).astype(F32) * 0.125).astype(BF), k.astype(BF), v.astype(BF)], axis=1
        )

    active = squash(stream_tokens.astype(F32)).astype(BF)
    qkv = project(active, bin_own, student_bias)
    numerators, context, inverse, teacher_blocks, up_parts = attention(
        qkv,
        docs,
        Moves(gather, Spread(teacher_up.shape, BF)),
        [teacher_tokens, teacher_up],
        True,
        2,
        "attention_student",
    )
    teacher_stream = teacher_blocks.reshape(seq, depth)
    full_qkv = own_columns(qkv_parts.transpose(1, 0, 2, 3).reshape(3, depth, depth))
    teacher_own = project(teacher_stream, full_qkv, teacher_bias)
    row_shape = (groups,) + row_block
    teacher_context, cot_blocks, down_parts, ctx_rows = attention(
        teacher_own,
        docs,
        Moves(swap, Spread(teacher_down.shape, BF), by_rows),
        [cotangent, teacher_down, context.reshape(row_shape)],
        False,
        3,
        "attention_teacher",
    )
    (tctx_rows,) = move(
        Moves(by_rows), [teacher_context.reshape(row_shape)], 4, "teacher_context_rows"
    )
    output, d_one, d_context, g_out, g_up, g_down, g_gain, g_bias, g_ub = middle(
        r,
        stream_tokens,
        teacher_stream,
        cot_blocks.reshape(rows, depth),
        ctx_rows,
        tctx_rows,
        [bin_out, bin_up, bin_down],
        [
            out_parts.reshape(-1, depth),
            up_parts.reshape(depth, -1),
            down_parts.reshape(-1, depth),
        ],
        [
            student_gain,
            student_bias,
            student_up_bias.reshape(1, -1),
            teacher_gain,
            teacher_bias,
            teacher_up_bias.reshape(1, -1),
        ],
    )
    small = jnp.concatenate(
        [g_gain, g_bias, g_ub.reshape(-1, depth), jnp.zeros((4, depth), F32)], axis=0
    )
    (d_ctx_rows,) = move(Moves(by_rows), [d_context], 5, "d_context_rows")
    grads = [[g_up], [g_down, g_out]]
    in_kernel = depth % (16 * blocks * lax.axis_size("dp")) == 0
    output_blocks, grad_tokens, early, late, small = attention_back(
        streams,
        groups,
        numerators,
        qkv,
        teacher_own,
        d_ctx_rows.reshape(seq, width),
        context,
        inverse,
        docs,
        in_big,
        small,
        active,
        bin_own,
        d_one,
        token_blocks,
        output.reshape(streams, shard_len, depth),
        grads if in_kernel else [],
        6,
    )
    if not in_kernel:
        early = lax.psum((g_up, g_down, g_out), ("dp", "blk"))
    up_rows = latent_up.shape[1] // depth
    grad_out, grad_up, grad_down = early_latents(
        [latent_out, latent_up, latent_down], [early[2], early[0], early[1]]
    )
    return (
        output_blocks,
        grad_tokens,
        late_latents(latent_qkv, late),
        grad_out,
        grad_up,
        grad_down,
        small[0:2],
        small[2:8],
        small[8 : 8 + up_rows].reshape(-1),
    )


def solution(mesh):
    return jax.shard_map(
        shards,
        mesh=mesh,
        in_specs=(
            P("dp", "blk", None),
            P("dp", "blk", None),
            P("dp", "blk"),
            P("dp", "blk", None),
            P(),
            P(),
            P(),
            P(),
            P(),
            P(),
            P(),
            P(None, "dp", None),
            P("dp", None),
            P("dp", None),
            P("dp", None),
            P(),
            P(),
            P(),
        ),
        out_specs=(P("dp", "blk", None), P("dp", "blk", None), P(), P(), P(), P(), P(), P(), P()),
        check_vma=False,
    )
```

```python
import functools

import jax
import jax.numpy as jnp
from jax import lax
from jax.experimental import pallas as pl
from jax.experimental.pallas import tpu as pltpu
from jax.sharding import PartitionSpec as P

HEADS = 8
BF = jnp.bfloat16
F32 = jnp.float32
LOG2E = 1.4426950408889634
clip_level = 2.5
masked_score = -1e30
VMEM_BYTES = 56 << 20
MESH = pl.DeviceIdType.MESH
NT = (((1,), (1,)), ((), ()))
TN = (((0,), (0,)), ((), ()))


def squash(tensor):
    return clip_level * jnp.tanh(tensor * (1.0 / clip_level))


def gelu_parts(tensor):
    phi = 0.5 * (1.0 + lax.erf(tensor * 0.7071067811865476))
    return tensor * phi, phi


def binarize(matrix):
    column_scale = jnp.sqrt(jnp.mean(matrix * matrix, axis=-2, keepdims=True) + 1e-06)
    return column_scale * jnp.tanh(2.0 * matrix / column_scale)


def layer_norm(tensor, gain_row, shift_row):
    centre = tensor - jnp.mean(tensor, axis=-1, keepdims=True)
    inverse_std = lax.rsqrt(jnp.mean(centre * centre, axis=-1, keepdims=True) + 1e-05)
    normed = centre * inverse_std
    return (normed * gain_row + shift_row, normed, inverse_std)


def norm_back(upstream, gain_row, normed, inverse_std):
    scaled = upstream * gain_row
    return inverse_std * (
        scaled
        - jnp.mean(scaled, axis=-1, keepdims=True)
        - normed * jnp.mean(scaled * normed, axis=-1, keepdims=True)
    )


def dot(a, b, dims=(((1,), (0,)), ((), ()))):
    return lax.dot_general(a, b, dims, preferred_element_type=F32)


def latent_grad(latent, binary_grad):
    matrix = latent.astype(F32)
    unused, pullback = jax.vjp(binarize, matrix)
    return pullback(binary_grad)[0]


def place(groups):
    here = lax.axis_index("blk")
    return here // groups, lax.rem(here, groups)


def greet(peers):
    barrier = pltpu.get_barrier_semaphore()
    for peer in peers:
        pl.semaphore_signal(barrier, inc=1, device_id=peer, device_id_type=MESH)
    pl.semaphore_wait(barrier, len(peers))


def stream_peers(streams, groups):
    s, r = place(groups)
    return [{"blk": lax.rem(s + d, streams) * groups + r} for d in range(1, streams)]


def core_peers(groups):
    s, r = place(groups)
    return [{"blk": s * groups + lax.rem(r + j, groups)} for j in range(1, groups)]


def dp_peers():
    size = lax.axis_size("dp")
    here = lax.axis_index("dp")
    return [{"dp": lax.rem(here + d, size)} for d in range(1, size)]


def unique(jobs):
    peers, kinds = [], []
    for job in jobs:
        for kind, found in job.peers():
            if kind not in kinds:
                kinds.append(kind)
                peers += found
    return peers


def remote(source, target, send, recv, peer):
    return pltpu.make_async_remote_copy(
        src_ref=source,
        dst_ref=target,
        send_sem=send,
        recv_sem=recv,
        device_id=peer,
        device_id_type=MESH,
    )


def dma(count):
    return pltpu.SemaphoreType.DMA((count,))


class Staged:
    def __init__(self, source, target, stage, sems):
        self.load = pltpu.make_async_copy(source, stage, sems.at[0])
        self.store = pltpu.make_async_copy(stage, target, sems.at[1])

    def first(self):
        self.load.start()

    def last(self):
        self.load.wait()
        self.store.start()
        self.store.wait()


class Gather:
    def __init__(self, streams, groups, block, dtype):
        self.streams, self.groups, self.block, self.dtype = streams, groups, block, dtype

    def scratch(self):
        b, g = self.streams, self.groups
        return [dma(b), dma(b), dma(b * g), dma(b * g), pltpu.VMEM(self.block, self.dtype), dma(2)]

    def out_shape(self):
        return jax.ShapeDtypeStruct((self.streams * self.groups,) + self.block, self.dtype)

    def peers(self):
        return [
            ("stream", stream_peers(self.streams, self.groups)),
            ("core", core_peers(self.groups)),
        ]

    def parts(self, source, target, send, recv, share_send, share_recv, stage, sems):
        b, g = self.streams, self.groups
        s, r = place(g)
        peers, cores = stream_peers(b, g), core_peers(g)
        swaps = [
            remote(
                source.at[lax.rem(s + d, b)],
                target.at[r * b + s],
                send.at[d],
                recv.at[d],
                peers[d - 1],
            )
            for d in range(1, b)
        ]
        shares = [
            [
                remote(
                    source.at[s] if d == 0 else target.at[r * b + lax.rem(s + b - d, b)],
                    target.at[r * b + lax.rem(s + b - d, b)],
                    share_send.at[j * b + d],
                    share_recv.at[j * b + d],
                    cores[j - 1],
                )
                for j in range(1, g)
            ]
            for d in range(b)
        ]
        own = Staged(source.at[s], target.at[r * b + s], stage, sems)
        return swaps, shares, own

    def first(self, *refs):
        swaps, shares, own = self.parts(*refs)
        for copy in swaps:
            copy.start()
        own.first()
        for copy in shares[0]:
            copy.start()

    def last(self, *refs):
        swaps, shares, own = self.parts(*refs)
        own.last()
        for d in [1, 3, 2] if self.streams == 4 else range(1, self.streams):
            swaps[d - 1].wait_recv()
            for copy in shares[d]:
                copy.start()
        for row in shares:
            for copy in row:
                copy.wait()
        for copy in swaps:
            copy.wait_send()


class Swap:
    def __init__(self, streams, groups, block, dtype):
        self.streams, self.groups, self.block, self.dtype = streams, groups, block, dtype

    def scratch(self):
        return [dma(self.streams), dma(self.streams), pltpu.VMEM(self.block, self.dtype), dma(2)]

    def out_shape(self):
        return jax.ShapeDtypeStruct((self.streams,) + self.block, self.dtype)

    def peers(self):
        return [("stream", stream_peers(self.streams, self.groups))]

    def parts(self, source, target, send, recv, stage, sems):
        b, g = self.streams, self.groups
        s, r = place(g)
        peers = stream_peers(b, g)
        swaps = [
            remote(source.at[lax.rem(s + d, b)], target.at[s], send.at[d], recv.at[d], peers[d - 1])
            for d in range(1, b)
        ]
        return swaps, Staged(source.at[s], target.at[s], stage, sems)

    def first(self, *refs):
        swaps, own = self.parts(*refs)
        for copy in swaps:
            copy.start()
        own.first()

    def last(self, *refs):
        swaps, own = self.parts(*refs)
        own.last()
        for copy in swaps:
            copy.wait()


class Spread:
    def __init__(self, block, dtype):
        self.block, self.dtype = block, dtype

    def scratch(self):
        size = lax.axis_size("dp")
        return [dma(size), dma(size), pltpu.VMEM(self.block, self.dtype), dma(2)]

    def out_shape(self):
        return jax.ShapeDtypeStruct((lax.axis_size("dp"),) + self.block, self.dtype)

    def peers(self):
        return [("dp", dp_peers())]

    def parts(self, source, target, send, recv, stage, sems):
        here = lax.axis_index("dp")
        copies = [
            remote(source, target.at[here], send.at[d], recv.at[d], peer)
            for d, peer in enumerate(dp_peers(), 1)
        ]
        return copies, Staged(source, target.at[here], stage, sems)

    first = Swap.first
    last = Swap.last


class Tiles:
    def __init__(self, bag, name, groups, pairs, per_owner):
        self.name, self.groups, self.pairs, self.per_owner = name, groups, pairs, per_owner
        count = pairs * per_owner
        bag.add(f"{name}_s", dma(groups * count))
        bag.add(f"{name}_r", dma(groups * count))

    def slot(self, who, pair, at):
        return (who * self.pairs + pair) * self.per_owner + at

    def copy(self, have, source, target, owner, pair, at):
        s, r = place(self.groups)
        return remote(
            source,
            target,
            have[f"{self.name}_s"].at[self.slot(owner, pair, at)],
            have[f"{self.name}_r"].at[self.slot(r, pair, at)],
            {"blk": s * self.groups + owner},
        )

    def own(self, have, source, target, pair, at):
        s, r = place(self.groups)
        return pltpu.make_async_copy(
            source, target, have[f"{self.name}_s"].at[self.slot(r, pair, at)]
        )

    def finish(self, have, source, target):
        s, r = place(self.groups)
        for pair in range(self.pairs):
            for at in range(self.per_owner):
                self.own(have, source, target, pair, at).wait()
                for j in range(1, self.groups):
                    other = lax.rem(r + j, self.groups)
                    remote(
                        source,
                        target,
                        have[f"{self.name}_s"].at[self.slot(other, pair, at)],
                        have[f"{self.name}_r"].at[self.slot(other, pair, at)],
                        {"blk": s * self.groups + other},
                    ).wait()


class Bag:
    def __init__(self):
        self.items = {}

    def add(self, name, item):
        self.items[name] = item

    def bind(self, refs):
        return dict(zip(self.items, refs))


class Reduce:
    def __init__(self, bag, name, streams, groups, shapes, over_cores):
        self.name, self.streams, self.groups = name, streams, groups
        self.size = lax.axis_size("dp")
        self.over_cores = over_cores
        self.count = len(shapes)
        share = self.size * (groups if over_cores else 1)
        self.shapes = [(rows // share, cols) for rows, cols in shapes]
        self.wires = [BF if (c // streams) % 16 == 0 else F32 for c, cols in self.shapes]
        for i, (chunk, cols) in enumerate(self.shapes):
            wire, slim = self.wires[i], chunk // streams
            bag.add(f"{name}half{i}", pltpu.VMEM((self.size, chunk, cols), wire))
            if over_cores:
                bag.add(f"{name}core{i}", pltpu.VMEM((groups - 1, self.size, chunk, cols), wire))
            bag.add(f"{name}dp{i}", pltpu.VMEM((self.size - 1, chunk, cols), wire))
            bag.add(f"{name}cut{i}", pltpu.VMEM((streams, slim, cols), wire))
            bag.add(f"{name}z{i}", pltpu.VMEM((streams - 1, slim, cols), wire))
            bag.add(f"{name}fin{i}", pltpu.VMEM((slim, cols), wire))
            for kind, n in self.sem_counts().items():
                bag.add(f"{name}{kind}s{i}", dma(n))
                bag.add(f"{name}{kind}r{i}", dma(n))
            bag.add(f"{name}local{i}", dma(2))

    def sem_counts(self):
        b, g, d = self.streams, self.groups, self.size
        return {"a": g, "b": d, "c": b, "d": b, "e": d, "f": g}

    def out_shapes(self):
        return [
            jax.ShapeDtypeStruct(
                (self.groups, self.size, self.streams, chunk // self.streams, cols), wire
            )
            for (chunk, cols), wire in zip(self.shapes, self.wires)
        ]

    def bind(self, sources, targets, scratch):
        self.sources, self.targets, self.scratch = sources, targets, scratch

    def get(self, what, i):
        return self.scratch[f"{self.name}{what}{i}"]

    def copies(self, kind, i):
        s, r = place(self.groups)
        here = lax.axis_index("dp")
        b, g, size = self.streams, self.groups, self.size
        send, recv = self.get(kind + "s", i), self.get(kind + "r", i)
        if kind in "af":
            peers = core_peers(g)
        elif kind in "be":
            peers = dp_peers()
        else:
            peers = stream_peers(b, g)
        order = list(enumerate(peers, 1))
        if kind in "cd" and b == 4:
            order = [order[1], order[0], order[2]]
        for d, peer in order:
            if kind == "a":
                pair = self.sources[i].at[lax.rem(r + d, g)], self.get("core", i).at[d - 1]
            elif kind == "b":
                pair = self.get("half", i).at[lax.rem(here + d, size)], self.get("dp", i).at[d - 1]
            elif kind == "c":
                pair = self.get("cut", i).at[lax.rem(s + d, b)], self.get("z", i).at[d - 1]
            elif kind == "d":
                pair = self.get("fin", i), self.targets[i].at[r, here, s]
            elif kind == "e":
                pair = self.targets[i].at[r, here], self.targets[i].at[r, here]
            else:
                pair = self.targets[i].at[r], self.targets[i].at[r]
            yield remote(*pair, send.at[d], recv.at[d], peer)

    def start(self, kind, i):
        for copy in self.copies(kind, i):
            copy.start()

    def arrive(self, kind, i):
        for copy in self.copies(kind, i):
            copy.wait_recv()

    def load(self, i):
        s, r = place(self.groups)
        return pltpu.make_async_copy(
            self.sources[i].at[r], self.get("half", i), self.get("local", i).at[0]
        )

    def keep(self, i):
        s, r = place(self.groups)
        return pltpu.make_async_copy(
            self.get("fin", i),
            self.targets[i].at[r, lax.axis_index("dp"), s],
            self.get("local", i).at[1],
        )

    def core_start(self):
        for i in range(self.count):
            self.start("a", i)
            self.load(i).start()

    def dp_start(self):
        for i in range(self.count):
            if self.over_cores:
                self.load(i).wait()
                self.arrive("a", i)
                half, box, wire = self.get("half", i), self.get("core", i), self.wires[i]
                for p in range(self.size):
                    total = half[p].astype(F32)
                    for j in range(self.groups - 1):
                        total = total + box[j, p].astype(F32)
                    half[p] = total.astype(wire)
            self.start("b", i)

    def z_start(self):
        here = lax.axis_index("dp")
        for i in range(self.count):
            self.arrive("b", i)
            half, box, cut, wire = (
                self.get("half", i),
                self.get("dp", i),
                self.get("cut", i),
                self.wires[i],
            )
            slim = self.shapes[i][0] // self.streams
            for z in range(self.streams):
                at = slice(z * slim, (z + 1) * slim)
                total = half[here, at, :].astype(F32)
                for d in range(self.size - 1):
                    total = total + box[d, at, :].astype(F32)
                cut[z] = total.astype(wire)
            self.start("c", i)

    def z_back(self):
        s, r = place(self.groups)
        for i in range(self.count):
            self.arrive("c", i)
            box = self.get("z", i)
            total = self.get("cut", i)[s].astype(F32)
            for d in range(self.streams - 1):
                total = total + box[d].astype(F32)
            self.get("fin", i)[...] = total.astype(self.wires[i])
            self.keep(i).start()
            self.start("d", i)

    def dp_back(self):
        for i in range(self.count):
            self.keep(i).wait()
            self.arrive("d", i)
            self.start("e", i)

    def core_back(self):
        for i in range(self.count):
            self.arrive("e", i)
            self.start("f", i)

    def end(self):
        for i in range(self.count):
            self.arrive("f", i)
            for kind in "abcdef" if self.over_cores else "bcdef":
                for copy in self.copies(kind, i):
                    copy.wait_send()


class Moves:
    def __init__(self, *jobs, others=()):
        self.jobs, self.others = list(jobs), list(others)
        self.counts = [len(job.scratch()) for job in jobs]

    def scratch(self):
        return [item for job in self.jobs for item in job.scratch()]

    def out_shapes(self):
        return [job.out_shape() for job in self.jobs]

    def spaces(self):
        return [pl.BlockSpec(memory_space=pl.ANY)] * len(self.jobs)

    def each(self, sources, targets, scratch):
        at = 0
        for job, count, source, target in zip(self.jobs, self.counts, sources, targets):
            yield job, (source, target, *scratch[at : at + count])
            at += count

    def first(self, sources, targets, scratch):
        greet(unique(self.jobs + self.others))
        for job, refs in self.each(sources, targets, scratch):
            job.first(*refs)

    def last(self, sources, targets, scratch):
        for job, refs in self.each(sources, targets, scratch):
            job.last(*refs)


def remote_params(collective_id):
    return pltpu.CompilerParams(
        collective_id=collective_id, has_side_effects=True, vmem_limit_bytes=VMEM_BYTES
    )


def binary_columns(latent):
    matrix = latent.astype(F32)
    scale = jnp.sqrt(jnp.mean(matrix * matrix, axis=0, keepdims=True) + 1e-06)
    return (scale * jnp.tanh(matrix * (2.0 / scale))).astype(BF)


def intake_kernel(moves, groups, qkv_ref, out_ref, up_ref, down_ref, *refs):
    count = len(moves.jobs)
    sources = refs[:count]
    own_bin, out_bin, up_bin, down_bin = refs[count : count + 4]
    targets = refs[count + 4 : 2 * count + 4]
    scratch = refs[2 * count + 4 :]
    moves.first(sources, targets, scratch)
    s, r = place(groups)
    width = own_bin.shape[3]
    own = pl.ds(pl.multiple_of(r * width, 128), width)
    for i in range(3):
        own_bin[0, i] = binary_columns(qkv_ref[i, :, own])
    out_bin[...] = binary_columns(out_ref[...])
    for i in range(0, up_ref.shape[1], 512):
        up_bin[:, i : i + 512] = binary_columns(up_ref[:, i : i + 512])
    for i in range(0, down_ref.shape[1], 128):
        down_bin[:, i : i + 128] = binary_columns(down_ref[:, i : i + 128])
    moves.last(sources, targets, scratch)


def intake(moves, groups, latents, arrays, collective_id):
    three, depth, unused = latents[0].shape
    shapes = [(1, three, depth, depth // groups)] + [a.shape for a in latents[1:]]
    vmem = pl.BlockSpec(memory_space=pltpu.VMEM)
    return pl.pallas_call(
        functools.partial(intake_kernel, moves, groups),
        out_shape=[jax.ShapeDtypeStruct(shape, BF) for shape in shapes] + moves.out_shapes(),
        in_specs=[vmem] * 4 + moves.spaces(),
        out_specs=[vmem] * 4 + moves.spaces(),
        scratch_shapes=moves.scratch(),
        compiler_params=remote_params(collective_id),
        name="intake",
    )(*latents, *arrays)


def lanes_of(shape):
    return lax.broadcasted_iota(jnp.int32, shape, 1)


def forward_kernel(
    moves, keep, streams, groups, tile, bag, tiles, x_ref, w_ref, bias_ref, row_ref, *rest
):
    count = len(moves.jobs)
    sources, rest = rest[:count], rest[count:]
    q_ref, k_ref, rows_ref, *rest = rest
    if keep:
        v_ref, e_ref, ctx_ref, inv_ref, active_ref, *rest = rest
    targets, rest = rest[:count], rest[count:]
    have = bag.bind(rest)
    scratch = tuple(have[f"moves{i}"] for i in range(len(moves.scratch())))
    k_aug, v_aug, ctx_all, mask, edges = (
        have["k_aug"],
        have["v_aug"],
        have["ctx_all"],
        have["mask"],
        have["edges"],
    )
    active = active_ref if keep else x_ref
    pair, step = pl.program_id(0), pl.program_id(1)
    pairs, steps = pl.num_programs(0), pl.num_programs(1)
    seq = k_ref.shape[0]
    s, r = place(groups)
    sub = min(256, tile)
    width = w_ref.shape[3]
    n_pairs = ctx_all.shape[0]
    offset = pair * 128 if width == n_pairs * 128 else (r * n_pairs + pair) * 128
    offset = pl.multiple_of(offset, 128)
    home = pl.multiple_of((r * n_pairs + pair) * 128, 128)

    @pl.when((pair == 0) & (step == 0))
    def _():
        moves.first(sources, targets, scratch)
        ids = row_ref[...]
        big_at = long_at(streams, groups, seq)
        big = ids[:, big_at : big_at + 1]
        mask[...] = jnp.where(ids == big, 0.0, masked_score)
        edges[0] = jnp.broadcast_to(ids[:, :sub], (128, sub)).T
        edges[1] = jnp.broadcast_to(ids[:, seq - sub :], (128, sub)).T
        if keep:
            for i in range(0, seq, 256):
                active_ref[i : i + 256, :] = squash(x_ref[i : i + 256, :].astype(F32)).astype(BF)

    @pl.when(step == 0)
    def _():
        columns = pl.ds(offset, 128)

        def project(i, bias):
            matrix = jnp.concatenate(
                [w_ref[d, i, :, columns] for d in range(w_ref.shape[0])], axis=0
            )
            result = dot(active[...], matrix)
            if bias is not None:
                result = result + bias_ref[bias : bias + 1, pl.ds(home, 128)]
            return result.astype(BF)

        low = lanes_of((seq, 128)) < 64
        lane = lanes_of((seq, 128))
        q_ref[...] = (project(0, 0).astype(F32) * 0.125).astype(BF)
        keys = project(1, None)
        k_ref[...] = keys
        keys = keys.astype(F32)
        turned = pltpu.roll(keys, 64, 1)
        k_aug[0] = jnp.where(low, keys, turned).astype(BF)
        k_aug[1] = jnp.where(low, turned, keys).astype(BF)
        values = project(2, 1)
        if keep:
            v_ref[...] = values
        values = values.astype(F32)
        v_aug[0] = jnp.where(low, values, jnp.where(lane < 66, 1.0, 0.0)).astype(BF)
        v_aug[1] = jnp.where(low, jnp.where(lane < 2, 1.0, 0.0), values).astype(BF)

    start = pl.multiple_of(step * tile, tile)

    def body(edge_at):
        low = lanes_of((sub, 128)) < 64
        parts = []
        for at in range(0, tile, sub):
            scaled = q_ref[pl.ds(start + at, sub), :].astype(F32) * LOG2E
            upper = scaled.astype(BF).astype(F32)
            lower = scaled - upper
            parts.append(
                (
                    jnp.where(low, upper, pltpu.roll(lower, 64, 1)).astype(BF),
                    jnp.where(low, pltpu.roll(upper, 64, 1), lower).astype(BF),
                )
            )
        chains = [(at, h) for at in range(0, tile, sub) for h in range(2)]

        def scores_of(at, h):
            scores = dot(parts[at // sub][h], k_aug[h], NT)
            if edge_at is not None and at == (0 if edge_at == 0 else tile - sub):
                return jnp.where(edges[edge_at][:, :1] == row_ref[...], scores, masked_score)
            return jnp.concatenate(
                [
                    scores[:, :sub] + mask[:, :sub],
                    scores[:, sub : seq - sub],
                    scores[:, seq - sub :] + mask[:, seq - sub :],
                ],
                axis=1,
            )

        scores = scores_of(*chains[0])
        results = {}
        for n, (at, h) in enumerate(chains):
            if n + 1 < len(chains):
                later = scores_of(*chains[n + 1])
            peak = jnp.max(scores, axis=1, keepdims=True)
            numerators = jnp.exp2(scores - peak).astype(BF)
            if keep:
                e_ref[h, at : at + sub, :] = numerators
            total = dot(numerators, v_aug[h])
            where_sum = 64 if h == 0 else 0
            inverse = 1.0 / total[:, where_sum : where_sum + 1]
            results[h] = (total * inverse, inverse)
            if n + 1 < len(chains):
                scores = later
            if h == 1:
                done = jnp.where(low, results[0][0], results[1][0]).astype(BF)
                ctx_all[pair, pl.ds(start + at, sub), :] = done
                if keep:
                    ctx_ref[at : at + sub, :] = done
                    inv_ref[at : at + sub, :] = jnp.where(low, results[0][1], results[1][1])

    @pl.when(step == 0)
    def _():
        body(0)

    @pl.when(step == steps - 1)
    def _():
        body(1)

    @pl.when((step > 0) & (step < steps - 1))
    def _():
        body(None)

    owned = seq // groups
    owner = start // owned
    at = lax.rem(step, owned // tile)
    source = ctx_all.at[pair, pl.ds(start, tile)]
    target = rows_ref.at[r, pair, pl.ds(pl.multiple_of(lax.rem(start, owned), tile), tile)]

    @pl.when(owner == r)
    def _():
        tiles.own(have, source, target, pair, at).start()

    @pl.when(owner != r)
    def _():
        tiles.copy(have, source, target, owner, pair, at).start()

    @pl.when((pair == pairs - 1) & (step == steps - 1))
    def _():
        tiles.finish(have, source, target)
        moves.last(sources, targets, scratch)


def long_at(streams, groups, seq):
    shard = seq // (streams * groups)
    return streams * shard if groups > 1 else shard


def attention(x, weights, bias, docs, streams, groups, moves, moved, keep, collective_id, name):
    seq, depth = x.shape
    width = depth // groups
    pairs = width // 128
    tile = 512
    owned = seq // groups
    bag = Bag()
    bag.add("k_aug", pltpu.VMEM((2, seq, 128), BF))
    bag.add("v_aug", pltpu.VMEM((2, seq, 128), BF))
    bag.add("ctx_all", pltpu.VMEM((pairs, seq, 128), BF))
    bag.add("mask", pltpu.VMEM((1, seq), F32))
    bag.add("edges", pltpu.VMEM((2, 256, 128), F32))
    tiles = Tiles(bag, "tiles", groups, pairs, owned // tile)
    for i, item in enumerate(moves.scratch()):
        bag.add(f"moves{i}", item)

    def constant(shape):
        return pl.BlockSpec(shape, lambda p, i: (0,) * len(shape))

    part = pl.BlockSpec((tile, 128), lambda p, i: (i, p))
    whole = pl.BlockSpec((seq, 128), lambda p, i: (0, p))
    any_space = pl.BlockSpec(memory_space=pl.ANY)
    wide = jax.ShapeDtypeStruct((seq, width), BF)
    outs = [whole, whole, any_space]
    shapes = [wide, wide, jax.ShapeDtypeStruct((groups, pairs, owned, 128), BF)]
    if keep:
        outs += [
            whole,
            pl.BlockSpec((2, tile, seq), lambda p, i: (p, i, 0)),
            part,
            part,
            constant((seq, depth)),
        ]
        shapes += [
            wide,
            jax.ShapeDtypeStruct((2 * pairs, seq, seq), BF),
            wide,
            jax.ShapeDtypeStruct((seq, width), F32),
            jax.ShapeDtypeStruct((seq, depth), BF),
        ]
    return pl.pallas_call(
        functools.partial(forward_kernel, moves, keep, streams, groups, tile, bag, tiles),
        grid=(pairs, seq // tile),
        in_specs=[constant(x.shape), constant(weights.shape), constant(bias.shape)]
        + [constant((1, seq))]
        + moves.spaces(),
        out_specs=outs + moves.spaces(),
        out_shape=shapes + moves.out_shapes(),
        scratch_shapes=list(bag.items.values()),
        compiler_params=remote_params(collective_id),
        name=name,
    )(x, weights, bias, docs, *moved)


def split(matrix):
    upper = matrix.astype(BF)
    return upper, (matrix - upper.astype(F32)).astype(BF)


def backward_kernel(
    streams,
    groups,
    tile,
    bag,
    early,
    late,
    e_ref,
    q_ref,
    k_ref,
    v_ref,
    tq_ref,
    tk_ref,
    dc_ref,
    ctx_ref,
    inv_ref,
    row_ref,
    small_ref,
    active_hbm,
    bin_hbm,
    d1_hbm,
    tokens_hbm,
    *rest,
):
    n_early = sum(job.count for job in early)
    sources, rest = rest[:n_early], rest[n_early:]
    grad_ref, *rest = rest
    early_out, rest = rest[:n_early], rest[n_early:]
    late_out, (sum_ref, *rest) = rest[: len(late)], rest[len(late) :]
    have = bag.bind(rest)
    at = 0
    for job in early:
        job.bind(sources[at : at + job.count], early_out[at : at + job.count], have)
        at += job.count
    for job, target in zip(late, late_out):
        job.bind(None, [target], have)

    pair, step = pl.program_id(0), pl.program_id(1)
    pairs, steps = len(late), q_ref.shape[0] // tile
    seq = k_ref.shape[0]
    share = 1.0 / seq
    time = pair * steps + step
    total_time = pairs * steps
    size = lax.axis_size("dp")
    here = lax.axis_index("dp")
    s, r = place(groups)
    rows, depth = d1_hbm.shape
    width = pairs * 128
    v_aug, dk_acc, dv_acc, grams = have["v_aug"], have["dk_acc"], have["dv_acc"], have["grams"]
    dq_all, d_act, active, weights = have["dq_all"], have["d_act"], have["active"], have["weights"]
    d_one, x_rows = have["d_one"], have["x_rows"]
    edges, in_big = have["edges"], have["in_big"]
    along_z, cores, along_dp = stream_peers(streams, groups), core_peers(groups), dp_peers()

    def loads():
        sems = have["load"]
        return [
            pltpu.make_async_copy(active_hbm, active, sems.at[0]),
            pltpu.make_async_copy(bin_hbm, weights, sems.at[1]),
            pltpu.make_async_copy(d1_hbm, d_one, sems.at[2]),
            pltpu.make_async_copy(tokens_hbm.at[pl.ds(r * streams, streams)], x_rows, sems.at[3]),
        ]

    def at_time(when, *work):
        @pl.when(time == when)
        def _():
            for item in work:
                item()

    def begin():
        greet(along_z + cores + along_dp)
        for job in early:
            job.core_start()
        for copy in loads():
            copy.start()
        ids = row_ref[...]
        big_at = long_at(streams, groups, seq)
        big = ids[:, big_at : big_at + 1]
        for n, first in enumerate((0, seq - tile)):
            column = jnp.broadcast_to(ids[:, first : first + tile], (128, tile)).T
            edges[n] = column
            in_big[n] = jnp.where(column == big, 1.0, 0.0)

    def big_rows(ref):
        return jnp.concatenate(
            [
                (ref[:tile, :].astype(F32) * in_big[0]).astype(BF),
                ref[tile : seq - tile, :],
                (ref[seq - tile :, :].astype(F32) * in_big[1]).astype(BF),
            ],
            axis=0,
        )

    at_time(0, begin)
    unit = total_time / 16
    for n, job in enumerate(early):
        for when, work in zip(EARLY_TIMES[n], (job.dp_start, job.z_start, job.z_back, job.dp_back)):
            at_time(int(when * unit), work)
    for p, job in enumerate(late[:-1]):
        first = (p + 1) * steps
        for when, work in zip(LATE_TIMES, (job.dp_start, job.z_start, job.z_back, job.dp_back)):
            at_time(first + when, work)

    @pl.when(step == 0)
    def _():
        lane = lanes_of((seq, 128))
        low = lane < 64
        values = v_ref[...].astype(F32)
        v_aug[0] = jnp.where(low, values, jnp.where(lane < 66, 1.0, 0.0)).astype(BF)
        v_aug[1] = jnp.where(low, jnp.where(lane < 2, 1.0, 0.0), values).astype(BF)
        dk_acc[...] = jnp.zeros_like(dk_acc)
        dv_acc[...] = jnp.zeros_like(dv_acc)
        kb, tkb, qb, tqb = (big_rows(ref) for ref in (k_ref, tk_ref, q_ref, tq_ref))
        same_head = (lax.broadcasted_iota(jnp.int32, (128, 128), 0) < 64) == (
            lanes_of((128, 128)) < 64
        )
        for i, (a, b) in enumerate(((kb, kb), (tkb, kb), (qb, qb), (tqb, qb))):
            gram = jnp.where(same_head, dot(a, b, TN) * share, 0.0)
            grams[2 * i], grams[2 * i + 1] = split(gram)

    start = pl.multiple_of(step * tile, tile)
    rows_here = pl.ds(start, tile)
    lane = lanes_of((tile, 128))
    low = lane < 64

    def body(whole, columns):
        edge = 0 if whole and columns.start == 0 else 1
        q8 = q_ref[rows_here, :]
        tq8 = tq_ref[rows_here, :]
        dc = dc_ref[...].astype(F32)
        inv = inv_ref[...]
        scaled = dc * inv
        product = scaled * ctx_ref[...].astype(F32)
        scaled_low = scaled.astype(BF)
        q_turned = q8.astype(F32).T.astype(BF)
        dc_turned = scaled_low.astype(F32).T.astype(BF)
        d_queries = []
        for h in range(2):
            mine = low if h == 0 else jnp.logical_not(low)
            delta = -jnp.sum(jnp.where(mine, product, 0.0), axis=1, keepdims=True)
            upper = delta.astype(BF).astype(F32)
            first = 64 if h == 0 else 0
            extra = jnp.where(
                lane == first, upper, jnp.where(lane == first + 1, delta - upper, 0.0)
            )
            dc_aug = jnp.where(mine, scaled, extra).astype(BF)
            numerators = e_ref[h]
            d_probs = dot(dc_aug, v_aug[h], NT)
            d_scores = numerators.astype(F32) * d_probs
            if whole:
                q_mine = jnp.where(mine, q8, 0.0).astype(BF)
                tq_mine = jnp.where(mine, tq8, 0.0).astype(BF)
                gap = dot(q_mine, k_ref[columns, :], NT) - dot(tq_mine, tk_ref[columns, :], NT)
                same = jnp.where(edges[edge][:, :1] == row_ref[:, columns], share, 0.0)
                gap = gap * (same * (1.0 - in_big[edge][:, :1]))
                if columns.start == 0:
                    d_scores = jnp.concatenate(
                        [d_scores[:, :tile] + gap, d_scores[:, tile:]], axis=1
                    )
                else:
                    d_scores = jnp.concatenate(
                        [d_scores[:, : seq - tile], d_scores[:, seq - tile :] + gap], axis=1
                    )
            d_scores = d_scores.astype(BF)
            d_queries.append(dot(d_scores, k_ref[...]))
            half = slice(64 * h, 64 * h + 64)
            dk_acc[half, :] += dot(q_turned[half, :], d_scores)
            dv_acc[half, :] += dot(dc_turned[half, :], numerators)
        d_query = jnp.where(low, d_queries[0], d_queries[1])
        qb, tqb = q8, tq8
        if whole:
            qb = (q8.astype(F32) * in_big[edge]).astype(BF)
            tqb = (tq8.astype(F32) * in_big[edge]).astype(BF)
        d_query += dot(qb, grams[0]) + dot(qb, grams[1]) - dot(tqb, grams[2]) - dot(tqb, grams[3])
        dq_all[rows_here, :] = (d_query * 0.125).astype(BF)

    @pl.when(step == 0)
    def _():
        body(True, slice(0, tile))

    @pl.when(step == steps - 1)
    def _():
        body(True, slice(seq - tile, seq))

    @pl.when((step > 0) & (step < steps - 1))
    def _():
        body(False, None)

    def pair_end(p):
        job = late[p]
        kb, tkb = big_rows(k_ref), big_rows(tk_ref)
        d_key = dk_acc[...].T
        d_key += dot(kb, grams[4]) + dot(kb, grams[5]) - dot(tkb, grams[6]) - dot(tkb, grams[7])
        d_value = dv_acc[...].T.astype(BF)
        d_query = dq_all[...]
        d_pair = jnp.concatenate([d_query, d_key.astype(BF), d_value], axis=1)
        if p == 0:
            for copy in loads():
                copy.wait()
        columns = slice(p * 128, (p + 1) * 128)
        bins = jnp.concatenate([weights[0, i, :, columns] for i in range(3)], axis=1)
        if p == 0:
            d_act[...] = dot(d_pair, bins, NT)
        else:
            d_act[...] += dot(d_pair, bins, NT)
        if p == pairs - 1:
            for j in range(1, groups):
                other = pl.multiple_of(lax.rem(r + j, groups) * rows, rows)
                have["outbox"][j - 1] = d_act[pl.ds(other, rows), :].astype(BF)
            for copy in core_copies():
                copy.start()
        partial = dot(active[...], d_pair, TN)
        chunk = depth // size
        half = job.get("half", 0)
        for d in range(size):
            half[d] = partial[d * chunk : (d + 1) * chunk, :].astype(job.wires[0])
        sums = have["sums"]
        sums[0:1, columns] = jnp.sum(d_query.astype(F32), axis=0, keepdims=True)
        sums[1:2, columns] = jnp.sum(d_value.astype(F32), axis=0, keepdims=True)

    def core_copies():
        return [
            remote(
                have["outbox"].at[j - 1],
                have["inbox"].at[j - 1],
                have["core_s"].at[j],
                have["core_r"].at[j],
                cores[j - 1],
            )
            for j in range(1, groups)
        ]

    def small_copies(stage, peers, base):
        return [
            remote(
                have["small"].at[stage],
                have["small_box"].at[base + d],
                have["small_s"].at[base + d],
                have["small_r"].at[base + d],
                peer,
            )
            for d, peer in enumerate(peers)
        ]

    def small_start(stage, peers, base):
        for copy in small_copies(stage, peers, base):
            copy.start()

    def small_sum(stage, peers, base):
        for copy in small_copies(stage, peers, base):
            copy.wait_recv()
        total = have["small"][stage]
        for d in range(len(peers)):
            total = total + have["small_box"][base + d]
        return total

    for p in range(pairs - 1):

        @pl.when((pair == p) & (step == steps - 1))
        def _():
            pair_end(p)

    @pl.when(time == total_time - 1)
    def _():
        pair_end(pairs - 1)
        last = late[-1]
        last.dp_start()
        small = have["small"]
        small[0] = small_ref[...]
        for i in range(2):
            vector = have["sums"][i : i + 1, :]
            small[0, 2 + i : 3 + i, :] = jnp.concatenate(
                [jnp.where(r == j, vector, 0.0) for j in range(groups)], axis=1
            )
        small_start(0, along_dp, 0)
        for copy in core_copies():
            copy.wait_recv()
        shard = rows // streams
        back_copies = []
        blocks = have["blocks"]
        order = [2, 1, 3] if streams == 4 else list(range(1, streams))
        for d in order + [0]:
            target = lax.rem(s + d, streams)
            here_rows = pl.ds(pl.multiple_of(target * shard, shard), shard)
            bent = jnp.tanh(x_rows[target].astype(F32) * (1.0 / clip_level))
            total = d_act[pl.ds(pl.multiple_of(r * rows + target * shard, shard), shard), :]
            for j in range(groups - 1):
                total = total + have["inbox"][j, here_rows, :].astype(F32)
            blocks[target] = (d_one[here_rows, :] + total * (1.0 - bent * bent)).astype(BF)
            if d:
                copy = remote(
                    blocks.at[target],
                    grad_ref.at[s],
                    have["grad_s"].at[d],
                    have["grad_r"].at[d],
                    along_z[d - 1],
                )
            else:
                copy = pltpu.make_async_copy(blocks.at[s], grad_ref.at[s], have["grad_s"].at[0])
            copy.start()
            back_copies.append(copy)
        for job in early[:1]:
            job.core_back()
        last.z_start()
        small[1] = small_sum(0, along_dp, 0)
        small_start(1, along_z, size)
        for job in late[:-1]:
            job.core_back()
        last.z_back()
        for job in early[1:]:
            job.core_back()
        small[2] = small_sum(1, along_z, size)
        small_start(2, cores, size + streams)
        last.dp_back()
        sum_ref[...] = small_sum(2, cores, size + streams)
        last.core_back()
        for copy in back_copies:
            copy.wait()
        for job in early + late:
            job.end()
        for copy in (
            core_copies()
            + small_copies(0, along_dp, 0)
            + small_copies(1, along_z, size)
            + small_copies(2, cores, size + streams)
        ):
            copy.wait_send()


EARLY_TIMES = ((1, 7, 10, 12), (2, 11, 13, 15))
LATE_TIMES = (0, 3, 5, 7)


def attention_back(
    streams,
    groups,
    numerators,
    queries,
    keys,
    values,
    teacher_queries,
    teacher_keys,
    d_context,
    context,
    inverse,
    docs,
    small,
    active,
    bin_own,
    d_one,
    tokens,
    early_arrays,
    collective_id,
):
    seq, width = queries.shape
    pairs = width // 128
    tile = 256
    rows, depth = d_one.shape
    size = lax.axis_size("dp")
    shard = rows // streams
    bag = Bag()
    bag.add("v_aug", pltpu.VMEM((2, seq, 128), BF))
    bag.add("dk_acc", pltpu.VMEM((128, seq), F32))
    bag.add("dv_acc", pltpu.VMEM((128, seq), F32))
    bag.add("grams", pltpu.VMEM((8, 128, 128), BF))
    bag.add("dq_all", pltpu.VMEM((seq, 128), BF))
    bag.add("d_act", pltpu.VMEM((seq, depth), F32))
    bag.add("active", pltpu.VMEM((seq, depth), BF))
    bag.add("weights", pltpu.VMEM((1, 3, depth, width), BF))
    bag.add("d_one", pltpu.VMEM((rows, depth), F32))
    bag.add("x_rows", pltpu.VMEM((streams, shard, depth), BF))
    bag.add("load", dma(4))
    bag.add("sums", pltpu.VMEM((8, width), F32))
    bag.add("outbox", pltpu.VMEM((groups - 1, rows, depth), BF))
    bag.add("inbox", pltpu.VMEM((groups - 1, rows, depth), BF))
    bag.add("core_s", dma(groups))
    bag.add("core_r", dma(groups))
    bag.add("blocks", pltpu.VMEM((streams, shard, depth), BF))
    bag.add("grad_s", dma(streams))
    bag.add("grad_r", dma(streams))
    count = size + streams + groups
    bag.add("small", pltpu.VMEM((3,) + small.shape, F32))
    bag.add("small_box", pltpu.VMEM((count,) + small.shape, F32))
    bag.add("small_s", dma(count))
    bag.add("small_r", dma(count))
    bag.add("edges", pltpu.VMEM((2, tile, 128), F32))
    bag.add("in_big", pltpu.VMEM((2, tile, 128), F32))
    early, flat = [], []
    for n, arrays in enumerate(early_arrays):
        job = Reduce(bag, f"early{n}", streams, groups, [a.shape for a in arrays], True)
        early.append(job)
        flat += [
            a.reshape(groups, size, chunk, cols) for a, (chunk, cols) in zip(arrays, job.shapes)
        ]
    late = [
        Reduce(bag, f"late{p}", streams, groups, [(depth, 3 * 128)], False) for p in range(pairs)
    ]
    part = pl.BlockSpec((tile, 128), lambda p, i: (i, p))
    any_space = pl.BlockSpec(memory_space=pl.ANY)

    whole = pl.BlockSpec((seq, 128), lambda p, i: (0, p))

    def constant(shape):
        return pl.BlockSpec(shape, lambda p, i: (0,) * len(shape))

    early_shapes = [shape for job in early for shape in job.out_shapes()]
    late_shapes = [shape for job in late for shape in job.out_shapes()]
    results = pl.pallas_call(
        functools.partial(backward_kernel, streams, groups, tile, bag, early, late),
        grid=(pairs, seq // tile),
        in_specs=[
            pl.BlockSpec((2, tile, seq), lambda p, i: (p, i, 0)),
            whole,
            whole,
            whole,
            whole,
            whole,
            part,
            part,
            part,
            constant((1, seq)),
            constant(small.shape),
        ]
        + [any_space] * (4 + len(flat)),
        out_specs=[any_space] * (1 + len(early_shapes) + len(late_shapes))
        + [constant(small.shape)],
        out_shape=[jax.ShapeDtypeStruct((streams, shard, depth), BF)]
        + early_shapes
        + late_shapes
        + [jax.ShapeDtypeStruct(small.shape, F32)],
        scratch_shapes=list(bag.items.values()),
        compiler_params=remote_params(collective_id),
        name="attention_back",
    )(
        numerators,
        queries,
        keys,
        values,
        teacher_queries,
        teacher_keys,
        d_context,
        context,
        inverse,
        docs,
        small,
        active,
        bin_own,
        d_one,
        tokens,
        *flat,
    )
    grad_tokens, *rest = results
    early_sums = rest[: len(flat)]
    late_sums = rest[len(flat) : -1]
    shapes = [a.shape for arrays in early_arrays for a in arrays]
    return (
        grad_tokens,
        [e.reshape(shape) for e, shape in zip(early_sums, shapes)],
        [l.reshape(groups, depth, 3 * 128) for l in late_sums],
        rest[-1],
    )


def middle_kernel(
    streams,
    groups,
    bag,
    tiles,
    x_ref,
    tx_ref,
    cot_ref,
    ctx_ref,
    tctx_ref,
    bo_ref,
    bup_ref,
    bdown_ref,
    to_ref,
    tup_ref,
    tdown_ref,
    sg_ref,
    sb_ref,
    sub_ref,
    tg_ref,
    tb_ref,
    tub_ref,
    out_ref,
    d1_ref,
    dctx_ref,
    gout_ref,
    gup_ref,
    gdown_ref,
    ggain_ref,
    gbias_ref,
    gub_ref,
    *rest,
):
    have = bag.bind(rest)
    gout_acc, gup_acc, gdown_acc = have["gout"], have["gup"], have["gdown"]
    out_box, d_box = have["out_box"], have["d_box"]
    step = pl.program_id(0)
    steps = pl.num_programs(0)
    width = ctx_ref.shape[1] * 128
    tile, depth = cot_ref.shape
    n_steps = out_box.shape[0]
    shard = n_steps * tile // streams
    s, r = place(groups)
    along_z = stream_peers(streams, groups)
    turned = row_tile(step, n_steps, streams, groups)
    start = pl.multiple_of(turned * tile, tile)

    @pl.when(step == 0)
    def _():
        greet(along_z + core_peers(groups))

    @pl.when(step == 0)
    def _():
        for ref in (gout_acc, gup_acc, gdown_acc, ggain_ref, gbias_ref, gub_ref):
            ref[...] = jnp.zeros_like(ref)

    def row(ref, i):
        return ref[i : i + 1, :]

    pieces = [(j, p) for j in range(groups) for p in range(ctx_ref.shape[1])]
    tctx = jnp.concatenate([tctx_ref[j, p] for j, p in pieces], axis=1)
    t_att = dot(tctx, to_ref[...]) + row(tb_ref, 2)
    t_hidden = layer_norm(tx_ref[...].astype(F32) + t_att, row(tg_ref, 0), row(tb_ref, 3))[0]
    t_inner = gelu_parts(dot(t_hidden.astype(BF), tup_ref[...]) + tub_ref[...])[0]
    t_out = layer_norm(
        t_hidden + dot(t_inner.astype(BF), tdown_ref[...]) + row(tb_ref, 4),
        row(tg_ref, 1),
        row(tb_ref, 5),
    )[0]

    context = jnp.concatenate([ctx_ref[j, p] for j, p in pieces], axis=1).astype(F32)
    bent = jnp.tanh(context * (1.0 / clip_level))
    ctx_active = (clip_level * bent).astype(BF)
    ctx_slope = 1.0 - bent * bent
    attended = dot(ctx_active, bo_ref[...]) + row(sb_ref, 2)
    hidden, normed_one, inverse_one = layer_norm(
        x_ref[...].astype(F32) + attended, row(sg_ref, 0), row(sb_ref, 3)
    )
    bent = jnp.tanh(hidden * (1.0 / clip_level))
    hidden_active = (clip_level * bent).astype(BF)
    hidden_slope = 1.0 - bent * bent
    inner_pre = dot(hidden_active, bup_ref[...]) + sub_ref[...]
    inner_act, phi = gelu_parts(inner_pre)
    bent = jnp.tanh(inner_act * (1.0 / clip_level))
    inner_active = (clip_level * bent).astype(BF)
    slope = (1.0 - bent * bent) * (
        phi + inner_pre * jnp.exp(-0.5 * inner_pre * inner_pre) * 0.3989422804014327
    )
    branch = dot(inner_active, bdown_ref[...]) + row(sb_ref, 4)
    output, normed_two, inverse_two = layer_norm(hidden + branch, row(sg_ref, 1), row(sb_ref, 5))
    out_box[step] = output.astype(BF)
    per_tile = tile // shard
    for n in range(per_tile):
        block = turned * per_tile + n
        source = out_box.at[step, pl.ds(n * shard, shard)]

        @pl.when(block == s)
        def _():
            pltpu.make_async_copy(source, out_ref.at[s], have["out_s"].at[s]).start()

        @pl.when(block != s)
        def _():
            remote(
                source,
                out_ref.at[s],
                have["out_s"].at[block],
                have["out_r"].at[s],
                {"blk": block * groups + r},
            ).start()

    upstream = cot_ref[...].astype(F32) + 0.5 * (output - t_out)
    d_two = norm_back(upstream, row(sg_ref, 1), normed_two, inverse_two)
    d_branch = d_two.astype(BF)
    gdown_acc[...] += dot(inner_active, d_branch, TN)
    d_inner = (dot(d_branch, bdown_ref[...], NT) * slope).astype(BF)
    gup_acc[...] += dot(hidden_active, d_inner, TN)
    d_hidden = d_two + dot(d_inner, bup_ref[...], NT) * hidden_slope
    d_one = norm_back(d_hidden, row(sg_ref, 0), normed_one, inverse_one)
    d1_ref[...] = d_one
    d_attended = d_one.astype(BF)
    gout_acc[...] += dot(ctx_active, d_attended, TN)
    d_context = (dot(d_attended, bo_ref[...], NT) * ctx_slope).astype(BF)
    place_rows = pl.ds(pl.multiple_of(r * n_steps * tile + start, tile), tile)
    for j in range(groups):
        d_box[step, j] = d_context[:, j * width : (j + 1) * width]
        piece, target = d_box.at[step, j], dctx_ref.at[place_rows]

        @pl.when(r == j)
        def _():
            tiles.own(have, piece, target, 0, step).start()

        @pl.when(r != j)
        def _():
            tiles.copy(have, piece, target, j, 0, step).start()


    def total(value):
        return jnp.sum(value, axis=0, keepdims=True)

    ggain_ref[0:1, :] += total(d_hidden * normed_one)
    ggain_ref[1:2, :] += total(upstream * normed_two)
    gbias_ref[2:3, :] += total(d_attended.astype(F32))
    gbias_ref[3:4, :] += total(d_hidden)
    gbias_ref[4:5, :] += total(d_branch.astype(F32))
    gbias_ref[5:6, :] += total(upstream)
    gub_ref[...] += total(d_inner.astype(F32))

    @pl.when(step == steps - 1)
    def _():
        tiles.finish(have, d_box.at[0, 0], dctx_ref.at[place_rows])
        source = out_box.at[0, pl.ds(0, shard)]
        pltpu.make_async_copy(source, out_ref.at[s], have["out_s"].at[s]).wait()
        for d, peer in enumerate(along_z, 1):
            block = lax.rem(s + d, streams)
            remote(
                source, out_ref.at[block], have["out_s"].at[block], have["out_r"].at[block], peer
            ).wait()
        gout_ref[...] = gout_acc[...].astype(BF)
        gup_ref[...] = gup_acc[...].astype(BF)
        gdown_ref[...] = gdown_acc[...].astype(BF)


def row_tile(step, steps, streams, groups):
    s, r = place(groups)
    return lax.rem(s // (streams // steps) + 1 + step, steps)


def middle(streams, groups, x, tx, cot, ctx, tctx, weights, teacher_weights, vectors, collective_id):
    rows, depth = cot.shape
    ff = weights[1].shape[1]
    tile = min(256, rows)
    pairs = ctx.shape[1]
    width = pairs * 128
    steps = rows // tile
    shard = rows // streams

    def turn(i):
        return row_tile(i, steps, streams, groups)

    def stream_tile(i):
        return lax.rem(lax.axis_index("blk"), groups) * steps + turn(i)

    tall = pl.BlockSpec((tile, depth), lambda i: (turn(i), 0))
    of_stream = pl.BlockSpec((tile, depth), lambda i: (stream_tile(i), 0))
    split_rows = pl.BlockSpec((groups, pairs, tile, 128), lambda i: (0, 0, turn(i), 0))
    any_space = pl.BlockSpec(memory_space=pl.ANY)

    def full(shape):
        return pl.BlockSpec(shape, lambda i: (0,) * len(shape))

    out_full = [(depth, depth), (depth, ff), (ff, depth), (2, depth), (6, depth), (1, ff)]
    bag = Bag()
    for name, shape in zip(("gout", "gup", "gdown"), out_full):
        bag.add(name, pltpu.VMEM(shape, F32))
    bag.add("out_box", pltpu.VMEM((steps, tile, depth), BF))
    bag.add("d_box", pltpu.VMEM((steps, groups, tile, width), BF))
    bag.add("out_s", dma(streams))
    bag.add("out_r", dma(streams))
    tiles = Tiles(bag, "tiles", groups, 1, steps)
    return pl.pallas_call(
        functools.partial(middle_kernel, streams, groups, bag, tiles),
        grid=(steps,),
        in_specs=[of_stream, of_stream, tall, split_rows, split_rows]
        + [full(a.shape) for a in weights + teacher_weights + vectors],
        out_specs=[any_space, tall, any_space] + [full(s) for s in out_full],
        out_shape=[
            jax.ShapeDtypeStruct((streams, shard, depth), BF),
            jax.ShapeDtypeStruct((rows, depth), F32),
            jax.ShapeDtypeStruct((rows * groups, width), BF),
        ]
        + [jax.ShapeDtypeStruct(s, BF if i < 3 else F32) for i, s in enumerate(out_full)],
        scratch_shapes=list(bag.items.values()),
        compiler_params=remote_params(collective_id),
        name="middle",
    )(x, tx, cot, ctx, tctx, *weights, *teacher_weights, *vectors)


def latent_columns(latent, binary_grad):
    matrix = latent.astype(F32)
    grad = binary_grad.astype(F32)
    scale = jnp.sqrt(jnp.mean(matrix * matrix, axis=0, keepdims=True) + 1e-06)
    inner = matrix * (2.0 / scale)
    bent = jnp.tanh(inner)
    slope = 1.0 - bent * bent
    through_scale = jnp.sum(grad * (bent - inner * slope), axis=0, keepdims=True)
    factor = through_scale / (matrix.shape[0] * scale)
    return 2.0 * grad * slope + matrix * factor


def early_latents_kernel(lo, lu, ld, go, gu, gd, oo, ou, od):
    oo[...] = latent_columns(lo[...], go[...])
    ou[...] = latent_columns(lu[...], gu[...])
    od[...] = latent_columns(ld[...], gd[...])


def early_latents(latents, grads):
    steps = 4
    specs = [
        pl.BlockSpec((a.shape[0], a.shape[1] // steps), lambda i: (0, i)) for a in latents
    ]
    return pl.pallas_call(
        early_latents_kernel,
        grid=(steps,),
        in_specs=specs * 2,
        out_specs=specs,
        out_shape=[jax.ShapeDtypeStruct(a.shape, F32) for a in latents],
        compiler_params=pltpu.CompilerParams(vmem_limit_bytes=VMEM_BYTES),
        name="early_latents",
    )(*latents, *grads)


def late_latents_kernel(pairs, latent, *refs):
    grads, out = refs[:pairs], refs[pairs]
    for p in range(pairs):
        columns = slice(p * 128, (p + 1) * 128)
        out[0, :, columns] = latent_columns(latent[0, :, columns], grads[p][0])


def late_latents(latent, grads):
    pairs = len(grads)
    groups, depth, wide = grads[0].shape
    spec = pl.BlockSpec((1, depth, pairs * 128), lambda m, j: (m, 0, j))
    return pl.pallas_call(
        functools.partial(late_latents_kernel, pairs),
        grid=(3, groups),
        in_specs=[spec] + [pl.BlockSpec((1, depth, 128), lambda m, j: (j, 0, m))] * pairs,
        out_specs=spec,
        out_shape=jax.ShapeDtypeStruct(latent.shape, F32),
        compiler_params=pltpu.CompilerParams(vmem_limit_bytes=VMEM_BYTES),
        name="late_latents",
    )(latent, *grads)


def shards(
    tokens,
    teacher_tokens,
    segment_ids,
    cotangent,
    latent_qkv,
    latent_out,
    latent_up,
    latent_down,
    student_gain,
    student_bias,
    student_up_bias,
    teacher_qkv,
    teacher_out,
    teacher_up,
    teacher_down,
    teacher_gain,
    teacher_bias,
    teacher_up_bias,
):
    streams, shard_len, depth = tokens.shape
    blocks = lax.axis_size("blk")
    groups = blocks // streams
    seq = shard_len * blocks
    rows = seq // groups
    block = (shard_len, depth)
    gather, swap = Gather(streams, groups, block, BF), Swap(streams, groups, block, BF)
    doc_block = (shard_len // 128, 128)
    bin_own, bin_out, bin_up, bin_down, token_blocks, docs, qkv_parts = intake(
        Moves(
            gather,
            Gather(streams, groups, doc_block, jnp.int32),
            Spread(teacher_qkv.shape, BF),
        ),
        groups,
        [latent_qkv, latent_out, latent_up, latent_down],
        [tokens, segment_ids.reshape((streams,) + doc_block), teacher_qkv],
        1,
    )
    docs = docs.reshape(1, seq).astype(F32)
    stream_tokens = token_blocks.reshape(seq, depth)
    (
        queries,
        keys,
        ctx_rows,
        values,
        numerators,
        context,
        inverse,
        active,
        teacher_blocks,
        up_parts,
        out_parts,
    ) = attention(
        stream_tokens,
        bin_own,
        student_bias,
        docs,
        streams,
        groups,
        Moves(gather, Spread(teacher_up.shape, BF), Spread(teacher_out.shape, BF)),
        [teacher_tokens, teacher_up, teacher_out],
        True,
        2,
        "attention_student",
    )
    teacher_stream = teacher_blocks.reshape(seq, depth)
    teacher_queries, teacher_keys, tctx_rows, cot_blocks, down_parts = attention(
        teacher_stream,
        qkv_parts,
        teacher_bias,
        docs,
        streams,
        groups,
        Moves(swap, Spread(teacher_down.shape, BF), others=[gather]),
        [cotangent, teacher_down],
        False,
        3,
        "attention_teacher",
    )
    output, d_one, d_context, g_out, g_up, g_down, g_gain, g_bias, g_ub = middle(
        streams,
        groups,
        stream_tokens,
        teacher_stream,
        cot_blocks.reshape(rows, depth),
        ctx_rows,
        tctx_rows,
        [bin_out, bin_up, bin_down],
        [
            out_parts.reshape(-1, depth),
            up_parts.reshape(depth, -1),
            down_parts.reshape(-1, depth),
        ],
        [
            student_gain,
            student_bias,
            student_up_bias.reshape(1, -1),
            teacher_gain,
            teacher_bias,
            teacher_up_bias.reshape(1, -1),
        ],
        4,
    )
    small = jnp.concatenate(
        [g_gain, g_bias, g_ub.reshape(-1, depth), jnp.zeros((4, depth), F32)], axis=0
    )
    grads = [[g_up], [g_down, g_out]]
    in_kernel = depth % (16 * blocks * lax.axis_size("dp")) == 0
    grad_tokens, early, late, small = attention_back(
        streams,
        groups,
        numerators,
        queries,
        keys,
        values,
        teacher_queries,
        teacher_keys,
        d_context,
        context,
        inverse,
        docs,
        small,
        active,
        bin_own,
        d_one,
        token_blocks,
        grads if in_kernel else [],
        6,
    )
    if not in_kernel:
        early = lax.psum((g_up, g_down, g_out), ("dp", "blk"))
    up_rows = latent_up.shape[1] // depth
    grad_out, grad_up, grad_down = early_latents(
        [latent_out, latent_up, latent_down], [early[2], early[0], early[1]]
    )
    return (
        output,
        grad_tokens,
        late_latents(latent_qkv, late),
        grad_out,
        grad_up,
        grad_down,
        small[0:2],
        small[2:8],
        small[8 : 8 + up_rows].reshape(-1),
    )


def solution(mesh):
    return jax.shard_map(
        shards,
        mesh=mesh,
        in_specs=(
            P("dp", "blk", None),
            P("dp", "blk", None),
            P("dp", "blk"),
            P("dp", "blk", None),
            P(),
            P(),
            P(),
            P(),
            P(),
            P(),
            P(),
            P(None, "dp", None),
            P("dp", None),
            P("dp", None),
            P("dp", None),
            P(),
            P(),
            P(),
        ),
        out_specs=(P("dp", "blk", None), P("dp", "blk", None), P(), P(), P(), P(), P(), P(), P()),
        check_vma=False,
    )
```

```python
import functools

import jax
import jax.numpy as jnp
from jax import lax
from jax.experimental import pallas as pl
from jax.experimental.pallas import tpu as pltpu
from jax.sharding import PartitionSpec as P

HEADS = 8
BF = jnp.bfloat16
F32 = jnp.float32
LOG2E = 1.4426950408889634
clip_level = 2.5
masked_score = -1e30
VMEM_BYTES = 56 << 20
MESH = pl.DeviceIdType.MESH
NT = (((1,), (1,)), ((), ()))
TN = (((0,), (0,)), ((), ()))


def squash(tensor):
    return clip_level * jnp.tanh(tensor * (1.0 / clip_level))


def gelu_parts(tensor):
    phi = 0.5 * (1.0 + lax.erf(tensor * 0.7071067811865476))
    return tensor * phi, phi


def binarize(matrix):
    column_scale = jnp.sqrt(jnp.mean(matrix * matrix, axis=-2, keepdims=True) + 1e-06)
    return column_scale * jnp.tanh(2.0 * matrix / column_scale)


def layer_norm(tensor, gain_row, shift_row):
    centre = tensor - jnp.mean(tensor, axis=-1, keepdims=True)
    inverse_std = lax.rsqrt(jnp.mean(centre * centre, axis=-1, keepdims=True) + 1e-05)
    normed = centre * inverse_std
    return (normed * gain_row + shift_row, normed, inverse_std)


def norm_back(upstream, gain_row, normed, inverse_std):
    scaled = upstream * gain_row
    return inverse_std * (
        scaled
        - jnp.mean(scaled, axis=-1, keepdims=True)
        - normed * jnp.mean(scaled * normed, axis=-1, keepdims=True)
    )


def dot(a, b, dims=(((1,), (0,)), ((), ()))):
    return lax.dot_general(a, b, dims, preferred_element_type=F32)


def latent_grad(latent, binary_grad):
    matrix = latent.astype(F32)
    unused, pullback = jax.vjp(binarize, matrix)
    return pullback(binary_grad)[0]


def place(groups):
    here = lax.axis_index("blk")
    return here // groups, lax.rem(here, groups)


def greet(peers):
    barrier = pltpu.get_barrier_semaphore()
    for peer in peers:
        pl.semaphore_signal(barrier, inc=1, device_id=peer, device_id_type=MESH)
    pl.semaphore_wait(barrier, len(peers))


def stream_peers(streams, groups):
    s, r = place(groups)
    return [{"blk": lax.rem(s + d, streams) * groups + r} for d in range(1, streams)]


def core_peers(groups):
    s, r = place(groups)
    return [{"blk": s * groups + lax.rem(r + j, groups)} for j in range(1, groups)]


def dp_peers():
    size = lax.axis_size("dp")
    here = lax.axis_index("dp")
    return [{"dp": lax.rem(here + d, size)} for d in range(1, size)]


def unique(jobs):
    peers, kinds = [], []
    for job in jobs:
        for kind, found in job.peers():
            if kind not in kinds:
                kinds.append(kind)
                peers += found
    return peers


def remote(source, target, send, recv, peer):
    return pltpu.make_async_remote_copy(
        src_ref=source,
        dst_ref=target,
        send_sem=send,
        recv_sem=recv,
        device_id=peer,
        device_id_type=MESH,
    )


def dma(count):
    return pltpu.SemaphoreType.DMA((count,))


class Staged:
    def __init__(self, source, target, stage, sems):
        self.load = pltpu.make_async_copy(source, stage, sems.at[0])
        self.store = pltpu.make_async_copy(stage, target, sems.at[1])

    def first(self):
        self.load.start()

    def last(self):
        self.load.wait()
        self.store.start()
        self.store.wait()


class Gather:
    def __init__(self, streams, groups, block, dtype):
        self.streams, self.groups, self.block, self.dtype = streams, groups, block, dtype

    def scratch(self):
        b, g = self.streams, self.groups
        return [dma(b), dma(b), dma(b * g), dma(b * g), pltpu.VMEM(self.block, self.dtype), dma(2)]

    def out_shape(self):
        return jax.ShapeDtypeStruct((self.streams * self.groups,) + self.block, self.dtype)

    def peers(self):
        return [
            ("stream", stream_peers(self.streams, self.groups)),
            ("core", core_peers(self.groups)),
        ]

    def parts(self, source, target, send, recv, share_send, share_recv, stage, sems):
        b, g = self.streams, self.groups
        s, r = place(g)
        peers, cores = stream_peers(b, g), core_peers(g)
        swaps = [
            remote(
                source.at[lax.rem(s + d, b)],
                target.at[r * b + s],
                send.at[d],
                recv.at[d],
                peers[d - 1],
            )
            for d in range(1, b)
        ]
        shares = [
            [
                remote(
                    source.at[s] if d == 0 else target.at[r * b + lax.rem(s + b - d, b)],
                    target.at[r * b + lax.rem(s + b - d, b)],
                    share_send.at[j * b + d],
                    share_recv.at[j * b + d],
                    cores[j - 1],
                )
                for j in range(1, g)
            ]
            for d in range(b)
        ]
        own = Staged(source.at[s], target.at[r * b + s], stage, sems)
        return swaps, shares, own

    def first(self, *refs):
        swaps, shares, own = self.parts(*refs)
        for copy in swaps:
            copy.start()
        own.first()
        for copy in shares[0]:
            copy.start()

    def middle(self, *refs):
        swaps, shares, own = self.parts(*refs)
        for d in [1, 3, 2] if self.streams == 4 else range(1, self.streams):
            swaps[d - 1].wait_recv()
            for copy in shares[d]:
                copy.start()

    def last(self, *refs):
        swaps, shares, own = self.parts(*refs)
        own.last()
        for row in shares:
            for copy in row:
                copy.wait()
        for copy in swaps:
            copy.wait_send()


class Swap:
    def __init__(self, streams, groups, block, dtype):
        self.streams, self.groups, self.block, self.dtype = streams, groups, block, dtype

    def scratch(self):
        return [dma(self.streams), dma(self.streams), pltpu.VMEM(self.block, self.dtype), dma(2)]

    def out_shape(self):
        return jax.ShapeDtypeStruct((self.streams,) + self.block, self.dtype)

    def peers(self):
        return [("stream", stream_peers(self.streams, self.groups))]

    def parts(self, source, target, send, recv, stage, sems):
        b, g = self.streams, self.groups
        s, r = place(g)
        peers = stream_peers(b, g)
        swaps = [
            remote(source.at[lax.rem(s + d, b)], target.at[s], send.at[d], recv.at[d], peers[d - 1])
            for d in range(1, b)
        ]
        return swaps, Staged(source.at[s], target.at[s], stage, sems)

    def first(self, *refs):
        swaps, own = self.parts(*refs)
        for copy in swaps:
            copy.start()
        own.first()

    def last(self, *refs):
        swaps, own = self.parts(*refs)
        own.last()
        for copy in swaps:
            copy.wait()


class Spread:
    def __init__(self, block, dtype):
        self.block, self.dtype = block, dtype

    def scratch(self):
        size = lax.axis_size("dp")
        return [dma(size), dma(size), pltpu.VMEM(self.block, self.dtype), dma(2)]

    def out_shape(self):
        return jax.ShapeDtypeStruct((lax.axis_size("dp"),) + self.block, self.dtype)

    def peers(self):
        return [("dp", dp_peers())]

    def parts(self, source, target, send, recv, stage, sems):
        here = lax.axis_index("dp")
        copies = [
            remote(source, target.at[here], send.at[d], recv.at[d], peer)
            for d, peer in enumerate(dp_peers(), 1)
        ]
        return copies, Staged(source, target.at[here], stage, sems)

    first = Swap.first
    last = Swap.last


class Tiles:
    def __init__(self, bag, name, groups, pairs, per_owner):
        self.name, self.groups, self.pairs, self.per_owner = name, groups, pairs, per_owner
        count = pairs * per_owner
        bag.add(f"{name}_s", dma(groups * count))
        bag.add(f"{name}_r", dma(groups * count))

    def slot(self, who, pair, at):
        return (who * self.pairs + pair) * self.per_owner + at

    def copy(self, have, source, target, owner, pair, at):
        s, r = place(self.groups)
        return remote(
            source,
            target,
            have[f"{self.name}_s"].at[self.slot(owner, pair, at)],
            have[f"{self.name}_r"].at[self.slot(r, pair, at)],
            {"blk": s * self.groups + owner},
        )

    def own(self, have, source, target, pair, at):
        s, r = place(self.groups)
        return pltpu.make_async_copy(
            source, target, have[f"{self.name}_s"].at[self.slot(r, pair, at)]
        )

    def finish(self, have, source, target):
        s, r = place(self.groups)
        for pair in range(self.pairs):
            for at in range(self.per_owner):
                self.own(have, source, target, pair, at).wait()
                for j in range(1, self.groups):
                    other = lax.rem(r + j, self.groups)
                    remote(
                        source,
                        target,
                        have[f"{self.name}_s"].at[self.slot(other, pair, at)],
                        have[f"{self.name}_r"].at[self.slot(other, pair, at)],
                        {"blk": s * self.groups + other},
                    ).wait()


class Bag:
    def __init__(self):
        self.items = {}

    def add(self, name, item):
        self.items[name] = item

    def bind(self, refs):
        return dict(zip(self.items, refs))


class Reduce:
    def __init__(self, bag, name, streams, groups, shapes, over_cores, two_step):
        self.name, self.streams, self.groups = name, streams, groups
        self.size = lax.axis_size("dp")
        self.over_cores = over_cores
        self.two_step = two_step and self.size == 4 and streams % 2 == 0
        self.count = len(shapes)
        share = self.size * (groups if over_cores else 1)
        self.shapes = [(rows // share, cols) for rows, cols in shapes]
        self.wires = [BF if (c // streams) % 16 == 0 else F32 for c, cols in self.shapes]
        for i, (chunk, cols) in enumerate(self.shapes):
            wire, slim = self.wires[i], chunk // streams
            bag.add(f"{name}half{i}", pltpu.VMEM((self.size, chunk, cols), wire))
            if over_cores:
                bag.add(f"{name}core{i}", pltpu.VMEM((groups - 1, self.size, chunk, cols), wire))
            if self.two_step:
                bag.add(f"{name}first{i}", pltpu.VMEM((4, chunk // 2, cols), wire))
                bag.add(f"{name}second{i}", pltpu.VMEM((2, chunk // 2, cols), wire))
            else:
                bag.add(f"{name}dp{i}", pltpu.VMEM((self.size - 1, chunk, cols), wire))
            bag.add(f"{name}cut{i}", pltpu.VMEM((streams, slim, cols), wire))
            bag.add(f"{name}z{i}", pltpu.VMEM((streams - 1, slim, cols), wire))
            bag.add(f"{name}fin{i}", pltpu.VMEM((slim, cols), wire))
            for kind in self.kinds():
                bag.add(f"{name}{kind}s{i}", dma(self.sem_count(kind)))
                bag.add(f"{name}{kind}r{i}", dma(self.sem_count(kind)))
            bag.add(f"{name}local{i}", dma(2))

    def kinds(self):
        along = ["b1", "b2", "c", "d", "e1", "e2"] if self.two_step else ["b", "c", "d", "e"]
        return (["a"] if self.over_cores else []) + along + ["f"]

    def sem_count(self, kind):
        if kind in ("a", "f"):
            return self.groups
        if kind in ("c", "d"):
            return self.streams
        return max(self.size, 4)

    def out_shapes(self):
        return [
            jax.ShapeDtypeStruct(
                (self.groups, self.size, self.streams, chunk // self.streams, cols), wire
            )
            for (chunk, cols), wire in zip(self.shapes, self.wires)
        ]

    def bind(self, sources, targets, scratch):
        self.sources, self.targets, self.scratch = sources, targets, scratch

    def get(self, what, i):
        return self.scratch[f"{self.name}{what}{i}"]

    def pairs(self, kind, i):
        s, r = place(self.groups)
        here = lax.axis_index("dp")
        b, g, size = self.streams, self.groups, self.size
        x, y = lax.rem(here, 2), here // 2
        beside_x, beside_y = {"dp": 2 * y + 1 - x}, {"dp": 2 * (1 - y) + x}
        if kind == "a":
            for d, peer in enumerate(core_peers(g), 1):
                yield d, self.sources[i].at[lax.rem(r + d, g)], self.get("core", i).at[d - 1], peer
        elif kind == "b":
            half, box = self.get("half", i), self.get("dp", i)
            for d, peer in enumerate(dp_peers(), 1):
                yield d, half.at[lax.rem(here + d, size)], box.at[d - 1], peer
        elif kind == "b1":
            half, box, h = self.get("half", i), self.get("first", i), self.shapes[i][0] // 2
            for n in range(2):
                yield n, half.at[2 * n + 1 - x, pl.ds(0, h)], box.at[n], beside_x
                yield 2 + n, half.at[2 * (1 - y) + n, pl.ds(h, h)], box.at[2 + n], beside_y
        elif kind == "b2":
            half, box, h = self.get("half", i), self.get("second", i), self.shapes[i][0] // 2
            yield 0, half.at[2 * (1 - y) + x, pl.ds(0, h)], box.at[0], beside_y
            yield 1, half.at[2 * y + 1 - x, pl.ds(h, h)], box.at[1], beside_x
        elif kind in "cd":
            peers = list(enumerate(stream_peers(b, g), 1))
            for d, peer in [peers[1], peers[0], peers[2]] if b == 4 else peers:
                if kind == "c":
                    cut = self.get("cut", i)
                    yield d, cut.at[lax.rem(s + d, b)], self.get("z", i).at[d - 1], peer
                else:
                    yield d, self.get("fin", i), self.targets[i].at[r, here, s], peer
        elif kind == "e":
            whole = self.targets[i].at[r, here]
            for d, peer in enumerate(dp_peers(), 1):
                yield d, whole, whole, peer
        elif kind == "e1":
            for n, peer in enumerate((beside_y, beside_x)):
                part = self.targets[i].at[r, here, pl.ds(n * b // 2, b // 2)]
                yield n, part, part, peer
        elif kind == "e2":
            for n in range(2):
                part = self.targets[i].at[r, 2 * n + x, pl.ds(0, b // 2)]
                yield n, part, part, beside_x
                part = self.targets[i].at[r, 2 * y + n, pl.ds(b // 2, b // 2)]
                yield 2 + n, part, part, beside_y
        else:
            whole = self.targets[i].at[r]
            for d, peer in enumerate(core_peers(g), 1):
                yield d, whole, whole, peer

    def copies(self, kind, i):
        send, recv = self.get(kind + "s", i), self.get(kind + "r", i)
        for n, source, target, peer in self.pairs(kind, i):
            yield remote(source, target, send.at[n], recv.at[n], peer)

    def start(self, kind, i):
        for copy in self.copies(kind, i):
            copy.start()

    def arrive(self, kind, i):
        for copy in self.copies(kind, i):
            copy.wait_recv()

    def load(self, i):
        s, r = place(self.groups)
        return pltpu.make_async_copy(
            self.sources[i].at[r], self.get("half", i), self.get("local", i).at[0]
        )

    def keep(self, i):
        s, r = place(self.groups)
        return pltpu.make_async_copy(
            self.get("fin", i),
            self.targets[i].at[r, lax.axis_index("dp"), s],
            self.get("local", i).at[1],
        )

    def stages(self):
        middle = [self.dp_middle] if self.two_step else []
        back = [self.dp_back_middle] if self.two_step else []
        return [self.dp_start, *middle, self.z_start, self.z_back, self.dp_back, *back, self.core_back]

    def core_start(self):
        for i in range(self.count):
            self.start("a", i)
            self.load(i).start()

    def dp_start(self):
        for i in range(self.count):
            if self.over_cores:
                self.load(i).wait()
                self.arrive("a", i)
                half, box, wire = self.get("half", i), self.get("core", i), self.wires[i]
                for p in range(self.size):
                    total = half[p].astype(F32)
                    for j in range(self.groups - 1):
                        total = total + box[j, p].astype(F32)
                    half[p] = total.astype(wire)
            self.start("b1" if self.two_step else "b", i)

    def dp_middle(self):
        here = lax.axis_index("dp")
        x, y = lax.rem(here, 2), here // 2
        for i in range(self.count):
            self.arrive("b1", i)
            half, box, wire = self.get("half", i), self.get("first", i), self.wires[i]
            h = self.shapes[i][0] // 2
            for n in range(2):
                for who, at, part in ((2 * n + x, pl.ds(0, h), n), (2 * y + n, pl.ds(h, h), 2 + n)):
                    total = half[who, at, :].astype(F32) + box[part].astype(F32)
                    half[who, at, :] = total.astype(wire)
            self.start("b2", i)

    def z_start(self):
        here = lax.axis_index("dp")
        for i in range(self.count):
            self.arrive("b2" if self.two_step else "b", i)
            half, cut, wire = self.get("half", i), self.get("cut", i), self.wires[i]
            chunk = self.shapes[i][0]
            slim = chunk // self.streams
            for z in range(self.streams):
                at = slice(z * slim, (z + 1) * slim)
                total = half[here, at, :].astype(F32)
                if self.two_step:
                    which, first = divmod(z * slim, chunk // 2)
                    total = total + self.get("second", i)[which, first : first + slim].astype(F32)
                else:
                    for d in range(self.size - 1):
                        total = total + self.get("dp", i)[d, at, :].astype(F32)
                cut[z] = total.astype(wire)
            self.start("c", i)

    def z_back(self):
        s, r = place(self.groups)
        for i in range(self.count):
            self.arrive("c", i)
            box = self.get("z", i)
            total = self.get("cut", i)[s].astype(F32)
            for d in range(self.streams - 1):
                total = total + box[d].astype(F32)
            self.get("fin", i)[...] = total.astype(self.wires[i])
            self.keep(i).start()
            self.start("d", i)

    def dp_back(self):
        for i in range(self.count):
            self.keep(i).wait()
            self.arrive("d", i)
            self.start("e1" if self.two_step else "e", i)

    def dp_back_middle(self):
        for i in range(self.count):
            self.arrive("e1", i)
            self.start("e2", i)

    def core_back(self):
        for i in range(self.count):
            self.arrive("e2" if self.two_step else "e", i)
            self.start("f", i)

    def end(self):
        for i in range(self.count):
            self.arrive("f", i)
            for kind in self.kinds():
                for copy in self.copies(kind, i):
                    copy.wait_send()


class Moves:
    def __init__(self, *jobs, others=()):
        self.jobs, self.others = list(jobs), list(others)
        self.counts = [len(job.scratch()) for job in jobs]

    def scratch(self):
        return [item for job in self.jobs for item in job.scratch()]

    def out_shapes(self):
        return [job.out_shape() for job in self.jobs]

    def spaces(self):
        return [pl.BlockSpec(memory_space=pl.ANY)] * len(self.jobs)

    def each(self, sources, targets, scratch):
        at = 0
        for job, count, source, target in zip(self.jobs, self.counts, sources, targets):
            yield job, (source, target, *scratch[at : at + count])
            at += count

    def first(self, sources, targets, scratch):
        greet(unique(self.jobs + self.others))
        for job, refs in self.each(sources, targets, scratch):
            job.first(*refs)

    def middle(self, sources, targets, scratch):
        for job, refs in self.each(sources, targets, scratch):
            if isinstance(job, Gather):
                job.middle(*refs)

    def last(self, sources, targets, scratch):
        for job, refs in self.each(sources, targets, scratch):
            job.last(*refs)


def remote_params(collective_id):
    return pltpu.CompilerParams(
        collective_id=collective_id, has_side_effects=True, vmem_limit_bytes=VMEM_BYTES
    )


def binary_columns(latent):
    matrix = latent.astype(F32)
    scale = jnp.sqrt(jnp.mean(matrix * matrix, axis=0, keepdims=True) + 1e-06)
    return (scale * jnp.tanh(matrix * (2.0 / scale))).astype(BF)


def intake_kernel(moves, groups, qkv_ref, out_ref, up_ref, down_ref, *refs):
    count = len(moves.jobs)
    sources = refs[:count]
    own_bin, out_bin, up_bin, down_bin = refs[count : count + 4]
    targets = refs[count + 4 : 2 * count + 4]
    scratch = refs[2 * count + 4 :]
    moves.first(sources, targets, scratch)
    s, r = place(groups)
    width = own_bin.shape[3]
    own = pl.ds(pl.multiple_of(r * width, 128), width)
    for i in range(3):
        own_bin[0, i] = binary_columns(qkv_ref[i, :, own])
    out_bin[...] = binary_columns(out_ref[...])
    for i in range(0, up_ref.shape[1], 512):
        up_bin[:, i : i + 512] = binary_columns(up_ref[:, i : i + 512])
    for i in range(0, down_ref.shape[1], 128):
        down_bin[:, i : i + 128] = binary_columns(down_ref[:, i : i + 128])
    moves.middle(sources, targets, scratch)
    moves.last(sources, targets, scratch)


def intake(moves, groups, latents, arrays, collective_id):
    three, depth, unused = latents[0].shape
    shapes = [(1, three, depth, depth // groups)] + [a.shape for a in latents[1:]]
    vmem = pl.BlockSpec(memory_space=pltpu.VMEM)
    return pl.pallas_call(
        functools.partial(intake_kernel, moves, groups),
        out_shape=[jax.ShapeDtypeStruct(shape, BF) for shape in shapes] + moves.out_shapes(),
        in_specs=[vmem] * 4 + moves.spaces(),
        out_specs=[vmem] * 4 + moves.spaces(),
        scratch_shapes=moves.scratch(),
        compiler_params=remote_params(collective_id),
        name="intake",
    )(*latents, *arrays)


def lanes_of(shape):
    return lax.broadcasted_iota(jnp.int32, shape, 1)


def forward_kernel(
    moves, keep, streams, groups, tile, bag, tiles, x_ref, w_ref, bias_ref, row_ref, *rest
):
    count = len(moves.jobs)
    sources, rest = rest[:count], rest[count:]
    q_ref, k_ref, rows_ref, *rest = rest
    if keep:
        v_ref, e_ref, ctx_ref, inv_ref, active_ref, *rest = rest
    targets, rest = rest[:count], rest[count:]
    have = bag.bind(rest)
    scratch = tuple(have[f"moves{i}"] for i in range(len(moves.scratch())))
    k_aug, v_aug, ctx_all, mask, edges = (
        have["k_aug"],
        have["v_aug"],
        have["ctx_all"],
        have["mask"],
        have["edges"],
    )
    active = active_ref if keep else x_ref
    pair, step = pl.program_id(0), pl.program_id(1)
    pairs, steps = pl.num_programs(0), pl.num_programs(1)
    seq = k_ref.shape[0]
    s, r = place(groups)
    sub = min(256, tile)
    width = w_ref.shape[3]
    n_pairs = ctx_all.shape[0]
    offset = pair * 128 if width == n_pairs * 128 else (r * n_pairs + pair) * 128
    offset = pl.multiple_of(offset, 128)
    home = pl.multiple_of((r * n_pairs + pair) * 128, 128)

    @pl.when((pair == 0) & (step == 0))
    def _():
        moves.first(sources, targets, scratch)
        ids = row_ref[...]
        big_at = long_at(streams, groups, seq)
        big = ids[:, big_at : big_at + 1]
        mask[...] = jnp.where(ids == big, 0.0, masked_score)
        edges[0] = jnp.broadcast_to(ids[:, :sub], (128, sub)).T
        edges[1] = jnp.broadcast_to(ids[:, seq - sub :], (128, sub)).T
        if keep:
            for i in range(0, seq, 256):
                active_ref[i : i + 256, :] = squash(x_ref[i : i + 256, :].astype(F32)).astype(BF)

    @pl.when((pair == pairs - 1) & (step == steps - 2))
    def _():
        moves.middle(sources, targets, scratch)

    @pl.when(step == 0)
    def _():
        columns = pl.ds(offset, 128)

        def project(i, bias):
            matrix = jnp.concatenate(
                [w_ref[d, i, :, columns] for d in range(w_ref.shape[0])], axis=0
            )
            result = dot(active[...], matrix)
            if bias is not None:
                result = result + bias_ref[bias : bias + 1, pl.ds(home, 128)]
            return result.astype(BF)

        low = lanes_of((seq, 128)) < 64
        lane = lanes_of((seq, 128))
        q_ref[...] = (project(0, 0).astype(F32) * 0.125).astype(BF)
        keys = project(1, None)
        k_ref[...] = keys
        keys = keys.astype(F32)
        turned = pltpu.roll(keys, 64, 1)
        k_aug[0] = jnp.where(low, keys, turned).astype(BF)
        k_aug[1] = jnp.where(low, turned, keys).astype(BF)
        values = project(2, 1)
        if keep:
            v_ref[...] = values
        values = values.astype(F32)
        v_aug[0] = jnp.where(low, values, jnp.where(lane < 66, 1.0, 0.0)).astype(BF)
        v_aug[1] = jnp.where(low, jnp.where(lane < 2, 1.0, 0.0), values).astype(BF)

    start = pl.multiple_of(step * tile, tile)

    def body(edge_at):
        low = lanes_of((sub, 128)) < 64
        parts = []
        for at in range(0, tile, sub):
            scaled = q_ref[pl.ds(start + at, sub), :].astype(F32) * LOG2E
            upper = scaled.astype(BF).astype(F32)
            lower = scaled - upper
            parts.append(
                (
                    jnp.where(low, upper, pltpu.roll(lower, 64, 1)).astype(BF),
                    jnp.where(low, pltpu.roll(upper, 64, 1), lower).astype(BF),
                )
            )
        chains = [(at, h) for at in range(0, tile, sub) for h in range(2)]

        def scores_of(at, h):
            scores = dot(parts[at // sub][h], k_aug[h], NT)
            if edge_at is not None and at == (0 if edge_at == 0 else tile - sub):
                return jnp.where(edges[edge_at][:, :1] == row_ref[...], scores, masked_score)
            return jnp.concatenate(
                [
                    scores[:, :sub] + mask[:, :sub],
                    scores[:, sub : seq - sub],
                    scores[:, seq - sub :] + mask[:, seq - sub :],
                ],
                axis=1,
            )

        scores = scores_of(*chains[0])
        results = {}
        for n, (at, h) in enumerate(chains):
            if n + 1 < len(chains):
                later = scores_of(*chains[n + 1])
            peak = jnp.max(scores, axis=1, keepdims=True)
            numerators = jnp.exp2(scores - peak).astype(BF)
            if keep:
                e_ref[h, at : at + sub, :] = numerators
            total = dot(numerators, v_aug[h])
            where_sum = 64 if h == 0 else 0
            inverse = 1.0 / total[:, where_sum : where_sum + 1]
            results[h] = (total * inverse, inverse)
            if n + 1 < len(chains):
                scores = later
            if h == 1:
                done = jnp.where(low, results[0][0], results[1][0]).astype(BF)
                ctx_all[pair, pl.ds(start + at, sub), :] = done
                if keep:
                    ctx_ref[at : at + sub, :] = done
                    inv_ref[at : at + sub, :] = jnp.where(low, results[0][1], results[1][1])

    @pl.when(step == 0)
    def _():
        body(0)

    @pl.when(step == steps - 1)
    def _():
        body(1)

    @pl.when((step > 0) & (step < steps - 1))
    def _():
        body(None)

    owned = seq // groups
    owner = start // owned
    at = lax.rem(step, owned // tile)
    source = ctx_all.at[pair, pl.ds(start, tile)]
    target = rows_ref.at[r, pair, pl.ds(pl.multiple_of(lax.rem(start, owned), tile), tile)]

    @pl.when(owner == r)
    def _():
        tiles.own(have, source, target, pair, at).start()

    @pl.when(owner != r)
    def _():
        tiles.copy(have, source, target, owner, pair, at).start()

    @pl.when((pair == pairs - 1) & (step == steps - 1))
    def _():
        tiles.finish(have, source, target)
        moves.last(sources, targets, scratch)


def long_at(streams, groups, seq):
    shard = seq // (streams * groups)
    return streams * shard if groups > 1 else shard


def attention(x, weights, bias, docs, streams, groups, moves, moved, keep, collective_id, name):
    seq, depth = x.shape
    width = depth // groups
    pairs = width // 128
    tile = 512
    owned = seq // groups
    bag = Bag()
    bag.add("k_aug", pltpu.VMEM((2, seq, 128), BF))
    bag.add("v_aug", pltpu.VMEM((2, seq, 128), BF))
    bag.add("ctx_all", pltpu.VMEM((pairs, seq, 128), BF))
    bag.add("mask", pltpu.VMEM((1, seq), F32))
    bag.add("edges", pltpu.VMEM((2, 256, 128), F32))
    tiles = Tiles(bag, "tiles", groups, pairs, owned // tile)
    for i, item in enumerate(moves.scratch()):
        bag.add(f"moves{i}", item)

    def constant(shape):
        return pl.BlockSpec(shape, lambda p, i: (0,) * len(shape))

    part = pl.BlockSpec((tile, 128), lambda p, i: (i, p))
    whole = pl.BlockSpec((seq, 128), lambda p, i: (0, p))
    any_space = pl.BlockSpec(memory_space=pl.ANY)
    wide = jax.ShapeDtypeStruct((seq, width), BF)
    outs = [whole, whole, any_space]
    shapes = [wide, wide, jax.ShapeDtypeStruct((groups, pairs, owned, 128), BF)]
    if keep:
        outs += [
            whole,
            pl.BlockSpec((2, tile, seq), lambda p, i: (p, i, 0)),
            part,
            part,
            constant((seq, depth)),
        ]
        shapes += [
            wide,
            jax.ShapeDtypeStruct((2 * pairs, seq, seq), BF),
            wide,
            jax.ShapeDtypeStruct((seq, width), F32),
            jax.ShapeDtypeStruct((seq, depth), BF),
        ]
    return pl.pallas_call(
        functools.partial(forward_kernel, moves, keep, streams, groups, tile, bag, tiles),
        grid=(pairs, seq // tile),
        in_specs=[constant(x.shape), constant(weights.shape), constant(bias.shape)]
        + [constant((1, seq))]
        + moves.spaces(),
        out_specs=outs + moves.spaces(),
        out_shape=shapes + moves.out_shapes(),
        scratch_shapes=list(bag.items.values()),
        compiler_params=remote_params(collective_id),
        name=name,
    )(x, weights, bias, docs, *moved)


def split(matrix):
    upper = matrix.astype(BF)
    return upper, (matrix - upper.astype(F32)).astype(BF)


def backward_kernel(
    streams,
    groups,
    tile,
    bag,
    early,
    late,
    e_ref,
    q_ref,
    k_ref,
    v_ref,
    tq_ref,
    tk_ref,
    dc_ref,
    ctx_ref,
    inv_ref,
    row_ref,
    small_ref,
    active_hbm,
    bin_hbm,
    d1_hbm,
    tokens_hbm,
    *rest,
):
    n_early = sum(job.count for job in early)
    sources, rest = rest[:n_early], rest[n_early:]
    grad_ref, *rest = rest
    early_out, rest = rest[:n_early], rest[n_early:]
    late_out, (gain_ref, bias_ref, shift_ref, *rest) = rest[: len(late)], rest[len(late) :]
    have = bag.bind(rest)
    at = 0
    for job in early:
        job.bind(sources[at : at + job.count], early_out[at : at + job.count], have)
        at += job.count
    for job, target in zip(late, late_out):
        job.bind(None, [target], have)

    pair, step = pl.program_id(0), pl.program_id(1)
    pairs, steps = len(late), q_ref.shape[0] // tile
    seq = k_ref.shape[0]
    share = 1.0 / seq
    time = pair * steps + step
    total_time = pairs * steps
    size = lax.axis_size("dp")
    here = lax.axis_index("dp")
    s, r = place(groups)
    rows, depth = d1_hbm.shape
    width = pairs * 128
    v_aug, dk_acc, dv_acc, grams = have["v_aug"], have["dk_acc"], have["dv_acc"], have["grams"]
    dq_all, d_act, active, weights = have["dq_all"], have["d_act"], have["active"], have["weights"]
    d_one, x_rows = have["d_one"], have["x_rows"]
    edges, in_big, pair_box = have["edges"], have["in_big"], have["pair_box"]
    along_z, cores, along_dp = stream_peers(streams, groups), core_peers(groups), dp_peers()

    def loads():
        sems = have["load"]
        return [
            pltpu.make_async_copy(active_hbm, active, sems.at[0]),
            pltpu.make_async_copy(bin_hbm, weights, sems.at[1]),
            pltpu.make_async_copy(d1_hbm, d_one, sems.at[2]),
            pltpu.make_async_copy(tokens_hbm.at[pl.ds(r * streams, streams)], x_rows, sems.at[3]),
        ]

    def at_time(when, *work):
        @pl.when(time == when)
        def _():
            for item in work:
                item()

    def begin():
        greet(along_z + cores + along_dp)
        for job in early:
            job.core_start()
        for copy in loads():
            copy.start()
        ids = row_ref[...]
        big_at = long_at(streams, groups, seq)
        big = ids[:, big_at : big_at + 1]
        for n, first in enumerate((0, seq - tile)):
            column = jnp.broadcast_to(ids[:, first : first + tile], (128, tile)).T
            edges[n] = column
            in_big[n] = jnp.where(column == big, 1.0, 0.0)

    def big_rows(ref):
        return jnp.concatenate(
            [
                (ref[:tile, :].astype(F32) * in_big[0]).astype(BF),
                ref[tile : seq - tile, :],
                (ref[seq - tile :, :].astype(F32) * in_big[1]).astype(BF),
            ],
            axis=0,
        )

    at_time(0, begin)
    unit = total_time / 16
    left = []
    for n, job in enumerate(early):
        stages, times = job.stages(), EARLY_TIMES[n]
        if not job.two_step:
            times = times[:1] + times[2:5] + times[6:]
        for when, work in zip(times, stages):
            at_time(int(when * unit), work)
        left.append(stages[len(times) :])
    for p, job in enumerate(late[:-1]):
        first = (p + 1) * steps
        for when, work in zip(LATE_TIMES, job.stages()):
            at_time(first + when, work)
        left.append(job.stages()[len(LATE_TIMES) :])

    def go_on(count):
        for unused in range(count):
            for queue in left:
                if queue:
                    queue.pop(0)()

    @pl.when(step == 0)
    def _():
        lane = lanes_of((seq, 128))
        low = lane < 64
        values = v_ref[...].astype(F32)
        v_aug[0] = jnp.where(low, values, jnp.where(lane < 66, 1.0, 0.0)).astype(BF)
        v_aug[1] = jnp.where(low, jnp.where(lane < 2, 1.0, 0.0), values).astype(BF)
        dk_acc[...] = jnp.zeros_like(dk_acc)
        dv_acc[...] = jnp.zeros_like(dv_acc)
        kb, tkb, qb, tqb = (big_rows(ref) for ref in (k_ref, tk_ref, q_ref, tq_ref))
        same_head = (lax.broadcasted_iota(jnp.int32, (128, 128), 0) < 64) == (
            lanes_of((128, 128)) < 64
        )
        for i, (a, b) in enumerate(((kb, kb), (tkb, kb), (qb, qb), (tqb, qb))):
            gram = jnp.where(same_head, dot(a, b, TN) * share, 0.0)
            grams[2 * i], grams[2 * i + 1] = split(gram)

    start = pl.multiple_of(step * tile, tile)
    rows_here = pl.ds(start, tile)
    lane = lanes_of((tile, 128))
    low = lane < 64

    def body(whole, columns):
        edge = 0 if whole and columns.start == 0 else 1
        q8 = q_ref[rows_here, :]
        tq8 = tq_ref[rows_here, :]
        dc = dc_ref[...].astype(F32)
        inv = inv_ref[...]
        scaled = dc * inv
        product = scaled * ctx_ref[...].astype(F32)
        scaled_low = scaled.astype(BF)
        q_turned = q8.astype(F32).T.astype(BF)
        dc_turned = scaled_low.astype(F32).T.astype(BF)
        d_queries = []
        for h in range(2):
            mine = low if h == 0 else jnp.logical_not(low)
            delta = -jnp.sum(jnp.where(mine, product, 0.0), axis=1, keepdims=True)
            upper = delta.astype(BF).astype(F32)
            first = 64 if h == 0 else 0
            extra = jnp.where(
                lane == first, upper, jnp.where(lane == first + 1, delta - upper, 0.0)
            )
            dc_aug = jnp.where(mine, scaled, extra).astype(BF)
            numerators = e_ref[h]
            d_probs = dot(dc_aug, v_aug[h], NT)
            d_scores = numerators.astype(F32) * d_probs
            if whole:
                q_mine = jnp.where(mine, q8, 0.0).astype(BF)
                tq_mine = jnp.where(mine, tq8, 0.0).astype(BF)
                gap = dot(q_mine, k_ref[columns, :], NT) - dot(tq_mine, tk_ref[columns, :], NT)
                same = jnp.where(edges[edge][:, :1] == row_ref[:, columns], share, 0.0)
                gap = gap * (same * (1.0 - in_big[edge][:, :1]))
                if columns.start == 0:
                    d_scores = jnp.concatenate(
                        [d_scores[:, :tile] + gap, d_scores[:, tile:]], axis=1
                    )
                else:
                    d_scores = jnp.concatenate(
                        [d_scores[:, : seq - tile], d_scores[:, seq - tile :] + gap], axis=1
                    )
            d_scores = d_scores.astype(BF)
            d_queries.append(dot(d_scores, k_ref[...]))
            half = slice(64 * h, 64 * h + 64)
            dk_acc[half, :] += dot(q_turned[half, :], d_scores)
            dv_acc[half, :] += dot(dc_turned[half, :], numerators)
        d_query = jnp.where(low, d_queries[0], d_queries[1])
        qb, tqb = q8, tq8
        if whole:
            qb = (q8.astype(F32) * in_big[edge]).astype(BF)
            tqb = (tq8.astype(F32) * in_big[edge]).astype(BF)
        d_query += dot(qb, grams[0]) + dot(qb, grams[1]) - dot(tqb, grams[2]) - dot(tqb, grams[3])
        dq_all[rows_here, :] = (d_query * 0.125).astype(BF)

    @pl.when(step == 0)
    def _():
        body(True, slice(0, tile))

    @pl.when(step == steps - 1)
    def _():
        body(True, slice(seq - tile, seq))

    @pl.when((step > 0) & (step < steps - 1))
    def _():
        body(False, None)

    def pair_end(p):
        job = late[p]
        kb, tkb = big_rows(k_ref), big_rows(tk_ref)
        d_key = dk_acc[...].T
        d_key += dot(kb, grams[4]) + dot(kb, grams[5]) - dot(tkb, grams[6]) - dot(tkb, grams[7])
        d_value = dv_acc[...].T.astype(BF)
        d_query = dq_all[...]
        d_pair = jnp.concatenate([d_query, d_key.astype(BF), d_value], axis=1)
        if p == 0:
            for copy in loads():
                copy.wait()
        columns = slice(p * 128, (p + 1) * 128)
        bins = jnp.concatenate([weights[0, i, :, columns] for i in range(3)], axis=1)
        if p < pairs - 1:
            if p == 0:
                d_act[...] = dot(d_pair, bins, NT)
            else:
                d_act[...] += dot(d_pair, bins, NT)
        else:
            pair_box[...] = d_pair
            for j in range(1, groups + 1):
                at = pl.ds(pl.multiple_of(lax.rem(r + j, groups) * rows, rows), rows)
                total = dot(pair_box[at, :], bins, NT)
                if p > 0:
                    total = total + d_act[at, :]
                if j < groups:
                    have["outbox"][j - 1] = total.astype(BF)
                    core_copies()[j - 1].start()
                else:
                    d_act[at, :] = total
        partial = dot(active[...], d_pair, TN)
        chunk = depth // size
        half = job.get("half", 0)
        for d in range(size):
            half[d] = partial[d * chunk : (d + 1) * chunk, :].astype(job.wires[0])
        sums = have["sums"]
        sums[0:1, columns] = jnp.sum(d_query.astype(F32), axis=0, keepdims=True)
        sums[1:2, columns] = jnp.sum(d_value.astype(F32), axis=0, keepdims=True)

    def core_copies():
        return [
            remote(
                have["outbox"].at[j - 1],
                have["inbox"].at[j - 1],
                have["core_s"].at[j],
                have["core_r"].at[j],
                cores[j - 1],
            )
            for j in range(1, groups)
        ]

    def small_copies(stage, peers, base):
        return [
            remote(
                have["small"].at[stage],
                have["small_box"].at[base + d],
                have["small_s"].at[base + d],
                have["small_r"].at[base + d],
                peer,
            )
            for d, peer in enumerate(peers)
        ]

    def small_start(stage, peers, base):
        for copy in small_copies(stage, peers, base):
            copy.start()

    def small_sum(stage, peers, base):
        for copy in small_copies(stage, peers, base):
            copy.wait_recv()
        total = have["small"][stage]
        for d in range(len(peers)):
            total = total + have["small_box"][base + d]
        return total

    for p in range(pairs - 1):

        @pl.when((pair == p) & (step == steps - 1))
        def _():
            pair_end(p)

    @pl.when(time == total_time - 1)
    def _():
        pair_end(pairs - 1)
        last = late[-1]
        last.dp_start()
        small = have["small"]
        small[0] = small_ref[...]
        for i in range(2):
            vector = have["sums"][i : i + 1, :]
            small[0, 2 + i : 3 + i, :] = jnp.concatenate(
                [jnp.where(r == j, vector, 0.0) for j in range(groups)], axis=1
            )
        small_start(0, along_dp, 0)
        go_on(TAIL[0])
        last.z_start()
        last.z_back()
        for copy in core_copies():
            copy.wait_recv()
        shard = rows // streams
        back_copies = []
        blocks = have["blocks"]
        order = [2, 1, 3] if streams == 4 else list(range(1, streams))
        for d in order + [0]:
            target = lax.rem(s + d, streams)
            here_rows = pl.ds(pl.multiple_of(target * shard, shard), shard)
            bent = jnp.tanh(x_rows[target].astype(F32) * (1.0 / clip_level))
            total = d_act[pl.ds(pl.multiple_of(r * rows + target * shard, shard), shard), :]
            for j in range(groups - 1):
                total = total + have["inbox"][j, here_rows, :].astype(F32)
            blocks[target] = (d_one[here_rows, :] + total * (1.0 - bent * bent)).astype(BF)
            if d:
                copy = remote(
                    blocks.at[target],
                    grad_ref.at[s],
                    have["grad_s"].at[d],
                    have["grad_r"].at[d],
                    along_z[d - 1],
                )
            else:
                copy = pltpu.make_async_copy(blocks.at[s], grad_ref.at[s], have["grad_s"].at[0])
            copy.start()
            back_copies.append(copy)
        small[1] = small_sum(0, along_dp, 0)
        small_start(1, along_z, size)
        go_on(TAIL[1])
        small[2] = small_sum(1, along_z, size)
        small_start(2, cores, size + streams)
        go_on(TAIL[2])
        last.dp_back()
        summed = small_sum(2, cores, size + streams)
        gain_ref[...] = summed[0:2, :]
        bias_ref[...] = summed[2:8, :]
        for i in range(shift_ref.shape[1] // depth):
            shift_ref[:, i * depth : (i + 1) * depth] = summed[8 + i : 9 + i, :]
        go_on(TAIL[3])
        last.core_back()
        go_on(8)
        for copy in back_copies:
            copy.wait()
        for job in early + late:
            job.end()
        for copy in (
            core_copies()
            + small_copies(0, along_dp, 0)
            + small_copies(1, along_z, size)
            + small_copies(2, cores, size + streams)
        ):
            copy.wait_send()


TWO_STEP = False
TAIL = (1, 1, 0, 0)
EARLY_TIMES = ((2, 0, 7, 9, 12), (4, 0, 12, 14))
LATE_TIMES = (0, 5, 7)


def attention_back(
    streams,
    groups,
    numerators,
    queries,
    keys,
    values,
    teacher_queries,
    teacher_keys,
    d_context,
    context,
    inverse,
    docs,
    small,
    active,
    bin_own,
    d_one,
    tokens,
    early_arrays,
    up_width,
    collective_id,
):
    seq, width = queries.shape
    pairs = width // 128
    tile = 256
    rows, depth = d_one.shape
    size = lax.axis_size("dp")
    shard = rows // streams
    bag = Bag()
    bag.add("v_aug", pltpu.VMEM((2, seq, 128), BF))
    bag.add("dk_acc", pltpu.VMEM((128, seq), F32))
    bag.add("dv_acc", pltpu.VMEM((128, seq), F32))
    bag.add("grams", pltpu.VMEM((8, 128, 128), BF))
    bag.add("dq_all", pltpu.VMEM((seq, 128), BF))
    bag.add("d_act", pltpu.VMEM((seq, depth), F32))
    bag.add("active", pltpu.VMEM((seq, depth), BF))
    bag.add("weights", pltpu.VMEM((1, 3, depth, width), BF))
    bag.add("d_one", pltpu.VMEM((rows, depth), F32))
    bag.add("x_rows", pltpu.VMEM((streams, shard, depth), BF))
    bag.add("load", dma(4))
    bag.add("sums", pltpu.VMEM((8, width), F32))
    bag.add("outbox", pltpu.VMEM((groups - 1, rows, depth), BF))
    bag.add("inbox", pltpu.VMEM((groups - 1, rows, depth), BF))
    bag.add("core_s", dma(groups))
    bag.add("core_r", dma(groups))
    bag.add("blocks", pltpu.VMEM((streams, shard, depth), BF))
    bag.add("grad_s", dma(streams))
    bag.add("grad_r", dma(streams))
    count = size + streams + groups
    bag.add("small", pltpu.VMEM((3,) + small.shape, F32))
    bag.add("small_box", pltpu.VMEM((count,) + small.shape, F32))
    bag.add("small_s", dma(count))
    bag.add("small_r", dma(count))
    bag.add("pair_box", pltpu.VMEM((seq, 3 * 128), BF))
    bag.add("edges", pltpu.VMEM((2, tile, 128), F32))
    bag.add("in_big", pltpu.VMEM((2, tile, 128), F32))
    early, flat = [], []
    for n, arrays in enumerate(early_arrays):
        job = Reduce(bag, f"early{n}", streams, groups, [a.shape for a in arrays], True, TWO_STEP)
        early.append(job)
        flat += [
            a.reshape(groups, size, chunk, cols) for a, (chunk, cols) in zip(arrays, job.shapes)
        ]
    late = [
        Reduce(bag, f"late{p}", streams, groups, [(depth, 3 * 128)], False, False)
        for p in range(pairs)
    ]
    part = pl.BlockSpec((tile, 128), lambda p, i: (i, p))
    any_space = pl.BlockSpec(memory_space=pl.ANY)

    whole = pl.BlockSpec((seq, 128), lambda p, i: (0, p))

    def constant(shape):
        return pl.BlockSpec(shape, lambda p, i: (0,) * len(shape))

    small_shapes = [(2, depth), (6, depth), (1, up_width)]
    early_shapes = [shape for job in early for shape in job.out_shapes()]
    late_shapes = [shape for job in late for shape in job.out_shapes()]
    results = pl.pallas_call(
        functools.partial(backward_kernel, streams, groups, tile, bag, early, late),
        grid=(pairs, seq // tile),
        in_specs=[
            pl.BlockSpec((2, tile, seq), lambda p, i: (p, i, 0)),
            whole,
            whole,
            whole,
            whole,
            whole,
            part,
            part,
            part,
            constant((1, seq)),
            constant(small.shape),
        ]
        + [any_space] * (4 + len(flat)),
        out_specs=[any_space] * (1 + len(early_shapes) + len(late_shapes))
        + [constant(shape) for shape in small_shapes],
        out_shape=[jax.ShapeDtypeStruct((streams, shard, depth), BF)]
        + early_shapes
        + late_shapes
        + [jax.ShapeDtypeStruct(shape, F32) for shape in small_shapes],
        scratch_shapes=list(bag.items.values()),
        compiler_params=remote_params(collective_id),
        name="attention_back",
    )(
        numerators,
        queries,
        keys,
        values,
        teacher_queries,
        teacher_keys,
        d_context,
        context,
        inverse,
        docs,
        small,
        active,
        bin_own,
        d_one,
        tokens,
        *flat,
    )
    grad_tokens, *rest = results
    early_sums = rest[: len(flat)]
    late_sums = rest[len(flat) : -3]
    shapes = [a.shape for arrays in early_arrays for a in arrays]
    return (
        grad_tokens,
        [e.reshape(shape) for e, shape in zip(early_sums, shapes)],
        [l.reshape(groups, depth, 3 * 128) for l in late_sums],
        rest[-3:],
    )


def middle_kernel(
    streams,
    groups,
    bag,
    tiles,
    x_ref,
    tx_ref,
    cot_ref,
    ctx_ref,
    tctx_ref,
    bo_ref,
    bup_ref,
    bdown_ref,
    to_ref,
    tup_ref,
    tdown_ref,
    sg_ref,
    sb_ref,
    sub_ref,
    tg_ref,
    tb_ref,
    tub_ref,
    out_ref,
    d1_ref,
    dctx_ref,
    gout_ref,
    gup_ref,
    gdown_ref,
    small_ref,
    *rest,
):
    have = bag.bind(rest)
    gout_acc, gup_acc, gdown_acc = have["gout"], have["gup"], have["gdown"]
    out_box, d_box = have["out_box"], have["d_box"]
    step = pl.program_id(0)
    steps = pl.num_programs(0)
    width = ctx_ref.shape[1] * 128
    tile, depth = cot_ref.shape
    n_steps = out_box.shape[0]
    shard = n_steps * tile // streams
    s, r = place(groups)
    along_z = stream_peers(streams, groups)
    turned = row_tile(step, n_steps, streams, groups)
    start = pl.multiple_of(turned * tile, tile)

    @pl.when(step == 0)
    def _():
        greet(along_z + core_peers(groups))

    @pl.when(step == 0)
    def _():
        for ref in (gout_acc, gup_acc, gdown_acc, small_ref):
            ref[...] = jnp.zeros_like(ref)

    def row(ref, i):
        return ref[i : i + 1, :]

    pieces = [(j, p) for j in range(groups) for p in range(ctx_ref.shape[1])]
    tctx = jnp.concatenate([tctx_ref[j, p] for j, p in pieces], axis=1)
    t_att = dot(tctx, to_ref[...]) + row(tb_ref, 2)
    t_hidden = layer_norm(tx_ref[...].astype(F32) + t_att, row(tg_ref, 0), row(tb_ref, 3))[0]
    t_inner = gelu_parts(dot(t_hidden.astype(BF), tup_ref[...]) + tub_ref[...])[0]
    t_out = layer_norm(
        t_hidden + dot(t_inner.astype(BF), tdown_ref[...]) + row(tb_ref, 4),
        row(tg_ref, 1),
        row(tb_ref, 5),
    )[0]

    context = jnp.concatenate([ctx_ref[j, p] for j, p in pieces], axis=1).astype(F32)
    bent = jnp.tanh(context * (1.0 / clip_level))
    ctx_active = (clip_level * bent).astype(BF)
    ctx_slope = 1.0 - bent * bent
    attended = dot(ctx_active, bo_ref[...]) + row(sb_ref, 2)
    hidden, normed_one, inverse_one = layer_norm(
        x_ref[...].astype(F32) + attended, row(sg_ref, 0), row(sb_ref, 3)
    )
    bent = jnp.tanh(hidden * (1.0 / clip_level))
    hidden_active = (clip_level * bent).astype(BF)
    hidden_slope = 1.0 - bent * bent
    inner_pre = dot(hidden_active, bup_ref[...]) + sub_ref[...]
    inner_act, phi = gelu_parts(inner_pre)
    bent = jnp.tanh(inner_act * (1.0 / clip_level))
    inner_active = (clip_level * bent).astype(BF)
    slope = (1.0 - bent * bent) * (
        phi + inner_pre * jnp.exp(-0.5 * inner_pre * inner_pre) * 0.3989422804014327
    )
    branch = dot(inner_active, bdown_ref[...]) + row(sb_ref, 4)
    output, normed_two, inverse_two = layer_norm(hidden + branch, row(sg_ref, 1), row(sb_ref, 5))
    out_box[step] = output.astype(BF)
    per_tile = tile // shard
    for n in range(per_tile):
        block = turned * per_tile + n
        source = out_box.at[step, pl.ds(n * shard, shard)]

        @pl.when(block == s)
        def _():
            pltpu.make_async_copy(source, out_ref.at[s], have["out_s"].at[s]).start()

        @pl.when(block != s)
        def _():
            remote(
                source,
                out_ref.at[s],
                have["out_s"].at[block],
                have["out_r"].at[s],
                {"blk": block * groups + r},
            ).start()

    upstream = cot_ref[...].astype(F32) + 0.5 * (output - t_out)
    d_two = norm_back(upstream, row(sg_ref, 1), normed_two, inverse_two)
    d_branch = d_two.astype(BF)
    gdown_acc[...] += dot(inner_active, d_branch, TN)
    d_inner = (dot(d_branch, bdown_ref[...], NT) * slope).astype(BF)
    gup_acc[...] += dot(hidden_active, d_inner, TN)
    d_hidden = d_two + dot(d_inner, bup_ref[...], NT) * hidden_slope
    d_one = norm_back(d_hidden, row(sg_ref, 0), normed_one, inverse_one)
    d1_ref[...] = d_one
    d_attended = d_one.astype(BF)
    gout_acc[...] += dot(ctx_active, d_attended, TN)
    d_context = (dot(d_attended, bo_ref[...], NT) * ctx_slope).astype(BF)
    place_rows = pl.ds(pl.multiple_of(r * n_steps * tile + start, tile), tile)
    for j in range(groups):
        d_box[step, j] = d_context[:, j * width : (j + 1) * width]
        piece, target = d_box.at[step, j], dctx_ref.at[place_rows]

        @pl.when(r == j)
        def _():
            tiles.own(have, piece, target, 0, step).start()

        @pl.when(r != j)
        def _():
            tiles.copy(have, piece, target, j, 0, step).start()


    def total(value):
        return jnp.sum(value, axis=0, keepdims=True)

    sums = [
        (0, d_hidden * normed_one),
        (1, upstream * normed_two),
        (4, d_attended.astype(F32)),
        (5, d_hidden),
        (6, d_branch.astype(F32)),
        (7, upstream),
    ]
    for i, value in sums:
        small_ref[i : i + 1, :] += total(value)
    d_shift = total(d_inner.astype(F32))
    for i in range(d_shift.shape[1] // depth):
        small_ref[8 + i : 9 + i, :] += d_shift[:, i * depth : (i + 1) * depth]

    @pl.when(step == steps - 1)
    def _():
        tiles.finish(have, d_box.at[0, 0], dctx_ref.at[place_rows])
        source = out_box.at[0, pl.ds(0, shard)]
        pltpu.make_async_copy(source, out_ref.at[s], have["out_s"].at[s]).wait()
        for d, peer in enumerate(along_z, 1):
            block = lax.rem(s + d, streams)
            remote(
                source, out_ref.at[block], have["out_s"].at[block], have["out_r"].at[block], peer
            ).wait()
        gout_ref[...] = gout_acc[...].astype(BF)
        gup_ref[...] = gup_acc[...].astype(BF)
        gdown_ref[...] = gdown_acc[...].astype(BF)


def row_tile(step, steps, streams, groups):
    s, r = place(groups)
    return lax.rem(s // (streams // steps) + 1 + step, steps)


def middle(streams, groups, x, tx, cot, ctx, tctx, weights, teacher_weights, vectors, collective_id):
    rows, depth = cot.shape
    ff = weights[1].shape[1]
    tile = min(256, rows)
    pairs = ctx.shape[1]
    width = pairs * 128
    steps = rows // tile
    shard = rows // streams

    def turn(i):
        return row_tile(i, steps, streams, groups)

    def stream_tile(i):
        return lax.rem(lax.axis_index("blk"), groups) * steps + turn(i)

    tall = pl.BlockSpec((tile, depth), lambda i: (turn(i), 0))
    of_stream = pl.BlockSpec((tile, depth), lambda i: (stream_tile(i), 0))
    split_rows = pl.BlockSpec((groups, pairs, tile, 128), lambda i: (0, 0, turn(i), 0))
    any_space = pl.BlockSpec(memory_space=pl.ANY)

    def full(shape):
        return pl.BlockSpec(shape, lambda i: (0,) * len(shape))

    out_full = [(depth, depth), (depth, ff), (ff, depth), (16, depth)]
    bag = Bag()
    for name, shape in zip(("gout", "gup", "gdown"), out_full):
        bag.add(name, pltpu.VMEM(shape, F32))
    bag.add("out_box", pltpu.VMEM((steps, tile, depth), BF))
    bag.add("d_box", pltpu.VMEM((steps, groups, tile, width), BF))
    bag.add("out_s", dma(streams))
    bag.add("out_r", dma(streams))
    tiles = Tiles(bag, "tiles", groups, 1, steps)
    return pl.pallas_call(
        functools.partial(middle_kernel, streams, groups, bag, tiles),
        grid=(steps,),
        in_specs=[of_stream, of_stream, tall, split_rows, split_rows]
        + [full(a.shape) for a in weights + teacher_weights + vectors],
        out_specs=[any_space, tall, any_space] + [full(s) for s in out_full],
        out_shape=[
            jax.ShapeDtypeStruct((streams, shard, depth), BF),
            jax.ShapeDtypeStruct((rows, depth), F32),
            jax.ShapeDtypeStruct((rows * groups, width), BF),
        ]
        + [jax.ShapeDtypeStruct(s, BF if i < 3 else F32) for i, s in enumerate(out_full)],
        scratch_shapes=list(bag.items.values()),
        compiler_params=remote_params(collective_id),
        name="middle",
    )(x, tx, cot, ctx, tctx, *weights, *teacher_weights, *vectors)


def latent_columns(latent, binary_grad):
    matrix = latent.astype(F32)
    grad = binary_grad.astype(F32)
    scale = jnp.sqrt(jnp.mean(matrix * matrix, axis=0, keepdims=True) + 1e-06)
    inner = matrix * (2.0 / scale)
    bent = jnp.tanh(inner)
    slope = 1.0 - bent * bent
    through_scale = jnp.sum(grad * (bent - inner * slope), axis=0, keepdims=True)
    factor = through_scale / (matrix.shape[0] * scale)
    return 2.0 * grad * slope + matrix * factor


def latent_grads_kernel(pairs, lq, lo, lu, ld, *refs):
    late, (go, gu, gd, oq, oo, ou, od) = refs[:pairs], refs[pairs:]
    for p in range(pairs):

        @pl.when(lax.rem(pl.program_id(0), pairs) == p)
        def _():
            for i in range(3):
                oq[i] = latent_columns(lq[i], late[p][0, :, i * 128 : (i + 1) * 128])

    oo[...] = latent_columns(lo[...], go[...])
    od[...] = latent_columns(ld[...], gd[...])
    for i in range(0, lu.shape[1], 128):
        at = slice(i, i + 128)
        ou[:, at] = latent_columns(lu[:, at], gu[:, at])


def latent_grads(latents, late, early):
    pairs = len(late)
    groups, depth, wide = late[0].shape
    steps = groups * pairs
    qkv = pl.BlockSpec((3, depth, depth // steps), lambda i: (0, 0, i))
    flat = [pl.BlockSpec((a.shape[0], a.shape[1] // steps), lambda i: (0, i)) for a in latents[1:]]
    return pl.pallas_call(
        functools.partial(latent_grads_kernel, pairs),
        grid=(steps,),
        in_specs=[qkv]
        + flat
        + [pl.BlockSpec((1, depth, wide), lambda i: (i // pairs, 0, 0))] * pairs
        + flat,
        out_specs=[qkv] + flat,
        out_shape=[jax.ShapeDtypeStruct(a.shape, F32) for a in latents],
        compiler_params=pltpu.CompilerParams(vmem_limit_bytes=VMEM_BYTES),
        name="latent_grads",
    )(*latents, *late, *early)


def shards(
    tokens,
    teacher_tokens,
    segment_ids,
    cotangent,
    latent_qkv,
    latent_out,
    latent_up,
    latent_down,
    student_gain,
    student_bias,
    student_up_bias,
    teacher_qkv,
    teacher_out,
    teacher_up,
    teacher_down,
    teacher_gain,
    teacher_bias,
    teacher_up_bias,
):
    streams, shard_len, depth = tokens.shape
    blocks = lax.axis_size("blk")
    groups = blocks // streams
    seq = shard_len * blocks
    rows = seq // groups
    block = (shard_len, depth)
    gather, swap = Gather(streams, groups, block, BF), Swap(streams, groups, block, BF)
    doc_block = (shard_len // 128, 128)
    bin_own, bin_out, bin_up, bin_down, token_blocks, docs, qkv_parts = intake(
        Moves(
            gather,
            Gather(streams, groups, doc_block, jnp.int32),
            Spread(teacher_qkv.shape, BF),
        ),
        groups,
        [latent_qkv, latent_out, latent_up, latent_down],
        [tokens, segment_ids.reshape((streams,) + doc_block), teacher_qkv],
        1,
    )
    docs = docs.reshape(1, seq).astype(F32)
    stream_tokens = token_blocks.reshape(seq, depth)
    (
        queries,
        keys,
        ctx_rows,
        values,
        numerators,
        context,
        inverse,
        active,
        teacher_blocks,
        up_parts,
        out_parts,
    ) = attention(
        stream_tokens,
        bin_own,
        student_bias,
        docs,
        streams,
        groups,
        Moves(gather, Spread(teacher_up.shape, BF), Spread(teacher_out.shape, BF)),
        [teacher_tokens, teacher_up, teacher_out],
        True,
        2,
        "attention_student",
    )
    teacher_stream = teacher_blocks.reshape(seq, depth)
    teacher_queries, teacher_keys, tctx_rows, cot_blocks, down_parts = attention(
        teacher_stream,
        qkv_parts,
        teacher_bias,
        docs,
        streams,
        groups,
        Moves(swap, Spread(teacher_down.shape, BF), others=[gather]),
        [cotangent, teacher_down],
        False,
        3,
        "attention_teacher",
    )
    output, d_one, d_context, g_out, g_up, g_down, small = middle(
        streams,
        groups,
        stream_tokens,
        teacher_stream,
        cot_blocks.reshape(rows, depth),
        ctx_rows,
        tctx_rows,
        [bin_out, bin_up, bin_down],
        [
            out_parts.reshape(-1, depth),
            up_parts.reshape(depth, -1),
            down_parts.reshape(-1, depth),
        ],
        [
            student_gain,
            student_bias,
            student_up_bias.reshape(1, -1),
            teacher_gain,
            teacher_bias,
            teacher_up_bias.reshape(1, -1),
        ],
        4,
    )
    grads = [[g_up], [g_down, g_out]]
    in_kernel = depth % (16 * blocks * lax.axis_size("dp")) == 0
    grad_tokens, early, late, small = attention_back(
        streams,
        groups,
        numerators,
        queries,
        keys,
        values,
        teacher_queries,
        teacher_keys,
        d_context,
        context,
        inverse,
        docs,
        small,
        active,
        bin_own,
        d_one,
        token_blocks,
        grads if in_kernel else [],
        latent_up.shape[1],
        6,
    )
    if not in_kernel:
        early = lax.psum((g_up, g_down, g_out), ("dp", "blk"))
    grad_qkv, grad_out, grad_up, grad_down = latent_grads(
        [latent_qkv, latent_out, latent_up, latent_down], late, [early[2], early[0], early[1]]
    )
    return (
        output,
        grad_tokens,
        grad_qkv,
        grad_out,
        grad_up,
        grad_down,
        small[0],
        small[1],
        small[2].reshape(-1),
    )


def solution(mesh):
    return jax.shard_map(
        shards,
        mesh=mesh,
        in_specs=(
            P("dp", "blk", None),
            P("dp", "blk", None),
            P("dp", "blk"),
            P("dp", "blk", None),
            P(),
            P(),
            P(),
            P(),
            P(),
            P(),
            P(),
            P(None, "dp", None),
            P("dp", None),
            P("dp", None),
            P("dp", None),
            P(),
            P(),
            P(),
        ),
        out_specs=(P("dp", "blk", None), P("dp", "blk", None), P(), P(), P(), P(), P(), P(), P()),
        check_vma=False,
    )
```

```python
import functools

import jax
import jax.numpy as jnp
from jax import lax
from jax.experimental import pallas as pl
from jax.experimental.pallas import tpu as pltpu
from jax.sharding import PartitionSpec as P

HEADS = 8
BF = jnp.bfloat16
F32 = jnp.float32
LOG2E = 1.4426950408889634
clip_level = 2.5
masked_score = -1e30
VMEM_BYTES = 56 << 20
MESH = pl.DeviceIdType.MESH
NT = (((1,), (1,)), ((), ()))
TN = (((0,), (0,)), ((), ()))


def squash(tensor):
    return clip_level * jnp.tanh(tensor * (1.0 / clip_level))


def gelu_parts(tensor):
    phi = 0.5 * (1.0 + lax.erf(tensor * 0.7071067811865476))
    return tensor * phi, phi


def binarize(matrix):
    column_scale = jnp.sqrt(jnp.mean(matrix * matrix, axis=-2, keepdims=True) + 1e-06)
    return column_scale * jnp.tanh(2.0 * matrix / column_scale)


def layer_norm(tensor, gain_row, shift_row):
    centre = tensor - jnp.mean(tensor, axis=-1, keepdims=True)
    inverse_std = lax.rsqrt(jnp.mean(centre * centre, axis=-1, keepdims=True) + 1e-05)
    normed = centre * inverse_std
    return (normed * gain_row + shift_row, normed, inverse_std)


def norm_back(upstream, gain_row, normed, inverse_std):
    scaled = upstream * gain_row
    return inverse_std * (
        scaled
        - jnp.mean(scaled, axis=-1, keepdims=True)
        - normed * jnp.mean(scaled * normed, axis=-1, keepdims=True)
    )


def dot(a, b, dims=(((1,), (0,)), ((), ()))):
    return lax.dot_general(a, b, dims, preferred_element_type=F32)


def latent_grad(latent, binary_grad):
    matrix = latent.astype(F32)
    unused, pullback = jax.vjp(binarize, matrix)
    return pullback(binary_grad)[0]


def place(groups):
    here = lax.axis_index("blk")
    return here // groups, lax.rem(here, groups)


def greet(peers):
    barrier = pltpu.get_barrier_semaphore()
    for peer in peers:
        pl.semaphore_signal(barrier, inc=1, device_id=peer, device_id_type=MESH)
    pl.semaphore_wait(barrier, len(peers))


def stream_peers(streams, groups):
    s, r = place(groups)
    return [{"blk": lax.rem(s + d, streams) * groups + r} for d in range(1, streams)]


def core_peers(groups):
    s, r = place(groups)
    return [{"blk": s * groups + lax.rem(r + j, groups)} for j in range(1, groups)]


def dp_peers():
    size = lax.axis_size("dp")
    here = lax.axis_index("dp")
    return [{"dp": lax.rem(here + d, size)} for d in range(1, size)]


def unique(jobs):
    peers, kinds = [], []
    for job in jobs:
        for kind, found in job.peers():
            if kind not in kinds:
                kinds.append(kind)
                peers += found
    return peers


def remote(source, target, send, recv, peer):
    return pltpu.make_async_remote_copy(
        src_ref=source,
        dst_ref=target,
        send_sem=send,
        recv_sem=recv,
        device_id=peer,
        device_id_type=MESH,
    )


def dma(count):
    return pltpu.SemaphoreType.DMA((count,))


class Staged:
    def __init__(self, source, target, stage, sems):
        self.load = pltpu.make_async_copy(source, stage, sems.at[0])
        self.store = pltpu.make_async_copy(stage, target, sems.at[1])

    def first(self):
        self.load.start()

    def last(self):
        self.load.wait()
        self.store.start()
        self.store.wait()


class Gather:
    def __init__(self, streams, groups, block, dtype):
        self.streams, self.groups, self.block, self.dtype = streams, groups, block, dtype

    def scratch(self):
        b, g = self.streams, self.groups
        return [dma(b), dma(b), dma(b * g), dma(b * g), pltpu.VMEM(self.block, self.dtype), dma(2)]

    def out_shape(self):
        return jax.ShapeDtypeStruct((self.streams * self.groups,) + self.block, self.dtype)

    def peers(self):
        return [
            ("stream", stream_peers(self.streams, self.groups)),
            ("core", core_peers(self.groups)),
        ]

    def parts(self, source, target, send, recv, share_send, share_recv, stage, sems):
        b, g = self.streams, self.groups
        s, r = place(g)
        peers, cores = stream_peers(b, g), core_peers(g)
        swaps = [
            remote(
                source.at[lax.rem(s + d, b)],
                target.at[r * b + s],
                send.at[d],
                recv.at[d],
                peers[d - 1],
            )
            for d in range(1, b)
        ]
        shares = [
            [
                remote(
                    source.at[s] if d == 0 else target.at[r * b + lax.rem(s + b - d, b)],
                    target.at[r * b + lax.rem(s + b - d, b)],
                    share_send.at[j * b + d],
                    share_recv.at[j * b + d],
                    cores[j - 1],
                )
                for j in range(1, g)
            ]
            for d in range(b)
        ]
        own = Staged(source.at[s], target.at[r * b + s], stage, sems)
        return swaps, shares, own

    def first(self, *refs):
        swaps, shares, own = self.parts(*refs)
        for copy in swaps:
            copy.start()
        own.first()
        for copy in shares[0]:
            copy.start()

    def middle(self, *refs):
        swaps, shares, own = self.parts(*refs)
        for d in [1, 3, 2] if self.streams == 4 else range(1, self.streams):
            swaps[d - 1].wait_recv()
            for copy in shares[d]:
                copy.start()

    def last(self, *refs):
        swaps, shares, own = self.parts(*refs)
        own.last()
        for row in shares:
            for copy in row:
                copy.wait()
        for copy in swaps:
            copy.wait_send()


class Swap:
    def __init__(self, streams, groups, block, dtype):
        self.streams, self.groups, self.block, self.dtype = streams, groups, block, dtype

    def scratch(self):
        return [dma(self.streams), dma(self.streams), pltpu.VMEM(self.block, self.dtype), dma(2)]

    def out_shape(self):
        return jax.ShapeDtypeStruct((self.streams,) + self.block, self.dtype)

    def peers(self):
        return [("stream", stream_peers(self.streams, self.groups))]

    def parts(self, source, target, send, recv, stage, sems):
        b, g = self.streams, self.groups
        s, r = place(g)
        peers = stream_peers(b, g)
        swaps = [
            remote(source.at[lax.rem(s + d, b)], target.at[s], send.at[d], recv.at[d], peers[d - 1])
            for d in range(1, b)
        ]
        return swaps, Staged(source.at[s], target.at[s], stage, sems)

    def first(self, *refs):
        swaps, own = self.parts(*refs)
        for copy in swaps:
            copy.start()
        own.first()

    def last(self, *refs):
        swaps, own = self.parts(*refs)
        own.last()
        for copy in swaps:
            copy.wait()


class Spread:
    def __init__(self, block, dtype):
        self.block, self.dtype = block, dtype

    def scratch(self):
        size = lax.axis_size("dp")
        return [dma(size), dma(size), pltpu.VMEM(self.block, self.dtype), dma(2)]

    def out_shape(self):
        return jax.ShapeDtypeStruct((lax.axis_size("dp"),) + self.block, self.dtype)

    def peers(self):
        return [("dp", dp_peers())]

    def parts(self, source, target, send, recv, stage, sems):
        here = lax.axis_index("dp")
        copies = [
            remote(source, target.at[here], send.at[d], recv.at[d], peer)
            for d, peer in enumerate(dp_peers(), 1)
        ]
        return copies, Staged(source, target.at[here], stage, sems)

    first = Swap.first
    last = Swap.last


class Tiles:
    def __init__(self, bag, name, groups, pairs, per_owner):
        self.name, self.groups, self.pairs, self.per_owner = name, groups, pairs, per_owner
        count = pairs * per_owner
        bag.add(f"{name}_s", dma(groups * count))
        bag.add(f"{name}_r", dma(groups * count))

    def slot(self, who, pair, at):
        return (who * self.pairs + pair) * self.per_owner + at

    def copy(self, have, source, target, owner, pair, at):
        s, r = place(self.groups)
        return remote(
            source,
            target,
            have[f"{self.name}_s"].at[self.slot(owner, pair, at)],
            have[f"{self.name}_r"].at[self.slot(r, pair, at)],
            {"blk": s * self.groups + owner},
        )

    def own(self, have, source, target, pair, at):
        s, r = place(self.groups)
        return pltpu.make_async_copy(
            source, target, have[f"{self.name}_s"].at[self.slot(r, pair, at)]
        )

    def finish(self, have, source, target):
        s, r = place(self.groups)
        for pair in range(self.pairs):
            for at in range(self.per_owner):
                self.own(have, source, target, pair, at).wait()
                for j in range(1, self.groups):
                    other = lax.rem(r + j, self.groups)
                    remote(
                        source,
                        target,
                        have[f"{self.name}_s"].at[self.slot(other, pair, at)],
                        have[f"{self.name}_r"].at[self.slot(other, pair, at)],
                        {"blk": s * self.groups + other},
                    ).wait()


class Bag:
    def __init__(self):
        self.items = {}

    def add(self, name, item):
        self.items[name] = item

    def bind(self, refs):
        return dict(zip(self.items, refs))


class Reduce:
    def __init__(self, bag, name, streams, groups, shapes, over_cores, two_step):
        self.name, self.streams, self.groups = name, streams, groups
        self.size = lax.axis_size("dp")
        self.over_cores = over_cores
        self.two_step = two_step and self.size == 4 and streams % 2 == 0
        self.count = len(shapes)
        share = self.size * (groups if over_cores else 1)
        self.shapes = [(rows // share, cols) for rows, cols in shapes]
        self.wires = [BF if (c // streams) % 16 == 0 else F32 for c, cols in self.shapes]
        for i, (chunk, cols) in enumerate(self.shapes):
            wire, slim = self.wires[i], chunk // streams
            bag.add(f"{name}half{i}", pltpu.VMEM((self.size, chunk, cols), wire))
            if over_cores:
                bag.add(f"{name}core{i}", pltpu.VMEM((groups - 1, self.size, chunk, cols), wire))
            if self.two_step:
                bag.add(f"{name}first{i}", pltpu.VMEM((4, chunk // 2, cols), wire))
                bag.add(f"{name}second{i}", pltpu.VMEM((2, chunk // 2, cols), wire))
            else:
                bag.add(f"{name}dp{i}", pltpu.VMEM((self.size - 1, chunk, cols), wire))
            bag.add(f"{name}cut{i}", pltpu.VMEM((streams, slim, cols), wire))
            bag.add(f"{name}z{i}", pltpu.VMEM((streams - 1, slim, cols), wire))
            bag.add(f"{name}fin{i}", pltpu.VMEM((slim, cols), wire))
            for kind in self.kinds():
                bag.add(f"{name}{kind}s{i}", dma(self.sem_count(kind)))
                bag.add(f"{name}{kind}r{i}", dma(self.sem_count(kind)))
            bag.add(f"{name}local{i}", dma(2))

    def kinds(self):
        along = ["b1", "b2", "c", "d", "e1", "e2"] if self.two_step else ["b", "c", "d", "e"]
        return (["a"] if self.over_cores else []) + along + ["f"]

    def sem_count(self, kind):
        if kind in ("a", "f"):
            return self.groups
        if kind in ("c", "d"):
            return self.streams
        return max(self.size, 4)

    def out_shapes(self):
        return [
            jax.ShapeDtypeStruct(
                (self.groups, self.size, self.streams, chunk // self.streams, cols), wire
            )
            for (chunk, cols), wire in zip(self.shapes, self.wires)
        ]

    def bind(self, sources, targets, scratch):
        self.sources, self.targets, self.scratch = sources, targets, scratch

    def get(self, what, i):
        return self.scratch[f"{self.name}{what}{i}"]

    def pairs(self, kind, i):
        s, r = place(self.groups)
        here = lax.axis_index("dp")
        b, g, size = self.streams, self.groups, self.size
        x, y = lax.rem(here, 2), here // 2
        beside_x, beside_y = {"dp": 2 * y + 1 - x}, {"dp": 2 * (1 - y) + x}
        if kind == "a":
            for d, peer in enumerate(core_peers(g), 1):
                yield d, self.sources[i].at[lax.rem(r + d, g)], self.get("core", i).at[d - 1], peer
        elif kind == "b":
            half, box = self.get("half", i), self.get("dp", i)
            for d, peer in enumerate(dp_peers(), 1):
                yield d, half.at[lax.rem(here + d, size)], box.at[d - 1], peer
        elif kind == "b1":
            half, box, h = self.get("half", i), self.get("first", i), self.shapes[i][0] // 2
            for n in range(2):
                yield n, half.at[2 * n + 1 - x, pl.ds(0, h)], box.at[n], beside_x
                yield 2 + n, half.at[2 * (1 - y) + n, pl.ds(h, h)], box.at[2 + n], beside_y
        elif kind == "b2":
            half, box, h = self.get("half", i), self.get("second", i), self.shapes[i][0] // 2
            yield 0, half.at[2 * (1 - y) + x, pl.ds(0, h)], box.at[0], beside_y
            yield 1, half.at[2 * y + 1 - x, pl.ds(h, h)], box.at[1], beside_x
        elif kind in "cd":
            peers = list(enumerate(stream_peers(b, g), 1))
            for d, peer in [peers[1], peers[0], peers[2]] if b == 4 else peers:
                if kind == "c":
                    cut = self.get("cut", i)
                    yield d, cut.at[lax.rem(s + d, b)], self.get("z", i).at[d - 1], peer
                else:
                    yield d, self.get("fin", i), self.targets[i].at[r, here, s], peer
        elif kind == "e":
            whole = self.targets[i].at[r, here]
            for d, peer in enumerate(dp_peers(), 1):
                yield d, whole, whole, peer
        elif kind == "e1":
            for n, peer in enumerate((beside_y, beside_x)):
                part = self.targets[i].at[r, here, pl.ds(n * b // 2, b // 2)]
                yield n, part, part, peer
        elif kind == "e2":
            for n in range(2):
                part = self.targets[i].at[r, 2 * n + x, pl.ds(0, b // 2)]
                yield n, part, part, beside_x
                part = self.targets[i].at[r, 2 * y + n, pl.ds(b // 2, b // 2)]
                yield 2 + n, part, part, beside_y
        else:
            whole = self.targets[i].at[r]
            for d, peer in enumerate(core_peers(g), 1):
                yield d, whole, whole, peer

    def copies(self, kind, i):
        send, recv = self.get(kind + "s", i), self.get(kind + "r", i)
        for n, source, target, peer in self.pairs(kind, i):
            yield remote(source, target, send.at[n], recv.at[n], peer)

    def start(self, kind, i):
        for copy in self.copies(kind, i):
            copy.start()

    def arrive(self, kind, i):
        for copy in self.copies(kind, i):
            copy.wait_recv()

    def load(self, i):
        s, r = place(self.groups)
        return pltpu.make_async_copy(
            self.sources[i].at[r], self.get("half", i), self.get("local", i).at[0]
        )

    def keep(self, i):
        s, r = place(self.groups)
        return pltpu.make_async_copy(
            self.get("fin", i),
            self.targets[i].at[r, lax.axis_index("dp"), s],
            self.get("local", i).at[1],
        )

    def stages(self):
        middle = [self.dp_middle] if self.two_step else []
        back = [self.dp_back_middle] if self.two_step else []
        return [self.dp_start, *middle, self.z_start, self.z_back, self.dp_back, *back, self.core_back]

    def core_start(self):
        for i in range(self.count):
            self.start("a", i)
            self.load(i).start()

    def dp_start(self):
        for i in range(self.count):
            if self.over_cores:
                self.load(i).wait()
                self.arrive("a", i)
                half, box, wire = self.get("half", i), self.get("core", i), self.wires[i]
                for p in range(self.size):
                    total = half[p].astype(F32)
                    for j in range(self.groups - 1):
                        total = total + box[j, p].astype(F32)
                    half[p] = total.astype(wire)
            self.start("b1" if self.two_step else "b", i)

    def dp_middle(self):
        here = lax.axis_index("dp")
        x, y = lax.rem(here, 2), here // 2
        for i in range(self.count):
            self.arrive("b1", i)
            half, box, wire = self.get("half", i), self.get("first", i), self.wires[i]
            h = self.shapes[i][0] // 2
            for n in range(2):
                for who, at, part in ((2 * n + x, pl.ds(0, h), n), (2 * y + n, pl.ds(h, h), 2 + n)):
                    total = half[who, at, :].astype(F32) + box[part].astype(F32)
                    half[who, at, :] = total.astype(wire)
            self.start("b2", i)

    def z_start(self):
        here = lax.axis_index("dp")
        for i in range(self.count):
            self.arrive("b2" if self.two_step else "b", i)
            half, cut, wire = self.get("half", i), self.get("cut", i), self.wires[i]
            chunk = self.shapes[i][0]
            slim = chunk // self.streams
            for z in range(self.streams):
                at = slice(z * slim, (z + 1) * slim)
                total = half[here, at, :].astype(F32)
                if self.two_step:
                    which, first = divmod(z * slim, chunk // 2)
                    total = total + self.get("second", i)[which, first : first + slim].astype(F32)
                else:
                    for d in range(self.size - 1):
                        total = total + self.get("dp", i)[d, at, :].astype(F32)
                cut[z] = total.astype(wire)
            self.start("c", i)

    def z_back(self):
        s, r = place(self.groups)
        for i in range(self.count):
            self.arrive("c", i)
            box = self.get("z", i)
            total = self.get("cut", i)[s].astype(F32)
            for d in range(self.streams - 1):
                total = total + box[d].astype(F32)
            self.get("fin", i)[...] = total.astype(self.wires[i])
            self.keep(i).start()
            self.start("d", i)

    def dp_back(self):
        for i in range(self.count):
            self.keep(i).wait()
            self.arrive("d", i)
            self.start("e1" if self.two_step else "e", i)

    def dp_back_middle(self):
        for i in range(self.count):
            self.arrive("e1", i)
            self.start("e2", i)

    def core_back(self):
        for i in range(self.count):
            self.arrive("e2" if self.two_step else "e", i)
            self.start("f", i)

    def end(self):
        for i in range(self.count):
            self.arrive("f", i)
            for kind in self.kinds():
                for copy in self.copies(kind, i):
                    copy.wait_send()


class Moves:
    def __init__(self, *jobs, others=()):
        self.jobs, self.others = list(jobs), list(others)
        self.counts = [len(job.scratch()) for job in jobs]

    def scratch(self):
        return [item for job in self.jobs for item in job.scratch()]

    def out_shapes(self):
        return [job.out_shape() for job in self.jobs]

    def spaces(self):
        return [pl.BlockSpec(memory_space=pl.ANY)] * len(self.jobs)

    def each(self, sources, targets, scratch):
        at = 0
        for job, count, source, target in zip(self.jobs, self.counts, sources, targets):
            yield job, (source, target, *scratch[at : at + count])
            at += count

    def first(self, sources, targets, scratch, count=None):
        greet(unique(self.jobs + self.others))
        for job, refs in list(self.each(sources, targets, scratch))[:count]:
            job.first(*refs)

    def start_last(self, sources, targets, scratch):
        for job, refs in list(self.each(sources, targets, scratch))[-1:]:
            job.first(*refs)

    def middle(self, sources, targets, scratch):
        for job, refs in self.each(sources, targets, scratch):
            if isinstance(job, Gather):
                job.middle(*refs)

    def last(self, sources, targets, scratch):
        for job, refs in self.each(sources, targets, scratch):
            job.last(*refs)


def remote_params(collective_id):
    return pltpu.CompilerParams(
        collective_id=collective_id, has_side_effects=True, vmem_limit_bytes=VMEM_BYTES
    )


def binary_columns(latent):
    matrix = latent.astype(F32)
    scale = jnp.sqrt(jnp.mean(matrix * matrix, axis=0, keepdims=True) + 1e-06)
    return (scale * jnp.tanh(matrix * (2.0 / scale))).astype(BF)


def intake_kernel(moves, groups, *refs):
    count = len(moves.jobs)
    latents, ids_ref, refs = refs[:4], refs[4], refs[5:]
    sources, refs = refs[: count - 1], refs[count - 1 :]
    results, refs = refs[:4], refs[4:]
    targets, refs = refs[:count], refs[count:]
    loaded, made, sems = refs[:4], refs[4:8], refs[8]
    ids_in, ids_box, *scratch = refs[9:]
    sources = (*sources, ids_box)
    moves.first(sources, targets, scratch, count - 1)
    s, r = place(groups)
    width = results[0].shape[3]
    own = pl.ds(pl.multiple_of(r * width, 128), width)
    places = [latents[0].at[:, :, own], *latents[1:]]
    loads = [
        pltpu.make_async_copy(source, target, sems.at[i])
        for i, (source, target) in enumerate(zip(places, loaded))
    ]
    stores = [
        pltpu.make_async_copy(source, target, sems.at[4 + i])
        for i, (source, target) in enumerate(zip(made, [results[0].at[0], *results[1:]]))
    ]
    fetch = pltpu.make_async_copy(ids_ref, ids_in, sems.at[8])
    fetch.start()
    for copy in loads:
        copy.start()
    fetch.wait()
    ids = ids_in[...].astype(F32)
    for i in range(ids.shape[0]):
        ids_box[i] = jnp.broadcast_to(ids[i : i + 1, :], ids_box.shape[1:])
    moves.start_last(sources, targets, scratch)
    loads[0].wait()
    for i in range(3):
        made[0][i] = binary_columns(loaded[0][i])
    stores[0].start()
    for n in range(1, 4):
        loads[n].wait()
        for i in range(0, loaded[n].shape[1], 128):
            made[n][:, i : i + 128] = binary_columns(loaded[n][:, i : i + 128])
        stores[n].start()
    moves.middle(sources, targets, scratch)
    for copy in stores:
        copy.wait()
    moves.last(sources, targets, scratch)


def intake(moves, groups, latents, ids, arrays, collective_id):
    three, depth, unused = latents[0].shape
    own_shape = (three, depth, depth // groups)
    shapes = [(1,) + own_shape] + [a.shape for a in latents[1:]]
    buffers = [pltpu.VMEM(shape, BF) for shape in [own_shape] + shapes[1:]]
    any_space = [pl.BlockSpec(memory_space=pl.ANY)] * 4
    return pl.pallas_call(
        functools.partial(intake_kernel, moves, groups),
        out_shape=[jax.ShapeDtypeStruct(shape, BF) for shape in shapes] + moves.out_shapes(),
        in_specs=any_space
        + moves.spaces(),
        out_specs=any_space + moves.spaces(),
        scratch_shapes=buffers * 2
        + [dma(9), pltpu.VMEM(ids.shape, ids.dtype)]
        + [pltpu.VMEM((ids.shape[0], 8, ids.shape[1]), F32)]
        + moves.scratch(),
        compiler_params=remote_params(collective_id),
        name="intake",
    )(*latents, ids, *arrays)


def lanes_of(shape):
    return lax.broadcasted_iota(jnp.int32, shape, 1)


def forward_kernel(
    moves, keep, streams, groups, tile, bag, tiles, x_ref, w_ref, bias_ref, docs_ref, *rest
):
    count = len(moves.jobs)
    sources, rest = rest[:count], rest[count:]
    q_ref, k_ref, rows_ref, *rest = rest
    if keep:
        v_ref, e_ref, ctx_ref, inv_ref, active_ref, *rest = rest
    targets, rest = rest[:count], rest[count:]
    have = bag.bind(rest)
    scratch = tuple(have[f"moves{i}"] for i in range(len(moves.scratch())))
    k_aug, v_aug, ctx_all, mask, edges = (
        have["k_aug"],
        have["v_aug"],
        have["ctx_all"],
        have["mask"],
        have["edges"],
    )
    active = active_ref if keep else x_ref
    row_ref = have["row"]
    pair, step = pl.program_id(0), pl.program_id(1)
    pairs, steps = pl.num_programs(0), pl.num_programs(1)
    seq = k_ref.shape[0]
    s, r = place(groups)
    sub = min(256, tile)
    width = w_ref.shape[3]
    n_pairs = ctx_all.shape[0]
    offset = pair * 128 if width == n_pairs * 128 else (r * n_pairs + pair) * 128
    offset = pl.multiple_of(offset, 128)
    home = pl.multiple_of((r * n_pairs + pair) * 128, 128)

    @pl.when((pair == 0) & (step == 0))
    def _():
        moves.first(sources, targets, scratch)
        ids = stream_row(docs_ref)
        row_ref[...] = ids
        big_at = long_at(streams, groups, seq)
        big = ids[:, big_at : big_at + 1]
        mask[...] = jnp.where(ids == big, 0.0, masked_score)
        edges[0] = jnp.broadcast_to(ids[:, :sub], (128, sub)).T
        edges[1] = jnp.broadcast_to(ids[:, seq - sub :], (128, sub)).T
        if keep:
            for i in range(0, seq, 256):
                active_ref[i : i + 256, :] = squash(x_ref[i : i + 256, :].astype(F32)).astype(BF)

    @pl.when((pair == pairs - 1) & (step == steps - 2))
    def _():
        moves.middle(sources, targets, scratch)

    @pl.when(step == 0)
    def _():
        columns = pl.ds(offset, 128)

        def project(i, bias):
            matrix = jnp.concatenate(
                [w_ref[d, i, :, columns] for d in range(w_ref.shape[0])], axis=0
            )
            result = dot(active[...], matrix)
            if bias is not None:
                result = result + bias_ref[bias : bias + 1, pl.ds(home, 128)]
            return result.astype(BF)

        low = lanes_of((seq, 128)) < 64
        lane = lanes_of((seq, 128))
        q_ref[...] = (project(0, 0).astype(F32) * 0.125).astype(BF)
        keys = project(1, None)
        k_ref[...] = keys
        keys = keys.astype(F32)
        turned = pltpu.roll(keys, 64, 1)
        k_aug[0] = jnp.where(low, keys, turned).astype(BF)
        k_aug[1] = jnp.where(low, turned, keys).astype(BF)
        values = project(2, 1)
        if keep:
            v_ref[...] = values
        values = values.astype(F32)
        v_aug[0] = jnp.where(low, values, jnp.where(lane < 66, 1.0, 0.0)).astype(BF)
        v_aug[1] = jnp.where(low, jnp.where(lane < 2, 1.0, 0.0), values).astype(BF)

    start = pl.multiple_of(step * tile, tile)

    def body(edge_at):
        low = lanes_of((sub, 128)) < 64
        parts = []
        for at in range(0, tile, sub):
            scaled = q_ref[pl.ds(start + at, sub), :].astype(F32) * LOG2E
            upper = scaled.astype(BF).astype(F32)
            lower = scaled - upper
            parts.append(
                (
                    jnp.where(low, upper, pltpu.roll(lower, 64, 1)).astype(BF),
                    jnp.where(low, pltpu.roll(upper, 64, 1), lower).astype(BF),
                )
            )
        chains = [(at, h) for at in range(0, tile, sub) for h in range(2)]

        def scores_of(at, h):
            scores = dot(parts[at // sub][h], k_aug[h], NT)
            if edge_at is not None and at == (0 if edge_at == 0 else tile - sub):
                return jnp.where(edges[edge_at][:, :1] == row_ref[...], scores, masked_score)
            return jnp.concatenate(
                [
                    scores[:, :sub] + mask[:, :sub],
                    scores[:, sub : seq - sub],
                    scores[:, seq - sub :] + mask[:, seq - sub :],
                ],
                axis=1,
            )

        scores = scores_of(*chains[0])
        results = {}
        for n, (at, h) in enumerate(chains):
            if n + 1 < len(chains):
                later = scores_of(*chains[n + 1])
            peak = jnp.max(scores, axis=1, keepdims=True)
            numerators = jnp.exp2(scores - peak).astype(BF)
            if keep:
                e_ref[h, at : at + sub, :] = numerators
            total = dot(numerators, v_aug[h])
            where_sum = 64 if h == 0 else 0
            inverse = 1.0 / total[:, where_sum : where_sum + 1]
            results[h] = (total * inverse, inverse)
            if n + 1 < len(chains):
                scores = later
            if h == 1:
                done = jnp.where(low, results[0][0], results[1][0]).astype(BF)
                ctx_all[pair, pl.ds(start + at, sub), :] = done
                if keep:
                    ctx_ref[at : at + sub, :] = done
                    inv_ref[at : at + sub, :] = jnp.where(low, results[0][1], results[1][1])

    @pl.when(step == 0)
    def _():
        body(0)

    @pl.when(step == steps - 1)
    def _():
        body(1)

    @pl.when((step > 0) & (step < steps - 1))
    def _():
        body(None)

    owned = seq // groups
    owner = start // owned
    at = lax.rem(step, owned // tile)
    source = ctx_all.at[pair, pl.ds(start, tile)]
    target = rows_ref.at[r, pair, pl.ds(pl.multiple_of(lax.rem(start, owned), tile), tile)]

    @pl.when(owner == r)
    def _():
        tiles.own(have, source, target, pair, at).start()

    @pl.when(owner != r)
    def _():
        tiles.copy(have, source, target, owner, pair, at).start()

    @pl.when((pair == pairs - 1) & (step == steps - 1))
    def _():
        tiles.finish(have, source, target)
        moves.last(sources, targets, scratch)


def stream_row(docs_ref):
    return jnp.concatenate([docs_ref[i, 0:1, :] for i in range(docs_ref.shape[0])], axis=1)


def long_at(streams, groups, seq):
    shard = seq // (streams * groups)
    return streams * shard if groups > 1 else shard


def attention(x, weights, bias, docs, streams, groups, moves, moved, keep, collective_id, name):
    seq, depth = x.shape
    width = depth // groups
    pairs = width // 128
    tile = 512
    owned = seq // groups
    bag = Bag()
    bag.add("k_aug", pltpu.VMEM((2, seq, 128), BF))
    bag.add("v_aug", pltpu.VMEM((2, seq, 128), BF))
    bag.add("ctx_all", pltpu.VMEM((pairs, seq, 128), BF))
    bag.add("mask", pltpu.VMEM((1, seq), F32))
    bag.add("row", pltpu.VMEM((1, seq), F32))
    bag.add("edges", pltpu.VMEM((2, 256, 128), F32))
    tiles = Tiles(bag, "tiles", groups, pairs, owned // tile)
    for i, item in enumerate(moves.scratch()):
        bag.add(f"moves{i}", item)

    def constant(shape):
        return pl.BlockSpec(shape, lambda p, i: (0,) * len(shape))

    part = pl.BlockSpec((tile, 128), lambda p, i: (i, p))
    whole = pl.BlockSpec((seq, 128), lambda p, i: (0, p))
    any_space = pl.BlockSpec(memory_space=pl.ANY)
    wide = jax.ShapeDtypeStruct((seq, width), BF)
    outs = [whole, whole, any_space]
    shapes = [wide, wide, jax.ShapeDtypeStruct((groups, pairs, owned, 128), BF)]
    if keep:
        outs += [
            whole,
            pl.BlockSpec((2, tile, seq), lambda p, i: (p, i, 0)),
            part,
            part,
            constant((seq, depth)),
        ]
        shapes += [
            wide,
            jax.ShapeDtypeStruct((2 * pairs, seq, seq), BF),
            wide,
            jax.ShapeDtypeStruct((seq, width), F32),
            jax.ShapeDtypeStruct((seq, depth), BF),
        ]
    return pl.pallas_call(
        functools.partial(forward_kernel, moves, keep, streams, groups, tile, bag, tiles),
        grid=(pairs, seq // tile),
        in_specs=[constant(a.shape) for a in (x, weights, bias, docs)]
        + moves.spaces(),
        out_specs=outs + moves.spaces(),
        out_shape=shapes + moves.out_shapes(),
        scratch_shapes=list(bag.items.values()),
        compiler_params=remote_params(collective_id),
        name=name,
    )(x, weights, bias, docs, *moved)


def split(matrix):
    upper = matrix.astype(BF)
    return upper, (matrix - upper.astype(F32)).astype(BF)


def backward_kernel(
    streams,
    groups,
    tile,
    bag,
    early,
    late,
    e_ref,
    q_ref,
    k_ref,
    v_ref,
    tq_ref,
    tk_ref,
    dc_ref,
    ctx_ref,
    inv_ref,
    docs_ref,
    small_ref,
    active_hbm,
    bin_hbm,
    d1_hbm,
    tokens_hbm,
    *rest,
):
    n_early = sum(job.count for job in early)
    sources, rest = rest[:n_early], rest[n_early:]
    grad_ref, *rest = rest
    early_out, rest = rest[:n_early], rest[n_early:]
    late_out, (gain_ref, bias_ref, shift_ref, *rest) = rest[: len(late)], rest[len(late) :]
    have = bag.bind(rest)
    at = 0
    for job in early:
        job.bind(sources[at : at + job.count], early_out[at : at + job.count], have)
        at += job.count
    for job, target in zip(late, late_out):
        job.bind(None, [target], have)

    pair, step = pl.program_id(0), pl.program_id(1)
    pairs, steps = len(late), q_ref.shape[0] // tile
    seq = k_ref.shape[0]
    share = 1.0 / seq
    time = pair * steps + step
    total_time = pairs * steps
    size = lax.axis_size("dp")
    here = lax.axis_index("dp")
    s, r = place(groups)
    rows, depth = d1_hbm.shape
    width = pairs * 128
    v_aug, dk_acc, dv_acc, grams = have["v_aug"], have["dk_acc"], have["dv_acc"], have["grams"]
    dq_all, d_act, active, weights = have["dq_all"], have["d_act"], have["active"], have["weights"]
    d_one, x_rows = have["d_one"], have["x_rows"]
    edges, in_big, pair_box = have["edges"], have["in_big"], have["pair_box"]
    row_ref = have["row"]
    along_z, cores, along_dp = stream_peers(streams, groups), core_peers(groups), dp_peers()

    def loads():
        sems = have["load"]
        return [
            pltpu.make_async_copy(active_hbm, active, sems.at[0]),
            pltpu.make_async_copy(bin_hbm, weights, sems.at[1]),
            pltpu.make_async_copy(d1_hbm, d_one, sems.at[2]),
            pltpu.make_async_copy(tokens_hbm.at[pl.ds(r * streams, streams)], x_rows, sems.at[3]),
        ]

    def at_time(when, *work):
        @pl.when(time == when)
        def _():
            for item in work:
                item()

    def begin():
        greet(along_z + cores + along_dp)
        for job in early:
            job.core_start()
        for copy in loads():
            copy.start()
        ids = stream_row(docs_ref)
        row_ref[...] = ids
        big_at = long_at(streams, groups, seq)
        big = ids[:, big_at : big_at + 1]
        for n, first in enumerate((0, seq - tile)):
            column = jnp.broadcast_to(ids[:, first : first + tile], (128, tile)).T
            edges[n] = column
            in_big[n] = jnp.where(column == big, 1.0, 0.0)

    def big_rows(ref):
        return jnp.concatenate(
            [
                (ref[:tile, :].astype(F32) * in_big[0]).astype(BF),
                ref[tile : seq - tile, :],
                (ref[seq - tile :, :].astype(F32) * in_big[1]).astype(BF),
            ],
            axis=0,
        )

    at_time(0, begin)
    unit = total_time / 16
    left = []
    for n, job in enumerate(early):
        stages, times = job.stages(), EARLY_TIMES[n]
        if not job.two_step:
            times = times[:1] + times[2:5] + times[6:]
        for when, work in zip(times, stages):
            at_time(int(when * unit), work)
        left.append(stages[len(times) :])
    for p, job in enumerate(late[:-1]):
        first = (p + 1) * steps
        for when, work in zip(LATE_TIMES, job.stages()):
            at_time(first + when, work)
        left.append(job.stages()[len(LATE_TIMES) :])

    def go_on(count):
        for unused in range(count):
            for queue in left:
                if queue:
                    queue.pop(0)()

    @pl.when(step == 0)
    def _():
        lane = lanes_of((seq, 128))
        low = lane < 64
        values = v_ref[...].astype(F32)
        v_aug[0] = jnp.where(low, values, jnp.where(lane < 66, 1.0, 0.0)).astype(BF)
        v_aug[1] = jnp.where(low, jnp.where(lane < 2, 1.0, 0.0), values).astype(BF)
        dk_acc[...] = jnp.zeros_like(dk_acc)
        dv_acc[...] = jnp.zeros_like(dv_acc)
        kb, tkb, qb, tqb = (big_rows(ref) for ref in (k_ref, tk_ref, q_ref, tq_ref))
        same_head = (lax.broadcasted_iota(jnp.int32, (128, 128), 0) < 64) == (
            lanes_of((128, 128)) < 64
        )
        for i, (a, b) in enumerate(((kb, kb), (tkb, kb), (qb, qb), (tqb, qb))):
            gram = jnp.where(same_head, dot(a, b, TN) * share, 0.0)
            grams[2 * i], grams[2 * i + 1] = split(gram)

    start = pl.multiple_of(step * tile, tile)
    rows_here = pl.ds(start, tile)
    lane = lanes_of((tile, 128))
    low = lane < 64

    def body(whole, columns):
        edge = 0 if whole and columns.start == 0 else 1
        q8 = q_ref[rows_here, :]
        tq8 = tq_ref[rows_here, :]
        dc = dc_ref[...].astype(F32)
        inv = inv_ref[...]
        scaled = dc * inv
        product = scaled * ctx_ref[...].astype(F32)
        scaled_low = scaled.astype(BF)
        q_turned = q8.astype(F32).T.astype(BF)
        dc_turned = scaled_low.astype(F32).T.astype(BF)
        d_queries = []
        for h in range(2):
            mine = low if h == 0 else jnp.logical_not(low)
            delta = -jnp.sum(jnp.where(mine, product, 0.0), axis=1, keepdims=True)
            upper = delta.astype(BF).astype(F32)
            first = 64 if h == 0 else 0
            extra = jnp.where(
                lane == first, upper, jnp.where(lane == first + 1, delta - upper, 0.0)
            )
            dc_aug = jnp.where(mine, scaled, extra).astype(BF)
            numerators = e_ref[h]
            d_probs = dot(dc_aug, v_aug[h], NT)
            d_scores = numerators.astype(F32) * d_probs
            if whole:
                q_mine = jnp.where(mine, q8, 0.0).astype(BF)
                tq_mine = jnp.where(mine, tq8, 0.0).astype(BF)
                gap = dot(q_mine, k_ref[columns, :], NT) - dot(tq_mine, tk_ref[columns, :], NT)
                same = jnp.where(edges[edge][:, :1] == row_ref[:, columns], share, 0.0)
                gap = gap * (same * (1.0 - in_big[edge][:, :1]))
                if columns.start == 0:
                    d_scores = jnp.concatenate(
                        [d_scores[:, :tile] + gap, d_scores[:, tile:]], axis=1
                    )
                else:
                    d_scores = jnp.concatenate(
                        [d_scores[:, : seq - tile], d_scores[:, seq - tile :] + gap], axis=1
                    )
            d_scores = d_scores.astype(BF)
            d_queries.append(dot(d_scores, k_ref[...]))
            half = slice(64 * h, 64 * h + 64)
            dk_acc[half, :] += dot(q_turned[half, :], d_scores)
            dv_acc[half, :] += dot(dc_turned[half, :], numerators)
        d_query = jnp.where(low, d_queries[0], d_queries[1])
        qb, tqb = q8, tq8
        if whole:
            qb = (q8.astype(F32) * in_big[edge]).astype(BF)
            tqb = (tq8.astype(F32) * in_big[edge]).astype(BF)
        d_query += dot(qb, grams[0]) + dot(qb, grams[1]) - dot(tqb, grams[2]) - dot(tqb, grams[3])
        dq_all[rows_here, :] = (d_query * 0.125).astype(BF)

    @pl.when(step == 0)
    def _():
        body(True, slice(0, tile))

    @pl.when(step == steps - 1)
    def _():
        body(True, slice(seq - tile, seq))

    @pl.when((step > 0) & (step < steps - 1))
    def _():
        body(False, None)

    def pair_end(p):
        job = late[p]
        kb, tkb = big_rows(k_ref), big_rows(tk_ref)
        d_key = dk_acc[...].T
        d_key += dot(kb, grams[4]) + dot(kb, grams[5]) - dot(tkb, grams[6]) - dot(tkb, grams[7])
        d_value = dv_acc[...].T.astype(BF)
        d_query = dq_all[...]
        d_pair = jnp.concatenate([d_query, d_key.astype(BF), d_value], axis=1)
        if p == 0:
            for copy in loads():
                copy.wait()
        columns = slice(p * 128, (p + 1) * 128)
        bins = jnp.concatenate([weights[0, i, :, columns] for i in range(3)], axis=1)
        chunk = depth // size
        half = job.get("half", 0)
        partial = dot(active[...], d_pair, TN).astype(job.wires[0])
        for d in range(size):
            half[d] = partial[d * chunk : (d + 1) * chunk, :]
        if p == pairs - 1:
            job.dp_start()
        if p < pairs - 1:
            if p == 0:
                d_act[...] = dot(d_pair, bins, NT)
            else:
                d_act[...] += dot(d_pair, bins, NT)
        else:
            pair_box[...] = d_pair
            for j in range(1, groups + 1):
                at = pl.ds(pl.multiple_of(lax.rem(r + j, groups) * rows, rows), rows)
                total = dot(pair_box[at, :], bins, NT)
                if p > 0:
                    total = total + d_act[at, :]
                if j < groups:
                    have["outbox"][j - 1] = total.astype(BF)
                    core_copies()[j - 1].start()
                else:
                    d_act[at, :] = total
        sums = have["sums"]
        sums[0:1, columns] = jnp.sum(d_query.astype(F32), axis=0, keepdims=True)
        sums[1:2, columns] = jnp.sum(d_value.astype(F32), axis=0, keepdims=True)

    def core_copies():
        return [
            remote(
                have["outbox"].at[j - 1],
                have["inbox"].at[j - 1],
                have["core_s"].at[j],
                have["core_r"].at[j],
                cores[j - 1],
            )
            for j in range(1, groups)
        ]

    def small_copies(stage, peers, base):
        return [
            remote(
                have["small"].at[stage],
                have["small_box"].at[base + d],
                have["small_s"].at[base + d],
                have["small_r"].at[base + d],
                peer,
            )
            for d, peer in enumerate(peers)
        ]

    def small_start(stage, peers, base):
        for copy in small_copies(stage, peers, base):
            copy.start()

    def small_sum(stage, peers, base):
        for copy in small_copies(stage, peers, base):
            copy.wait_recv()
        total = have["small"][stage]
        for d in range(len(peers)):
            total = total + have["small_box"][base + d]
        return total

    for p in range(pairs - 1):

        @pl.when((pair == p) & (step == steps - 1))
        def _():
            pair_end(p)

    @pl.when(time == total_time - 1)
    def _():
        pair_end(pairs - 1)
        last = late[-1]
        small = have["small"]
        small[0] = small_ref[...]
        for i in range(2):
            vector = have["sums"][i : i + 1, :]
            small[0, 2 + i : 3 + i, :] = jnp.concatenate(
                [jnp.where(r == j, vector, 0.0) for j in range(groups)], axis=1
            )
        small_start(0, along_dp, 0)
        go_on(TAIL[0])
        last.z_start()
        last.z_back()
        for copy in core_copies():
            copy.wait_recv()
        shard = rows // streams
        back_copies = []
        blocks = have["blocks"]
        order = [2, 1, 3] if streams == 4 else list(range(1, streams))
        for d in order + [0]:
            target = lax.rem(s + d, streams)
            here_rows = pl.ds(pl.multiple_of(target * shard, shard), shard)
            bent = jnp.tanh(x_rows[target].astype(F32) * (1.0 / clip_level))
            total = d_act[pl.ds(pl.multiple_of(r * rows + target * shard, shard), shard), :]
            for j in range(groups - 1):
                total = total + have["inbox"][j, here_rows, :].astype(F32)
            blocks[target] = (d_one[here_rows, :] + total * (1.0 - bent * bent)).astype(BF)
            if d:
                copy = remote(
                    blocks.at[target],
                    grad_ref.at[s],
                    have["grad_s"].at[d],
                    have["grad_r"].at[d],
                    along_z[d - 1],
                )
            else:
                copy = pltpu.make_async_copy(blocks.at[s], grad_ref.at[s], have["grad_s"].at[0])
            copy.start()
            back_copies.append(copy)
        small[1] = small_sum(0, along_dp, 0)
        small_start(1, along_z, size)
        go_on(TAIL[1])
        small[2] = small_sum(1, along_z, size)
        small_start(2, cores, size + streams)
        go_on(TAIL[2])
        last.dp_back()
        summed = small_sum(2, cores, size + streams)
        gain_ref[...] = summed[0:2, :]
        bias_ref[...] = summed[2:8, :]
        for i in range(shift_ref.shape[1] // depth):
            shift_ref[:, i * depth : (i + 1) * depth] = summed[8 + i : 9 + i, :]
        go_on(TAIL[3])
        last.core_back()
        go_on(8)
        for copy in back_copies:
            copy.wait()
        for job in early + late:
            job.end()
        for copy in (
            core_copies()
            + small_copies(0, along_dp, 0)
            + small_copies(1, along_z, size)
            + small_copies(2, cores, size + streams)
        ):
            copy.wait_send()


TWO_STEP = False
TAIL = (1, 1, 0, 0)
EARLY_TIMES = ((2, 0, 7, 9, 12), (4, 0, 12, 14))
LATE_TIMES = (0, 5, 7)


def attention_back(
    streams,
    groups,
    numerators,
    queries,
    keys,
    values,
    teacher_queries,
    teacher_keys,
    d_context,
    context,
    inverse,
    docs,
    small,
    active,
    bin_own,
    d_one,
    tokens,
    early_arrays,
    up_width,
    collective_id,
):
    seq, width = queries.shape
    pairs = width // 128
    tile = 256
    rows, depth = d_one.shape
    size = lax.axis_size("dp")
    shard = rows // streams
    bag = Bag()
    bag.add("v_aug", pltpu.VMEM((2, seq, 128), BF))
    bag.add("dk_acc", pltpu.VMEM((128, seq), F32))
    bag.add("dv_acc", pltpu.VMEM((128, seq), F32))
    bag.add("grams", pltpu.VMEM((8, 128, 128), BF))
    bag.add("dq_all", pltpu.VMEM((seq, 128), BF))
    bag.add("d_act", pltpu.VMEM((seq, depth), F32))
    bag.add("active", pltpu.VMEM((seq, depth), BF))
    bag.add("weights", pltpu.VMEM((1, 3, depth, width), BF))
    bag.add("d_one", pltpu.VMEM((rows, depth), F32))
    bag.add("x_rows", pltpu.VMEM((streams, shard, depth), BF))
    bag.add("load", dma(4))
    bag.add("sums", pltpu.VMEM((8, width), F32))
    bag.add("outbox", pltpu.VMEM((groups - 1, rows, depth), BF))
    bag.add("inbox", pltpu.VMEM((groups - 1, rows, depth), BF))
    bag.add("core_s", dma(groups))
    bag.add("core_r", dma(groups))
    bag.add("blocks", pltpu.VMEM((streams, shard, depth), BF))
    bag.add("grad_s", dma(streams))
    bag.add("grad_r", dma(streams))
    count = size + streams + groups
    bag.add("small", pltpu.VMEM((3,) + small.shape, F32))
    bag.add("small_box", pltpu.VMEM((count,) + small.shape, F32))
    bag.add("small_s", dma(count))
    bag.add("small_r", dma(count))
    bag.add("row", pltpu.VMEM((1, seq), F32))
    bag.add("pair_box", pltpu.VMEM((seq, 3 * 128), BF))
    bag.add("edges", pltpu.VMEM((2, tile, 128), F32))
    bag.add("in_big", pltpu.VMEM((2, tile, 128), F32))
    early, flat = [], []
    for n, arrays in enumerate(early_arrays):
        job = Reduce(bag, f"early{n}", streams, groups, [a.shape for a in arrays], True, TWO_STEP)
        early.append(job)
        flat += [
            a.reshape(groups, size, chunk, cols) for a, (chunk, cols) in zip(arrays, job.shapes)
        ]
    late = [
        Reduce(bag, f"late{p}", streams, groups, [(depth, 3 * 128)], False, False)
        for p in range(pairs)
    ]
    part = pl.BlockSpec((tile, 128), lambda p, i: (i, p))
    any_space = pl.BlockSpec(memory_space=pl.ANY)

    whole = pl.BlockSpec((seq, 128), lambda p, i: (0, p))

    def constant(shape):
        return pl.BlockSpec(shape, lambda p, i: (0,) * len(shape))

    small_shapes = [(2, depth), (6, depth), (1, up_width)]
    early_shapes = [shape for job in early for shape in job.out_shapes()]
    late_shapes = [shape for job in late for shape in job.out_shapes()]
    results = pl.pallas_call(
        functools.partial(backward_kernel, streams, groups, tile, bag, early, late),
        grid=(pairs, seq // tile),
        in_specs=[
            pl.BlockSpec((2, tile, seq), lambda p, i: (p, i, 0)),
            whole,
            whole,
            whole,
            whole,
            whole,
            part,
            part,
            part,
            constant(docs.shape),
            constant(small.shape),
        ]
        + [any_space] * (4 + len(flat)),
        out_specs=[any_space] * (1 + len(early_shapes) + len(late_shapes))
        + [constant(shape) for shape in small_shapes],
        out_shape=[jax.ShapeDtypeStruct((streams, shard, depth), BF)]
        + early_shapes
        + late_shapes
        + [jax.ShapeDtypeStruct(shape, F32) for shape in small_shapes],
        scratch_shapes=list(bag.items.values()),
        compiler_params=remote_params(collective_id),
        name="attention_back",
    )(
        numerators,
        queries,
        keys,
        values,
        teacher_queries,
        teacher_keys,
        d_context,
        context,
        inverse,
        docs,
        small,
        active,
        bin_own,
        d_one,
        tokens,
        *flat,
    )
    grad_tokens, *rest = results
    early_sums = rest[: len(flat)]
    late_sums = rest[len(flat) : -3]
    shapes = [a.shape for arrays in early_arrays for a in arrays]
    return (
        grad_tokens,
        [e.reshape(shape) for e, shape in zip(early_sums, shapes)],
        [l.reshape(groups, depth, 3 * 128) for l in late_sums],
        list(rest[-3:]),
    )


def middle_kernel(
    streams,
    groups,
    bag,
    tiles,
    x_ref,
    tx_ref,
    cot_ref,
    ctx_ref,
    tctx_ref,
    bo_ref,
    bup_ref,
    bdown_ref,
    to_ref,
    tup_ref,
    tdown_ref,
    sg_ref,
    sb_ref,
    sub_ref,
    tg_ref,
    tb_ref,
    tub_ref,
    out_ref,
    d1_ref,
    dctx_ref,
    gout_ref,
    gup_ref,
    gdown_ref,
    small_ref,
    *rest,
):
    have = bag.bind(rest)
    gout_acc, gup_acc, gdown_acc = have["gout"], have["gup"], have["gdown"]
    out_box, d_box = have["out_box"], have["d_box"]
    step = pl.program_id(0)
    steps = pl.num_programs(0)
    width = ctx_ref.shape[1] * 128
    tile, depth = cot_ref.shape
    n_steps = out_box.shape[0]
    shard = n_steps * tile // streams
    s, r = place(groups)
    along_z = stream_peers(streams, groups)
    turned = row_tile(step, n_steps, streams, groups)
    start = pl.multiple_of(turned * tile, tile)

    @pl.when(step == 0)
    def _():
        greet(along_z + core_peers(groups))

    @pl.when(step == 0)
    def _():
        for ref in (gout_acc, gup_acc, gdown_acc, small_ref):
            ref[...] = jnp.zeros_like(ref)

    def row(ref, i):
        return ref[i : i + 1, :]

    pieces = [(j, p) for j in range(groups) for p in range(ctx_ref.shape[1])]
    ff = bup_ref.shape[1]
    wide = min(512, ff)
    chunks = [slice(i, i + wide) for i in range(0, ff, wide)]

    tctx = jnp.concatenate([tctx_ref[j, p] for j, p in pieces], axis=1)
    t_att = dot(tctx, to_ref[...]) + row(tb_ref, 2)
    context = jnp.concatenate([ctx_ref[j, p] for j, p in pieces], axis=1).astype(F32)
    bent = jnp.tanh(context * (1.0 / clip_level))
    ctx_active = (clip_level * bent).astype(BF)
    ctx_slope = 1.0 - bent * bent
    attended = dot(ctx_active, bo_ref[...]) + row(sb_ref, 2)
    t_hidden = layer_norm(tx_ref[...].astype(F32) + t_att, row(tg_ref, 0), row(tb_ref, 3))[0]
    hidden, normed_one, inverse_one = layer_norm(
        x_ref[...].astype(F32) + attended, row(sg_ref, 0), row(sb_ref, 3)
    )
    bent = jnp.tanh(hidden * (1.0 / clip_level))
    hidden_active = (clip_level * bent).astype(BF)
    hidden_slope = 1.0 - bent * bent
    t_low = t_hidden.astype(BF)

    def up(i):
        return dot(t_low, tup_ref[:, chunks[i]]), dot(hidden_active, bup_ref[:, chunks[i]])

    ahead = up(0)
    t_branch, branch, actives, slopes = None, None, [], []
    for i, at in enumerate(chunks):
        t_pre, inner_pre = ahead
        if i + 1 < len(chunks):
            ahead = up(i + 1)
        t_inner = gelu_parts(t_pre + tub_ref[:, at])[0]
        inner_pre = inner_pre + sub_ref[:, at]
        inner_act, phi = gelu_parts(inner_pre)
        bent = jnp.tanh(inner_act * (1.0 / clip_level))
        inner_active = (clip_level * bent).astype(BF)
        t_term = dot(t_inner.astype(BF), tdown_ref[at, :])
        term = dot(inner_active, bdown_ref[at, :])
        t_branch = t_term if i == 0 else t_branch + t_term
        branch = term if i == 0 else branch + term
        actives.append(inner_active)
        slopes.append(
            (1.0 - bent * bent)
            * (phi + inner_pre * jnp.exp(-0.5 * inner_pre * inner_pre) * 0.3989422804014327)
        )
    t_out = layer_norm(t_hidden + t_branch + row(tb_ref, 4), row(tg_ref, 1), row(tb_ref, 5))[0]
    branch = branch + row(sb_ref, 4)
    output, normed_two, inverse_two = layer_norm(hidden + branch, row(sg_ref, 1), row(sb_ref, 5))
    out_box[step] = output.astype(BF)
    per_tile = tile // shard
    for n in range(per_tile):
        block = turned * per_tile + n
        source = out_box.at[step, pl.ds(n * shard, shard)]

        @pl.when(block == s)
        def _():
            pltpu.make_async_copy(source, out_ref.at[s], have["out_s"].at[s]).start()

        @pl.when(block != s)
        def _():
            remote(
                source,
                out_ref.at[s],
                have["out_s"].at[block],
                have["out_r"].at[s],
                {"blk": block * groups + r},
            ).start()
    upstream = cot_ref[...].astype(F32) + 0.5 * (output - t_out)
    d_two = norm_back(upstream, row(sg_ref, 1), normed_two, inverse_two)
    d_branch = d_two.astype(BF)

    def down(i):
        return dot(d_branch, bdown_ref[chunks[i], :], NT)

    ahead = down(0)
    through = None
    for i, at in enumerate(chunks):
        d_inner = ahead
        if i + 1 < len(chunks):
            ahead = down(i + 1)
        d_inner = (d_inner * slopes[i]).astype(BF)
        gdown_acc[at, :] += dot(actives[i], d_branch, TN)
        gup_acc[:, at] += dot(hidden_active, d_inner, TN)
        term = dot(d_inner, bup_ref[:, at], NT)
        through = term if i == 0 else through + term
        d_shift = jnp.sum(d_inner.astype(F32), axis=0, keepdims=True)
        for n in range(wide // depth):
            line = 8 + (i * wide) // depth + n
            small_ref[line : line + 1, :] += d_shift[:, n * depth : (n + 1) * depth]
    d_hidden = d_two + through * hidden_slope
    d_one = norm_back(d_hidden, row(sg_ref, 0), normed_one, inverse_one)
    d1_ref[...] = d_one
    d_attended = d_one.astype(BF)
    gout_acc[...] += dot(ctx_active, d_attended, TN)
    d_context = (dot(d_attended, bo_ref[...], NT) * ctx_slope).astype(BF)
    place_rows = pl.ds(pl.multiple_of(r * n_steps * tile + start, tile), tile)
    for j in range(groups):
        d_box[step, j] = d_context[:, j * width : (j + 1) * width]
        piece, target = d_box.at[step, j], dctx_ref.at[place_rows]

        @pl.when(r == j)
        def _():
            tiles.own(have, piece, target, 0, step).start()

        @pl.when(r != j)
        def _():
            tiles.copy(have, piece, target, j, 0, step).start()


    def total(value):
        return jnp.sum(value, axis=0, keepdims=True)

    sums = [
        (0, d_hidden * normed_one),
        (1, upstream * normed_two),
        (4, d_attended.astype(F32)),
        (5, d_hidden),
        (6, d_branch.astype(F32)),
        (7, upstream),
    ]
    for i, value in sums:
        small_ref[i : i + 1, :] += total(value)
    @pl.when(step == steps - 1)
    def _():
        tiles.finish(have, d_box.at[0, 0], dctx_ref.at[place_rows])
        source = out_box.at[0, pl.ds(0, shard)]
        pltpu.make_async_copy(source, out_ref.at[s], have["out_s"].at[s]).wait()
        for d, peer in enumerate(along_z, 1):
            block = lax.rem(s + d, streams)
            remote(
                source, out_ref.at[block], have["out_s"].at[block], have["out_r"].at[block], peer
            ).wait()
        gout_ref[...] = gout_acc[...].astype(BF)
        gup_ref[...] = gup_acc[...].astype(BF)
        gdown_ref[...] = gdown_acc[...].astype(BF)


def row_tile(step, steps, streams, groups):
    s, r = place(groups)
    return lax.rem(s // (streams // steps) + 1 + step, steps)


def middle(streams, groups, x, tx, cot, ctx, tctx, weights, teacher_weights, vectors, collective_id):
    rows, depth = cot.shape
    ff = weights[1].shape[1]
    tile = min(256, rows)
    pairs = ctx.shape[1]
    width = pairs * 128
    steps = rows // tile
    shard = rows // streams

    def turn(i):
        return row_tile(i, steps, streams, groups)

    def stream_tile(i):
        return lax.rem(lax.axis_index("blk"), groups) * steps + turn(i)

    tall = pl.BlockSpec((tile, depth), lambda i: (turn(i), 0))
    of_stream = pl.BlockSpec((tile, depth), lambda i: (stream_tile(i), 0))
    split_rows = pl.BlockSpec((groups, pairs, tile, 128), lambda i: (0, 0, turn(i), 0))
    any_space = pl.BlockSpec(memory_space=pl.ANY)

    def full(shape):
        return pl.BlockSpec(shape, lambda i: (0,) * len(shape))

    out_full = [(depth, depth), (depth, ff), (ff, depth), (16, depth)]
    bag = Bag()
    for name, shape in zip(("gout", "gup", "gdown"), out_full):
        bag.add(name, pltpu.VMEM(shape, F32))
    bag.add("out_box", pltpu.VMEM((steps, tile, depth), BF))
    bag.add("d_box", pltpu.VMEM((steps, groups, tile, width), BF))
    bag.add("out_s", dma(streams))
    bag.add("out_r", dma(streams))
    tiles = Tiles(bag, "tiles", groups, 1, steps)
    return pl.pallas_call(
        functools.partial(middle_kernel, streams, groups, bag, tiles),
        grid=(steps,),
        in_specs=[of_stream, of_stream, tall, split_rows, split_rows]
        + [full(a.shape) for a in weights + teacher_weights + vectors],
        out_specs=[any_space, tall, any_space] + [full(s) for s in out_full],
        out_shape=[
            jax.ShapeDtypeStruct((streams, shard, depth), BF),
            jax.ShapeDtypeStruct((rows, depth), F32),
            jax.ShapeDtypeStruct((rows * groups, width), BF),
        ]
        + [jax.ShapeDtypeStruct(s, BF if i < 3 else F32) for i, s in enumerate(out_full)],
        scratch_shapes=list(bag.items.values()),
        compiler_params=remote_params(collective_id),
        name="middle",
    )(x, tx, cot, ctx, tctx, *weights, *teacher_weights, *vectors)


def latent_columns(latent, grad, out):
    rows = latent.shape[0]
    size = min(256, rows)
    chunks = [slice(i, i + size) for i in range(0, rows, size)]
    squares = jnp.zeros((1, latent.shape[1]), F32)
    for at in chunks:
        matrix = latent[at, :].astype(F32)
        squares = squares + jnp.sum(matrix * matrix, axis=0, keepdims=True)
    scale = jnp.sqrt(squares * (1.0 / rows) + 1e-06)
    twice = 2.0 / scale
    through_scale = jnp.zeros_like(squares)
    for at in chunks:
        matrix, upstream = latent[at, :].astype(F32), grad[at, :].astype(F32)
        inner = matrix * twice
        bent = jnp.tanh(inner)
        slope = 1.0 - bent * bent
        through_scale = through_scale + jnp.sum(
            upstream * (bent - inner * slope), axis=0, keepdims=True
        )
        out[at, :] = upstream * (2.0 * slope)
    factor = through_scale / (rows * scale)
    for at in chunks:
        out[at, :] = out[at, :] + latent[at, :].astype(F32) * factor


def latent_grads_kernel(pairs, passed, lq, lo, lu, ld, *refs):
    late, (go, gu, gd, *refs) = refs[:pairs], refs[pairs:]
    come, (oq, oo, ou, od, *gone) = refs[:passed], refs[passed:]
    for source, target in zip(come, gone):
        target[...] = source[...]
    for p in range(pairs):

        @pl.when(lax.rem(pl.program_id(0), pairs) == p)
        def _():
            for i in range(3):
                latent_columns(lq.at[i], late[p].at[0, :, i * 128 : (i + 1) * 128], oq.at[i])

    latent_columns(lo, go, oo)
    latent_columns(ld, gd, od)
    for i in range(0, lu.shape[1], 128):
        at = slice(i, i + 128)
        latent_columns(lu.at[:, at], gu.at[:, at], ou.at[:, at])


def latent_grads(latents, late, early, tall, small):
    pairs = len(late)
    groups, depth, wide = late[0].shape
    steps = groups * pairs
    qkv = pl.BlockSpec((3, depth, depth // steps), lambda i: (0, 0, i))
    flat = [pl.BlockSpec((a.shape[0], a.shape[1] // steps), lambda i: (0, i)) for a in latents[1:]]
    handed = [
        pl.BlockSpec((a.shape[0] // steps,) + a.shape[1:], lambda i: (i, 0, 0)) for a in tall
    ] + [pl.BlockSpec(a.shape, lambda i: (0, 0)) for a in small]
    return pl.pallas_call(
        functools.partial(latent_grads_kernel, pairs, len(handed)),
        grid=(steps,),
        in_specs=[qkv]
        + flat
        + [pl.BlockSpec((1, depth, wide), lambda i: (i // pairs, 0, 0))] * pairs
        + flat
        + handed,
        out_specs=[qkv] + flat + handed,
        out_shape=[jax.ShapeDtypeStruct(a.shape, F32) for a in latents]
        + [jax.ShapeDtypeStruct(a.shape, a.dtype) for a in tall + small],
        compiler_params=pltpu.CompilerParams(vmem_limit_bytes=VMEM_BYTES),
        name="latent_grads",
    )(*latents, *late, *early, *tall, *small)


def shards(
    tokens,
    teacher_tokens,
    segment_ids,
    cotangent,
    latent_qkv,
    latent_out,
    latent_up,
    latent_down,
    student_gain,
    student_bias,
    student_up_bias,
    teacher_qkv,
    teacher_out,
    teacher_up,
    teacher_down,
    teacher_gain,
    teacher_bias,
    teacher_up_bias,
):
    streams, shard_len, depth = tokens.shape
    blocks = lax.axis_size("blk")
    groups = blocks // streams
    seq = shard_len * blocks
    rows = seq // groups
    block = (shard_len, depth)
    gather, swap = Gather(streams, groups, block, BF), Swap(streams, groups, block, BF)
    bin_own, bin_out, bin_up, bin_down, token_blocks, qkv_parts, docs = intake(
        Moves(
            gather,
            Spread(teacher_qkv.shape, BF),
            Gather(streams, groups, (8, shard_len), F32),
        ),
        groups,
        [latent_qkv, latent_out, latent_up, latent_down],
        segment_ids,
        [tokens, teacher_qkv],
        1,
    )
    stream_tokens = token_blocks.reshape(seq, depth)
    (
        queries,
        keys,
        ctx_rows,
        values,
        numerators,
        context,
        inverse,
        active,
        teacher_blocks,
        up_parts,
        out_parts,
    ) = attention(
        stream_tokens,
        bin_own,
        student_bias,
        docs,
        streams,
        groups,
        Moves(gather, Spread(teacher_up.shape, BF), Spread(teacher_out.shape, BF)),
        [teacher_tokens, teacher_up, teacher_out],
        True,
        2,
        "attention_student",
    )
    teacher_stream = teacher_blocks.reshape(seq, depth)
    teacher_queries, teacher_keys, tctx_rows, cot_blocks, down_parts = attention(
        teacher_stream,
        qkv_parts,
        teacher_bias,
        docs,
        streams,
        groups,
        Moves(swap, Spread(teacher_down.shape, BF), others=[gather]),
        [cotangent, teacher_down],
        False,
        3,
        "attention_teacher",
    )
    output, d_one, d_context, g_out, g_up, g_down, small = middle(
        streams,
        groups,
        stream_tokens,
        teacher_stream,
        cot_blocks.reshape(rows, depth),
        ctx_rows,
        tctx_rows,
        [bin_out, bin_up, bin_down],
        [
            out_parts.reshape(-1, depth),
            up_parts.reshape(depth, -1),
            down_parts.reshape(-1, depth),
        ],
        [
            student_gain,
            student_bias,
            student_up_bias.reshape(1, -1),
            teacher_gain,
            teacher_bias,
            teacher_up_bias.reshape(1, -1),
        ],
        4,
    )
    grads = [[g_up], [g_down, g_out]]
    in_kernel = depth % (16 * blocks * lax.axis_size("dp")) == 0
    grad_tokens, early, late, small = attention_back(
        streams,
        groups,
        numerators,
        queries,
        keys,
        values,
        teacher_queries,
        teacher_keys,
        d_context,
        context,
        inverse,
        docs,
        small,
        active,
        bin_own,
        d_one,
        token_blocks,
        grads if in_kernel else [],
        latent_up.shape[1],
        6,
    )
    if not in_kernel:
        early = lax.psum((g_up, g_down, g_out), ("dp", "blk"))
    grad_qkv, grad_out, grad_up, grad_down, output, grad_tokens, gain, bias, shift = latent_grads(
        [latent_qkv, latent_out, latent_up, latent_down],
        late,
        [early[2], early[0], early[1]],
        [output, grad_tokens],
        small,
    )
    return (
        output,
        grad_tokens,
        grad_qkv,
        grad_out,
        grad_up,
        grad_down,
        gain,
        bias,
        shift.reshape(-1),
    )


def solution(mesh):
    return jax.shard_map(
        shards,
        mesh=mesh,
        in_specs=(
            P("dp", "blk", None),
            P("dp", "blk", None),
            P("dp", "blk"),
            P("dp", "blk", None),
            P(),
            P(),
            P(),
            P(),
            P(),
            P(),
            P(),
            P(None, "dp", None),
            P("dp", None),
            P("dp", None),
            P("dp", None),
            P(),
            P(),
            P(),
        ),
        out_specs=(P("dp", "blk", None), P("dp", "blk", None), P(), P(), P(), P(), P(), P(), P()),
        check_vma=False,
    )
```

```python
import functools

import jax
import jax.numpy as jnp
from jax import lax
from jax.experimental import pallas as pl
from jax.experimental.pallas import tpu as pltpu
from jax.sharding import PartitionSpec as P

HEADS = 8
BF = jnp.bfloat16
F32 = jnp.float32
LOG2E = 1.4426950408889634
clip_level = 2.5
masked_score = -1e30
VMEM_BYTES = 56 << 20
MESH = pl.DeviceIdType.MESH
NT = (((1,), (1,)), ((), ()))
TN = (((0,), (0,)), ((), ()))


def squash(tensor):
    return clip_level * jnp.tanh(tensor * (1.0 / clip_level))


def gelu_parts(tensor):
    phi = 0.5 * (1.0 + lax.erf(tensor * 0.7071067811865476))
    return tensor * phi, phi


def binarize(matrix):
    column_scale = jnp.sqrt(jnp.mean(matrix * matrix, axis=-2, keepdims=True) + 1e-06)
    return column_scale * jnp.tanh(2.0 * matrix / column_scale)


def layer_norm(tensor, gain_row, shift_row):
    centre = tensor - jnp.mean(tensor, axis=-1, keepdims=True)
    inverse_std = lax.rsqrt(jnp.mean(centre * centre, axis=-1, keepdims=True) + 1e-05)
    normed = centre * inverse_std
    return (normed * gain_row + shift_row, normed, inverse_std)


def norm_back(upstream, gain_row, normed, inverse_std):
    scaled = upstream * gain_row
    return inverse_std * (
        scaled
        - jnp.mean(scaled, axis=-1, keepdims=True)
        - normed * jnp.mean(scaled * normed, axis=-1, keepdims=True)
    )


def dot(a, b, dims=(((1,), (0,)), ((), ()))):
    return lax.dot_general(a, b, dims, preferred_element_type=F32)


def latent_grad(latent, binary_grad):
    matrix = latent.astype(F32)
    unused, pullback = jax.vjp(binarize, matrix)
    return pullback(binary_grad)[0]


def place(groups):
    here = lax.axis_index("blk")
    return here // groups, lax.rem(here, groups)


def greet(peers):
    barrier = pltpu.get_barrier_semaphore()
    for peer in peers:
        pl.semaphore_signal(barrier, inc=1, device_id=peer, device_id_type=MESH)
    pl.semaphore_wait(barrier, len(peers))


def stream_peers(streams, groups):
    s, r = place(groups)
    return [{"blk": lax.rem(s + d, streams) * groups + r} for d in range(1, streams)]


def core_peers(groups):
    s, r = place(groups)
    return [{"blk": s * groups + lax.rem(r + j, groups)} for j in range(1, groups)]


def dp_peers():
    size = lax.axis_size("dp")
    here = lax.axis_index("dp")
    return [{"dp": lax.rem(here + d, size)} for d in range(1, size)]


def unique(jobs):
    peers, kinds = [], []
    for job in jobs:
        for kind, found in job.peers():
            if kind not in kinds:
                kinds.append(kind)
                peers += found
    return peers


def remote(source, target, send, recv, peer):
    return pltpu.make_async_remote_copy(
        src_ref=source,
        dst_ref=target,
        send_sem=send,
        recv_sem=recv,
        device_id=peer,
        device_id_type=MESH,
    )


def dma(count):
    return pltpu.SemaphoreType.DMA((count,))


class Staged:
    def __init__(self, source, target, stage, sems):
        self.load = pltpu.make_async_copy(source, stage, sems.at[0])
        self.store = pltpu.make_async_copy(stage, target, sems.at[1])

    def first(self):
        self.load.start()

    def last(self):
        self.load.wait()
        self.store.start()
        self.store.wait()


class Gather:
    def __init__(self, streams, groups, block, dtype):
        self.streams, self.groups, self.block, self.dtype = streams, groups, block, dtype

    def scratch(self):
        b, g = self.streams, self.groups
        return [dma(b), dma(b), dma(b * g), dma(b * g), pltpu.VMEM(self.block, self.dtype), dma(2)]

    def out_shape(self):
        return jax.ShapeDtypeStruct((self.streams * self.groups,) + self.block, self.dtype)

    def peers(self):
        return [
            ("stream", stream_peers(self.streams, self.groups)),
            ("core", core_peers(self.groups)),
        ]

    def parts(self, source, target, send, recv, share_send, share_recv, stage, sems):
        b, g = self.streams, self.groups
        s, r = place(g)
        peers, cores = stream_peers(b, g), core_peers(g)
        swaps = [
            remote(
                source.at[lax.rem(s + d, b)],
                target.at[r * b + s],
                send.at[d],
                recv.at[d],
                peers[d - 1],
            )
            for d in range(1, b)
        ]
        shares = [
            [
                remote(
                    source.at[s] if d == 0 else target.at[r * b + lax.rem(s + b - d, b)],
                    target.at[r * b + lax.rem(s + b - d, b)],
                    share_send.at[j * b + d],
                    share_recv.at[j * b + d],
                    cores[j - 1],
                )
                for j in range(1, g)
            ]
            for d in range(b)
        ]
        own = Staged(source.at[s], target.at[r * b + s], stage, sems)
        return swaps, shares, own

    def first(self, *refs):
        swaps, shares, own = self.parts(*refs)
        for copy in swaps:
            copy.start()
        own.first()
        for copy in shares[0]:
            copy.start()

    def middle(self, *refs):
        swaps, shares, own = self.parts(*refs)
        for d in [1, 3, 2] if self.streams == 4 else range(1, self.streams):
            swaps[d - 1].wait_recv()
            for copy in shares[d]:
                copy.start()

    def last(self, *refs):
        swaps, shares, own = self.parts(*refs)
        own.last()
        for row in shares:
            for copy in row:
                copy.wait()
        for copy in swaps:
            copy.wait_send()


class Swap:
    def __init__(self, streams, groups, block, dtype):
        self.streams, self.groups, self.block, self.dtype = streams, groups, block, dtype

    def scratch(self):
        return [dma(self.streams), dma(self.streams), pltpu.VMEM(self.block, self.dtype), dma(2)]

    def out_shape(self):
        return jax.ShapeDtypeStruct((self.streams,) + self.block, self.dtype)

    def peers(self):
        return [("stream", stream_peers(self.streams, self.groups))]

    def parts(self, source, target, send, recv, stage, sems):
        b, g = self.streams, self.groups
        s, r = place(g)
        peers = stream_peers(b, g)
        swaps = [
            remote(source.at[lax.rem(s + d, b)], target.at[s], send.at[d], recv.at[d], peers[d - 1])
            for d in range(1, b)
        ]
        return swaps, Staged(source.at[s], target.at[s], stage, sems)

    def first(self, *refs):
        swaps, own = self.parts(*refs)
        for copy in swaps:
            copy.start()
        own.first()

    def last(self, *refs):
        swaps, own = self.parts(*refs)
        own.last()
        for copy in swaps:
            copy.wait()


class Spread:
    def __init__(self, block, dtype):
        self.block, self.dtype = block, dtype

    def scratch(self):
        size = lax.axis_size("dp")
        return [dma(size), dma(size), pltpu.VMEM(self.block, self.dtype), dma(2)]

    def out_shape(self):
        return jax.ShapeDtypeStruct((lax.axis_size("dp"),) + self.block, self.dtype)

    def peers(self):
        return [("dp", dp_peers())]

    def parts(self, source, target, send, recv, stage, sems):
        here = lax.axis_index("dp")
        copies = [
            remote(source, target.at[here], send.at[d], recv.at[d], peer)
            for d, peer in enumerate(dp_peers(), 1)
        ]
        return copies, Staged(source, target.at[here], stage, sems)

    first = Swap.first
    last = Swap.last


class Tiles:
    def __init__(self, bag, name, groups, pairs, per_owner):
        self.name, self.groups, self.pairs, self.per_owner = name, groups, pairs, per_owner
        count = pairs * per_owner
        bag.add(f"{name}_s", dma(groups * count))
        bag.add(f"{name}_r", dma(groups * count))

    def slot(self, who, pair, at):
        return (who * self.pairs + pair) * self.per_owner + at

    def copy(self, have, source, target, owner, pair, at):
        s, r = place(self.groups)
        return remote(
            source,
            target,
            have[f"{self.name}_s"].at[self.slot(owner, pair, at)],
            have[f"{self.name}_r"].at[self.slot(r, pair, at)],
            {"blk": s * self.groups + owner},
        )

    def own(self, have, source, target, pair, at):
        s, r = place(self.groups)
        return pltpu.make_async_copy(
            source, target, have[f"{self.name}_s"].at[self.slot(r, pair, at)]
        )

    def finish(self, have, source, target):
        s, r = place(self.groups)
        for pair in range(self.pairs):
            for at in range(self.per_owner):
                self.own(have, source, target, pair, at).wait()
                for j in range(1, self.groups):
                    other = lax.rem(r + j, self.groups)
                    remote(
                        source,
                        target,
                        have[f"{self.name}_s"].at[self.slot(other, pair, at)],
                        have[f"{self.name}_r"].at[self.slot(other, pair, at)],
                        {"blk": s * self.groups + other},
                    ).wait()


class Bag:
    def __init__(self):
        self.items = {}

    def add(self, name, item):
        self.items[name] = item

    def bind(self, refs):
        return dict(zip(self.items, refs))


class Reduce:
    def __init__(self, bag, name, streams, groups, shapes, over_cores, two_step):
        self.name, self.streams, self.groups = name, streams, groups
        self.size = lax.axis_size("dp")
        self.over_cores = over_cores
        self.two_step = two_step and self.size == 4 and streams % 2 == 0
        self.count = len(shapes)
        share = self.size * (groups if over_cores else 1)
        self.shapes = [(rows // share, cols) for rows, cols in shapes]
        self.wires = [BF if (c // streams) % 16 == 0 else F32 for c, cols in self.shapes]
        for i, (chunk, cols) in enumerate(self.shapes):
            wire, slim = self.wires[i], chunk // streams
            bag.add(f"{name}half{i}", pltpu.VMEM((self.size, chunk, cols), wire))
            if over_cores:
                bag.add(f"{name}core{i}", pltpu.VMEM((groups - 1, self.size, chunk, cols), wire))
            if self.two_step:
                bag.add(f"{name}first{i}", pltpu.VMEM((4, chunk // 2, cols), wire))
                bag.add(f"{name}second{i}", pltpu.VMEM((2, chunk // 2, cols), wire))
            else:
                bag.add(f"{name}dp{i}", pltpu.VMEM((self.size - 1, chunk, cols), wire))
            bag.add(f"{name}cut{i}", pltpu.VMEM((streams, slim, cols), wire))
            bag.add(f"{name}z{i}", pltpu.VMEM((streams - 1, slim, cols), wire))
            bag.add(f"{name}fin{i}", pltpu.VMEM((slim, cols), wire))
            for kind in self.kinds():
                bag.add(f"{name}{kind}s{i}", dma(self.sem_count(kind)))
                bag.add(f"{name}{kind}r{i}", dma(self.sem_count(kind)))
            bag.add(f"{name}local{i}", dma(2))

    def kinds(self):
        along = ["b1", "b2", "c", "d", "e1", "e2"] if self.two_step else ["b", "c", "d", "e"]
        return (["a"] if self.over_cores else []) + along + ["f"]

    def sem_count(self, kind):
        if kind in ("a", "f"):
            return self.groups
        if kind in ("c", "d"):
            return self.streams
        return max(self.size, 4)

    def out_shapes(self):
        return [
            jax.ShapeDtypeStruct(
                (self.groups, self.size, self.streams, chunk // self.streams, cols), wire
            )
            for (chunk, cols), wire in zip(self.shapes, self.wires)
        ]

    def bind(self, sources, targets, scratch):
        self.sources, self.targets, self.scratch = sources, targets, scratch

    def get(self, what, i):
        return self.scratch[f"{self.name}{what}{i}"]

    def pairs(self, kind, i):
        s, r = place(self.groups)
        here = lax.axis_index("dp")
        b, g, size = self.streams, self.groups, self.size
        x, y = lax.rem(here, 2), here // 2
        beside_x, beside_y = {"dp": 2 * y + 1 - x}, {"dp": 2 * (1 - y) + x}
        if kind == "a":
            for d, peer in enumerate(core_peers(g), 1):
                yield d, self.sources[i].at[lax.rem(r + d, g)], self.get("core", i).at[d - 1], peer
        elif kind == "b":
            half, box = self.get("half", i), self.get("dp", i)
            for d, peer in enumerate(dp_peers(), 1):
                yield d, half.at[lax.rem(here + d, size)], box.at[d - 1], peer
        elif kind == "b1":
            half, box, h = self.get("half", i), self.get("first", i), self.shapes[i][0] // 2
            for n in range(2):
                yield n, half.at[2 * n + 1 - x, pl.ds(0, h)], box.at[n], beside_x
                yield 2 + n, half.at[2 * (1 - y) + n, pl.ds(h, h)], box.at[2 + n], beside_y
        elif kind == "b2":
            half, box, h = self.get("half", i), self.get("second", i), self.shapes[i][0] // 2
            yield 0, half.at[2 * (1 - y) + x, pl.ds(0, h)], box.at[0], beside_y
            yield 1, half.at[2 * y + 1 - x, pl.ds(h, h)], box.at[1], beside_x
        elif kind in "cd":
            peers = list(enumerate(stream_peers(b, g), 1))
            for d, peer in [peers[1], peers[0], peers[2]] if b == 4 else peers:
                if kind == "c":
                    cut = self.get("cut", i)
                    yield d, cut.at[lax.rem(s + d, b)], self.get("z", i).at[d - 1], peer
                else:
                    yield d, self.get("fin", i), self.targets[i].at[r, here, s], peer
        elif kind == "e":
            whole = self.targets[i].at[r, here]
            for d, peer in enumerate(dp_peers(), 1):
                yield d, whole, whole, peer
        elif kind == "e1":
            for n, peer in enumerate((beside_y, beside_x)):
                part = self.targets[i].at[r, here, pl.ds(n * b // 2, b // 2)]
                yield n, part, part, peer
        elif kind == "e2":
            for n in range(2):
                part = self.targets[i].at[r, 2 * n + x, pl.ds(0, b // 2)]
                yield n, part, part, beside_x
                part = self.targets[i].at[r, 2 * y + n, pl.ds(b // 2, b // 2)]
                yield 2 + n, part, part, beside_y
        else:
            whole = self.targets[i].at[r]
            for d, peer in enumerate(core_peers(g), 1):
                yield d, whole, whole, peer

    def copies(self, kind, i):
        send, recv = self.get(kind + "s", i), self.get(kind + "r", i)
        for n, source, target, peer in self.pairs(kind, i):
            yield remote(source, target, send.at[n], recv.at[n], peer)

    def start(self, kind, i):
        for copy in self.copies(kind, i):
            copy.start()

    def arrive(self, kind, i):
        for copy in self.copies(kind, i):
            copy.wait_recv()

    def load(self, i):
        s, r = place(self.groups)
        return pltpu.make_async_copy(
            self.sources[i].at[r], self.get("half", i), self.get("local", i).at[0]
        )

    def keep(self, i):
        s, r = place(self.groups)
        return pltpu.make_async_copy(
            self.get("fin", i),
            self.targets[i].at[r, lax.axis_index("dp"), s],
            self.get("local", i).at[1],
        )

    def stages(self):
        middle = [self.dp_middle] if self.two_step else []
        back = [self.dp_back_middle] if self.two_step else []
        return [self.dp_start, *middle, self.z_start, self.z_back, self.dp_back, *back, self.core_back]

    def core_start(self):
        for i in range(self.count):
            self.start("a", i)
            self.load(i).start()

    def dp_start(self):
        for i in range(self.count):
            if self.over_cores:
                self.load(i).wait()
                self.arrive("a", i)
                half, box, wire = self.get("half", i), self.get("core", i), self.wires[i]
                for p in range(self.size):
                    total = half[p].astype(F32)
                    for j in range(self.groups - 1):
                        total = total + box[j, p].astype(F32)
                    half[p] = total.astype(wire)
            self.start("b1" if self.two_step else "b", i)

    def dp_middle(self):
        here = lax.axis_index("dp")
        x, y = lax.rem(here, 2), here // 2
        for i in range(self.count):
            self.arrive("b1", i)
            half, box, wire = self.get("half", i), self.get("first", i), self.wires[i]
            h = self.shapes[i][0] // 2
            for n in range(2):
                for who, at, part in ((2 * n + x, pl.ds(0, h), n), (2 * y + n, pl.ds(h, h), 2 + n)):
                    total = half[who, at, :].astype(F32) + box[part].astype(F32)
                    half[who, at, :] = total.astype(wire)
            self.start("b2", i)

    def z_start(self):
        here = lax.axis_index("dp")
        for i in range(self.count):
            self.arrive("b2" if self.two_step else "b", i)
            half, cut, wire = self.get("half", i), self.get("cut", i), self.wires[i]
            chunk = self.shapes[i][0]
            slim = chunk // self.streams
            for z in range(self.streams):
                at = slice(z * slim, (z + 1) * slim)
                total = half[here, at, :].astype(F32)
                if self.two_step:
                    which, first = divmod(z * slim, chunk // 2)
                    total = total + self.get("second", i)[which, first : first + slim].astype(F32)
                else:
                    for d in range(self.size - 1):
                        total = total + self.get("dp", i)[d, at, :].astype(F32)
                cut[z] = total.astype(wire)
            self.start("c", i)

    def z_back(self):
        s, r = place(self.groups)
        for i in range(self.count):
            self.arrive("c", i)
            box = self.get("z", i)
            total = self.get("cut", i)[s].astype(F32)
            for d in range(self.streams - 1):
                total = total + box[d].astype(F32)
            self.get("fin", i)[...] = total.astype(self.wires[i])
            self.keep(i).start()
            self.start("d", i)

    def dp_back(self):
        for i in range(self.count):
            self.keep(i).wait()
            self.arrive("d", i)
            self.start("e1" if self.two_step else "e", i)

    def dp_back_middle(self):
        for i in range(self.count):
            self.arrive("e1", i)
            self.start("e2", i)

    def core_back(self):
        for i in range(self.count):
            self.arrive("e2" if self.two_step else "e", i)
            self.start("f", i)

    def end(self):
        for i in range(self.count):
            self.arrive("f", i)
            for kind in self.kinds():
                for copy in self.copies(kind, i):
                    copy.wait_send()


class Moves:
    def __init__(self, *jobs, others=()):
        self.jobs, self.others = list(jobs), list(others)
        self.counts = [len(job.scratch()) for job in jobs]

    def scratch(self):
        return [item for job in self.jobs for item in job.scratch()]

    def out_shapes(self):
        return [job.out_shape() for job in self.jobs]

    def spaces(self):
        return [pl.BlockSpec(memory_space=pl.ANY)] * len(self.jobs)

    def each(self, sources, targets, scratch):
        at = 0
        for job, count, source, target in zip(self.jobs, self.counts, sources, targets):
            yield job, (source, target, *scratch[at : at + count])
            at += count

    def first(self, sources, targets, scratch, count=None):
        greet(unique(self.jobs + self.others))
        for job, refs in list(self.each(sources, targets, scratch))[:count]:
            job.first(*refs)

    def start_last(self, sources, targets, scratch):
        for job, refs in list(self.each(sources, targets, scratch))[-1:]:
            job.first(*refs)

    def middle(self, sources, targets, scratch):
        for job, refs in self.each(sources, targets, scratch):
            if isinstance(job, Gather):
                job.middle(*refs)

    def last(self, sources, targets, scratch):
        for job, refs in self.each(sources, targets, scratch):
            job.last(*refs)


def remote_params(collective_id):
    return pltpu.CompilerParams(
        collective_id=collective_id, has_side_effects=True, vmem_limit_bytes=VMEM_BYTES
    )


def binary_columns(latent):
    matrix = latent.astype(F32)
    scale = jnp.sqrt(jnp.mean(matrix * matrix, axis=0, keepdims=True) + 1e-06)
    return (scale * jnp.tanh(matrix * (2.0 / scale))).astype(BF)


def intake_kernel(moves, groups, *refs):
    count = len(moves.jobs)
    latents, ids_ref, refs = refs[:4], refs[4], refs[5:]
    sources, refs = refs[: count - 1], refs[count - 1 :]
    results, refs = refs[:4], refs[4:]
    targets, refs = refs[:count], refs[count:]
    loaded, made, sems = refs[:4], refs[4:8], refs[8]
    ids_in, ids_box, *scratch = refs[9:]
    sources = (*sources, ids_box)
    moves.first(sources, targets, scratch, count - 1)
    s, r = place(groups)
    width = results[0].shape[3]
    own = pl.ds(pl.multiple_of(r * width, 128), width)
    places = [latents[0].at[:, :, own], *latents[1:]]
    loads = [
        pltpu.make_async_copy(source, target, sems.at[i])
        for i, (source, target) in enumerate(zip(places, loaded))
    ]
    stores = [
        pltpu.make_async_copy(source, target, sems.at[4 + i])
        for i, (source, target) in enumerate(zip(made, [results[0].at[0], *results[1:]]))
    ]
    fetch = pltpu.make_async_copy(ids_ref, ids_in, sems.at[8])
    fetch.start()
    for copy in loads:
        copy.start()
    fetch.wait()
    ids = ids_in[...].astype(F32)
    for i in range(ids.shape[0]):
        ids_box[i] = jnp.broadcast_to(ids[i : i + 1, :], ids_box.shape[1:])
    moves.start_last(sources, targets, scratch)
    loads[0].wait()
    for i in range(3):
        made[0][i] = binary_columns(loaded[0][i])
    stores[0].start()
    for n in range(1, 4):
        loads[n].wait()
        for i in range(0, loaded[n].shape[1], 128):
            made[n][:, i : i + 128] = binary_columns(loaded[n][:, i : i + 128])
        stores[n].start()
    moves.middle(sources, targets, scratch)
    for copy in stores:
        copy.wait()
    moves.last(sources, targets, scratch)


def intake(moves, groups, latents, ids, arrays, collective_id):
    three, depth, unused = latents[0].shape
    own_shape = (three, depth, depth // groups)
    shapes = [(1,) + own_shape] + [a.shape for a in latents[1:]]
    buffers = [pltpu.VMEM(shape, BF) for shape in [own_shape] + shapes[1:]]
    any_space = [pl.BlockSpec(memory_space=pl.ANY)] * 4
    return pl.pallas_call(
        functools.partial(intake_kernel, moves, groups),
        out_shape=[jax.ShapeDtypeStruct(shape, BF) for shape in shapes] + moves.out_shapes(),
        in_specs=any_space
        + moves.spaces(),
        out_specs=any_space + moves.spaces(),
        scratch_shapes=buffers * 2
        + [dma(9), pltpu.VMEM(ids.shape, ids.dtype)]
        + [pltpu.VMEM((ids.shape[0], 8, ids.shape[1]), F32)]
        + moves.scratch(),
        compiler_params=remote_params(collective_id),
        name="intake",
    )(*latents, ids, *arrays)


def lanes_of(shape):
    return lax.broadcasted_iota(jnp.int32, shape, 1)


def forward_kernel(
    moves, keep, streams, groups, tile, bag, tiles, x_ref, w_ref, bias_ref, docs_ref, *rest
):
    count = len(moves.jobs)
    sources, rest = rest[:count], rest[count:]
    q_ref, k_ref, rows_ref, *rest = rest
    if keep:
        v_ref, e_ref, ctx_ref, inv_ref, active_ref, *rest = rest
    targets, rest = rest[:count], rest[count:]
    have = bag.bind(rest)
    scratch = tuple(have[f"moves{i}"] for i in range(len(moves.scratch())))
    k_aug, v_aug, ctx_all, mask, edges = (
        have["k_aug"],
        have["v_aug"],
        have["ctx_all"],
        have["mask"],
        have["edges"],
    )
    active = active_ref if keep else x_ref
    row_ref = have["row"]
    pair, step = pl.program_id(0), pl.program_id(1)
    pairs, steps = pl.num_programs(0), pl.num_programs(1)
    seq = k_ref.shape[0]
    s, r = place(groups)
    sub = min(256, tile)
    width = w_ref.shape[3]
    n_pairs = ctx_all.shape[0]
    offset = pair * 128 if width == n_pairs * 128 else (r * n_pairs + pair) * 128
    offset = pl.multiple_of(offset, 128)
    home = pl.multiple_of((r * n_pairs + pair) * 128, 128)

    @pl.when((pair == 0) & (step == 0))
    def _():
        moves.first(sources, targets, scratch)
        ids = stream_row(docs_ref)
        row_ref[...] = ids
        big_at = long_at(streams, groups, seq)
        big = ids[:, big_at : big_at + 1]
        mask[...] = jnp.where(ids == big, 0.0, masked_score)
        edges[0] = jnp.broadcast_to(ids[:, :sub], (128, sub)).T
        edges[1] = jnp.broadcast_to(ids[:, seq - sub :], (128, sub)).T
        if keep:
            for i in range(0, seq, 256):
                active_ref[i : i + 256, :] = squash(x_ref[i : i + 256, :].astype(F32)).astype(BF)

    @pl.when((pair == pairs - 1) & (step == steps - 2))
    def _():
        moves.middle(sources, targets, scratch)

    @pl.when(step == 0)
    def _():
        columns = pl.ds(offset, 128)

        def project(i, bias):
            matrix = jnp.concatenate(
                [w_ref[d, i, :, columns] for d in range(w_ref.shape[0])], axis=0
            )
            result = dot(active[...], matrix)
            if bias is not None:
                result = result + bias_ref[bias : bias + 1, pl.ds(home, 128)]
            return result.astype(BF)

        low = lanes_of((seq, 128)) < 64
        lane = lanes_of((seq, 128))
        q_ref[...] = (project(0, 0).astype(F32) * 0.125).astype(BF)
        keys = project(1, None)
        k_ref[...] = keys
        keys = keys.astype(F32)
        turned = pltpu.roll(keys, 64, 1)
        k_aug[0] = jnp.where(low, keys, turned).astype(BF)
        k_aug[1] = jnp.where(low, turned, keys).astype(BF)
        values = project(2, 1)
        if keep:
            v_ref[...] = values
        values = values.astype(F32)
        v_aug[0] = jnp.where(low, values, jnp.where(lane < 66, 1.0, 0.0)).astype(BF)
        v_aug[1] = jnp.where(low, jnp.where(lane < 2, 1.0, 0.0), values).astype(BF)

    turned = own_rows_last(step, seq, tile, groups)
    start = pl.multiple_of(turned * tile, tile)

    def body(edge_at):
        low = lanes_of((sub, 128)) < 64
        parts = []
        for at in range(0, tile, sub):
            scaled = q_ref[pl.ds(start + at, sub), :].astype(F32) * LOG2E
            upper = scaled.astype(BF).astype(F32)
            lower = scaled - upper
            parts.append(
                (
                    jnp.where(low, upper, pltpu.roll(lower, 64, 1)).astype(BF),
                    jnp.where(low, pltpu.roll(upper, 64, 1), lower).astype(BF),
                )
            )
        chains = [(at, h) for at in range(0, tile, sub) for h in range(2)]

        def scores_of(at, h):
            scores = dot(parts[at // sub][h], k_aug[h], NT)
            if edge_at is not None and at == (0 if edge_at == 0 else tile - sub):
                return jnp.where(edges[edge_at][:, :1] == row_ref[...], scores, masked_score)
            return jnp.concatenate(
                [
                    scores[:, :sub] + mask[:, :sub],
                    scores[:, sub : seq - sub],
                    scores[:, seq - sub :] + mask[:, seq - sub :],
                ],
                axis=1,
            )

        scores = scores_of(*chains[0])
        results = {}
        for n, (at, h) in enumerate(chains):
            if n + 1 < len(chains):
                later = scores_of(*chains[n + 1])
            peak = jnp.max(scores, axis=1, keepdims=True)
            numerators = jnp.exp2(scores - peak).astype(BF)
            if keep:
                e_ref[h, at : at + sub, :] = numerators
            total = dot(numerators, v_aug[h])
            where_sum = 64 if h == 0 else 0
            inverse = 1.0 / total[:, where_sum : where_sum + 1]
            results[h] = (total * inverse, inverse)
            if n + 1 < len(chains):
                scores = later
            if h == 1:
                done = jnp.where(low, results[0][0], results[1][0]).astype(BF)
                ctx_all[pair, pl.ds(start + at, sub), :] = done
                if keep:
                    ctx_ref[at : at + sub, :] = done
                    inv_ref[at : at + sub, :] = jnp.where(low, results[0][1], results[1][1])

    @pl.when(turned == 0)
    def _():
        body(0)

    @pl.when(turned == steps - 1)
    def _():
        body(1)

    @pl.when((turned > 0) & (turned < steps - 1))
    def _():
        body(None)

    owned = seq // groups
    owner = start // owned
    at = lax.rem(turned, owned // tile)
    source = ctx_all.at[pair, pl.ds(start, tile)]
    target = rows_ref.at[r, pair, pl.ds(pl.multiple_of(lax.rem(start, owned), tile), tile)]

    @pl.when(owner == r)
    def _():
        tiles.own(have, source, target, pair, at).start()

    @pl.when(owner != r)
    def _():
        tiles.copy(have, source, target, owner, pair, at).start()

    @pl.when((pair == pairs - 1) & (step == steps - 1))
    def _():
        tiles.finish(have, source, target)
        moves.last(sources, targets, scratch)


def own_rows_last(step, seq, tile, groups):
    s, r = place(groups)
    steps = seq // tile
    return lax.rem(step + (r + 1) * (steps // groups), steps)


def stream_row(docs_ref):
    return jnp.concatenate([docs_ref[i, 0:1, :] for i in range(docs_ref.shape[0])], axis=1)


def long_at(streams, groups, seq):
    shard = seq // (streams * groups)
    return streams * shard if groups > 1 else shard


def attention(x, weights, bias, docs, streams, groups, moves, moved, keep, collective_id, name):
    seq, depth = x.shape
    width = depth // groups
    pairs = width // 128
    tile = 512
    owned = seq // groups
    bag = Bag()
    bag.add("k_aug", pltpu.VMEM((2, seq, 128), BF))
    bag.add("v_aug", pltpu.VMEM((2, seq, 128), BF))
    bag.add("ctx_all", pltpu.VMEM((pairs, seq, 128), BF))
    bag.add("mask", pltpu.VMEM((1, seq), F32))
    bag.add("row", pltpu.VMEM((1, seq), F32))
    bag.add("edges", pltpu.VMEM((2, 256, 128), F32))
    tiles = Tiles(bag, "tiles", groups, pairs, owned // tile)
    for i, item in enumerate(moves.scratch()):
        bag.add(f"moves{i}", item)

    def constant(shape):
        return pl.BlockSpec(shape, lambda p, i: (0,) * len(shape))

    def turn(i):
        return own_rows_last(i, seq, tile, groups)

    part = pl.BlockSpec((tile, 128), lambda p, i: (turn(i), p))
    whole = pl.BlockSpec((seq, 128), lambda p, i: (0, p))
    any_space = pl.BlockSpec(memory_space=pl.ANY)
    wide = jax.ShapeDtypeStruct((seq, width), BF)
    outs = [whole, whole, any_space]
    shapes = [wide, wide, jax.ShapeDtypeStruct((groups, pairs, owned, 128), BF)]
    if keep:
        outs += [
            whole,
            pl.BlockSpec((2, tile, seq), lambda p, i: (p, turn(i), 0)),
            part,
            part,
            constant((seq, depth)),
        ]
        shapes += [
            wide,
            jax.ShapeDtypeStruct((2 * pairs, seq, seq), BF),
            wide,
            jax.ShapeDtypeStruct((seq, width), F32),
            jax.ShapeDtypeStruct((seq, depth), BF),
        ]
    return pl.pallas_call(
        functools.partial(forward_kernel, moves, keep, streams, groups, tile, bag, tiles),
        grid=(pairs, seq // tile),
        in_specs=[constant(a.shape) for a in (x, weights, bias, docs)]
        + moves.spaces(),
        out_specs=outs + moves.spaces(),
        out_shape=shapes + moves.out_shapes(),
        scratch_shapes=list(bag.items.values()),
        compiler_params=remote_params(collective_id),
        name=name,
    )(x, weights, bias, docs, *moved)


def split(matrix):
    upper = matrix.astype(BF)
    return upper, (matrix - upper.astype(F32)).astype(BF)


def backward_kernel(
    streams,
    groups,
    tile,
    bag,
    early,
    late,
    e_ref,
    q_ref,
    k_ref,
    v_ref,
    tq_ref,
    tk_ref,
    dc_ref,
    ctx_ref,
    inv_ref,
    docs_ref,
    small_ref,
    active_hbm,
    bin_hbm,
    d1_hbm,
    tokens_hbm,
    *rest,
):
    n_early = sum(job.count for job in early)
    sources, rest = rest[:n_early], rest[n_early:]
    grad_ref, *rest = rest
    early_out, rest = rest[:n_early], rest[n_early:]
    late_out, (gain_ref, bias_ref, shift_ref, *rest) = rest[: len(late)], rest[len(late) :]
    have = bag.bind(rest)
    at = 0
    for job in early:
        job.bind(sources[at : at + job.count], early_out[at : at + job.count], have)
        at += job.count
    for job, target in zip(late, late_out):
        job.bind(None, [target], have)

    pair, step = pl.program_id(0), pl.program_id(1)
    pairs, steps = len(late), q_ref.shape[0] // tile
    sub = min(256, tile)
    seq = k_ref.shape[0]
    share = 1.0 / seq
    time = pair * steps + step
    total_time = pairs * steps
    size = lax.axis_size("dp")
    here = lax.axis_index("dp")
    s, r = place(groups)
    rows, depth = d1_hbm.shape
    width = pairs * 128
    v_aug, dk_acc, dv_acc, grams = have["v_aug"], have["dk_acc"], have["dv_acc"], have["grams"]
    dq_all, d_act, active, weights = have["dq_all"], have["d_act"], have["active"], have["weights"]
    d_one, x_rows = have["d_one"], have["x_rows"]
    edges, in_big, pair_box = have["edges"], have["in_big"], have["pair_box"]
    row_ref = have["row"]
    along_z, cores, along_dp = stream_peers(streams, groups), core_peers(groups), dp_peers()

    def loads():
        sems = have["load"]
        return [
            pltpu.make_async_copy(active_hbm, active, sems.at[0]),
            pltpu.make_async_copy(bin_hbm, weights, sems.at[1]),
            pltpu.make_async_copy(d1_hbm, d_one, sems.at[2]),
            pltpu.make_async_copy(tokens_hbm.at[pl.ds(r * streams, streams)], x_rows, sems.at[3]),
        ]

    halves = tile // sub
    plan = []

    def at_time(when, work):
        plan.append((when, work))

    def due(half):
        for when, work in plan:
            if when % halves == half:
                pl.when(time == when // halves)(work)

    def begin():
        greet(along_z + cores + along_dp)
        for job in early:
            job.core_start()
        for copy in loads():
            copy.start()
        ids = stream_row(docs_ref)
        row_ref[...] = ids
        big_at = long_at(streams, groups, seq)
        big = ids[:, big_at : big_at + 1]
        for n, first in enumerate((0, seq - sub)):
            column = jnp.broadcast_to(ids[:, first : first + sub], (128, sub)).T
            edges[n] = column
            in_big[n] = jnp.where(column == big, 1.0, 0.0)

    def big_rows(ref):
        return jnp.concatenate(
            [
                (ref[:sub, :].astype(F32) * in_big[0]).astype(BF),
                ref[sub : seq - sub, :],
                (ref[seq - sub :, :].astype(F32) * in_big[1]).astype(BF),
            ],
            axis=0,
        )

    at_time(0, begin)
    unit = total_time * halves / 16
    left = []
    for n, job in enumerate(early):
        stages, times = job.stages(), EARLY_TIMES[n]
        if not job.two_step:
            times = times[:1] + times[2:5] + times[6:]
        for when, work in zip(times, stages):
            at_time(int(when * unit), work)
        left.append(stages[len(times) :])
    for p, job in enumerate(late[:-1]):
        first = (p + 1) * steps * halves
        for when, work in zip(LATE_TIMES, job.stages()):
            at_time(first + when, work)
        left.append(job.stages()[len(LATE_TIMES) :])

    def go_on(count):
        for unused in range(count):
            for queue in left:
                if queue:
                    queue.pop(0)()

    due(0)

    @pl.when(step == 0)
    def _():
        lane = lanes_of((seq, 128))
        low = lane < 64
        values = v_ref[...].astype(F32)
        v_aug[0] = jnp.where(low, values, jnp.where(lane < 66, 1.0, 0.0)).astype(BF)
        v_aug[1] = jnp.where(low, jnp.where(lane < 2, 1.0, 0.0), values).astype(BF)
        dk_acc[...] = jnp.zeros_like(dk_acc)
        dv_acc[...] = jnp.zeros_like(dv_acc)
        kb, tkb, qb, tqb = (big_rows(ref) for ref in (k_ref, tk_ref, q_ref, tq_ref))
        same_head = (lax.broadcasted_iota(jnp.int32, (128, 128), 0) < 64) == (
            lanes_of((128, 128)) < 64
        )
        for i, (a, b) in enumerate(((kb, kb), (tkb, kb), (qb, qb), (tqb, qb))):
            gram = jnp.where(same_head, dot(a, b, TN) * share, 0.0)
            grams[2 * i], grams[2 * i + 1] = split(gram)

    start = pl.multiple_of(step * tile, tile)
    low = lanes_of((sub, 128)) < 64
    lane = lanes_of((sub, 128))

    def prepare(at):
        here_rows = pl.ds(start + at, sub)
        q8, tq8 = q_ref[here_rows, :], tq_ref[here_rows, :]
        scaled = dc_ref[at : at + sub, :].astype(F32) * inv_ref[at : at + sub, :]
        product = scaled * ctx_ref[at : at + sub, :].astype(F32)
        augmented = []
        for h in range(2):
            mine = low if h == 0 else jnp.logical_not(low)
            delta = -jnp.sum(jnp.where(mine, product, 0.0), axis=1, keepdims=True)
            upper = delta.astype(BF).astype(F32)
            first = 64 if h == 0 else 0
            extra = jnp.where(
                lane == first, upper, jnp.where(lane == first + 1, delta - upper, 0.0)
            )
            augmented.append(jnp.where(mine, scaled, extra).astype(BF))
        q_turned = q8.astype(F32).T.astype(BF)
        dc_turned = scaled.T.astype(BF)
        return here_rows, q8, tq8, augmented, q_turned, dc_turned

    def body(edge, half):
        ready = {half * sub: prepare(half * sub)}
        chains = [(half * sub, h) for h in range(2)]
        edge_at = {None: None, 0: 0, 1: tile - sub}[edge]
        columns = slice(0, sub) if edge == 0 else slice(seq - sub, seq)

        def d_probs_of(at, h):
            return dot(ready[at][3][h], v_aug[h], NT)

        d_probs = d_probs_of(*chains[0])
        d_queries = {}
        for n, (at, h) in enumerate(chains):
            if n + 1 < len(chains):
                later = d_probs_of(*chains[n + 1])
            here_rows, q8, tq8, unused, q_turned, dc_turned = ready[at]
            mine = low if h == 0 else jnp.logical_not(low)
            numerators = e_ref[h, at : at + sub, :]
            d_scores = numerators.astype(F32) * d_probs
            if edge is not None and at == edge_at:
                q_mine = jnp.where(mine, q8, 0.0).astype(BF)
                tq_mine = jnp.where(mine, tq8, 0.0).astype(BF)
                gap = dot(q_mine, k_ref[columns, :], NT) - dot(tq_mine, tk_ref[columns, :], NT)
                same = jnp.where(edges[edge][:, :1] == row_ref[:, columns], share, 0.0)
                gap = gap * (same * (1.0 - in_big[edge][:, :1]))
                if edge == 0:
                    d_scores = jnp.concatenate(
                        [d_scores[:, :sub] + gap, d_scores[:, sub:]], axis=1
                    )
                else:
                    d_scores = jnp.concatenate(
                        [d_scores[:, : seq - sub], d_scores[:, seq - sub :] + gap], axis=1
                    )
            d_scores = d_scores.astype(BF)
            mine = slice(64 * h, 64 * h + 64)
            dv_acc[mine, :] += dot(dc_turned[mine, :], numerators)
            d_queries[h] = dot(d_scores, k_ref[...])
            dk_acc[mine, :] += dot(q_turned[mine, :], d_scores)
            if h == 1:
                d_query = jnp.where(low, d_queries[0], d_queries[1])
                qb, tqb = q8, tq8
                if edge is not None and at == edge_at:
                    qb = (q8.astype(F32) * in_big[edge]).astype(BF)
                    tqb = (tq8.astype(F32) * in_big[edge]).astype(BF)
                d_query += dot(qb, grams[0]) + dot(qb, grams[1])
                d_query -= dot(tqb, grams[2]) + dot(tqb, grams[3])
                dq_all[here_rows, :] = (d_query * 0.125).astype(BF)
            if n + 1 < len(chains):
                d_probs = later

    for half in range(halves):
        if half:
            due(half)
        edge, at_edge = None, None
        if half == 0:
            edge, at_edge = 0, step == 0
        elif half == halves - 1:
            edge, at_edge = 1, step == steps - 1
        if edge is not None:
            pl.when(at_edge)(functools.partial(body, edge, half))
            pl.when(jnp.logical_not(at_edge))(functools.partial(body, None, half))
        else:
            body(None, half)

    def pair_end(p):
        job = late[p]
        kb, tkb = big_rows(k_ref), big_rows(tk_ref)
        d_key = dk_acc[...].T
        d_key += dot(kb, grams[4]) + dot(kb, grams[5]) - dot(tkb, grams[6]) - dot(tkb, grams[7])
        d_value = dv_acc[...].T.astype(BF)
        d_query = dq_all[...]
        d_pair = jnp.concatenate([d_query, d_key.astype(BF), d_value], axis=1)
        if p == 0:
            for copy in loads():
                copy.wait()
        columns = slice(p * 128, (p + 1) * 128)
        bins = jnp.concatenate([weights[0, i, :, columns] for i in range(3)], axis=1)
        chunk = depth // size
        half = job.get("half", 0)
        partial = dot(active[...], d_pair, TN).astype(job.wires[0])
        for d in range(size):
            half[d] = partial[d * chunk : (d + 1) * chunk, :]
        if p == pairs - 1:
            job.dp_start()
        if p < pairs - 1:
            if p == 0:
                d_act[...] = dot(d_pair, bins, NT)
            else:
                d_act[...] += dot(d_pair, bins, NT)
        else:
            pair_box[...] = d_pair
            for j in range(1, groups + 1):
                at = pl.ds(pl.multiple_of(lax.rem(r + j, groups) * rows, rows), rows)
                total = dot(pair_box[at, :], bins, NT)
                if p > 0:
                    total = total + d_act[at, :]
                if j < groups:
                    have["outbox"][j - 1] = total.astype(BF)
                    core_copies()[j - 1].start()
                else:
                    d_act[at, :] = total
        sums = have["sums"]
        sums[0:1, columns] = jnp.sum(d_query.astype(F32), axis=0, keepdims=True)
        sums[1:2, columns] = jnp.sum(d_value.astype(F32), axis=0, keepdims=True)

    def core_copies():
        return [
            remote(
                have["outbox"].at[j - 1],
                have["inbox"].at[j - 1],
                have["core_s"].at[j],
                have["core_r"].at[j],
                cores[j - 1],
            )
            for j in range(1, groups)
        ]

    def small_copies(stage, peers, base):
        return [
            remote(
                have["small"].at[stage],
                have["small_box"].at[base + d],
                have["small_s"].at[base + d],
                have["small_r"].at[base + d],
                peer,
            )
            for d, peer in enumerate(peers)
        ]

    def small_start(stage, peers, base):
        for copy in small_copies(stage, peers, base):
            copy.start()

    def small_sum(stage, peers, base):
        for copy in small_copies(stage, peers, base):
            copy.wait_recv()
        total = have["small"][stage]
        for d in range(len(peers)):
            total = total + have["small_box"][base + d]
        return total

    for p in range(pairs - 1):

        @pl.when((pair == p) & (step == steps - 1))
        def _():
            pair_end(p)

    @pl.when(time == total_time - 1)
    def _():
        pair_end(pairs - 1)
        last = late[-1]
        small = have["small"]
        small[0] = small_ref[...]
        for i in range(2):
            vector = have["sums"][i : i + 1, :]
            small[0, 2 + i : 3 + i, :] = jnp.concatenate(
                [jnp.where(r == j, vector, 0.0) for j in range(groups)], axis=1
            )
        small_start(0, along_dp, 0)
        go_on(TAIL[0])
        last.z_start()
        last.z_back()
        for copy in core_copies():
            copy.wait_recv()
        shard = rows // streams
        back_copies = []
        blocks = have["blocks"]
        order = [2, 1, 3] if streams == 4 else list(range(1, streams))
        for d in order + [0]:
            target = lax.rem(s + d, streams)
            here_rows = pl.ds(pl.multiple_of(target * shard, shard), shard)
            bent = jnp.tanh(x_rows[target].astype(F32) * (1.0 / clip_level))
            total = d_act[pl.ds(pl.multiple_of(r * rows + target * shard, shard), shard), :]
            for j in range(groups - 1):
                total = total + have["inbox"][j, here_rows, :].astype(F32)
            blocks[target] = (d_one[here_rows, :] + total * (1.0 - bent * bent)).astype(BF)
            if d:
                copy = remote(
                    blocks.at[target],
                    grad_ref.at[s],
                    have["grad_s"].at[d],
                    have["grad_r"].at[d],
                    along_z[d - 1],
                )
            else:
                copy = pltpu.make_async_copy(blocks.at[s], grad_ref.at[s], have["grad_s"].at[0])
            copy.start()
            back_copies.append(copy)
        small[1] = small_sum(0, along_dp, 0)
        small_start(1, along_z, size)
        go_on(TAIL[1])
        small[2] = small_sum(1, along_z, size)
        small_start(2, cores, size + streams)
        go_on(TAIL[2])
        last.dp_back()
        summed = small_sum(2, cores, size + streams)
        gain_ref[...] = summed[0:2, :]
        bias_ref[...] = summed[2:8, :]
        for i in range(shift_ref.shape[1] // depth):
            shift_ref[:, i * depth : (i + 1) * depth] = summed[8 + i : 9 + i, :]
        go_on(TAIL[3])
        last.core_back()
        go_on(8)
        for copy in back_copies:
            copy.wait()
        for job in early + late:
            job.end()
        for copy in (
            core_copies()
            + small_copies(0, along_dp, 0)
            + small_copies(1, along_z, size)
            + small_copies(2, cores, size + streams)
        ):
            copy.wait_send()


TWO_STEP = False
TAIL = (1, 1, 0, 0)
EARLY_TIMES = ((2, 0, 7, 9, 12), (4, 0, 12, 14))
LATE_TIMES = (0, 5, 7)


def attention_back(
    streams,
    groups,
    numerators,
    queries,
    keys,
    values,
    teacher_queries,
    teacher_keys,
    d_context,
    context,
    inverse,
    docs,
    small,
    active,
    bin_own,
    d_one,
    tokens,
    early_arrays,
    up_width,
    collective_id,
):
    seq, width = queries.shape
    pairs = width // 128
    tile = 512
    rows, depth = d_one.shape
    size = lax.axis_size("dp")
    shard = rows // streams
    bag = Bag()
    bag.add("v_aug", pltpu.VMEM((2, seq, 128), BF))
    bag.add("dk_acc", pltpu.VMEM((128, seq), F32))
    bag.add("dv_acc", pltpu.VMEM((128, seq), F32))
    bag.add("grams", pltpu.VMEM((8, 128, 128), BF))
    bag.add("dq_all", pltpu.VMEM((seq, 128), BF))
    bag.add("d_act", pltpu.VMEM((seq, depth), F32))
    bag.add("active", pltpu.VMEM((seq, depth), BF))
    bag.add("weights", pltpu.VMEM((1, 3, depth, width), BF))
    bag.add("d_one", pltpu.VMEM((rows, depth), F32))
    bag.add("x_rows", pltpu.VMEM((streams, shard, depth), BF))
    bag.add("load", dma(4))
    bag.add("sums", pltpu.VMEM((8, width), F32))
    bag.add("outbox", pltpu.VMEM((groups - 1, rows, depth), BF))
    bag.add("inbox", pltpu.VMEM((groups - 1, rows, depth), BF))
    bag.add("core_s", dma(groups))
    bag.add("core_r", dma(groups))
    bag.add("blocks", pltpu.VMEM((streams, shard, depth), BF))
    bag.add("grad_s", dma(streams))
    bag.add("grad_r", dma(streams))
    count = size + streams + groups
    bag.add("small", pltpu.VMEM((3,) + small.shape, F32))
    bag.add("small_box", pltpu.VMEM((count,) + small.shape, F32))
    bag.add("small_s", dma(count))
    bag.add("small_r", dma(count))
    bag.add("row", pltpu.VMEM((1, seq), F32))
    bag.add("pair_box", pltpu.VMEM((seq, 3 * 128), BF))
    bag.add("edges", pltpu.VMEM((2, 256, 128), F32))
    bag.add("in_big", pltpu.VMEM((2, 256, 128), F32))
    early, flat = [], []
    for n, arrays in enumerate(early_arrays):
        job = Reduce(bag, f"early{n}", streams, groups, [a.shape for a in arrays], True, TWO_STEP)
        early.append(job)
        flat += [
            a.reshape(groups, size, chunk, cols) for a, (chunk, cols) in zip(arrays, job.shapes)
        ]
    late = [
        Reduce(bag, f"late{p}", streams, groups, [(depth, 3 * 128)], False, False)
        for p in range(pairs)
    ]
    part = pl.BlockSpec((tile, 128), lambda p, i: (i, p))
    any_space = pl.BlockSpec(memory_space=pl.ANY)

    whole = pl.BlockSpec((seq, 128), lambda p, i: (0, p))

    def constant(shape):
        return pl.BlockSpec(shape, lambda p, i: (0,) * len(shape))

    small_shapes = [(2, depth), (6, depth), (1, up_width)]
    early_shapes = [shape for job in early for shape in job.out_shapes()]
    late_shapes = [shape for job in late for shape in job.out_shapes()]
    results = pl.pallas_call(
        functools.partial(backward_kernel, streams, groups, tile, bag, early, late),
        grid=(pairs, seq // tile),
        in_specs=[
            pl.BlockSpec((2, tile, seq), lambda p, i: (p, i, 0)),
            whole,
            whole,
            whole,
            whole,
            whole,
            part,
            part,
            part,
            constant(docs.shape),
            constant(small.shape),
        ]
        + [any_space] * (4 + len(flat)),
        out_specs=[any_space] * (1 + len(early_shapes) + len(late_shapes))
        + [constant(shape) for shape in small_shapes],
        out_shape=[jax.ShapeDtypeStruct((streams, shard, depth), BF)]
        + early_shapes
        + late_shapes
        + [jax.ShapeDtypeStruct(shape, F32) for shape in small_shapes],
        scratch_shapes=list(bag.items.values()),
        compiler_params=remote_params(collective_id),
        name="attention_back",
    )(
        numerators,
        queries,
        keys,
        values,
        teacher_queries,
        teacher_keys,
        d_context,
        context,
        inverse,
        docs,
        small,
        active,
        bin_own,
        d_one,
        tokens,
        *flat,
    )
    grad_tokens, *rest = results
    early_sums = rest[: len(flat)]
    late_sums = rest[len(flat) : -3]
    shapes = [a.shape for arrays in early_arrays for a in arrays]
    return (
        grad_tokens,
        [e.reshape(shape) for e, shape in zip(early_sums, shapes)],
        [l.reshape(groups, depth, 3 * 128) for l in late_sums],
        list(rest[-3:]),
    )


def middle_kernel(
    streams,
    groups,
    bag,
    tiles,
    x_ref,
    tx_ref,
    cot_ref,
    ctx_ref,
    tctx_ref,
    bo_hbm,
    bup_hbm,
    bdown_hbm,
    to_hbm,
    tup_hbm,
    tdown_hbm,
    sg_ref,
    sb_ref,
    sub_ref,
    tg_ref,
    tb_ref,
    tub_ref,
    out_ref,
    d1_ref,
    dctx_ref,
    gout_ref,
    gup_ref,
    gdown_ref,
    small_ref,
    *rest,
):
    have = bag.bind(rest)
    gout_acc, gup_acc, gdown_acc = have["gout"], have["gup"], have["gdown"]
    out_box, d_box = have["out_box"], have["d_box"]
    step = pl.program_id(0)
    far = (to_hbm, bo_hbm, tup_hbm, bup_hbm, tdown_hbm, bdown_hbm)
    to_ref, bo_ref, tup_ref, bup_ref, tdown_ref, bdown_ref = near = [
        have[f"weight{i}"] for i in range(6)
    ]
    loads = [
        pltpu.make_async_copy(source, target, have["weight_sems"].at[i])
        for i, (source, target) in enumerate(zip(far, near))
    ]

    def ready(which):
        @pl.when(step == 0)
        def _():
            for i in which:
                loads[i].wait()

    steps = pl.num_programs(0)
    width = ctx_ref.shape[1] * 128
    tile, depth = cot_ref.shape
    n_steps = out_box.shape[0]
    shard = n_steps * tile // streams
    s, r = place(groups)
    along_z = stream_peers(streams, groups)
    turned = row_tile(step, n_steps, streams, groups)
    start = pl.multiple_of(turned * tile, tile)

    @pl.when(step == 0)
    def _():
        for copy in loads:
            copy.start()
        greet(along_z + core_peers(groups))

    @pl.when(step == 0)
    def _():
        for ref in (gout_acc, gup_acc, gdown_acc, small_ref):
            ref[...] = jnp.zeros_like(ref)

    def row(ref, i):
        return ref[i : i + 1, :]

    pieces = [(j, p) for j in range(groups) for p in range(ctx_ref.shape[1])]
    ff = bup_ref.shape[1]
    wide = min(512, ff)
    chunks = [slice(i, i + wide) for i in range(0, ff, wide)]

    ready((0, 1))
    tctx = jnp.concatenate([tctx_ref[j, p] for j, p in pieces], axis=1)
    t_att = dot(tctx, to_ref[...]) + row(tb_ref, 2)
    context = jnp.concatenate([ctx_ref[j, p] for j, p in pieces], axis=1).astype(F32)
    bent = jnp.tanh(context * (1.0 / clip_level))
    ctx_active = (clip_level * bent).astype(BF)
    ctx_slope = 1.0 - bent * bent
    attended = dot(ctx_active, bo_ref[...]) + row(sb_ref, 2)
    t_hidden = layer_norm(tx_ref[...].astype(F32) + t_att, row(tg_ref, 0), row(tb_ref, 3))[0]
    hidden, normed_one, inverse_one = layer_norm(
        x_ref[...].astype(F32) + attended, row(sg_ref, 0), row(sb_ref, 3)
    )
    bent = jnp.tanh(hidden * (1.0 / clip_level))
    hidden_active = (clip_level * bent).astype(BF)
    hidden_slope = 1.0 - bent * bent
    t_low = t_hidden.astype(BF)

    def up(i):
        return dot(t_low, tup_ref[:, chunks[i]]), dot(hidden_active, bup_ref[:, chunks[i]])

    ready((2, 3, 4, 5))
    ahead = up(0)
    t_branch, branch, actives, slopes = None, None, [], []
    for i, at in enumerate(chunks):
        t_pre, inner_pre = ahead
        if i + 1 < len(chunks):
            ahead = up(i + 1)
        t_inner = gelu_parts(t_pre + tub_ref[:, at])[0]
        inner_pre = inner_pre + sub_ref[:, at]
        inner_act, phi = gelu_parts(inner_pre)
        bent = jnp.tanh(inner_act * (1.0 / clip_level))
        inner_active = (clip_level * bent).astype(BF)
        t_term = dot(t_inner.astype(BF), tdown_ref[at, :])
        term = dot(inner_active, bdown_ref[at, :])
        t_branch = t_term if i == 0 else t_branch + t_term
        branch = term if i == 0 else branch + term
        actives.append(inner_active)
        slopes.append(
            (1.0 - bent * bent)
            * (phi + inner_pre * jnp.exp(-0.5 * inner_pre * inner_pre) * 0.3989422804014327)
        )
    t_out = layer_norm(t_hidden + t_branch + row(tb_ref, 4), row(tg_ref, 1), row(tb_ref, 5))[0]
    branch = branch + row(sb_ref, 4)
    output, normed_two, inverse_two = layer_norm(hidden + branch, row(sg_ref, 1), row(sb_ref, 5))
    out_box[step] = output.astype(BF)
    per_tile = tile // shard
    for n in range(per_tile):
        block = turned * per_tile + n
        source = out_box.at[step, pl.ds(n * shard, shard)]

        @pl.when(block == s)
        def _():
            pltpu.make_async_copy(source, out_ref.at[s], have["out_s"].at[s]).start()

        @pl.when(block != s)
        def _():
            remote(
                source,
                out_ref.at[s],
                have["out_s"].at[block],
                have["out_r"].at[s],
                {"blk": block * groups + r},
            ).start()
    upstream = cot_ref[...].astype(F32) + 0.5 * (output - t_out)
    d_two = norm_back(upstream, row(sg_ref, 1), normed_two, inverse_two)
    d_branch = d_two.astype(BF)

    def down(i):
        return dot(d_branch, bdown_ref[chunks[i], :], NT)

    ahead = down(0)
    through = None
    for i, at in enumerate(chunks):
        d_inner = ahead
        if i + 1 < len(chunks):
            ahead = down(i + 1)
        d_inner = (d_inner * slopes[i]).astype(BF)
        gdown_acc[at, :] += dot(actives[i], d_branch, TN)
        gup_acc[:, at] += dot(hidden_active, d_inner, TN)
        term = dot(d_inner, bup_ref[:, at], NT)
        through = term if i == 0 else through + term
        d_shift = jnp.sum(d_inner.astype(F32), axis=0, keepdims=True)
        for n in range(wide // depth):
            line = 8 + (i * wide) // depth + n
            small_ref[line : line + 1, :] += d_shift[:, n * depth : (n + 1) * depth]
    d_hidden = d_two + through * hidden_slope
    d_one = norm_back(d_hidden, row(sg_ref, 0), normed_one, inverse_one)
    d1_ref[...] = d_one
    d_attended = d_one.astype(BF)
    gout_acc[...] += dot(ctx_active, d_attended, TN)
    d_context = (dot(d_attended, bo_ref[...], NT) * ctx_slope).astype(BF)
    place_rows = pl.ds(pl.multiple_of(r * n_steps * tile + start, tile), tile)
    for j in range(groups):
        d_box[step, j] = d_context[:, j * width : (j + 1) * width]
        piece, target = d_box.at[step, j], dctx_ref.at[place_rows]

        @pl.when(r == j)
        def _():
            tiles.own(have, piece, target, 0, step).start()

        @pl.when(r != j)
        def _():
            tiles.copy(have, piece, target, j, 0, step).start()


    def total(value):
        return jnp.sum(value, axis=0, keepdims=True)

    sums = [
        (0, d_hidden * normed_one),
        (1, upstream * normed_two),
        (4, d_attended.astype(F32)),
        (5, d_hidden),
        (6, d_branch.astype(F32)),
        (7, upstream),
    ]
    for i, value in sums:
        small_ref[i : i + 1, :] += total(value)
    @pl.when(step == steps - 1)
    def _():
        tiles.finish(have, d_box.at[0, 0], dctx_ref.at[place_rows])
        source = out_box.at[0, pl.ds(0, shard)]
        pltpu.make_async_copy(source, out_ref.at[s], have["out_s"].at[s]).wait()
        for d, peer in enumerate(along_z, 1):
            block = lax.rem(s + d, streams)
            remote(
                source, out_ref.at[block], have["out_s"].at[block], have["out_r"].at[block], peer
            ).wait()
        gout_ref[...] = gout_acc[...].astype(BF)
        gup_ref[...] = gup_acc[...].astype(BF)
        gdown_ref[...] = gdown_acc[...].astype(BF)


def row_tile(step, steps, streams, groups):
    s, r = place(groups)
    return lax.rem(s // (streams // steps) + 1 + step, steps)


def middle(streams, groups, x, tx, cot, ctx, tctx, weights, teacher_weights, vectors, collective_id):
    rows, depth = cot.shape
    ff = weights[1].shape[1]
    tile = min(256, rows)
    pairs = ctx.shape[1]
    width = pairs * 128
    steps = rows // tile
    shard = rows // streams

    def turn(i):
        return row_tile(i, steps, streams, groups)

    def stream_tile(i):
        return lax.rem(lax.axis_index("blk"), groups) * steps + turn(i)

    tall = pl.BlockSpec((tile, depth), lambda i: (turn(i), 0))
    of_stream = pl.BlockSpec((tile, depth), lambda i: (stream_tile(i), 0))
    split_rows = pl.BlockSpec((groups, pairs, tile, 128), lambda i: (0, 0, turn(i), 0))
    any_space = pl.BlockSpec(memory_space=pl.ANY)

    def full(shape):
        return pl.BlockSpec(shape, lambda i: (0,) * len(shape))

    out_full = [(depth, depth), (depth, ff), (ff, depth), (16, depth)]
    bag = Bag()
    for name, shape in zip(("gout", "gup", "gdown"), out_full):
        bag.add(name, pltpu.VMEM(shape, F32))
    for i in range(3):
        bag.add(f"weight{2 * i}", pltpu.VMEM(teacher_weights[i].shape, BF))
        bag.add(f"weight{2 * i + 1}", pltpu.VMEM(weights[i].shape, BF))
    bag.add("weight_sems", dma(6))
    bag.add("out_box", pltpu.VMEM((steps, tile, depth), BF))
    bag.add("d_box", pltpu.VMEM((steps, groups, tile, width), BF))
    bag.add("out_s", dma(streams))
    bag.add("out_r", dma(streams))
    tiles = Tiles(bag, "tiles", groups, 1, steps)
    return pl.pallas_call(
        functools.partial(middle_kernel, streams, groups, bag, tiles),
        grid=(steps,),
        in_specs=[of_stream, of_stream, tall, split_rows, split_rows]
        + [any_space] * 6
        + [full(a.shape) for a in vectors],
        out_specs=[any_space, tall, any_space] + [full(s) for s in out_full],
        out_shape=[
            jax.ShapeDtypeStruct((streams, shard, depth), BF),
            jax.ShapeDtypeStruct((rows, depth), F32),
            jax.ShapeDtypeStruct((rows * groups, width), BF),
        ]
        + [jax.ShapeDtypeStruct(s, BF if i < 3 else F32) for i, s in enumerate(out_full)],
        scratch_shapes=list(bag.items.values()),
        compiler_params=remote_params(collective_id),
        name="middle",
    )(x, tx, cot, ctx, tctx, *weights, *teacher_weights, *vectors)


def latent_columns(latent, grad, out):
    rows = latent.shape[0]
    size = min(256, rows)
    chunks = [slice(i, i + size) for i in range(0, rows, size)]
    squares = jnp.zeros((1, latent.shape[1]), F32)
    for at in chunks:
        matrix = latent[at, :].astype(F32)
        squares = squares + jnp.sum(matrix * matrix, axis=0, keepdims=True)
    scale = jnp.sqrt(squares * (1.0 / rows) + 1e-06)
    twice = 2.0 / scale
    through_scale = jnp.zeros_like(squares)
    for at in chunks:
        matrix, upstream = latent[at, :].astype(F32), grad[at, :].astype(F32)
        inner = matrix * twice
        bent = jnp.tanh(inner)
        slope = 1.0 - bent * bent
        through_scale = through_scale + jnp.sum(
            upstream * (bent - inner * slope), axis=0, keepdims=True
        )
        out[at, :] = upstream * (2.0 * slope)
    factor = through_scale / (rows * scale)
    for at in chunks:
        out[at, :] = out[at, :] + latent[at, :].astype(F32) * factor


def latent_grads_kernel(pairs, passed, lq, lo, lu, ld, *refs):
    late, (go, gu, gd, *refs) = refs[:pairs], refs[pairs:]
    come, (oq, oo, ou, od, *gone) = refs[:passed], refs[passed:]
    for source, target in zip(come, gone):
        target[...] = source[...]
    for p in range(pairs):

        @pl.when(lax.rem(pl.program_id(0), pairs) == p)
        def _():
            for i in range(3):
                latent_columns(lq.at[i], late[p].at[0, :, i * 128 : (i + 1) * 128], oq.at[i])

    latent_columns(lo, go, oo)
    latent_columns(ld, gd, od)
    for i in range(0, lu.shape[1], 128):
        at = slice(i, i + 128)
        latent_columns(lu.at[:, at], gu.at[:, at], ou.at[:, at])


def latent_grads(latents, late, early, tall, small):
    pairs = len(late)
    groups, depth, wide = late[0].shape
    steps = groups * pairs
    qkv = pl.BlockSpec((3, depth, depth // steps), lambda i: (0, 0, i))
    flat = [pl.BlockSpec((a.shape[0], a.shape[1] // steps), lambda i: (0, i)) for a in latents[1:]]
    handed = [
        pl.BlockSpec((a.shape[0] // steps,) + a.shape[1:], lambda i: (i, 0, 0)) for a in tall
    ] + [pl.BlockSpec(a.shape, lambda i: (0, 0)) for a in small]
    return pl.pallas_call(
        functools.partial(latent_grads_kernel, pairs, len(handed)),
        grid=(steps,),
        in_specs=[qkv]
        + flat
        + [pl.BlockSpec((1, depth, wide), lambda i: (i // pairs, 0, 0))] * pairs
        + flat
        + handed,
        out_specs=[qkv] + flat + handed,
        out_shape=[jax.ShapeDtypeStruct(a.shape, F32) for a in latents]
        + [jax.ShapeDtypeStruct(a.shape, a.dtype) for a in tall + small],
        compiler_params=pltpu.CompilerParams(vmem_limit_bytes=VMEM_BYTES),
        name="latent_grads",
    )(*latents, *late, *early, *tall, *small)


def shards(
    tokens,
    teacher_tokens,
    segment_ids,
    cotangent,
    latent_qkv,
    latent_out,
    latent_up,
    latent_down,
    student_gain,
    student_bias,
    student_up_bias,
    teacher_qkv,
    teacher_out,
    teacher_up,
    teacher_down,
    teacher_gain,
    teacher_bias,
    teacher_up_bias,
):
    streams, shard_len, depth = tokens.shape
    blocks = lax.axis_size("blk")
    groups = blocks // streams
    seq = shard_len * blocks
    rows = seq // groups
    block = (shard_len, depth)
    gather, swap = Gather(streams, groups, block, BF), Swap(streams, groups, block, BF)
    bin_own, bin_out, bin_up, bin_down, token_blocks, qkv_parts, docs = intake(
        Moves(
            gather,
            Spread(teacher_qkv.shape, BF),
            Gather(streams, groups, (8, shard_len), F32),
        ),
        groups,
        [latent_qkv, latent_out, latent_up, latent_down],
        segment_ids,
        [tokens, teacher_qkv],
        1,
    )
    stream_tokens = token_blocks.reshape(seq, depth)
    (
        queries,
        keys,
        ctx_rows,
        values,
        numerators,
        context,
        inverse,
        active,
        teacher_blocks,
        up_parts,
        out_parts,
    ) = attention(
        stream_tokens,
        bin_own,
        student_bias,
        docs,
        streams,
        groups,
        Moves(gather, Spread(teacher_up.shape, BF), Spread(teacher_out.shape, BF)),
        [teacher_tokens, teacher_up, teacher_out],
        True,
        2,
        "attention_student",
    )
    teacher_stream = teacher_blocks.reshape(seq, depth)
    teacher_queries, teacher_keys, tctx_rows, cot_blocks, down_parts = attention(
        teacher_stream,
        qkv_parts,
        teacher_bias,
        docs,
        streams,
        groups,
        Moves(swap, Spread(teacher_down.shape, BF), others=[gather]),
        [cotangent, teacher_down],
        False,
        3,
        "attention_teacher",
    )
    output, d_one, d_context, g_out, g_up, g_down, small = middle(
        streams,
        groups,
        stream_tokens,
        teacher_stream,
        cot_blocks.reshape(rows, depth),
        ctx_rows,
        tctx_rows,
        [bin_out, bin_up, bin_down],
        [
            out_parts.reshape(-1, depth),
            up_parts.reshape(depth, -1),
            down_parts.reshape(-1, depth),
        ],
        [
            student_gain,
            student_bias,
            student_up_bias.reshape(1, -1),
            teacher_gain,
            teacher_bias,
            teacher_up_bias.reshape(1, -1),
        ],
        4,
    )
    grads = [[g_up], [g_down, g_out]]
    in_kernel = depth % (16 * blocks * lax.axis_size("dp")) == 0
    grad_tokens, early, late, small = attention_back(
        streams,
        groups,
        numerators,
        queries,
        keys,
        values,
        teacher_queries,
        teacher_keys,
        d_context,
        context,
        inverse,
        docs,
        small,
        active,
        bin_own,
        d_one,
        token_blocks,
        grads if in_kernel else [],
        latent_up.shape[1],
        6,
    )
    if not in_kernel:
        early = lax.psum((g_up, g_down, g_out), ("dp", "blk"))
    grad_qkv, grad_out, grad_up, grad_down, output, grad_tokens, gain, bias, shift = latent_grads(
        [latent_qkv, latent_out, latent_up, latent_down],
        late,
        [early[2], early[0], early[1]],
        [output, grad_tokens],
        small,
    )
    return (
        output,
        grad_tokens,
        grad_qkv,
        grad_out,
        grad_up,
        grad_down,
        gain,
        bias,
        shift.reshape(-1),
    )


def solution(mesh):
    return jax.shard_map(
        shards,
        mesh=mesh,
        in_specs=(
            P("dp", "blk", None),
            P("dp", "blk", None),
            P("dp", "blk"),
            P("dp", "blk", None),
            P(),
            P(),
            P(),
            P(),
            P(),
            P(),
            P(),
            P(None, "dp", None),
            P("dp", None),
            P("dp", None),
            P("dp", None),
            P(),
            P(),
            P(),
        ),
        out_specs=(P("dp", "blk", None), P("dp", "blk", None), P(), P(), P(), P(), P(), P(), P()),
        check_vma=False,
    )
```

```python
import functools

import jax
import jax.numpy as jnp
from jax import lax
from jax.experimental import pallas as pl
from jax.experimental.pallas import tpu as pltpu
from jax.sharding import PartitionSpec as P

HEADS = 8
BF = jnp.bfloat16
F32 = jnp.float32
LOG2E = 1.4426950408889634
clip_level = 2.5
masked_score = -1e30
VMEM_BYTES = 56 << 20
MESH = pl.DeviceIdType.MESH
NT = (((1,), (1,)), ((), ()))
TN = (((0,), (0,)), ((), ()))


def squash(tensor):
    return clip_level * jnp.tanh(tensor * (1.0 / clip_level))


def gelu_parts(tensor):
    phi = 0.5 * (1.0 + lax.erf(tensor * 0.7071067811865476))
    return tensor * phi, phi


def binarize(matrix):
    column_scale = jnp.sqrt(jnp.mean(matrix * matrix, axis=-2, keepdims=True) + 1e-06)
    return column_scale * jnp.tanh(2.0 * matrix / column_scale)


def layer_norm(tensor, gain_row, shift_row):
    centre = tensor - jnp.mean(tensor, axis=-1, keepdims=True)
    inverse_std = lax.rsqrt(jnp.mean(centre * centre, axis=-1, keepdims=True) + 1e-05)
    normed = centre * inverse_std
    return (normed * gain_row + shift_row, normed, inverse_std)


def norm_back(upstream, gain_row, normed, inverse_std):
    scaled = upstream * gain_row
    return inverse_std * (
        scaled
        - jnp.mean(scaled, axis=-1, keepdims=True)
        - normed * jnp.mean(scaled * normed, axis=-1, keepdims=True)
    )


def dot(a, b, dims=(((1,), (0,)), ((), ()))):
    return lax.dot_general(a, b, dims, preferred_element_type=F32)


def latent_grad(latent, binary_grad):
    matrix = latent.astype(F32)
    unused, pullback = jax.vjp(binarize, matrix)
    return pullback(binary_grad)[0]


def place(groups):
    here = lax.axis_index("blk")
    return here // groups, lax.rem(here, groups)


def greet(peers):
    barrier = pltpu.get_barrier_semaphore()
    for peer in peers:
        pl.semaphore_signal(barrier, inc=1, device_id=peer, device_id_type=MESH)
    pl.semaphore_wait(barrier, len(peers))


def stream_peers(streams, groups):
    s, r = place(groups)
    return [{"blk": lax.rem(s + d, streams) * groups + r} for d in range(1, streams)]


def core_peers(groups):
    s, r = place(groups)
    return [{"blk": s * groups + lax.rem(r + j, groups)} for j in range(1, groups)]


def dp_peers():
    size = lax.axis_size("dp")
    here = lax.axis_index("dp")
    return [{"dp": lax.rem(here + d, size)} for d in range(1, size)]


def unique(jobs):
    peers, kinds = [], []
    for job in jobs:
        for kind, found in job.peers():
            if kind not in kinds:
                kinds.append(kind)
                peers += found
    return peers


def remote(source, target, send, recv, peer):
    return pltpu.make_async_remote_copy(
        src_ref=source,
        dst_ref=target,
        send_sem=send,
        recv_sem=recv,
        device_id=peer,
        device_id_type=MESH,
    )


def dma(count):
    return pltpu.SemaphoreType.DMA((count,))


class Staged:
    def __init__(self, source, target, stage, sems):
        self.load = pltpu.make_async_copy(source, stage, sems.at[0])
        self.store = pltpu.make_async_copy(stage, target, sems.at[1])

    def first(self):
        self.load.start()

    def last(self):
        self.load.wait()
        self.store.start()
        self.store.wait()


class Gather:
    def __init__(self, streams, groups, block, dtype):
        self.streams, self.groups, self.block, self.dtype = streams, groups, block, dtype

    def scratch(self):
        b, g = self.streams, self.groups
        return [dma(b), dma(b), dma(b * g), dma(b * g), pltpu.VMEM(self.block, self.dtype), dma(2)]

    def out_shape(self):
        return jax.ShapeDtypeStruct((self.streams * self.groups,) + self.block, self.dtype)

    def peers(self):
        return [
            ("stream", stream_peers(self.streams, self.groups)),
            ("core", core_peers(self.groups)),
        ]

    def parts(self, source, target, send, recv, share_send, share_recv, stage, sems):
        b, g = self.streams, self.groups
        s, r = place(g)
        peers, cores = stream_peers(b, g), core_peers(g)
        swaps = [
            remote(
                source.at[lax.rem(s + d, b)],
                target.at[r * b + s],
                send.at[d],
                recv.at[d],
                peers[d - 1],
            )
            for d in range(1, b)
        ]
        shares = [
            [
                remote(
                    source.at[s] if d == 0 else target.at[r * b + lax.rem(s + b - d, b)],
                    target.at[r * b + lax.rem(s + b - d, b)],
                    share_send.at[j * b + d],
                    share_recv.at[j * b + d],
                    cores[j - 1],
                )
                for j in range(1, g)
            ]
            for d in range(b)
        ]
        own = Staged(source.at[s], target.at[r * b + s], stage, sems)
        return swaps, shares, own

    def first(self, *refs):
        swaps, shares, own = self.parts(*refs)
        for copy in swaps:
            copy.start()
        own.first()
        for copy in shares[0]:
            copy.start()

    def middle(self, *refs):
        swaps, shares, own = self.parts(*refs)
        for d in [1, 3, 2] if self.streams == 4 else range(1, self.streams):
            swaps[d - 1].wait_recv()
            for copy in shares[d]:
                copy.start()

    def last(self, *refs):
        swaps, shares, own = self.parts(*refs)
        own.last()
        for row in shares:
            for copy in row:
                copy.wait()
        for copy in swaps:
            copy.wait_send()


class Swap:
    def __init__(self, streams, groups, block, dtype):
        self.streams, self.groups, self.block, self.dtype = streams, groups, block, dtype

    def scratch(self):
        return [dma(self.streams), dma(self.streams), pltpu.VMEM(self.block, self.dtype), dma(2)]

    def out_shape(self):
        return jax.ShapeDtypeStruct((self.streams,) + self.block, self.dtype)

    def peers(self):
        return [("stream", stream_peers(self.streams, self.groups))]

    def parts(self, source, target, send, recv, stage, sems):
        b, g = self.streams, self.groups
        s, r = place(g)
        peers = stream_peers(b, g)
        swaps = [
            remote(source.at[lax.rem(s + d, b)], target.at[s], send.at[d], recv.at[d], peers[d - 1])
            for d in range(1, b)
        ]
        return swaps, Staged(source.at[s], target.at[s], stage, sems)

    def first(self, *refs):
        swaps, own = self.parts(*refs)
        for copy in swaps:
            copy.start()
        own.first()

    def last(self, *refs):
        swaps, own = self.parts(*refs)
        own.last()
        for copy in swaps:
            copy.wait()


class Spread:
    def __init__(self, block, dtype):
        self.block, self.dtype = block, dtype

    def scratch(self):
        size = lax.axis_size("dp")
        return [dma(size), dma(size), pltpu.VMEM(self.block, self.dtype), dma(2)]

    def out_shape(self):
        return jax.ShapeDtypeStruct((lax.axis_size("dp"),) + self.block, self.dtype)

    def peers(self):
        return [("dp", dp_peers())]

    def parts(self, source, target, send, recv, stage, sems):
        here = lax.axis_index("dp")
        copies = [
            remote(source, target.at[here], send.at[d], recv.at[d], peer)
            for d, peer in enumerate(dp_peers(), 1)
        ]
        return copies, Staged(source, target.at[here], stage, sems)

    first = Swap.first
    last = Swap.last


class Tiles:
    def __init__(self, bag, name, groups, pairs, per_owner):
        self.name, self.groups, self.pairs, self.per_owner = name, groups, pairs, per_owner
        count = pairs * per_owner
        bag.add(f"{name}_s", dma(groups * count))
        bag.add(f"{name}_r", dma(groups * count))

    def slot(self, who, pair, at):
        return (who * self.pairs + pair) * self.per_owner + at

    def copy(self, have, source, target, owner, pair, at):
        s, r = place(self.groups)
        return remote(
            source,
            target,
            have[f"{self.name}_s"].at[self.slot(owner, pair, at)],
            have[f"{self.name}_r"].at[self.slot(r, pair, at)],
            {"blk": s * self.groups + owner},
        )

    def own(self, have, source, target, pair, at):
        s, r = place(self.groups)
        return pltpu.make_async_copy(
            source, target, have[f"{self.name}_s"].at[self.slot(r, pair, at)]
        )

    def finish(self, have, source, target):
        s, r = place(self.groups)
        for pair in range(self.pairs):
            for at in range(self.per_owner):
                self.own(have, source, target, pair, at).wait()
                for j in range(1, self.groups):
                    other = lax.rem(r + j, self.groups)
                    remote(
                        source,
                        target,
                        have[f"{self.name}_s"].at[self.slot(other, pair, at)],
                        have[f"{self.name}_r"].at[self.slot(other, pair, at)],
                        {"blk": s * self.groups + other},
                    ).wait()


class Bag:
    def __init__(self):
        self.items = {}

    def add(self, name, item):
        self.items[name] = item

    def bind(self, refs):
        return dict(zip(self.items, refs))


class Reduce:
    def __init__(self, bag, name, streams, groups, shapes, over_cores, two_step):
        self.name, self.streams, self.groups = name, streams, groups
        self.size = lax.axis_size("dp")
        self.over_cores = over_cores
        self.two_step = two_step and self.size == 4 and streams % 2 == 0
        self.count = len(shapes)
        share = self.size * (groups if over_cores else 1)
        self.shapes = [(rows // share, cols) for rows, cols in shapes]
        self.wires = [BF if (c // streams) % 16 == 0 else F32 for c, cols in self.shapes]
        for i, (chunk, cols) in enumerate(self.shapes):
            wire, slim = self.wires[i], chunk // streams
            bag.add(f"{name}half{i}", pltpu.VMEM((self.size, chunk, cols), wire))
            if over_cores:
                bag.add(f"{name}core{i}", pltpu.VMEM((groups - 1, self.size, chunk, cols), wire))
            if self.two_step:
                bag.add(f"{name}first{i}", pltpu.VMEM((4, chunk // 2, cols), wire))
                bag.add(f"{name}second{i}", pltpu.VMEM((2, chunk // 2, cols), wire))
            else:
                bag.add(f"{name}dp{i}", pltpu.VMEM((self.size - 1, chunk, cols), wire))
            bag.add(f"{name}cut{i}", pltpu.VMEM((streams, slim, cols), wire))
            bag.add(f"{name}z{i}", pltpu.VMEM((streams - 1, slim, cols), wire))
            bag.add(f"{name}fin{i}", pltpu.VMEM((slim, cols), wire))
            for kind in self.kinds():
                bag.add(f"{name}{kind}s{i}", dma(self.sem_count(kind)))
                bag.add(f"{name}{kind}r{i}", dma(self.sem_count(kind)))
            bag.add(f"{name}local{i}", dma(2))

    def kinds(self):
        along = ["b1", "b2", "c", "d", "e1", "e2"] if self.two_step else ["b", "c", "d", "e"]
        return (["a"] if self.over_cores else []) + along + ["f"]

    def sem_count(self, kind):
        if kind in ("a", "f"):
            return self.groups
        if kind in ("c", "d"):
            return self.streams
        return max(self.size, 4)

    def out_shapes(self):
        return [
            jax.ShapeDtypeStruct(
                (self.groups, self.size, self.streams, chunk // self.streams, cols), wire
            )
            for (chunk, cols), wire in zip(self.shapes, self.wires)
        ]

    def bind(self, sources, targets, scratch):
        self.sources, self.targets, self.scratch = sources, targets, scratch

    def get(self, what, i):
        return self.scratch[f"{self.name}{what}{i}"]

    def pairs(self, kind, i):
        s, r = place(self.groups)
        here = lax.axis_index("dp")
        b, g, size = self.streams, self.groups, self.size
        x, y = lax.rem(here, 2), here // 2
        beside_x, beside_y = {"dp": 2 * y + 1 - x}, {"dp": 2 * (1 - y) + x}
        if kind == "a":
            for d, peer in enumerate(core_peers(g), 1):
                yield d, self.sources[i].at[lax.rem(r + d, g)], self.get("core", i).at[d - 1], peer
        elif kind == "b":
            half, box = self.get("half", i), self.get("dp", i)
            for d, peer in enumerate(dp_peers(), 1):
                yield d, half.at[lax.rem(here + d, size)], box.at[d - 1], peer
        elif kind == "b1":
            half, box, h = self.get("half", i), self.get("first", i), self.shapes[i][0] // 2
            for n in range(2):
                yield n, half.at[2 * n + 1 - x, pl.ds(0, h)], box.at[n], beside_x
                yield 2 + n, half.at[2 * (1 - y) + n, pl.ds(h, h)], box.at[2 + n], beside_y
        elif kind == "b2":
            half, box, h = self.get("half", i), self.get("second", i), self.shapes[i][0] // 2
            yield 0, half.at[2 * (1 - y) + x, pl.ds(0, h)], box.at[0], beside_y
            yield 1, half.at[2 * y + 1 - x, pl.ds(h, h)], box.at[1], beside_x
        elif kind in "cd":
            peers = list(enumerate(stream_peers(b, g), 1))
            for d, peer in [peers[1], peers[0], peers[2]] if b == 4 else peers:
                if kind == "c":
                    cut = self.get("cut", i)
                    yield d, cut.at[lax.rem(s + d, b)], self.get("z", i).at[d - 1], peer
                else:
                    yield d, self.get("fin", i), self.targets[i].at[r, here, s], peer
        elif kind == "e":
            whole = self.targets[i].at[r, here]
            for d, peer in enumerate(dp_peers(), 1):
                yield d, whole, whole, peer
        elif kind == "e1":
            for n, peer in enumerate((beside_y, beside_x)):
                part = self.targets[i].at[r, here, pl.ds(n * b // 2, b // 2)]
                yield n, part, part, peer
        elif kind == "e2":
            for n in range(2):
                part = self.targets[i].at[r, 2 * n + x, pl.ds(0, b // 2)]
                yield n, part, part, beside_x
                part = self.targets[i].at[r, 2 * y + n, pl.ds(b // 2, b // 2)]
                yield 2 + n, part, part, beside_y
        else:
            whole = self.targets[i].at[r]
            for d, peer in enumerate(core_peers(g), 1):
                yield d, whole, whole, peer

    def copies(self, kind, i):
        send, recv = self.get(kind + "s", i), self.get(kind + "r", i)
        for n, source, target, peer in self.pairs(kind, i):
            yield remote(source, target, send.at[n], recv.at[n], peer)

    def start(self, kind, i):
        for copy in self.copies(kind, i):
            copy.start()

    def arrive(self, kind, i):
        for copy in self.copies(kind, i):
            copy.wait_recv()

    def load(self, i):
        s, r = place(self.groups)
        return pltpu.make_async_copy(
            self.sources[i].at[r], self.get("half", i), self.get("local", i).at[0]
        )

    def keep(self, i):
        s, r = place(self.groups)
        return pltpu.make_async_copy(
            self.get("fin", i),
            self.targets[i].at[r, lax.axis_index("dp"), s],
            self.get("local", i).at[1],
        )

    def stages(self):
        middle = [self.dp_middle] if self.two_step else []
        back = [self.dp_back_middle] if self.two_step else []
        return [self.dp_start, *middle, self.z_start, self.z_back, self.dp_back, *back, self.core_back]

    def core_start(self):
        for i in range(self.count):
            self.start("a", i)
            self.load(i).start()

    def dp_start(self):
        for i in range(self.count):
            if self.over_cores:
                self.load(i).wait()
                self.arrive("a", i)
                half, box, wire = self.get("half", i), self.get("core", i), self.wires[i]
                for p in range(self.size):
                    total = half[p].astype(F32)
                    for j in range(self.groups - 1):
                        total = total + box[j, p].astype(F32)
                    half[p] = total.astype(wire)
            self.start("b1" if self.two_step else "b", i)

    def dp_middle(self):
        here = lax.axis_index("dp")
        x, y = lax.rem(here, 2), here // 2
        for i in range(self.count):
            self.arrive("b1", i)
            half, box, wire = self.get("half", i), self.get("first", i), self.wires[i]
            h = self.shapes[i][0] // 2
            for n in range(2):
                for who, at, part in ((2 * n + x, pl.ds(0, h), n), (2 * y + n, pl.ds(h, h), 2 + n)):
                    total = half[who, at, :].astype(F32) + box[part].astype(F32)
                    half[who, at, :] = total.astype(wire)
            self.start("b2", i)

    def z_start(self):
        here = lax.axis_index("dp")
        for i in range(self.count):
            self.arrive("b2" if self.two_step else "b", i)
            half, cut, wire = self.get("half", i), self.get("cut", i), self.wires[i]
            chunk = self.shapes[i][0]
            slim = chunk // self.streams
            for z in range(self.streams):
                at = slice(z * slim, (z + 1) * slim)
                total = half[here, at, :].astype(F32)
                if self.two_step:
                    which, first = divmod(z * slim, chunk // 2)
                    total = total + self.get("second", i)[which, first : first + slim].astype(F32)
                else:
                    for d in range(self.size - 1):
                        total = total + self.get("dp", i)[d, at, :].astype(F32)
                cut[z] = total.astype(wire)
            self.start("c", i)

    def z_back(self):
        s, r = place(self.groups)
        for i in range(self.count):
            self.arrive("c", i)
            box = self.get("z", i)
            total = self.get("cut", i)[s].astype(F32)
            for d in range(self.streams - 1):
                total = total + box[d].astype(F32)
            self.get("fin", i)[...] = total.astype(self.wires[i])
            self.keep(i).start()
            self.start("d", i)

    def dp_back(self):
        for i in range(self.count):
            self.keep(i).wait()
            self.arrive("d", i)
            self.start("e1" if self.two_step else "e", i)

    def dp_back_middle(self):
        for i in range(self.count):
            self.arrive("e1", i)
            self.start("e2", i)

    def core_back(self):
        for i in range(self.count):
            self.arrive("e2" if self.two_step else "e", i)
            self.start("f", i)

    def end(self):
        for i in range(self.count):
            self.arrive("f", i)
            for kind in self.kinds():
                for copy in self.copies(kind, i):
                    copy.wait_send()


class Moves:
    def __init__(self, *jobs, others=()):
        self.jobs, self.others = list(jobs), list(others)
        self.counts = [len(job.scratch()) for job in jobs]

    def scratch(self):
        return [item for job in self.jobs for item in job.scratch()]

    def out_shapes(self):
        return [job.out_shape() for job in self.jobs]

    def spaces(self):
        return [pl.BlockSpec(memory_space=pl.ANY)] * len(self.jobs)

    def each(self, sources, targets, scratch):
        at = 0
        for job, count, source, target in zip(self.jobs, self.counts, sources, targets):
            yield job, (source, target, *scratch[at : at + count])
            at += count

    def first(self, sources, targets, scratch, count=None, meet=True):
        if meet:
            greet(unique(self.jobs + self.others))
        for job, refs in list(self.each(sources, targets, scratch))[:count]:
            job.first(*refs)

    def start_last(self, sources, targets, scratch):
        for job, refs in list(self.each(sources, targets, scratch))[-1:]:
            job.first(*refs)

    def middle(self, sources, targets, scratch):
        for job, refs in self.each(sources, targets, scratch):
            if isinstance(job, Gather):
                job.middle(*refs)

    def last(self, sources, targets, scratch):
        for job, refs in self.each(sources, targets, scratch):
            job.last(*refs)


def remote_params(collective_id):
    return pltpu.CompilerParams(
        collective_id=collective_id, has_side_effects=True, vmem_limit_bytes=VMEM_BYTES
    )


def binary_columns(latent):
    matrix = latent.astype(F32)
    scale = jnp.sqrt(jnp.mean(matrix * matrix, axis=0, keepdims=True) + 1e-06)
    return (scale * jnp.tanh(matrix * (2.0 / scale))).astype(BF)


class Intake:
    def __init__(self, bag, moves, groups, latents, ids, seq):
        three, depth, unused = latents[0].shape
        own = (three, depth, depth // groups)
        self.moves, self.groups = moves, groups
        self.shapes = [(1,) + own] + [a.shape for a in latents[1:]]
        self.blocks = [job.out_shape() for job in moves.jobs]
        for i, shape in enumerate(self.shapes):
            bag.add(f"loaded{i}", pltpu.VMEM(own if i == 0 else shape, BF))
            bag.add(f"made{i}", pltpu.VMEM(shape, BF))
        bag.add("weight_sems", dma(4))
        bag.add("made_sems", dma(4))
        bag.add("in_sems", dma(3))
        bag.add("ids_in", pltpu.VMEM(ids.shape, ids.dtype))
        bag.add("ids_box", pltpu.VMEM((ids.shape[0], 8, ids.shape[1]), F32))
        bag.add("x_all", pltpu.VMEM(self.blocks[0].shape, BF))
        bag.add("docs", pltpu.VMEM(self.blocks[-1].shape, F32))
        for i, item in enumerate(moves.scratch()):
            bag.add(f"early{i}", item)

    def run(self, have, latents, ids_ref, sources, results, targets, begin):
        moves = self.moves
        scratch = [have[f"early{i}"] for i in range(len(moves.scratch()))]
        loaded = [have[f"loaded{i}"] for i in range(4)]
        made = [have[f"made{i}"] for i in range(4)]
        sources = (*sources, have["ids_box"])
        moves.first(sources, targets, scratch, len(sources) - 1, False)
        s, r = place(self.groups)
        width = results[0].shape[3]
        own = pl.ds(pl.multiple_of(r * width, 128), width)
        places = [latents[0].at[:, :, own], *latents[1:]]
        loads = [
            pltpu.make_async_copy(places[i], loaded[i], have["weight_sems"].at[i])
            for i in range(4)
        ]
        stores = [
            pltpu.make_async_copy(made[i], results[i], have["made_sems"].at[i]) for i in range(4)
        ]
        fetch = pltpu.make_async_copy(ids_ref, have["ids_in"], have["in_sems"].at[0])
        fetch.start()
        for copy in loads:
            copy.start()
        fetch.wait()
        ids = have["ids_in"][...].astype(F32)
        for i in range(ids.shape[0]):
            have["ids_box"][i] = jnp.broadcast_to(ids[i : i + 1, :], have["ids_box"].shape[1:])
        moves.start_last(sources, targets, scratch)
        loads[0].wait()
        for i in range(3):
            made[0][0, i] = binary_columns(loaded[0][i])
        stores[0].start()
        for n in range(1, 4):
            loads[n].wait()
            for i in range(0, loaded[n].shape[1], 128):
                made[n][:, i : i + 128] = binary_columns(loaded[n][:, i : i + 128])
            stores[n].start()
        moves.middle(sources, targets, scratch)
        for copy in stores:
            copy.wait()
        moves.last(sources, targets, scratch)
        begin()
        inward = [
            pltpu.make_async_copy(targets[0], have["x_all"], have["in_sems"].at[1]),
            pltpu.make_async_copy(targets[-1], have["docs"], have["in_sems"].at[2]),
        ]
        for copy in inward:
            copy.start()
        for copy in inward:
            copy.wait()


def lanes_of(shape):
    return lax.broadcasted_iota(jnp.int32, shape, 1)


def forward_kernel(intake, moves, streams, groups, tile, bag, tiles, *refs):
    keep = intake is not None
    refs = list(refs)

    def take(n):
        return [refs.pop(0) for unused in range(n)]

    count = len(moves.jobs)
    if keep:
        (bias_ref,), latents, (ids_ref,) = take(1), take(4), take(1)
        early_sources = take(len(intake.moves.jobs) - 1)
    else:
        x_ref, w_ref, bias_ref, docs_ref = take(4)
    sources = take(count)
    q_ref, k_ref, rows_ref = take(3)
    if keep:
        v_ref, e_ref, ctx_ref, inv_ref, active_ref = take(5)
        results, early_targets = take(4), take(len(intake.moves.jobs))
    targets = take(count)
    have = bag.bind(refs)
    if keep:
        w_ref, docs_ref = have["made0"], have["docs"]
    scratch = tuple(have[f"moves{i}"] for i in range(len(moves.scratch())))
    k_aug, v_aug, ctx_all, mask, edges = (
        have["k_aug"],
        have["v_aug"],
        have["ctx_all"],
        have["mask"],
        have["edges"],
    )
    active = active_ref if keep else x_ref
    row_ref = have["row"]
    pair, step = pl.program_id(0), pl.program_id(1)
    pairs, steps = pl.num_programs(0), pl.num_programs(1)
    seq = k_ref.shape[0]
    s, r = place(groups)
    sub = min(256, tile)
    width = w_ref.shape[3]
    n_pairs = ctx_all.shape[0]
    offset = pair * 128 if width == n_pairs * 128 else (r * n_pairs + pair) * 128
    offset = pl.multiple_of(offset, 128)
    home = pl.multiple_of((r * n_pairs + pair) * 128, 128)

    @pl.when((pair == 0) & (step == 0))
    def _():
        if keep:
            greet(unique(intake.moves.jobs + moves.jobs + moves.others))

            def begin():
                moves.first(sources, targets, scratch, None, False)

            intake.run(have, latents, ids_ref, early_sources, results, early_targets, begin)
        else:
            moves.first(sources, targets, scratch)
        ids = stream_row(docs_ref)
        row_ref[...] = ids
        big_at = long_at(streams, groups, seq)
        big = ids[:, big_at : big_at + 1]
        mask[...] = jnp.where(ids == big, 0.0, masked_score)
        edges[0] = jnp.broadcast_to(ids[:, :sub], (128, sub)).T
        edges[1] = jnp.broadcast_to(ids[:, seq - sub :], (128, sub)).T
        if keep:
            x_all = have["x_all"]
            shard = x_all.shape[1]
            for i in range(x_all.shape[0]):
                piece = squash(x_all[i].astype(F32)).astype(BF)
                active_ref[i * shard : (i + 1) * shard, :] = piece

    @pl.when((pair == pairs - 1) & (step == steps - 2))
    def _():
        moves.middle(sources, targets, scratch)

    @pl.when(step == 0)
    def _():
        columns = pl.ds(offset, 128)

        def project(i, bias):
            matrix = jnp.concatenate(
                [w_ref[d, i, :, columns] for d in range(w_ref.shape[0])], axis=0
            )
            result = dot(active[...], matrix)
            if bias is not None:
                result = result + bias_ref[bias : bias + 1, pl.ds(home, 128)]
            return result.astype(BF)

        low = lanes_of((seq, 128)) < 64
        lane = lanes_of((seq, 128))
        q_ref[...] = (project(0, 0).astype(F32) * 0.125).astype(BF)
        keys = project(1, None)
        k_ref[...] = keys
        keys = keys.astype(F32)
        turned = pltpu.roll(keys, 64, 1)
        k_aug[0] = jnp.where(low, keys, turned).astype(BF)
        k_aug[1] = jnp.where(low, turned, keys).astype(BF)
        values = project(2, 1)
        if keep:
            v_ref[...] = values
        values = values.astype(F32)
        v_aug[0] = jnp.where(low, values, jnp.where(lane < 66, 1.0, 0.0)).astype(BF)
        v_aug[1] = jnp.where(low, jnp.where(lane < 2, 1.0, 0.0), values).astype(BF)

    turned = own_rows_last(step, seq, tile, groups)
    start = pl.multiple_of(turned * tile, tile)

    def body(edge_at):
        low = lanes_of((sub, 128)) < 64
        parts = []
        for at in range(0, tile, sub):
            scaled = q_ref[pl.ds(start + at, sub), :].astype(F32) * LOG2E
            upper = scaled.astype(BF).astype(F32)
            lower = scaled - upper
            parts.append(
                (
                    jnp.where(low, upper, pltpu.roll(lower, 64, 1)).astype(BF),
                    jnp.where(low, pltpu.roll(upper, 64, 1), lower).astype(BF),
                )
            )
        chains = [(at, h) for at in range(0, tile, sub) for h in range(2)]

        def scores_of(at, h):
            scores = dot(parts[at // sub][h], k_aug[h], NT)
            if edge_at is not None and at == (0 if edge_at == 0 else tile - sub):
                return jnp.where(edges[edge_at][:, :1] == row_ref[...], scores, masked_score)
            return jnp.concatenate(
                [
                    scores[:, :sub] + mask[:, :sub],
                    scores[:, sub : seq - sub],
                    scores[:, seq - sub :] + mask[:, seq - sub :],
                ],
                axis=1,
            )

        scores = scores_of(*chains[0])
        results = {}
        for n, (at, h) in enumerate(chains):
            if n + 1 < len(chains):
                later = scores_of(*chains[n + 1])
            peak = jnp.max(scores, axis=1, keepdims=True)
            numerators = jnp.exp2(scores - peak).astype(BF)
            if keep:
                e_ref[h, at : at + sub, :] = numerators
            total = dot(numerators, v_aug[h])
            where_sum = 64 if h == 0 else 0
            inverse = 1.0 / total[:, where_sum : where_sum + 1]
            results[h] = (total * inverse, inverse)
            if n + 1 < len(chains):
                scores = later
            if h == 1:
                done = jnp.where(low, results[0][0], results[1][0]).astype(BF)
                ctx_all[pair, pl.ds(start + at, sub), :] = done
                if keep:
                    ctx_ref[at : at + sub, :] = done
                    inv_ref[at : at + sub, :] = jnp.where(low, results[0][1], results[1][1])

    @pl.when(turned == 0)
    def _():
        body(0)

    @pl.when(turned == steps - 1)
    def _():
        body(1)

    @pl.when((turned > 0) & (turned < steps - 1))
    def _():
        body(None)

    owned = seq // groups
    owner = start // owned
    at = lax.rem(turned, owned // tile)
    source = ctx_all.at[pair, pl.ds(start, tile)]
    target = rows_ref.at[r, pair, pl.ds(pl.multiple_of(lax.rem(start, owned), tile), tile)]

    @pl.when(owner == r)
    def _():
        tiles.own(have, source, target, pair, at).start()

    @pl.when(owner != r)
    def _():
        tiles.copy(have, source, target, owner, pair, at).start()

    @pl.when((pair == pairs - 1) & (step == steps - 1))
    def _():
        tiles.finish(have, source, target)
        moves.last(sources, targets, scratch)


def own_rows_last(step, seq, tile, groups):
    s, r = place(groups)
    steps = seq // tile
    return lax.rem(step + (r + 1) * (steps // groups), steps)


def stream_row(docs_ref):
    return jnp.concatenate([docs_ref[i, 0:1, :] for i in range(docs_ref.shape[0])], axis=1)


def long_at(streams, groups, seq):
    shard = seq // (streams * groups)
    return streams * shard if groups > 1 else shard


def attention(operands, seq, streams, groups, early, moves, moved, collective_id, name):
    keep = early is not None
    depth = operands[0].shape[-1]
    width = depth // groups
    pairs = width // 128
    tile = 512
    owned = seq // groups
    bag = Bag()
    bag.add("k_aug", pltpu.VMEM((2, seq, 128), BF))
    bag.add("v_aug", pltpu.VMEM((2, seq, 128), BF))
    bag.add("ctx_all", pltpu.VMEM((pairs, seq, 128), BF))
    bag.add("mask", pltpu.VMEM((1, seq), F32))
    bag.add("row", pltpu.VMEM((1, seq), F32))
    bag.add("edges", pltpu.VMEM((2, 256, 128), F32))
    tiles = Tiles(bag, "tiles", groups, pairs, owned // tile)
    for i, item in enumerate(moves.scratch()):
        bag.add(f"moves{i}", item)
    intake = Intake(bag, early, groups, operands[1:5], operands[5], seq) if keep else None

    def constant(shape):
        return pl.BlockSpec(shape, lambda p, i: (0,) * len(shape))

    def turn(i):
        return own_rows_last(i, seq, tile, groups)

    part = pl.BlockSpec((tile, 128), lambda p, i: (turn(i), p))
    whole = pl.BlockSpec((seq, 128), lambda p, i: (0, p))
    any_space = pl.BlockSpec(memory_space=pl.ANY)
    wide = jax.ShapeDtypeStruct((seq, width), BF)
    outs = [whole, whole, any_space]
    shapes = [wide, wide, jax.ShapeDtypeStruct((groups, pairs, owned, 128), BF)]
    ins = [constant(a.shape) for a in operands]
    if keep:
        ins = ins[:1] + [any_space] * (len(operands) - 1)
        outs += [
            whole,
            pl.BlockSpec((2, tile, seq), lambda p, i: (p, turn(i), 0)),
            part,
            part,
            constant((seq, depth)),
        ]
        outs += [any_space] * (4 + len(early.jobs))
        shapes += [
            wide,
            jax.ShapeDtypeStruct((2 * pairs, seq, seq), BF),
            wide,
            jax.ShapeDtypeStruct((seq, width), F32),
            jax.ShapeDtypeStruct((seq, depth), BF),
        ]
        shapes += [jax.ShapeDtypeStruct(shape, BF) for shape in intake.shapes] + intake.blocks
    return pl.pallas_call(
        functools.partial(forward_kernel, intake, moves, streams, groups, tile, bag, tiles),
        grid=(pairs, seq // tile),
        in_specs=ins + moves.spaces(),
        out_specs=outs + moves.spaces(),
        out_shape=shapes + moves.out_shapes(),
        scratch_shapes=list(bag.items.values()),
        compiler_params=remote_params(collective_id),
        name=name,
    )(*operands, *moved)


def split(matrix):
    upper = matrix.astype(BF)
    return upper, (matrix - upper.astype(F32)).astype(BF)


def backward_kernel(
    streams,
    groups,
    tile,
    bag,
    early,
    late,
    e_ref,
    q_ref,
    k_ref,
    v_ref,
    tq_ref,
    tk_ref,
    dc_ref,
    ctx_ref,
    inv_ref,
    docs_ref,
    small_ref,
    active_hbm,
    bin_hbm,
    d1_hbm,
    tokens_hbm,
    *rest,
):
    n_early = sum(job.count for job in early)
    sources, rest = rest[:n_early], rest[n_early:]
    grad_ref, *rest = rest
    early_out, rest = rest[:n_early], rest[n_early:]
    late_out, (gain_ref, bias_ref, shift_ref, *rest) = rest[: len(late)], rest[len(late) :]
    have = bag.bind(rest)
    at = 0
    for job in early:
        job.bind(sources[at : at + job.count], early_out[at : at + job.count], have)
        at += job.count
    for job, target in zip(late, late_out):
        job.bind(None, [target], have)

    pair, step = pl.program_id(0), pl.program_id(1)
    pairs, steps = len(late), q_ref.shape[0] // tile
    sub = min(256, tile)
    seq = k_ref.shape[0]
    share = 1.0 / seq
    time = pair * steps + step
    total_time = pairs * steps
    size = lax.axis_size("dp")
    here = lax.axis_index("dp")
    s, r = place(groups)
    rows, depth = d1_hbm.shape
    width = pairs * 128
    v_aug, dk_acc, dv_acc, grams = have["v_aug"], have["dk_acc"], have["dv_acc"], have["grams"]
    dq_all, d_act, active, weights = have["dq_all"], have["d_act"], have["active"], have["weights"]
    d_one, x_rows = have["d_one"], have["x_rows"]
    edges, in_big, pair_box = have["edges"], have["in_big"], have["pair_box"]
    row_ref = have["row"]
    along_z, cores, along_dp = stream_peers(streams, groups), core_peers(groups), dp_peers()

    def loads():
        sems = have["load"]
        return [
            pltpu.make_async_copy(active_hbm, active, sems.at[0]),
            pltpu.make_async_copy(bin_hbm, weights, sems.at[1]),
            pltpu.make_async_copy(d1_hbm, d_one, sems.at[2]),
            pltpu.make_async_copy(tokens_hbm.at[pl.ds(r * streams, streams)], x_rows, sems.at[3]),
        ]

    halves = tile // sub
    plan = []

    def at_time(when, work):
        plan.append((when, work))

    def due(half):
        for when, work in plan:
            if when % halves == half:
                pl.when(time == when // halves)(work)

    def begin():
        greet(along_z + cores + along_dp)
        for job in early:
            job.core_start()
        for copy in loads():
            copy.start()
        ids = stream_row(docs_ref)
        row_ref[...] = ids
        big_at = long_at(streams, groups, seq)
        big = ids[:, big_at : big_at + 1]
        for n, first in enumerate((0, seq - sub)):
            column = jnp.broadcast_to(ids[:, first : first + sub], (128, sub)).T
            edges[n] = column
            in_big[n] = jnp.where(column == big, 1.0, 0.0)

    def big_rows(ref):
        return jnp.concatenate(
            [
                (ref[:sub, :].astype(F32) * in_big[0]).astype(BF),
                ref[sub : seq - sub, :],
                (ref[seq - sub :, :].astype(F32) * in_big[1]).astype(BF),
            ],
            axis=0,
        )

    at_time(0, begin)
    unit = total_time * halves / 16
    left = []
    for n, job in enumerate(early):
        stages, times = job.stages(), EARLY_TIMES[n]
        if not job.two_step:
            times = times[:1] + times[2:5] + times[6:]
        for when, work in zip(times, stages):
            at_time(int(when * unit), work)
        left.append(stages[len(times) :])
    for p, job in enumerate(late[:-1]):
        first = (p + 1) * steps * halves
        for when, work in zip(LATE_TIMES, job.stages()):
            at_time(first + when, work)
        left.append(job.stages()[len(LATE_TIMES) :])

    def go_on(count):
        for unused in range(count):
            for queue in left:
                if queue:
                    queue.pop(0)()

    due(0)

    @pl.when(step == 0)
    def _():
        lane = lanes_of((seq, 128))
        low = lane < 64
        values = v_ref[...].astype(F32)
        v_aug[0] = jnp.where(low, values, jnp.where(lane < 66, 1.0, 0.0)).astype(BF)
        v_aug[1] = jnp.where(low, jnp.where(lane < 2, 1.0, 0.0), values).astype(BF)
        dk_acc[...] = jnp.zeros_like(dk_acc)
        dv_acc[...] = jnp.zeros_like(dv_acc)
        kb, tkb, qb, tqb = (big_rows(ref) for ref in (k_ref, tk_ref, q_ref, tq_ref))
        same_head = (lax.broadcasted_iota(jnp.int32, (128, 128), 0) < 64) == (
            lanes_of((128, 128)) < 64
        )
        for i, (a, b) in enumerate(((kb, kb), (tkb, kb), (qb, qb), (tqb, qb))):
            gram = jnp.where(same_head, dot(a, b, TN) * share, 0.0)
            grams[2 * i], grams[2 * i + 1] = split(gram)

    start = pl.multiple_of(step * tile, tile)
    low = lanes_of((sub, 128)) < 64
    lane = lanes_of((sub, 128))

    def prepare(at):
        here_rows = pl.ds(start + at, sub)
        q8, tq8 = q_ref[here_rows, :], tq_ref[here_rows, :]
        scaled = dc_ref[at : at + sub, :].astype(F32) * inv_ref[at : at + sub, :]
        product = scaled * ctx_ref[at : at + sub, :].astype(F32)
        augmented = []
        for h in range(2):
            mine = low if h == 0 else jnp.logical_not(low)
            delta = -jnp.sum(jnp.where(mine, product, 0.0), axis=1, keepdims=True)
            upper = delta.astype(BF).astype(F32)
            first = 64 if h == 0 else 0
            extra = jnp.where(
                lane == first, upper, jnp.where(lane == first + 1, delta - upper, 0.0)
            )
            augmented.append(jnp.where(mine, scaled, extra).astype(BF))
        q_turned = q8.astype(F32).T.astype(BF)
        dc_turned = scaled.T.astype(BF)
        return here_rows, q8, tq8, augmented, q_turned, dc_turned

    def body(edge, half):
        ready = {half * sub: prepare(half * sub)}
        chains = [(half * sub, h) for h in range(2)]
        edge_at = {None: None, 0: 0, 1: tile - sub}[edge]
        columns = slice(0, sub) if edge == 0 else slice(seq - sub, seq)

        def d_probs_of(at, h):
            return dot(ready[at][3][h], v_aug[h], NT)

        d_probs = d_probs_of(*chains[0])
        d_queries = {}
        for n, (at, h) in enumerate(chains):
            if n + 1 < len(chains):
                later = d_probs_of(*chains[n + 1])
            here_rows, q8, tq8, unused, q_turned, dc_turned = ready[at]
            mine = low if h == 0 else jnp.logical_not(low)
            numerators = e_ref[h, at : at + sub, :]
            d_scores = numerators.astype(F32) * d_probs
            if edge is not None and at == edge_at:
                q_mine = jnp.where(mine, q8, 0.0).astype(BF)
                tq_mine = jnp.where(mine, tq8, 0.0).astype(BF)
                gap = dot(q_mine, k_ref[columns, :], NT) - dot(tq_mine, tk_ref[columns, :], NT)
                same = jnp.where(edges[edge][:, :1] == row_ref[:, columns], share, 0.0)
                gap = gap * (same * (1.0 - in_big[edge][:, :1]))
                if edge == 0:
                    d_scores = jnp.concatenate(
                        [d_scores[:, :sub] + gap, d_scores[:, sub:]], axis=1
                    )
                else:
                    d_scores = jnp.concatenate(
                        [d_scores[:, : seq - sub], d_scores[:, seq - sub :] + gap], axis=1
                    )
            d_scores = d_scores.astype(BF)
            mine = slice(64 * h, 64 * h + 64)
            dv_acc[mine, :] += dot(dc_turned[mine, :], numerators)
            d_queries[h] = dot(d_scores, k_ref[...])
            dk_acc[mine, :] += dot(q_turned[mine, :], d_scores)
            if h == 1:
                d_query = jnp.where(low, d_queries[0], d_queries[1])
                qb, tqb = q8, tq8
                if edge is not None and at == edge_at:
                    qb = (q8.astype(F32) * in_big[edge]).astype(BF)
                    tqb = (tq8.astype(F32) * in_big[edge]).astype(BF)
                d_query += dot(qb, grams[0]) + dot(qb, grams[1])
                d_query -= dot(tqb, grams[2]) + dot(tqb, grams[3])
                dq_all[here_rows, :] = (d_query * 0.125).astype(BF)
            if n + 1 < len(chains):
                d_probs = later

    for half in range(halves):
        if half:
            due(half)
        edge, at_edge = None, None
        if half == 0:
            edge, at_edge = 0, step == 0
        elif half == halves - 1:
            edge, at_edge = 1, step == steps - 1
        if edge is not None:
            pl.when(at_edge)(functools.partial(body, edge, half))
            pl.when(jnp.logical_not(at_edge))(functools.partial(body, None, half))
        else:
            body(None, half)

    def pair_end(p):
        job = late[p]
        kb, tkb = big_rows(k_ref), big_rows(tk_ref)
        d_key = dk_acc[...].T
        d_key += dot(kb, grams[4]) + dot(kb, grams[5]) - dot(tkb, grams[6]) - dot(tkb, grams[7])
        d_value = dv_acc[...].T.astype(BF)
        d_query = dq_all[...]
        d_pair = jnp.concatenate([d_query, d_key.astype(BF), d_value], axis=1)
        if p == 0:
            for copy in loads():
                copy.wait()
        columns = slice(p * 128, (p + 1) * 128)
        bins = jnp.concatenate([weights[0, i, :, columns] for i in range(3)], axis=1)
        chunk = depth // size
        half = job.get("half", 0)
        partial = dot(active[...], d_pair, TN).astype(job.wires[0])
        for d in range(size):
            half[d] = partial[d * chunk : (d + 1) * chunk, :]
        if p == pairs - 1:
            job.dp_start()
        if p < pairs - 1:
            if p == 0:
                d_act[...] = dot(d_pair, bins, NT)
            else:
                d_act[...] += dot(d_pair, bins, NT)
        else:
            pair_box[...] = d_pair
            for j in range(1, groups + 1):
                at = pl.ds(pl.multiple_of(lax.rem(r + j, groups) * rows, rows), rows)
                total = dot(pair_box[at, :], bins, NT)
                if p > 0:
                    total = total + d_act[at, :]
                if j < groups:
                    have["outbox"][j - 1] = total.astype(BF)
                    core_copies()[j - 1].start()
                else:
                    d_act[at, :] = total
        sums = have["sums"]
        sums[0:1, columns] = jnp.sum(d_query.astype(F32), axis=0, keepdims=True)
        sums[1:2, columns] = jnp.sum(d_value.astype(F32), axis=0, keepdims=True)

    def core_copies():
        return [
            remote(
                have["outbox"].at[j - 1],
                have["inbox"].at[j - 1],
                have["core_s"].at[j],
                have["core_r"].at[j],
                cores[j - 1],
            )
            for j in range(1, groups)
        ]

    def small_copies(stage, peers, base):
        return [
            remote(
                have["small"].at[stage],
                have["small_box"].at[base + d],
                have["small_s"].at[base + d],
                have["small_r"].at[base + d],
                peer,
            )
            for d, peer in enumerate(peers)
        ]

    def small_start(stage, peers, base):
        for copy in small_copies(stage, peers, base):
            copy.start()

    def small_sum(stage, peers, base):
        for copy in small_copies(stage, peers, base):
            copy.wait_recv()
        total = have["small"][stage]
        for d in range(len(peers)):
            total = total + have["small_box"][base + d]
        return total

    for p in range(pairs - 1):

        @pl.when((pair == p) & (step == steps - 1))
        def _():
            pair_end(p)

    @pl.when(time == total_time - 1)
    def _():
        pair_end(pairs - 1)
        last = late[-1]
        small = have["small"]
        small[0] = small_ref[...]
        for i in range(2):
            vector = have["sums"][i : i + 1, :]
            small[0, 2 + i : 3 + i, :] = jnp.concatenate(
                [jnp.where(r == j, vector, 0.0) for j in range(groups)], axis=1
            )
        small_start(0, along_dp, 0)
        go_on(TAIL[0])
        last.z_start()
        last.z_back()
        for copy in core_copies():
            copy.wait_recv()
        shard = rows // streams
        back_copies = []
        blocks = have["blocks"]
        order = [2, 1, 3] if streams == 4 else list(range(1, streams))
        for d in order + [0]:
            target = lax.rem(s + d, streams)
            here_rows = pl.ds(pl.multiple_of(target * shard, shard), shard)
            bent = jnp.tanh(x_rows[target].astype(F32) * (1.0 / clip_level))
            total = d_act[pl.ds(pl.multiple_of(r * rows + target * shard, shard), shard), :]
            for j in range(groups - 1):
                total = total + have["inbox"][j, here_rows, :].astype(F32)
            blocks[target] = (d_one[here_rows, :] + total * (1.0 - bent * bent)).astype(BF)
            if d:
                copy = remote(
                    blocks.at[target],
                    grad_ref.at[s],
                    have["grad_s"].at[d],
                    have["grad_r"].at[d],
                    along_z[d - 1],
                )
            else:
                copy = pltpu.make_async_copy(blocks.at[s], grad_ref.at[s], have["grad_s"].at[0])
            copy.start()
            back_copies.append(copy)
        small[1] = small_sum(0, along_dp, 0)
        small_start(1, along_z, size)
        go_on(TAIL[1])
        small[2] = small_sum(1, along_z, size)
        small_start(2, cores, size + streams)
        go_on(TAIL[2])
        last.dp_back()
        summed = small_sum(2, cores, size + streams)
        gain_ref[...] = summed[0:2, :]
        bias_ref[...] = summed[2:8, :]
        for i in range(shift_ref.shape[1] // depth):
            shift_ref[:, i * depth : (i + 1) * depth] = summed[8 + i : 9 + i, :]
        go_on(TAIL[3])
        last.core_back()
        go_on(8)
        for copy in back_copies:
            copy.wait()
        for job in early + late:
            job.end()
        for copy in (
            core_copies()
            + small_copies(0, along_dp, 0)
            + small_copies(1, along_z, size)
            + small_copies(2, cores, size + streams)
        ):
            copy.wait_send()


TWO_STEP = False
TAIL = (1, 1, 0, 0)
EARLY_TIMES = ((2, 0, 7, 9, 12), (4, 0, 12, 14))
LATE_TIMES = (0, 5, 7)


def attention_back(
    streams,
    groups,
    numerators,
    queries,
    keys,
    values,
    teacher_queries,
    teacher_keys,
    d_context,
    context,
    inverse,
    docs,
    small,
    active,
    bin_own,
    d_one,
    tokens,
    early_arrays,
    up_width,
    collective_id,
):
    seq, width = queries.shape
    pairs = width // 128
    tile = 512
    rows, depth = d_one.shape
    size = lax.axis_size("dp")
    shard = rows // streams
    bag = Bag()
    bag.add("v_aug", pltpu.VMEM((2, seq, 128), BF))
    bag.add("dk_acc", pltpu.VMEM((128, seq), F32))
    bag.add("dv_acc", pltpu.VMEM((128, seq), F32))
    bag.add("grams", pltpu.VMEM((8, 128, 128), BF))
    bag.add("dq_all", pltpu.VMEM((seq, 128), BF))
    bag.add("d_act", pltpu.VMEM((seq, depth), F32))
    bag.add("active", pltpu.VMEM((seq, depth), BF))
    bag.add("weights", pltpu.VMEM((1, 3, depth, width), BF))
    bag.add("d_one", pltpu.VMEM((rows, depth), F32))
    bag.add("x_rows", pltpu.VMEM((streams, shard, depth), BF))
    bag.add("load", dma(4))
    bag.add("sums", pltpu.VMEM((8, width), F32))
    bag.add("outbox", pltpu.VMEM((groups - 1, rows, depth), BF))
    bag.add("inbox", pltpu.VMEM((groups - 1, rows, depth), BF))
    bag.add("core_s", dma(groups))
    bag.add("core_r", dma(groups))
    bag.add("blocks", pltpu.VMEM((streams, shard, depth), BF))
    bag.add("grad_s", dma(streams))
    bag.add("grad_r", dma(streams))
    count = size + streams + groups
    bag.add("small", pltpu.VMEM((3,) + small.shape, F32))
    bag.add("small_box", pltpu.VMEM((count,) + small.shape, F32))
    bag.add("small_s", dma(count))
    bag.add("small_r", dma(count))
    bag.add("row", pltpu.VMEM((1, seq), F32))
    bag.add("pair_box", pltpu.VMEM((seq, 3 * 128), BF))
    bag.add("edges", pltpu.VMEM((2, 256, 128), F32))
    bag.add("in_big", pltpu.VMEM((2, 256, 128), F32))
    early, flat = [], []
    for n, arrays in enumerate(early_arrays):
        job = Reduce(bag, f"early{n}", streams, groups, [a.shape for a in arrays], True, TWO_STEP)
        early.append(job)
        flat += [
            a.reshape(groups, size, chunk, cols) for a, (chunk, cols) in zip(arrays, job.shapes)
        ]
    late = [
        Reduce(bag, f"late{p}", streams, groups, [(depth, 3 * 128)], False, False)
        for p in range(pairs)
    ]
    part = pl.BlockSpec((tile, 128), lambda p, i: (i, p))
    any_space = pl.BlockSpec(memory_space=pl.ANY)

    whole = pl.BlockSpec((seq, 128), lambda p, i: (0, p))

    def constant(shape):
        return pl.BlockSpec(shape, lambda p, i: (0,) * len(shape))

    small_shapes = [(2, depth), (6, depth), (1, up_width)]
    early_shapes = [shape for job in early for shape in job.out_shapes()]
    late_shapes = [shape for job in late for shape in job.out_shapes()]
    results = pl.pallas_call(
        functools.partial(backward_kernel, streams, groups, tile, bag, early, late),
        grid=(pairs, seq // tile),
        in_specs=[
            pl.BlockSpec((2, tile, seq), lambda p, i: (p, i, 0)),
            whole,
            whole,
            whole,
            whole,
            whole,
            part,
            part,
            part,
            constant(docs.shape),
            constant(small.shape),
        ]
        + [any_space] * (4 + len(flat)),
        out_specs=[any_space] * (1 + len(early_shapes) + len(late_shapes))
        + [constant(shape) for shape in small_shapes],
        out_shape=[jax.ShapeDtypeStruct((streams, shard, depth), BF)]
        + early_shapes
        + late_shapes
        + [jax.ShapeDtypeStruct(shape, F32) for shape in small_shapes],
        scratch_shapes=list(bag.items.values()),
        compiler_params=remote_params(collective_id),
        name="attention_back",
    )(
        numerators,
        queries,
        keys,
        values,
        teacher_queries,
        teacher_keys,
        d_context,
        context,
        inverse,
        docs,
        small,
        active,
        bin_own,
        d_one,
        tokens,
        *flat,
    )
    grad_tokens, *rest = results
    early_sums = rest[: len(flat)]
    late_sums = rest[len(flat) : -3]
    shapes = [a.shape for arrays in early_arrays for a in arrays]
    return (
        grad_tokens,
        [e.reshape(shape) for e, shape in zip(early_sums, shapes)],
        [l.reshape(groups, depth, 3 * 128) for l in late_sums],
        list(rest[-3:]),
    )


def middle_kernel(
    streams,
    groups,
    bag,
    tiles,
    x_ref,
    tx_ref,
    cot_ref,
    ctx_ref,
    tctx_ref,
    bo_hbm,
    bup_hbm,
    bdown_hbm,
    to_hbm,
    tup_hbm,
    tdown_hbm,
    sg_ref,
    sb_ref,
    sub_ref,
    tg_ref,
    tb_ref,
    tub_ref,
    out_ref,
    d1_ref,
    dctx_ref,
    gout_ref,
    gup_ref,
    gdown_ref,
    small_ref,
    *rest,
):
    have = bag.bind(rest)
    gout_acc, gup_acc, gdown_acc = have["gout"], have["gup"], have["gdown"]
    out_box, d_box = have["out_box"], have["d_box"]
    step = pl.program_id(0)
    far = (to_hbm, bo_hbm, tup_hbm, bup_hbm, tdown_hbm, bdown_hbm)
    to_ref, bo_ref, tup_ref, bup_ref, tdown_ref, bdown_ref = near = [
        have[f"weight{i}"] for i in range(6)
    ]
    loads = [
        pltpu.make_async_copy(source, target, have["weight_sems"].at[i])
        for i, (source, target) in enumerate(zip(far, near))
    ]

    def ready(which):
        @pl.when(step == 0)
        def _():
            for i in which:
                loads[i].wait()

    steps = pl.num_programs(0)
    width = ctx_ref.shape[1] * 128
    tile, depth = cot_ref.shape
    n_steps = out_box.shape[0]
    shard = n_steps * tile // streams
    s, r = place(groups)
    along_z = stream_peers(streams, groups)
    turned = row_tile(step, n_steps, streams, groups)
    start = pl.multiple_of(turned * tile, tile)

    @pl.when(step == 0)
    def _():
        for copy in loads:
            copy.start()
        greet(along_z + core_peers(groups))

    @pl.when(step == 0)
    def _():
        for ref in (gout_acc, gup_acc, gdown_acc, small_ref):
            ref[...] = jnp.zeros_like(ref)

    def row(ref, i):
        return ref[i : i + 1, :]

    pieces = [(j, p) for j in range(groups) for p in range(ctx_ref.shape[1])]
    ff = bup_ref.shape[1]
    wide = min(512, ff)
    chunks = [slice(i, i + wide) for i in range(0, ff, wide)]

    ready((0, 1))
    tctx = jnp.concatenate([tctx_ref[j, p] for j, p in pieces], axis=1)
    t_att = dot(tctx, to_ref[...]) + row(tb_ref, 2)
    context = jnp.concatenate([ctx_ref[j, p] for j, p in pieces], axis=1).astype(F32)
    bent = jnp.tanh(context * (1.0 / clip_level))
    ctx_active = (clip_level * bent).astype(BF)
    ctx_slope = 1.0 - bent * bent
    attended = dot(ctx_active, bo_ref[...]) + row(sb_ref, 2)
    t_hidden = layer_norm(tx_ref[...].astype(F32) + t_att, row(tg_ref, 0), row(tb_ref, 3))[0]
    hidden, normed_one, inverse_one = layer_norm(
        x_ref[...].astype(F32) + attended, row(sg_ref, 0), row(sb_ref, 3)
    )
    bent = jnp.tanh(hidden * (1.0 / clip_level))
    hidden_active = (clip_level * bent).astype(BF)
    hidden_slope = 1.0 - bent * bent
    t_low = t_hidden.astype(BF)

    def up(i):
        return dot(t_low, tup_ref[:, chunks[i]]), dot(hidden_active, bup_ref[:, chunks[i]])

    ready((2, 3, 4, 5))
    ahead = up(0)
    t_branch, branch, actives, slopes = None, None, [], []
    for i, at in enumerate(chunks):
        t_pre, inner_pre = ahead
        if i + 1 < len(chunks):
            ahead = up(i + 1)
        t_inner = gelu_parts(t_pre + tub_ref[:, at])[0]
        inner_pre = inner_pre + sub_ref[:, at]
        inner_act, phi = gelu_parts(inner_pre)
        bent = jnp.tanh(inner_act * (1.0 / clip_level))
        inner_active = (clip_level * bent).astype(BF)
        t_term = dot(t_inner.astype(BF), tdown_ref[at, :])
        term = dot(inner_active, bdown_ref[at, :])
        t_branch = t_term if i == 0 else t_branch + t_term
        branch = term if i == 0 else branch + term
        actives.append(inner_active)
        slopes.append(
            (1.0 - bent * bent)
            * (phi + inner_pre * jnp.exp(-0.5 * inner_pre * inner_pre) * 0.3989422804014327)
        )
    t_out = layer_norm(t_hidden + t_branch + row(tb_ref, 4), row(tg_ref, 1), row(tb_ref, 5))[0]
    branch = branch + row(sb_ref, 4)
    output, normed_two, inverse_two = layer_norm(hidden + branch, row(sg_ref, 1), row(sb_ref, 5))
    out_box[step] = output.astype(BF)
    per_tile = tile // shard
    for n in range(per_tile):
        block = turned * per_tile + n
        source = out_box.at[step, pl.ds(n * shard, shard)]

        @pl.when(block == s)
        def _():
            pltpu.make_async_copy(source, out_ref.at[s], have["out_s"].at[s]).start()

        @pl.when(block != s)
        def _():
            remote(
                source,
                out_ref.at[s],
                have["out_s"].at[block],
                have["out_r"].at[s],
                {"blk": block * groups + r},
            ).start()
    upstream = cot_ref[...].astype(F32) + 0.5 * (output - t_out)
    d_two = norm_back(upstream, row(sg_ref, 1), normed_two, inverse_two)
    d_branch = d_two.astype(BF)

    def down(i):
        return dot(d_branch, bdown_ref[chunks[i], :], NT)

    ahead = down(0)
    through = None
    for i, at in enumerate(chunks):
        d_inner = ahead
        if i + 1 < len(chunks):
            ahead = down(i + 1)
        d_inner = (d_inner * slopes[i]).astype(BF)
        gdown_acc[at, :] += dot(actives[i], d_branch, TN)
        gup_acc[:, at] += dot(hidden_active, d_inner, TN)
        term = dot(d_inner, bup_ref[:, at], NT)
        through = term if i == 0 else through + term
        d_shift = jnp.sum(d_inner.astype(F32), axis=0, keepdims=True)
        for n in range(wide // depth):
            line = 8 + (i * wide) // depth + n
            small_ref[line : line + 1, :] += d_shift[:, n * depth : (n + 1) * depth]
    d_hidden = d_two + through * hidden_slope
    d_one = norm_back(d_hidden, row(sg_ref, 0), normed_one, inverse_one)
    d1_ref[...] = d_one
    d_attended = d_one.astype(BF)
    gout_acc[...] += dot(ctx_active, d_attended, TN)
    d_context = (dot(d_attended, bo_ref[...], NT) * ctx_slope).astype(BF)
    place_rows = pl.ds(pl.multiple_of(r * n_steps * tile + start, tile), tile)
    for j in range(groups):
        d_box[step, j] = d_context[:, j * width : (j + 1) * width]
        piece, target = d_box.at[step, j], dctx_ref.at[place_rows]

        @pl.when(r == j)
        def _():
            tiles.own(have, piece, target, 0, step).start()

        @pl.when(r != j)
        def _():
            tiles.copy(have, piece, target, j, 0, step).start()


    def total(value):
        return jnp.sum(value, axis=0, keepdims=True)

    sums = [
        (0, d_hidden * normed_one),
        (1, upstream * normed_two),
        (4, d_attended.astype(F32)),
        (5, d_hidden),
        (6, d_branch.astype(F32)),
        (7, upstream),
    ]
    for i, value in sums:
        small_ref[i : i + 1, :] += total(value)
    @pl.when(step == steps - 1)
    def _():
        tiles.finish(have, d_box.at[0, 0], dctx_ref.at[place_rows])
        source = out_box.at[0, pl.ds(0, shard)]
        pltpu.make_async_copy(source, out_ref.at[s], have["out_s"].at[s]).wait()
        for d, peer in enumerate(along_z, 1):
            block = lax.rem(s + d, streams)
            remote(
                source, out_ref.at[block], have["out_s"].at[block], have["out_r"].at[block], peer
            ).wait()
        gout_ref[...] = gout_acc[...].astype(BF)
        gup_ref[...] = gup_acc[...].astype(BF)
        gdown_ref[...] = gdown_acc[...].astype(BF)


def row_tile(step, steps, streams, groups):
    s, r = place(groups)
    return lax.rem(s // (streams // steps) + 1 + step, steps)


def middle(streams, groups, x, tx, cot, ctx, tctx, weights, teacher_weights, vectors, collective_id):
    rows, depth = cot.shape
    ff = weights[1].shape[1]
    tile = min(256, rows)
    pairs = ctx.shape[1]
    width = pairs * 128
    steps = rows // tile
    shard = rows // streams

    def turn(i):
        return row_tile(i, steps, streams, groups)

    def stream_tile(i):
        return lax.rem(lax.axis_index("blk"), groups) * steps + turn(i)

    tall = pl.BlockSpec((tile, depth), lambda i: (turn(i), 0))
    of_stream = pl.BlockSpec((tile, depth), lambda i: (stream_tile(i), 0))
    split_rows = pl.BlockSpec((groups, pairs, tile, 128), lambda i: (0, 0, turn(i), 0))
    any_space = pl.BlockSpec(memory_space=pl.ANY)

    def full(shape):
        return pl.BlockSpec(shape, lambda i: (0,) * len(shape))

    out_full = [(depth, depth), (depth, ff), (ff, depth), (16, depth)]
    bag = Bag()
    for name, shape in zip(("gout", "gup", "gdown"), out_full):
        bag.add(name, pltpu.VMEM(shape, F32))
    for i in range(3):
        bag.add(f"weight{2 * i}", pltpu.VMEM(teacher_weights[i].shape, BF))
        bag.add(f"weight{2 * i + 1}", pltpu.VMEM(weights[i].shape, BF))
    bag.add("weight_sems", dma(6))
    bag.add("out_box", pltpu.VMEM((steps, tile, depth), BF))
    bag.add("d_box", pltpu.VMEM((steps, groups, tile, width), BF))
    bag.add("out_s", dma(streams))
    bag.add("out_r", dma(streams))
    tiles = Tiles(bag, "tiles", groups, 1, steps)
    return pl.pallas_call(
        functools.partial(middle_kernel, streams, groups, bag, tiles),
        grid=(steps,),
        in_specs=[of_stream, of_stream, tall, split_rows, split_rows]
        + [any_space] * 6
        + [full(a.shape) for a in vectors],
        out_specs=[any_space, tall, any_space] + [full(s) for s in out_full],
        out_shape=[
            jax.ShapeDtypeStruct((streams, shard, depth), BF),
            jax.ShapeDtypeStruct((rows, depth), F32),
            jax.ShapeDtypeStruct((rows * groups, width), BF),
        ]
        + [jax.ShapeDtypeStruct(s, BF if i < 3 else F32) for i, s in enumerate(out_full)],
        scratch_shapes=list(bag.items.values()),
        compiler_params=remote_params(collective_id),
        name="middle",
    )(x, tx, cot, ctx, tctx, *weights, *teacher_weights, *vectors)


def latent_columns(latent, grad, out):
    rows = latent.shape[0]
    size = min(256, rows)
    chunks = [slice(i, i + size) for i in range(0, rows, size)]
    squares = jnp.zeros((1, latent.shape[1]), F32)
    for at in chunks:
        matrix = latent[at, :].astype(F32)
        squares = squares + jnp.sum(matrix * matrix, axis=0, keepdims=True)
    scale = jnp.sqrt(squares * (1.0 / rows) + 1e-06)
    twice = 2.0 / scale
    through_scale = jnp.zeros_like(squares)
    for at in chunks:
        matrix, upstream = latent[at, :].astype(F32), grad[at, :].astype(F32)
        inner = matrix * twice
        bent = jnp.tanh(inner)
        slope = 1.0 - bent * bent
        through_scale = through_scale + jnp.sum(
            upstream * (bent - inner * slope), axis=0, keepdims=True
        )
        out[at, :] = upstream * (2.0 * slope)
    factor = through_scale / (rows * scale)
    for at in chunks:
        out[at, :] = out[at, :] + latent[at, :].astype(F32) * factor


def latent_grads_kernel(pairs, passed, lq, lo, lu, ld, *refs):
    late, (go, gu, gd, *refs) = refs[:pairs], refs[pairs:]
    come, (oq, oo, ou, od, *gone) = refs[:passed], refs[passed:]
    for source, target in zip(come, gone):
        target[...] = source[...]
    for p in range(pairs):

        @pl.when(lax.rem(pl.program_id(0), pairs) == p)
        def _():
            for i in range(3):
                latent_columns(lq.at[i], late[p].at[0, :, i * 128 : (i + 1) * 128], oq.at[i])

    latent_columns(lo, go, oo)
    latent_columns(ld, gd, od)
    for i in range(0, lu.shape[1], 128):
        at = slice(i, i + 128)
        latent_columns(lu.at[:, at], gu.at[:, at], ou.at[:, at])


def latent_grads(latents, late, early, tall, small):
    pairs = len(late)
    groups, depth, wide = late[0].shape
    steps = groups * pairs
    qkv = pl.BlockSpec((3, depth, depth // steps), lambda i: (0, 0, i))
    flat = [pl.BlockSpec((a.shape[0], a.shape[1] // steps), lambda i: (0, i)) for a in latents[1:]]
    handed = [
        pl.BlockSpec((a.shape[0] // steps,) + a.shape[1:], lambda i: (i, 0, 0)) for a in tall
    ] + [pl.BlockSpec(a.shape, lambda i: (0, 0)) for a in small]
    return pl.pallas_call(
        functools.partial(latent_grads_kernel, pairs, len(handed)),
        grid=(steps,),
        in_specs=[qkv]
        + flat
        + [pl.BlockSpec((1, depth, wide), lambda i: (i // pairs, 0, 0))] * pairs
        + flat
        + handed,
        out_specs=[qkv] + flat + handed,
        out_shape=[jax.ShapeDtypeStruct(a.shape, F32) for a in latents]
        + [jax.ShapeDtypeStruct(a.shape, a.dtype) for a in tall + small],
        compiler_params=pltpu.CompilerParams(vmem_limit_bytes=VMEM_BYTES),
        name="latent_grads",
    )(*latents, *late, *early, *tall, *small)


def shards(
    tokens,
    teacher_tokens,
    segment_ids,
    cotangent,
    latent_qkv,
    latent_out,
    latent_up,
    latent_down,
    student_gain,
    student_bias,
    student_up_bias,
    teacher_qkv,
    teacher_out,
    teacher_up,
    teacher_down,
    teacher_gain,
    teacher_bias,
    teacher_up_bias,
):
    streams, shard_len, depth = tokens.shape
    blocks = lax.axis_size("blk")
    groups = blocks // streams
    seq = shard_len * blocks
    rows = seq // groups
    block = (shard_len, depth)
    gather, swap = Gather(streams, groups, block, BF), Swap(streams, groups, block, BF)
    (
        queries,
        keys,
        ctx_rows,
        values,
        numerators,
        context,
        inverse,
        active,
        bin_own,
        bin_out,
        bin_up,
        bin_down,
        token_blocks,
        qkv_parts,
        docs,
        teacher_blocks,
        up_parts,
        out_parts,
    ) = attention(
        [
            student_bias,
            latent_qkv,
            latent_out,
            latent_up,
            latent_down,
            segment_ids,
            tokens,
            teacher_qkv,
        ],
        seq,
        streams,
        groups,
        Moves(
            gather,
            Spread(teacher_qkv.shape, BF),
            Gather(streams, groups, (8, shard_len), F32),
        ),
        Moves(gather, Spread(teacher_up.shape, BF), Spread(teacher_out.shape, BF)),
        [teacher_tokens, teacher_up, teacher_out],
        2,
        "attention_student",
    )
    stream_tokens = token_blocks.reshape(seq, depth)
    teacher_stream = teacher_blocks.reshape(seq, depth)
    teacher_queries, teacher_keys, tctx_rows, cot_blocks, down_parts = attention(
        [teacher_stream, qkv_parts, teacher_bias, docs],
        seq,
        streams,
        groups,
        None,
        Moves(swap, Spread(teacher_down.shape, BF), others=[gather]),
        [cotangent, teacher_down],
        3,
        "attention_teacher",
    )
    output, d_one, d_context, g_out, g_up, g_down, small = middle(
        streams,
        groups,
        stream_tokens,
        teacher_stream,
        cot_blocks.reshape(rows, depth),
        ctx_rows,
        tctx_rows,
        [bin_out, bin_up, bin_down],
        [
            out_parts.reshape(-1, depth),
            up_parts.reshape(depth, -1),
            down_parts.reshape(-1, depth),
        ],
        [
            student_gain,
            student_bias,
            student_up_bias.reshape(1, -1),
            teacher_gain,
            teacher_bias,
            teacher_up_bias.reshape(1, -1),
        ],
        4,
    )
    grads = [[g_up], [g_down, g_out]]
    in_kernel = depth % (16 * blocks * lax.axis_size("dp")) == 0
    grad_tokens, early, late, small = attention_back(
        streams,
        groups,
        numerators,
        queries,
        keys,
        values,
        teacher_queries,
        teacher_keys,
        d_context,
        context,
        inverse,
        docs,
        small,
        active,
        bin_own,
        d_one,
        token_blocks,
        grads if in_kernel else [],
        latent_up.shape[1],
        6,
    )
    if not in_kernel:
        early = lax.psum((g_up, g_down, g_out), ("dp", "blk"))
    grad_qkv, grad_out, grad_up, grad_down, output, grad_tokens, gain, bias, shift = latent_grads(
        [latent_qkv, latent_out, latent_up, latent_down],
        late,
        [early[2], early[0], early[1]],
        [output, grad_tokens],
        small,
    )
    return (
        output,
        grad_tokens,
        grad_qkv,
        grad_out,
        grad_up,
        grad_down,
        gain,
        bias,
        shift.reshape(-1),
    )


def solution(mesh):
    return jax.shard_map(
        shards,
        mesh=mesh,
        in_specs=(
            P("dp", "blk", None),
            P("dp", "blk", None),
            P("dp", "blk"),
            P("dp", "blk", None),
            P(),
            P(),
            P(),
            P(),
            P(),
            P(),
            P(),
            P(None, "dp", None),
            P("dp", None),
            P("dp", None),
            P("dp", None),
            P(),
            P(),
            P(),
        ),
        out_specs=(P("dp", "blk", None), P("dp", "blk", None), P(), P(), P(), P(), P(), P(), P()),
        check_vma=False,
    )
```

```python
import functools

import jax
import jax.numpy as jnp
from jax import lax
from jax.experimental import pallas as pl
from jax.experimental.pallas import tpu as pltpu
from jax.sharding import PartitionSpec as P

HEADS = 8
BF = jnp.bfloat16
F32 = jnp.float32
LOG2E = 1.4426950408889634
clip_level = 2.5
masked_score = -1e30
VMEM_BYTES = 56 << 20
MESH = pl.DeviceIdType.MESH
NT = (((1,), (1,)), ((), ()))
TN = (((0,), (0,)), ((), ()))


def squash(tensor):
    return clip_level * jnp.tanh(tensor * (1.0 / clip_level))


def gelu_parts(tensor):
    phi = 0.5 * (1.0 + lax.erf(tensor * 0.7071067811865476))
    return tensor * phi, phi


def binarize(matrix):
    column_scale = jnp.sqrt(jnp.mean(matrix * matrix, axis=-2, keepdims=True) + 1e-06)
    return column_scale * jnp.tanh(2.0 * matrix / column_scale)


def layer_norm(tensor, gain_row, shift_row):
    centre = tensor - jnp.mean(tensor, axis=-1, keepdims=True)
    inverse_std = lax.rsqrt(jnp.mean(centre * centre, axis=-1, keepdims=True) + 1e-05)
    normed = centre * inverse_std
    return (normed * gain_row + shift_row, normed, inverse_std)


def norm_back(upstream, gain_row, normed, inverse_std):
    scaled = upstream * gain_row
    return inverse_std * (
        scaled
        - jnp.mean(scaled, axis=-1, keepdims=True)
        - normed * jnp.mean(scaled * normed, axis=-1, keepdims=True)
    )


def dot(a, b, dims=(((1,), (0,)), ((), ()))):
    return lax.dot_general(a, b, dims, preferred_element_type=F32)


def latent_grad(latent, binary_grad):
    matrix = latent.astype(F32)
    unused, pullback = jax.vjp(binarize, matrix)
    return pullback(binary_grad)[0]


def place(groups):
    here = lax.axis_index("blk")
    return here // groups, lax.rem(here, groups)


def greet(peers):
    barrier = pltpu.get_barrier_semaphore()
    for peer in peers:
        pl.semaphore_signal(barrier, inc=1, device_id=peer, device_id_type=MESH)
    pl.semaphore_wait(barrier, len(peers))


def stream_peers(streams, groups):
    s, r = place(groups)
    return [{"blk": lax.rem(s + d, streams) * groups + r} for d in range(1, streams)]


def core_peers(groups):
    s, r = place(groups)
    return [{"blk": s * groups + lax.rem(r + j, groups)} for j in range(1, groups)]


def dp_peers():
    size = lax.axis_size("dp")
    here = lax.axis_index("dp")
    return [{"dp": lax.rem(here + d, size)} for d in range(1, size)]


def unique(jobs):
    peers, kinds = [], []
    for job in jobs:
        for kind, found in job.peers():
            if kind not in kinds:
                kinds.append(kind)
                peers += found
    return peers


def remote(source, target, send, recv, peer):
    return pltpu.make_async_remote_copy(
        src_ref=source,
        dst_ref=target,
        send_sem=send,
        recv_sem=recv,
        device_id=peer,
        device_id_type=MESH,
    )


def dma(count):
    return pltpu.SemaphoreType.DMA((count,))


class Staged:
    def __init__(self, source, target, stage, sems):
        self.load = pltpu.make_async_copy(source, stage, sems.at[0])
        self.store = pltpu.make_async_copy(stage, target, sems.at[1])

    def first(self):
        self.load.start()

    def last(self):
        self.load.wait()
        self.store.start()
        self.store.wait()


class Gather:
    def __init__(self, streams, groups, block, dtype):
        self.streams, self.groups, self.block, self.dtype = streams, groups, block, dtype

    def scratch(self):
        b, g = self.streams, self.groups
        return [dma(b), dma(b), dma(b * g), dma(b * g), pltpu.VMEM(self.block, self.dtype), dma(2)]

    def out_shape(self):
        return jax.ShapeDtypeStruct((self.streams * self.groups,) + self.block, self.dtype)

    def peers(self):
        return [
            ("stream", stream_peers(self.streams, self.groups)),
            ("core", core_peers(self.groups)),
        ]

    def parts(self, source, target, send, recv, share_send, share_recv, stage, sems):
        b, g = self.streams, self.groups
        s, r = place(g)
        peers, cores = stream_peers(b, g), core_peers(g)
        swaps = [
            remote(
                source.at[lax.rem(s + d, b)],
                target.at[r * b + s],
                send.at[d],
                recv.at[d],
                peers[d - 1],
            )
            for d in range(1, b)
        ]
        shares = [
            [
                remote(
                    source.at[s] if d == 0 else target.at[r * b + lax.rem(s + b - d, b)],
                    target.at[r * b + lax.rem(s + b - d, b)],
                    share_send.at[j * b + d],
                    share_recv.at[j * b + d],
                    cores[j - 1],
                )
                for j in range(1, g)
            ]
            for d in range(b)
        ]
        own = Staged(source.at[s], target.at[r * b + s], stage, sems)
        return swaps, shares, own

    def first(self, *refs):
        swaps, shares, own = self.parts(*refs)
        for copy in swaps:
            copy.start()
        own.first()
        for copy in shares[0]:
            copy.start()

    def middle(self, *refs):
        swaps, shares, own = self.parts(*refs)
        for d in [1, 3, 2] if self.streams == 4 else range(1, self.streams):
            swaps[d - 1].wait_recv()
            for copy in shares[d]:
                copy.start()

    def last(self, *refs):
        swaps, shares, own = self.parts(*refs)
        own.last()
        for row in shares:
            for copy in row:
                copy.wait()
        for copy in swaps:
            copy.wait_send()


class Swap:
    def __init__(self, streams, groups, block, dtype):
        self.streams, self.groups, self.block, self.dtype = streams, groups, block, dtype

    def scratch(self):
        return [dma(self.streams), dma(self.streams), pltpu.VMEM(self.block, self.dtype), dma(2)]

    def out_shape(self):
        return jax.ShapeDtypeStruct((self.streams,) + self.block, self.dtype)

    def peers(self):
        return [("stream", stream_peers(self.streams, self.groups))]

    def parts(self, source, target, send, recv, stage, sems):
        b, g = self.streams, self.groups
        s, r = place(g)
        peers = stream_peers(b, g)
        swaps = [
            remote(source.at[lax.rem(s + d, b)], target.at[s], send.at[d], recv.at[d], peers[d - 1])
            for d in range(1, b)
        ]
        return swaps, Staged(source.at[s], target.at[s], stage, sems)

    def first(self, *refs):
        swaps, own = self.parts(*refs)
        for copy in swaps:
            copy.start()
        own.first()

    def last(self, *refs):
        swaps, own = self.parts(*refs)
        own.last()
        for copy in swaps:
            copy.wait()


class Spread:
    def __init__(self, block, dtype):
        self.block, self.dtype = block, dtype

    def scratch(self):
        size = lax.axis_size("dp")
        return [dma(size), dma(size), pltpu.VMEM(self.block, self.dtype), dma(2)]

    def out_shape(self):
        return jax.ShapeDtypeStruct((lax.axis_size("dp"),) + self.block, self.dtype)

    def peers(self):
        return [("dp", dp_peers())]

    def parts(self, source, target, send, recv, stage, sems):
        here = lax.axis_index("dp")
        copies = [
            remote(source, target.at[here], send.at[d], recv.at[d], peer)
            for d, peer in enumerate(dp_peers(), 1)
        ]
        return copies, Staged(source, target.at[here], stage, sems)

    first = Swap.first
    last = Swap.last


class Tiles:
    def __init__(self, bag, name, groups, pairs, per_owner):
        self.name, self.groups, self.pairs, self.per_owner = name, groups, pairs, per_owner
        count = pairs * per_owner
        bag.add(f"{name}_s", dma(groups * count))
        bag.add(f"{name}_r", dma(groups * count))

    def slot(self, who, pair, at):
        return (who * self.pairs + pair) * self.per_owner + at

    def copy(self, have, source, target, owner, pair, at):
        s, r = place(self.groups)
        return remote(
            source,
            target,
            have[f"{self.name}_s"].at[self.slot(owner, pair, at)],
            have[f"{self.name}_r"].at[self.slot(r, pair, at)],
            {"blk": s * self.groups + owner},
        )

    def own(self, have, source, target, pair, at):
        s, r = place(self.groups)
        return pltpu.make_async_copy(
            source, target, have[f"{self.name}_s"].at[self.slot(r, pair, at)]
        )

    def finish(self, have, source, target):
        s, r = place(self.groups)
        for pair in range(self.pairs):
            for at in range(self.per_owner):
                self.own(have, source, target, pair, at).wait()
                for j in range(1, self.groups):
                    other = lax.rem(r + j, self.groups)
                    remote(
                        source,
                        target,
                        have[f"{self.name}_s"].at[self.slot(other, pair, at)],
                        have[f"{self.name}_r"].at[self.slot(other, pair, at)],
                        {"blk": s * self.groups + other},
                    ).wait()


class Bag:
    def __init__(self):
        self.items = {}

    def add(self, name, item):
        self.items[name] = item

    def bind(self, refs):
        return dict(zip(self.items, refs))


class Reduce:
    def __init__(self, bag, name, streams, groups, shapes, over_cores, two_step):
        self.name, self.streams, self.groups = name, streams, groups
        self.size = lax.axis_size("dp")
        self.over_cores = over_cores
        self.two_step = two_step and self.size == 4 and streams % 2 == 0
        self.count = len(shapes)
        share = self.size * (groups if over_cores else 1)
        self.shapes = [(rows // share, cols) for rows, cols in shapes]
        self.wires = [BF if (c // streams) % 16 == 0 else F32 for c, cols in self.shapes]
        for i, (chunk, cols) in enumerate(self.shapes):
            wire, slim = self.wires[i], chunk // streams
            bag.add(f"{name}half{i}", pltpu.VMEM((self.size, chunk, cols), wire))
            if over_cores:
                bag.add(f"{name}core{i}", pltpu.VMEM((groups - 1, self.size, chunk, cols), wire))
            if self.two_step:
                bag.add(f"{name}first{i}", pltpu.VMEM((4, chunk // 2, cols), wire))
                bag.add(f"{name}second{i}", pltpu.VMEM((2, chunk // 2, cols), wire))
            else:
                bag.add(f"{name}dp{i}", pltpu.VMEM((self.size - 1, chunk, cols), wire))
            bag.add(f"{name}cut{i}", pltpu.VMEM((streams, slim, cols), wire))
            bag.add(f"{name}z{i}", pltpu.VMEM((streams - 1, slim, cols), wire))
            bag.add(f"{name}fin{i}", pltpu.VMEM((slim, cols), wire))
            for kind in self.kinds():
                bag.add(f"{name}{kind}s{i}", dma(self.sem_count(kind)))
                bag.add(f"{name}{kind}r{i}", dma(self.sem_count(kind)))
            bag.add(f"{name}local{i}", dma(2))

    def kinds(self):
        along = ["b1", "b2", "c", "d", "e1", "e2"] if self.two_step else ["b", "c", "d", "e"]
        return (["a"] if self.over_cores else []) + along + ["f"]

    def sem_count(self, kind):
        if kind in ("a", "f"):
            return self.groups
        if kind in ("c", "d"):
            return self.streams
        return max(self.size, 4)

    def out_shapes(self):
        return [
            jax.ShapeDtypeStruct(
                (self.groups, self.size, self.streams, chunk // self.streams, cols), wire
            )
            for (chunk, cols), wire in zip(self.shapes, self.wires)
        ]

    def bind(self, sources, targets, scratch):
        self.sources, self.targets, self.scratch = sources, targets, scratch

    def get(self, what, i):
        return self.scratch[f"{self.name}{what}{i}"]

    def pairs(self, kind, i):
        s, r = place(self.groups)
        here = lax.axis_index("dp")
        b, g, size = self.streams, self.groups, self.size
        x, y = lax.rem(here, 2), here // 2
        beside_x, beside_y = {"dp": 2 * y + 1 - x}, {"dp": 2 * (1 - y) + x}
        if kind == "a":
            for d, peer in enumerate(core_peers(g), 1):
                yield d, self.sources[i].at[lax.rem(r + d, g)], self.get("core", i).at[d - 1], peer
        elif kind == "b":
            half, box = self.get("half", i), self.get("dp", i)
            for d, peer in enumerate(dp_peers(), 1):
                yield d, half.at[lax.rem(here + d, size)], box.at[d - 1], peer
        elif kind == "b1":
            half, box, h = self.get("half", i), self.get("first", i), self.shapes[i][0] // 2
            for n in range(2):
                yield n, half.at[2 * n + 1 - x, pl.ds(0, h)], box.at[n], beside_x
                yield 2 + n, half.at[2 * (1 - y) + n, pl.ds(h, h)], box.at[2 + n], beside_y
        elif kind == "b2":
            half, box, h = self.get("half", i), self.get("second", i), self.shapes[i][0] // 2
            yield 0, half.at[2 * (1 - y) + x, pl.ds(0, h)], box.at[0], beside_y
            yield 1, half.at[2 * y + 1 - x, pl.ds(h, h)], box.at[1], beside_x
        elif kind in "cd":
            peers = list(enumerate(stream_peers(b, g), 1))
            for d, peer in [peers[1], peers[0], peers[2]] if b == 4 else peers:
                if kind == "c":
                    cut = self.get("cut", i)
                    yield d, cut.at[lax.rem(s + d, b)], self.get("z", i).at[d - 1], peer
                else:
                    yield d, self.get("fin", i), self.targets[i].at[r, here, s], peer
        elif kind == "e":
            whole = self.targets[i].at[r, here]
            for d, peer in enumerate(dp_peers(), 1):
                yield d, whole, whole, peer
        elif kind == "e1":
            for n, peer in enumerate((beside_y, beside_x)):
                part = self.targets[i].at[r, here, pl.ds(n * b // 2, b // 2)]
                yield n, part, part, peer
        elif kind == "e2":
            for n in range(2):
                part = self.targets[i].at[r, 2 * n + x, pl.ds(0, b // 2)]
                yield n, part, part, beside_x
                part = self.targets[i].at[r, 2 * y + n, pl.ds(b // 2, b // 2)]
                yield 2 + n, part, part, beside_y
        else:
            whole = self.targets[i].at[r]
            for d, peer in enumerate(core_peers(g), 1):
                yield d, whole, whole, peer

    def copies(self, kind, i):
        send, recv = self.get(kind + "s", i), self.get(kind + "r", i)
        for n, source, target, peer in self.pairs(kind, i):
            yield remote(source, target, send.at[n], recv.at[n], peer)

    def start(self, kind, i):
        for copy in self.copies(kind, i):
            copy.start()

    def arrive(self, kind, i):
        for copy in self.copies(kind, i):
            copy.wait_recv()

    def load(self, i):
        s, r = place(self.groups)
        return pltpu.make_async_copy(
            self.sources[i].at[r], self.get("half", i), self.get("local", i).at[0]
        )

    def keep(self, i):
        s, r = place(self.groups)
        return pltpu.make_async_copy(
            self.get("fin", i),
            self.targets[i].at[r, lax.axis_index("dp"), s],
            self.get("local", i).at[1],
        )

    def stages(self):
        middle = [self.dp_middle] if self.two_step else []
        back = [self.dp_back_middle] if self.two_step else []
        return [self.dp_start, *middle, self.z_start, self.z_back, self.dp_back, *back, self.core_back]

    def core_start(self):
        for i in range(self.count):
            self.start("a", i)
            self.load(i).start()

    def dp_start(self):
        for i in range(self.count):
            if self.over_cores:
                self.load(i).wait()
                self.arrive("a", i)
                half, box, wire = self.get("half", i), self.get("core", i), self.wires[i]
                for p in range(self.size):
                    total = half[p].astype(F32)
                    for j in range(self.groups - 1):
                        total = total + box[j, p].astype(F32)
                    half[p] = total.astype(wire)
            self.start("b1" if self.two_step else "b", i)

    def dp_middle(self):
        here = lax.axis_index("dp")
        x, y = lax.rem(here, 2), here // 2
        for i in range(self.count):
            self.arrive("b1", i)
            half, box, wire = self.get("half", i), self.get("first", i), self.wires[i]
            h = self.shapes[i][0] // 2
            for n in range(2):
                for who, at, part in ((2 * n + x, pl.ds(0, h), n), (2 * y + n, pl.ds(h, h), 2 + n)):
                    total = half[who, at, :].astype(F32) + box[part].astype(F32)
                    half[who, at, :] = total.astype(wire)
            self.start("b2", i)

    def z_start(self):
        here = lax.axis_index("dp")
        for i in range(self.count):
            self.arrive("b2" if self.two_step else "b", i)
            half, cut, wire = self.get("half", i), self.get("cut", i), self.wires[i]
            chunk = self.shapes[i][0]
            slim = chunk // self.streams
            for z in range(self.streams):
                at = slice(z * slim, (z + 1) * slim)
                total = half[here, at, :].astype(F32)
                if self.two_step:
                    which, first = divmod(z * slim, chunk // 2)
                    total = total + self.get("second", i)[which, first : first + slim].astype(F32)
                else:
                    for d in range(self.size - 1):
                        total = total + self.get("dp", i)[d, at, :].astype(F32)
                cut[z] = total.astype(wire)
            self.start("c", i)

    def z_back(self):
        s, r = place(self.groups)
        for i in range(self.count):
            self.arrive("c", i)
            box = self.get("z", i)
            total = self.get("cut", i)[s].astype(F32)
            for d in range(self.streams - 1):
                total = total + box[d].astype(F32)
            self.get("fin", i)[...] = total.astype(self.wires[i])
            self.keep(i).start()
            self.start("d", i)

    def dp_back(self):
        for i in range(self.count):
            self.keep(i).wait()
            self.arrive("d", i)
            self.start("e1" if self.two_step else "e", i)

    def dp_back_middle(self):
        for i in range(self.count):
            self.arrive("e1", i)
            self.start("e2", i)

    def core_back(self):
        for i in range(self.count):
            self.arrive("e2" if self.two_step else "e", i)
            self.start("f", i)

    def end(self):
        for i in range(self.count):
            self.arrive("f", i)
            for kind in self.kinds():
                for copy in self.copies(kind, i):
                    copy.wait_send()


class Moves:
    def __init__(self, *jobs, others=()):
        self.jobs, self.others = list(jobs), list(others)
        self.counts = [len(job.scratch()) for job in jobs]

    def scratch(self):
        return [item for job in self.jobs for item in job.scratch()]

    def out_shapes(self):
        return [job.out_shape() for job in self.jobs]

    def spaces(self):
        return [pl.BlockSpec(memory_space=pl.ANY)] * len(self.jobs)

    def each(self, sources, targets, scratch):
        at = 0
        for job, count, source, target in zip(self.jobs, self.counts, sources, targets):
            yield job, (source, target, *scratch[at : at + count])
            at += count

    def first(self, sources, targets, scratch, count=None):
        greet(unique(self.jobs + self.others))
        for job, refs in list(self.each(sources, targets, scratch))[:count]:
            job.first(*refs)

    def start_last(self, sources, targets, scratch):
        for job, refs in list(self.each(sources, targets, scratch))[-1:]:
            job.first(*refs)

    def middle(self, sources, targets, scratch):
        for job, refs in self.each(sources, targets, scratch):
            if isinstance(job, Gather):
                job.middle(*refs)

    def last(self, sources, targets, scratch):
        for job, refs in self.each(sources, targets, scratch):
            job.last(*refs)


def remote_params(collective_id):
    return pltpu.CompilerParams(
        collective_id=collective_id, has_side_effects=True, vmem_limit_bytes=VMEM_BYTES
    )


def binary_columns(latent):
    matrix = latent.astype(F32)
    scale = jnp.sqrt(jnp.mean(matrix * matrix, axis=0, keepdims=True) + 1e-06)
    return (scale * jnp.tanh(matrix * (2.0 / scale))).astype(BF)


def intake_kernel(moves, groups, *refs):
    count = len(moves.jobs)
    latents, ids_ref, refs = refs[:4], refs[4], refs[5:]
    sources, refs = refs[: count - 1], refs[count - 1 :]
    results, refs = refs[:4], refs[4:]
    targets, refs = refs[:count], refs[count:]
    loaded, made, sems = refs[:4], refs[4:8], refs[8]
    ids_in, ids_box, *scratch = refs[9:]
    sources = (*sources, ids_box)
    moves.first(sources, targets, scratch, count - 1)
    s, r = place(groups)
    width = results[0].shape[3]
    own = pl.ds(pl.multiple_of(r * width, 128), width)
    places = [latents[0].at[:, :, own], *latents[1:]]
    loads = [
        pltpu.make_async_copy(source, target, sems.at[i])
        for i, (source, target) in enumerate(zip(places, loaded))
    ]
    stores = [
        pltpu.make_async_copy(source, target, sems.at[4 + i])
        for i, (source, target) in enumerate(zip(made, [results[0].at[0], *results[1:]]))
    ]
    fetch = pltpu.make_async_copy(ids_ref, ids_in, sems.at[8])
    fetch.start()
    for copy in loads:
        copy.start()
    fetch.wait()
    ids = ids_in[...].astype(F32)
    for i in range(ids.shape[0]):
        ids_box[i] = jnp.broadcast_to(ids[i : i + 1, :], ids_box.shape[1:])
    moves.start_last(sources, targets, scratch)
    loads[0].wait()
    for i in range(3):
        made[0][i] = binary_columns(loaded[0][i])
    stores[0].start()
    for n in range(1, 4):
        loads[n].wait()
        for i in range(0, loaded[n].shape[1], 128):
            made[n][:, i : i + 128] = binary_columns(loaded[n][:, i : i + 128])
        stores[n].start()
    moves.middle(sources, targets, scratch)
    for copy in stores:
        copy.wait()
    moves.last(sources, targets, scratch)


def intake(moves, groups, latents, ids, arrays, collective_id):
    three, depth, unused = latents[0].shape
    own_shape = (three, depth, depth // groups)
    shapes = [(1,) + own_shape] + [a.shape for a in latents[1:]]
    buffers = [pltpu.VMEM(shape, BF) for shape in [own_shape] + shapes[1:]]
    any_space = [pl.BlockSpec(memory_space=pl.ANY)] * 4
    return pl.pallas_call(
        functools.partial(intake_kernel, moves, groups),
        out_shape=[jax.ShapeDtypeStruct(shape, BF) for shape in shapes] + moves.out_shapes(),
        in_specs=any_space
        + moves.spaces(),
        out_specs=any_space + moves.spaces(),
        scratch_shapes=buffers * 2
        + [dma(9), pltpu.VMEM(ids.shape, ids.dtype)]
        + [pltpu.VMEM((ids.shape[0], 8, ids.shape[1]), F32)]
        + moves.scratch(),
        compiler_params=remote_params(collective_id),
        name="intake",
    )(*latents, ids, *arrays)


def lanes_of(shape):
    return lax.broadcasted_iota(jnp.int32, shape, 1)


def forward_kernel(
    moves, keep, streams, groups, tile, bag, tiles, x_ref, w_ref, bias_ref, docs_ref, *rest
):
    count = len(moves.jobs)
    sources, rest = rest[:count], rest[count:]
    q_ref, k_ref, rows_ref, *rest = rest
    if keep:
        v_ref, e_ref, ctx_ref, inv_ref, active_ref, *rest = rest
    targets, rest = rest[:count], rest[count:]
    have = bag.bind(rest)
    scratch = tuple(have[f"moves{i}"] for i in range(len(moves.scratch())))
    k_aug, v_aug, ctx_all, mask, edges = (
        have["k_aug"],
        have["v_aug"],
        have["ctx_all"],
        have["mask"],
        have["edges"],
    )
    active = have["active"] if keep else x_ref
    row_ref = have["row"]
    pair, step = pl.program_id(0), pl.program_id(1)
    pairs, steps = pl.num_programs(0), pl.num_programs(1)
    seq = k_ref.shape[0]
    s, r = place(groups)
    sub = min(256, tile)
    width = w_ref.shape[3]
    n_pairs = ctx_all.shape[0]
    offset = pair * 128 if width == n_pairs * 128 else (r * n_pairs + pair) * 128
    offset = pl.multiple_of(offset, 128)
    home = pl.multiple_of((r * n_pairs + pair) * 128, 128)

    @pl.when((pair == 0) & (step == 0))
    def _():
        moves.first(sources, targets, scratch)
        ids = stream_row(docs_ref)
        row_ref[...] = ids
        big_at = long_at(streams, groups, seq)
        big = ids[:, big_at : big_at + 1]
        mask[...] = jnp.where(ids == big, 0.0, masked_score)
        edges[0] = jnp.broadcast_to(ids[:, :sub], (128, sub)).T
        edges[1] = jnp.broadcast_to(ids[:, seq - sub :], (128, sub)).T
        if keep:
            for i in range(0, seq, 256):
                active[i : i + 256, :] = squash(x_ref[i : i + 256, :].astype(F32)).astype(BF)
            pltpu.make_async_copy(active, active_ref, have["active_sem"].at[0]).start()

    @pl.when((pair == pairs - 1) & (step == steps - 2))
    def _():
        moves.middle(sources, targets, scratch)

    @pl.when(step == 0)
    def _():
        columns = pl.ds(offset, 128)

        def project(i, bias):
            matrix = jnp.concatenate(
                [w_ref[d, i, :, columns] for d in range(w_ref.shape[0])], axis=0
            )
            result = dot(active[...], matrix)
            if bias is not None:
                result = result + bias_ref[bias : bias + 1, pl.ds(home, 128)]
            return result.astype(BF)

        low = lanes_of((seq, 128)) < 64
        lane = lanes_of((seq, 128))
        q_ref[...] = (project(0, 0).astype(F32) * 0.125).astype(BF)
        keys = project(1, None)
        k_ref[...] = keys
        keys = keys.astype(F32)
        turned = pltpu.roll(keys, 64, 1)
        k_aug[0] = jnp.where(low, keys, turned).astype(BF)
        k_aug[1] = jnp.where(low, turned, keys).astype(BF)
        values = project(2, 1)
        if keep:
            v_ref[...] = values
        values = values.astype(F32)
        v_aug[0] = jnp.where(low, values, jnp.where(lane < 66, 1.0, 0.0)).astype(BF)
        v_aug[1] = jnp.where(low, jnp.where(lane < 2, 1.0, 0.0), values).astype(BF)

    turned = own_rows_last(step, seq, tile, groups)
    start = pl.multiple_of(turned * tile, tile)

    def body(edge_at):
        low = lanes_of((sub, 128)) < 64
        parts = []
        for at in range(0, tile, sub):
            scaled = q_ref[pl.ds(start + at, sub), :].astype(F32) * LOG2E
            upper = scaled.astype(BF).astype(F32)
            lower = scaled - upper
            parts.append(
                (
                    jnp.where(low, upper, pltpu.roll(lower, 64, 1)).astype(BF),
                    jnp.where(low, pltpu.roll(upper, 64, 1), lower).astype(BF),
                )
            )
        chains = [(at, h) for at in range(0, tile, sub) for h in range(2)]

        def scores_of(at, h):
            scores = dot(parts[at // sub][h], k_aug[h], NT)
            if edge_at is not None and at == (0 if edge_at == 0 else tile - sub):
                return jnp.where(edges[edge_at][:, :1] == row_ref[...], scores, masked_score)
            return jnp.concatenate(
                [
                    scores[:, :sub] + mask[:, :sub],
                    scores[:, sub : seq - sub],
                    scores[:, seq - sub :] + mask[:, seq - sub :],
                ],
                axis=1,
            )

        scores = scores_of(*chains[0])
        results = {}
        for n, (at, h) in enumerate(chains):
            if n + 1 < len(chains):
                later = scores_of(*chains[n + 1])
            peak = jnp.max(scores, axis=1, keepdims=True)
            numerators = jnp.exp2(scores - peak).astype(BF)
            if keep:
                e_ref[h, at : at + sub, :] = numerators
            total = dot(numerators, v_aug[h])
            where_sum = 64 if h == 0 else 0
            inverse = 1.0 / total[:, where_sum : where_sum + 1]
            results[h] = (total * inverse, inverse)
            if n + 1 < len(chains):
                scores = later
            if h == 1:
                done = jnp.where(low, results[0][0], results[1][0]).astype(BF)
                ctx_all[pair, pl.ds(start + at, sub), :] = done
                if keep:
                    ctx_ref[at : at + sub, :] = done
                    inv_ref[at : at + sub, :] = jnp.where(low, results[0][1], results[1][1])

    @pl.when(turned == 0)
    def _():
        body(0)

    @pl.when(turned == steps - 1)
    def _():
        body(1)

    @pl.when((turned > 0) & (turned < steps - 1))
    def _():
        body(None)

    owned = seq // groups
    owner = start // owned
    at = lax.rem(turned, owned // tile)
    source = ctx_all.at[pair, pl.ds(start, tile)]
    target = rows_ref.at[r, pair, pl.ds(pl.multiple_of(lax.rem(start, owned), tile), tile)]

    @pl.when(owner == r)
    def _():
        tiles.own(have, source, target, pair, at).start()

    @pl.when(owner != r)
    def _():
        tiles.copy(have, source, target, owner, pair, at).start()

    @pl.when((pair == pairs - 1) & (step == steps - 1))
    def _():
        tiles.finish(have, source, target)
        moves.last(sources, targets, scratch)
        if keep:
            pltpu.make_async_copy(active, active_ref, have["active_sem"].at[0]).wait()


def own_rows_last(step, seq, tile, groups):
    s, r = place(groups)
    steps = seq // tile
    return lax.rem(step + (r + 1) * (steps // groups), steps)


def stream_row(docs_ref):
    return jnp.concatenate([docs_ref[i, 0:1, :] for i in range(docs_ref.shape[0])], axis=1)


def long_at(streams, groups, seq):
    shard = seq // (streams * groups)
    return streams * shard if groups > 1 else shard


def attention(x, weights, bias, docs, streams, groups, moves, moved, keep, collective_id, name):
    seq, depth = x.shape
    width = depth // groups
    pairs = width // 128
    tile = 512
    owned = seq // groups
    bag = Bag()
    bag.add("k_aug", pltpu.VMEM((2, seq, 128), BF))
    bag.add("v_aug", pltpu.VMEM((2, seq, 128), BF))
    bag.add("ctx_all", pltpu.VMEM((pairs, seq, 128), BF))
    bag.add("mask", pltpu.VMEM((1, seq), F32))
    bag.add("row", pltpu.VMEM((1, seq), F32))
    if keep:
        bag.add("active", pltpu.VMEM((seq, depth), BF))
        bag.add("active_sem", dma(1))
    bag.add("edges", pltpu.VMEM((2, 256, 128), F32))
    tiles = Tiles(bag, "tiles", groups, pairs, owned // tile)
    for i, item in enumerate(moves.scratch()):
        bag.add(f"moves{i}", item)

    def constant(shape):
        return pl.BlockSpec(shape, lambda p, i: (0,) * len(shape))

    def turn(i):
        return own_rows_last(i, seq, tile, groups)

    part = pl.BlockSpec((tile, 128), lambda p, i: (turn(i), p))
    whole = pl.BlockSpec((seq, 128), lambda p, i: (0, p))
    any_space = pl.BlockSpec(memory_space=pl.ANY)
    wide = jax.ShapeDtypeStruct((seq, width), BF)
    outs = [whole, whole, any_space]
    shapes = [wide, wide, jax.ShapeDtypeStruct((groups, pairs, owned, 128), BF)]
    if keep:
        outs += [
            whole,
            pl.BlockSpec((2, tile, seq), lambda p, i: (p, turn(i), 0)),
            part,
            part,
            any_space,
        ]
        shapes += [
            wide,
            jax.ShapeDtypeStruct((2 * pairs, seq, seq), BF),
            wide,
            jax.ShapeDtypeStruct((seq, width), F32),
            jax.ShapeDtypeStruct((seq, depth), BF),
        ]
    return pl.pallas_call(
        functools.partial(forward_kernel, moves, keep, streams, groups, tile, bag, tiles),
        grid=(pairs, seq // tile),
        in_specs=[constant(a.shape) for a in (x, weights, bias, docs)]
        + moves.spaces(),
        out_specs=outs + moves.spaces(),
        out_shape=shapes + moves.out_shapes(),
        scratch_shapes=list(bag.items.values()),
        compiler_params=remote_params(collective_id),
        name=name,
    )(x, weights, bias, docs, *moved)


def split(matrix):
    upper = matrix.astype(BF)
    return upper, (matrix - upper.astype(F32)).astype(BF)


def backward_kernel(
    streams,
    groups,
    tile,
    bag,
    early,
    late,
    e_ref,
    q_ref,
    k_ref,
    v_ref,
    tq_ref,
    tk_ref,
    dc_ref,
    ctx_ref,
    inv_ref,
    docs_ref,
    small_ref,
    active_hbm,
    bin_hbm,
    d1_hbm,
    tokens_hbm,
    *rest,
):
    n_early = sum(job.count for job in early)
    sources, rest = rest[:n_early], rest[n_early:]
    grad_ref, *rest = rest
    early_out, rest = rest[:n_early], rest[n_early:]
    late_out, (gain_ref, bias_ref, shift_ref, *rest) = rest[: len(late)], rest[len(late) :]
    have = bag.bind(rest)
    at = 0
    for job in early:
        job.bind(sources[at : at + job.count], early_out[at : at + job.count], have)
        at += job.count
    for job, target in zip(late, late_out):
        job.bind(None, [target], have)

    pair, step = pl.program_id(0), pl.program_id(1)
    pairs, steps = len(late), q_ref.shape[0] // tile
    sub = min(256, tile)
    seq = k_ref.shape[0]
    share = 1.0 / seq
    time = pair * steps + step
    total_time = pairs * steps
    size = lax.axis_size("dp")
    here = lax.axis_index("dp")
    s, r = place(groups)
    rows, depth = d1_hbm.shape
    width = pairs * 128
    v_aug, dk_acc, dv_acc, grams = have["v_aug"], have["dk_acc"], have["dv_acc"], have["grams"]
    dq_all, d_act, active, weights = have["dq_all"], have["d_act"], have["active"], have["weights"]
    d_one, x_rows = have["d_one"], have["x_rows"]
    edges, in_big, pair_box = have["edges"], have["in_big"], have["pair_box"]
    row_ref = have["row"]
    along_z, cores, along_dp = stream_peers(streams, groups), core_peers(groups), dp_peers()

    def loads():
        sems = have["load"]
        return [
            pltpu.make_async_copy(active_hbm, active, sems.at[0]),
            pltpu.make_async_copy(bin_hbm, weights, sems.at[1]),
            pltpu.make_async_copy(d1_hbm, d_one, sems.at[2]),
            pltpu.make_async_copy(tokens_hbm.at[pl.ds(r * streams, streams)], x_rows, sems.at[3]),
        ]

    halves = tile // sub
    plan = []

    def at_time(when, work):
        plan.append((when, work))

    def due(half):
        for when, work in plan:
            if when % halves == half:
                pl.when(time == when // halves)(work)

    def begin():
        greet(along_z + cores + along_dp)
        for job in early:
            job.core_start()
        for copy in loads():
            copy.start()
        ids = stream_row(docs_ref)
        row_ref[...] = ids
        big_at = long_at(streams, groups, seq)
        big = ids[:, big_at : big_at + 1]
        for n, first in enumerate((0, seq - sub)):
            column = jnp.broadcast_to(ids[:, first : first + sub], (128, sub)).T
            edges[n] = column
            in_big[n] = jnp.where(column == big, 1.0, 0.0)

    def big_rows(ref):
        return jnp.concatenate(
            [
                (ref[:sub, :].astype(F32) * in_big[0]).astype(BF),
                ref[sub : seq - sub, :],
                (ref[seq - sub :, :].astype(F32) * in_big[1]).astype(BF),
            ],
            axis=0,
        )

    at_time(0, begin)
    unit = total_time * halves / 16
    left = []
    for n, job in enumerate(early):
        stages, times = job.stages(), EARLY_TIMES[n]
        if not job.two_step:
            times = times[:1] + times[2:5] + times[6:]
        for when, work in zip(times, stages):
            at_time(int(when * unit), work)
        left.append(stages[len(times) :])
    for p, job in enumerate(late[:-1]):
        first = (p + 1) * steps * halves
        for when, work in zip(LATE_TIMES, job.stages()):
            at_time(first + when, work)
        left.append(job.stages()[len(LATE_TIMES) :])

    def go_on(count):
        for unused in range(count):
            for queue in left:
                if queue:
                    queue.pop(0)()

    due(0)

    @pl.when(step == 0)
    def _():
        lane = lanes_of((seq, 128))
        low = lane < 64
        values = v_ref[...].astype(F32)
        v_aug[0] = jnp.where(low, values, jnp.where(lane < 66, 1.0, 0.0)).astype(BF)
        v_aug[1] = jnp.where(low, jnp.where(lane < 2, 1.0, 0.0), values).astype(BF)
        dk_acc[...] = jnp.zeros_like(dk_acc)
        dv_acc[...] = jnp.zeros_like(dv_acc)
        kb, tkb, qb, tqb = (big_rows(ref) for ref in (k_ref, tk_ref, q_ref, tq_ref))
        same_head = (lax.broadcasted_iota(jnp.int32, (128, 128), 0) < 64) == (
            lanes_of((128, 128)) < 64
        )
        for i, (a, b) in enumerate(((kb, kb), (tkb, kb), (qb, qb), (tqb, qb))):
            gram = jnp.where(same_head, dot(a, b, TN) * share, 0.0)
            grams[2 * i], grams[2 * i + 1] = split(gram)

    start = pl.multiple_of(step * tile, tile)
    low = lanes_of((sub, 128)) < 64
    lane = lanes_of((sub, 128))

    def prepare(at):
        here_rows = pl.ds(start + at, sub)
        q8, tq8 = q_ref[here_rows, :], tq_ref[here_rows, :]
        scaled = dc_ref[at : at + sub, :].astype(F32) * inv_ref[at : at + sub, :]
        product = scaled * ctx_ref[at : at + sub, :].astype(F32)
        augmented = []
        for h in range(2):
            mine = low if h == 0 else jnp.logical_not(low)
            delta = -jnp.sum(jnp.where(mine, product, 0.0), axis=1, keepdims=True)
            upper = delta.astype(BF).astype(F32)
            first = 64 if h == 0 else 0
            extra = jnp.where(
                lane == first, upper, jnp.where(lane == first + 1, delta - upper, 0.0)
            )
            augmented.append(jnp.where(mine, scaled, extra).astype(BF))
        q_turned = q8.astype(F32).T.astype(BF)
        dc_turned = scaled.T.astype(BF)
        return here_rows, q8, tq8, augmented, q_turned, dc_turned

    def body(edge, half):
        ready = {half * sub: prepare(half * sub)}
        chains = [(half * sub, h) for h in range(2)]
        edge_at = {None: None, 0: 0, 1: tile - sub}[edge]
        columns = slice(0, sub) if edge == 0 else slice(seq - sub, seq)

        def d_probs_of(at, h):
            return dot(ready[at][3][h], v_aug[h], NT)

        d_probs = d_probs_of(*chains[0])
        d_queries = {}
        for n, (at, h) in enumerate(chains):
            if n + 1 < len(chains):
                later = d_probs_of(*chains[n + 1])
            here_rows, q8, tq8, unused, q_turned, dc_turned = ready[at]
            mine = low if h == 0 else jnp.logical_not(low)
            numerators = e_ref[h, at : at + sub, :]
            d_scores = numerators.astype(F32) * d_probs
            if edge is not None and at == edge_at:
                q_mine = jnp.where(mine, q8, 0.0).astype(BF)
                tq_mine = jnp.where(mine, tq8, 0.0).astype(BF)
                gap = dot(q_mine, k_ref[columns, :], NT) - dot(tq_mine, tk_ref[columns, :], NT)
                same = jnp.where(edges[edge][:, :1] == row_ref[:, columns], share, 0.0)
                gap = gap * (same * (1.0 - in_big[edge][:, :1]))
                if edge == 0:
                    d_scores = jnp.concatenate(
                        [d_scores[:, :sub] + gap, d_scores[:, sub:]], axis=1
                    )
                else:
                    d_scores = jnp.concatenate(
                        [d_scores[:, : seq - sub], d_scores[:, seq - sub :] + gap], axis=1
                    )
            d_scores = d_scores.astype(BF)
            mine = slice(64 * h, 64 * h + 64)
            dv_acc[mine, :] += dot(dc_turned[mine, :], numerators)
            d_queries[h] = dot(d_scores, k_ref[...])
            dk_acc[mine, :] += dot(q_turned[mine, :], d_scores)
            if h == 1:
                d_query = jnp.where(low, d_queries[0], d_queries[1])
                qb, tqb = q8, tq8
                if edge is not None and at == edge_at:
                    qb = (q8.astype(F32) * in_big[edge]).astype(BF)
                    tqb = (tq8.astype(F32) * in_big[edge]).astype(BF)
                d_query += dot(qb, grams[0]) + dot(qb, grams[1])
                d_query -= dot(tqb, grams[2]) + dot(tqb, grams[3])
                dq_all[here_rows, :] = (d_query * 0.125).astype(BF)
            if n + 1 < len(chains):
                d_probs = later

    for half in range(halves):
        if half:
            due(half)
        edge, at_edge = None, None
        if half == 0:
            edge, at_edge = 0, step == 0
        elif half == halves - 1:
            edge, at_edge = 1, step == steps - 1
        if edge is not None:
            pl.when(at_edge)(functools.partial(body, edge, half))
            pl.when(jnp.logical_not(at_edge))(functools.partial(body, None, half))
        else:
            body(None, half)

    def pair_end(p):
        job = late[p]
        kb, tkb = big_rows(k_ref), big_rows(tk_ref)
        d_key = dk_acc[...].T
        d_key += dot(kb, grams[4]) + dot(kb, grams[5]) - dot(tkb, grams[6]) - dot(tkb, grams[7])
        d_value = dv_acc[...].T.astype(BF)
        d_query = dq_all[...]
        d_pair = jnp.concatenate([d_query, d_key.astype(BF), d_value], axis=1)
        if p == 0:
            for copy in loads():
                copy.wait()
        columns = slice(p * 128, (p + 1) * 128)
        bins = jnp.concatenate([weights[0, i, :, columns] for i in range(3)], axis=1)
        chunk = depth // size
        half = job.get("half", 0)
        partial = dot(active[...], d_pair, TN).astype(job.wires[0])
        for d in range(size):
            half[d] = partial[d * chunk : (d + 1) * chunk, :]
        if p == pairs - 1:
            job.dp_start()
        if p < pairs - 1:
            if p == 0:
                d_act[...] = dot(d_pair, bins, NT)
            else:
                d_act[...] += dot(d_pair, bins, NT)
        else:
            pair_box[...] = d_pair
            for j in range(1, groups + 1):
                at = pl.ds(pl.multiple_of(lax.rem(r + j, groups) * rows, rows), rows)
                total = dot(pair_box[at, :], bins, NT)
                if p > 0:
                    total = total + d_act[at, :]
                if j < groups:
                    have["outbox"][j - 1] = total.astype(BF)
                    core_copies()[j - 1].start()
                else:
                    d_act[at, :] = total
        sums = have["sums"]
        sums[0:1, columns] = jnp.sum(d_query.astype(F32), axis=0, keepdims=True)
        sums[1:2, columns] = jnp.sum(d_value.astype(F32), axis=0, keepdims=True)

    def core_copies():
        return [
            remote(
                have["outbox"].at[j - 1],
                have["inbox"].at[j - 1],
                have["core_s"].at[j],
                have["core_r"].at[j],
                cores[j - 1],
            )
            for j in range(1, groups)
        ]

    def small_copies(stage, peers, base):
        return [
            remote(
                have["small"].at[stage],
                have["small_box"].at[base + d],
                have["small_s"].at[base + d],
                have["small_r"].at[base + d],
                peer,
            )
            for d, peer in enumerate(peers)
        ]

    def small_start(stage, peers, base):
        for copy in small_copies(stage, peers, base):
            copy.start()

    def small_sum(stage, peers, base):
        for copy in small_copies(stage, peers, base):
            copy.wait_recv()
        total = have["small"][stage]
        for d in range(len(peers)):
            total = total + have["small_box"][base + d]
        return total

    for p in range(pairs - 1):

        @pl.when((pair == p) & (step == steps - 1))
        def _():
            pair_end(p)

    @pl.when(time == total_time - 1)
    def _():
        pair_end(pairs - 1)
        last = late[-1]
        small = have["small"]
        small[0] = small_ref[...]
        for i in range(2):
            vector = have["sums"][i : i + 1, :]
            small[0, 2 + i : 3 + i, :] = jnp.concatenate(
                [jnp.where(r == j, vector, 0.0) for j in range(groups)], axis=1
            )
        small_start(0, along_dp, 0)
        go_on(TAIL[0])
        last.z_start()
        last.z_back()
        for copy in core_copies():
            copy.wait_recv()
        shard = rows // streams
        back_copies = []
        blocks = have["blocks"]
        order = [2, 1, 3] if streams == 4 else list(range(1, streams))
        for d in order + [0]:
            target = lax.rem(s + d, streams)
            here_rows = pl.ds(pl.multiple_of(target * shard, shard), shard)
            bent = jnp.tanh(x_rows[target].astype(F32) * (1.0 / clip_level))
            total = d_act[pl.ds(pl.multiple_of(r * rows + target * shard, shard), shard), :]
            for j in range(groups - 1):
                total = total + have["inbox"][j, here_rows, :].astype(F32)
            blocks[target] = (d_one[here_rows, :] + total * (1.0 - bent * bent)).astype(BF)
            if d:
                copy = remote(
                    blocks.at[target],
                    grad_ref.at[s],
                    have["grad_s"].at[d],
                    have["grad_r"].at[d],
                    along_z[d - 1],
                )
            else:
                copy = pltpu.make_async_copy(blocks.at[s], grad_ref.at[s], have["grad_s"].at[0])
            copy.start()
            back_copies.append(copy)
        small[1] = small_sum(0, along_dp, 0)
        small_start(1, along_z, size)
        go_on(TAIL[1])
        small[2] = small_sum(1, along_z, size)
        small_start(2, cores, size + streams)
        go_on(TAIL[2])
        last.dp_back()
        summed = small_sum(2, cores, size + streams)
        gain_ref[...] = summed[0:2, :]
        bias_ref[...] = summed[2:8, :]
        for i in range(shift_ref.shape[1] // depth):
            shift_ref[:, i * depth : (i + 1) * depth] = summed[8 + i : 9 + i, :]
        go_on(TAIL[3])
        last.core_back()
        go_on(8)
        for copy in back_copies:
            copy.wait()
        for job in early + late:
            job.end()
        for copy in (
            core_copies()
            + small_copies(0, along_dp, 0)
            + small_copies(1, along_z, size)
            + small_copies(2, cores, size + streams)
        ):
            copy.wait_send()


TWO_STEP = False
TAIL = (1, 1, 0, 0)
EARLY_TIMES = ((2, 0, 7, 9, 12), (4, 0, 12, 14))
LATE_TIMES = (0, 5, 7)


def attention_back(
    streams,
    groups,
    numerators,
    queries,
    keys,
    values,
    teacher_queries,
    teacher_keys,
    d_context,
    context,
    inverse,
    docs,
    small,
    active,
    bin_own,
    d_one,
    tokens,
    early_arrays,
    up_width,
    collective_id,
):
    seq, width = queries.shape
    pairs = width // 128
    tile = 512
    rows, depth = d_one.shape
    size = lax.axis_size("dp")
    shard = rows // streams
    bag = Bag()
    bag.add("v_aug", pltpu.VMEM((2, seq, 128), BF))
    bag.add("dk_acc", pltpu.VMEM((128, seq), F32))
    bag.add("dv_acc", pltpu.VMEM((128, seq), F32))
    bag.add("grams", pltpu.VMEM((8, 128, 128), BF))
    bag.add("dq_all", pltpu.VMEM((seq, 128), BF))
    bag.add("d_act", pltpu.VMEM((seq, depth), F32))
    bag.add("active", pltpu.VMEM((seq, depth), BF))
    bag.add("weights", pltpu.VMEM((1, 3, depth, width), BF))
    bag.add("d_one", pltpu.VMEM((rows, depth), F32))
    bag.add("x_rows", pltpu.VMEM((streams, shard, depth), BF))
    bag.add("load", dma(4))
    bag.add("sums", pltpu.VMEM((8, width), F32))
    bag.add("outbox", pltpu.VMEM((groups - 1, rows, depth), BF))
    bag.add("inbox", pltpu.VMEM((groups - 1, rows, depth), BF))
    bag.add("core_s", dma(groups))
    bag.add("core_r", dma(groups))
    bag.add("blocks", pltpu.VMEM((streams, shard, depth), BF))
    bag.add("grad_s", dma(streams))
    bag.add("grad_r", dma(streams))
    count = size + streams + groups
    bag.add("small", pltpu.VMEM((3,) + small.shape, F32))
    bag.add("small_box", pltpu.VMEM((count,) + small.shape, F32))
    bag.add("small_s", dma(count))
    bag.add("small_r", dma(count))
    bag.add("row", pltpu.VMEM((1, seq), F32))
    bag.add("pair_box", pltpu.VMEM((seq, 3 * 128), BF))
    bag.add("edges", pltpu.VMEM((2, 256, 128), F32))
    bag.add("in_big", pltpu.VMEM((2, 256, 128), F32))
    early, flat = [], []
    for n, arrays in enumerate(early_arrays):
        job = Reduce(bag, f"early{n}", streams, groups, [a.shape for a in arrays], True, TWO_STEP)
        early.append(job)
        flat += [
            a.reshape(groups, size, chunk, cols) for a, (chunk, cols) in zip(arrays, job.shapes)
        ]
    late = [
        Reduce(bag, f"late{p}", streams, groups, [(depth, 3 * 128)], False, False)
        for p in range(pairs)
    ]
    part = pl.BlockSpec((tile, 128), lambda p, i: (i, p))
    any_space = pl.BlockSpec(memory_space=pl.ANY)

    whole = pl.BlockSpec((seq, 128), lambda p, i: (0, p))

    def constant(shape):
        return pl.BlockSpec(shape, lambda p, i: (0,) * len(shape))

    small_shapes = [(2, depth), (6, depth), (1, up_width)]
    early_shapes = [shape for job in early for shape in job.out_shapes()]
    late_shapes = [shape for job in late for shape in job.out_shapes()]
    results = pl.pallas_call(
        functools.partial(backward_kernel, streams, groups, tile, bag, early, late),
        grid=(pairs, seq // tile),
        in_specs=[
            pl.BlockSpec((2, tile, seq), lambda p, i: (p, i, 0)),
            whole,
            whole,
            whole,
            whole,
            whole,
            part,
            part,
            part,
            constant(docs.shape),
            constant(small.shape),
        ]
        + [any_space] * (4 + len(flat)),
        out_specs=[any_space] * (1 + len(early_shapes) + len(late_shapes))
        + [constant(shape) for shape in small_shapes],
        out_shape=[jax.ShapeDtypeStruct((streams, shard, depth), BF)]
        + early_shapes
        + late_shapes
        + [jax.ShapeDtypeStruct(shape, F32) for shape in small_shapes],
        scratch_shapes=list(bag.items.values()),
        compiler_params=remote_params(collective_id),
        name="attention_back",
    )(
        numerators,
        queries,
        keys,
        values,
        teacher_queries,
        teacher_keys,
        d_context,
        context,
        inverse,
        docs,
        small,
        active,
        bin_own,
        d_one,
        tokens,
        *flat,
    )
    grad_tokens, *rest = results
    early_sums = rest[: len(flat)]
    late_sums = rest[len(flat) : -3]
    shapes = [a.shape for arrays in early_arrays for a in arrays]
    return (
        grad_tokens,
        [e.reshape(shape) for e, shape in zip(early_sums, shapes)],
        [l.reshape(groups, depth, 3 * 128) for l in late_sums],
        list(rest[-3:]),
    )


def middle_kernel(
    streams,
    groups,
    bag,
    tiles,
    x_ref,
    tx_ref,
    cot_ref,
    ctx_ref,
    tctx_ref,
    bo_hbm,
    bup_hbm,
    bdown_hbm,
    to_hbm,
    tup_hbm,
    tdown_hbm,
    sg_ref,
    sb_ref,
    sub_ref,
    tg_ref,
    tb_ref,
    tub_ref,
    out_ref,
    d1_ref,
    dctx_ref,
    gout_ref,
    gup_ref,
    gdown_ref,
    small_ref,
    *rest,
):
    have = bag.bind(rest)
    gout_acc, gup_acc, gdown_acc = have["gout"], have["gup"], have["gdown"]
    out_box, d_box = have["out_box"], have["d_box"]
    step = pl.program_id(0)
    far = (to_hbm, bo_hbm, tup_hbm, bup_hbm, tdown_hbm, bdown_hbm)
    to_ref, bo_ref, tup_ref, bup_ref, tdown_ref, bdown_ref = near = [
        have[f"weight{i}"] for i in range(6)
    ]
    loads = [
        pltpu.make_async_copy(source, target, have["weight_sems"].at[i])
        for i, (source, target) in enumerate(zip(far, near))
    ]

    def ready(which):
        @pl.when(step == 0)
        def _():
            for i in which:
                loads[i].wait()

    steps = pl.num_programs(0)
    width = ctx_ref.shape[1] * 128
    tile, depth = cot_ref.shape
    n_steps = out_box.shape[0]
    shard = n_steps * tile // streams
    s, r = place(groups)
    along_z = stream_peers(streams, groups)
    turned = row_tile(step, n_steps, streams, groups)
    start = pl.multiple_of(turned * tile, tile)

    @pl.when(step == 0)
    def _():
        for copy in loads:
            copy.start()
        greet(along_z + core_peers(groups))

    @pl.when(step == 0)
    def _():
        for ref in (gout_acc, gup_acc, gdown_acc, small_ref):
            ref[...] = jnp.zeros_like(ref)

    def row(ref, i):
        return ref[i : i + 1, :]

    pieces = [(j, p) for j in range(groups) for p in range(ctx_ref.shape[1])]
    ff = bup_ref.shape[1]
    wide = min(512, ff)
    chunks = [slice(i, i + wide) for i in range(0, ff, wide)]

    ready((0, 1))
    tctx = jnp.concatenate([tctx_ref[j, p] for j, p in pieces], axis=1)
    t_att = dot(tctx, to_ref[...]) + row(tb_ref, 2)
    context = jnp.concatenate([ctx_ref[j, p] for j, p in pieces], axis=1).astype(F32)
    bent = jnp.tanh(context * (1.0 / clip_level))
    ctx_active = (clip_level * bent).astype(BF)
    ctx_slope = 1.0 - bent * bent
    attended = dot(ctx_active, bo_ref[...]) + row(sb_ref, 2)
    t_hidden = layer_norm(tx_ref[...].astype(F32) + t_att, row(tg_ref, 0), row(tb_ref, 3))[0]
    hidden, normed_one, inverse_one = layer_norm(
        x_ref[...].astype(F32) + attended, row(sg_ref, 0), row(sb_ref, 3)
    )
    bent = jnp.tanh(hidden * (1.0 / clip_level))
    hidden_active = (clip_level * bent).astype(BF)
    hidden_slope = 1.0 - bent * bent
    t_low = t_hidden.astype(BF)

    def up(i):
        return dot(t_low, tup_ref[:, chunks[i]]), dot(hidden_active, bup_ref[:, chunks[i]])

    ready((2, 3, 4, 5))
    ahead = up(0)
    t_branch, branch, actives, slopes = None, None, [], []
    for i, at in enumerate(chunks):
        t_pre, inner_pre = ahead
        if i + 1 < len(chunks):
            ahead = up(i + 1)
        t_inner = gelu_parts(t_pre + tub_ref[:, at])[0]
        inner_pre = inner_pre + sub_ref[:, at]
        inner_act, phi = gelu_parts(inner_pre)
        bent = jnp.tanh(inner_act * (1.0 / clip_level))
        inner_active = (clip_level * bent).astype(BF)
        t_term = dot(t_inner.astype(BF), tdown_ref[at, :])
        term = dot(inner_active, bdown_ref[at, :])
        t_branch = t_term if i == 0 else t_branch + t_term
        branch = term if i == 0 else branch + term
        actives.append(inner_active)
        slopes.append(
            (1.0 - bent * bent)
            * (phi + inner_pre * jnp.exp(-0.5 * inner_pre * inner_pre) * 0.3989422804014327)
        )
    t_out = layer_norm(t_hidden + t_branch + row(tb_ref, 4), row(tg_ref, 1), row(tb_ref, 5))[0]
    branch = branch + row(sb_ref, 4)
    output, normed_two, inverse_two = layer_norm(hidden + branch, row(sg_ref, 1), row(sb_ref, 5))
    out_box[step] = output.astype(BF)
    per_tile = tile // shard
    for n in range(per_tile):
        block = turned * per_tile + n
        source = out_box.at[step, pl.ds(n * shard, shard)]

        @pl.when(block == s)
        def _():
            pltpu.make_async_copy(source, out_ref.at[s], have["out_s"].at[s]).start()

        @pl.when(block != s)
        def _():
            remote(
                source,
                out_ref.at[s],
                have["out_s"].at[block],
                have["out_r"].at[s],
                {"blk": block * groups + r},
            ).start()
    upstream = cot_ref[...].astype(F32) + 0.5 * (output - t_out)
    d_two = norm_back(upstream, row(sg_ref, 1), normed_two, inverse_two)
    d_branch = d_two.astype(BF)

    def down(i):
        return dot(d_branch, bdown_ref[chunks[i], :], NT)

    ahead = down(0)
    through = None
    for i, at in enumerate(chunks):
        d_inner = ahead
        if i + 1 < len(chunks):
            ahead = down(i + 1)
        d_inner = (d_inner * slopes[i]).astype(BF)
        gdown_acc[at, :] += dot(actives[i], d_branch, TN)
        gup_acc[:, at] += dot(hidden_active, d_inner, TN)
        term = dot(d_inner, bup_ref[:, at], NT)
        through = term if i == 0 else through + term
        d_shift = jnp.sum(d_inner.astype(F32), axis=0, keepdims=True)
        for n in range(wide // depth):
            line = 8 + (i * wide) // depth + n
            small_ref[line : line + 1, :] += d_shift[:, n * depth : (n + 1) * depth]
    d_hidden = d_two + through * hidden_slope
    d_one = norm_back(d_hidden, row(sg_ref, 0), normed_one, inverse_one)
    d1_ref[...] = d_one
    d_attended = d_one.astype(BF)
    gout_acc[...] += dot(ctx_active, d_attended, TN)
    d_context = (dot(d_attended, bo_ref[...], NT) * ctx_slope).astype(BF)
    place_rows = pl.ds(pl.multiple_of(r * n_steps * tile + start, tile), tile)
    for j in range(groups):
        d_box[step, j] = d_context[:, j * width : (j + 1) * width]
        piece, target = d_box.at[step, j], dctx_ref.at[place_rows]

        @pl.when(r == j)
        def _():
            tiles.own(have, piece, target, 0, step).start()

        @pl.when(r != j)
        def _():
            tiles.copy(have, piece, target, j, 0, step).start()


    def total(value):
        return jnp.sum(value, axis=0, keepdims=True)

    sums = [
        (0, d_hidden * normed_one),
        (1, upstream * normed_two),
        (4, d_attended.astype(F32)),
        (5, d_hidden),
        (6, d_branch.astype(F32)),
        (7, upstream),
    ]
    for i, value in sums:
        small_ref[i : i + 1, :] += total(value)
    @pl.when(step == steps - 1)
    def _():
        writes = []
        for i, (total_ref, target) in enumerate(
            ((gdown_acc, gdown_ref), (gup_acc, gup_ref), (gout_acc, gout_ref))
        ):
            narrow = have[f"narrow{i}"]
            narrow[...] = total_ref[...].astype(BF)
            copy = pltpu.make_async_copy(narrow, target, have["narrow_sems"].at[i])
            copy.start()
            writes.append(copy)
        tiles.finish(have, d_box.at[0, 0], dctx_ref.at[place_rows])
        source = out_box.at[0, pl.ds(0, shard)]
        pltpu.make_async_copy(source, out_ref.at[s], have["out_s"].at[s]).wait()
        for d, peer in enumerate(along_z, 1):
            block = lax.rem(s + d, streams)
            remote(
                source, out_ref.at[block], have["out_s"].at[block], have["out_r"].at[block], peer
            ).wait()
        for copy in writes:
            copy.wait()


def row_tile(step, steps, streams, groups):
    s, r = place(groups)
    return lax.rem(s // (streams // steps) + 1 + step, steps)


def middle(streams, groups, x, tx, cot, ctx, tctx, weights, teacher_weights, vectors, collective_id):
    rows, depth = cot.shape
    ff = weights[1].shape[1]
    tile = min(256, rows)
    pairs = ctx.shape[1]
    width = pairs * 128
    steps = rows // tile
    shard = rows // streams

    def turn(i):
        return row_tile(i, steps, streams, groups)

    def stream_tile(i):
        return lax.rem(lax.axis_index("blk"), groups) * steps + turn(i)

    tall = pl.BlockSpec((tile, depth), lambda i: (turn(i), 0))
    of_stream = pl.BlockSpec((tile, depth), lambda i: (stream_tile(i), 0))
    split_rows = pl.BlockSpec((groups, pairs, tile, 128), lambda i: (0, 0, turn(i), 0))
    any_space = pl.BlockSpec(memory_space=pl.ANY)

    def full(shape):
        return pl.BlockSpec(shape, lambda i: (0,) * len(shape))

    out_full = [(depth, depth), (depth, ff), (ff, depth), (16, depth)]
    bag = Bag()
    for name, shape in zip(("gout", "gup", "gdown"), out_full):
        bag.add(name, pltpu.VMEM(shape, F32))
    for i in range(3):
        bag.add(f"weight{2 * i}", pltpu.VMEM(teacher_weights[i].shape, BF))
        bag.add(f"weight{2 * i + 1}", pltpu.VMEM(weights[i].shape, BF))
    bag.add("weight_sems", dma(6))
    for i in range(3):
        bag.add(f"narrow{i}", pltpu.VMEM(out_full[2 - i], BF))
    bag.add("narrow_sems", dma(3))
    bag.add("out_box", pltpu.VMEM((steps, tile, depth), BF))
    bag.add("d_box", pltpu.VMEM((steps, groups, tile, width), BF))
    bag.add("out_s", dma(streams))
    bag.add("out_r", dma(streams))
    tiles = Tiles(bag, "tiles", groups, 1, steps)
    return pl.pallas_call(
        functools.partial(middle_kernel, streams, groups, bag, tiles),
        grid=(steps,),
        in_specs=[of_stream, of_stream, tall, split_rows, split_rows]
        + [any_space] * 6
        + [full(a.shape) for a in vectors],
        out_specs=[any_space, tall, any_space] + [any_space] * 3 + [full(out_full[3])],
        out_shape=[
            jax.ShapeDtypeStruct((streams, shard, depth), BF),
            jax.ShapeDtypeStruct((rows, depth), F32),
            jax.ShapeDtypeStruct((rows * groups, width), BF),
        ]
        + [jax.ShapeDtypeStruct(s, BF if i < 3 else F32) for i, s in enumerate(out_full)],
        scratch_shapes=list(bag.items.values()),
        compiler_params=remote_params(collective_id),
        name="middle",
    )(x, tx, cot, ctx, tctx, *weights, *teacher_weights, *vectors)


def latent_columns(latent, grad, out):
    rows = latent.shape[0]
    size = min(256, rows)
    chunks = [slice(i, i + size) for i in range(0, rows, size)]
    squares = jnp.zeros((1, latent.shape[1]), F32)
    for at in chunks:
        matrix = latent[at, :].astype(F32)
        squares = squares + jnp.sum(matrix * matrix, axis=0, keepdims=True)
    scale = jnp.sqrt(squares * (1.0 / rows) + 1e-06)
    twice = 2.0 / scale
    through_scale = jnp.zeros_like(squares)
    for at in chunks:
        matrix, upstream = latent[at, :].astype(F32), grad[at, :].astype(F32)
        inner = matrix * twice
        bent = jnp.tanh(inner)
        slope = 1.0 - bent * bent
        through_scale = through_scale + jnp.sum(
            upstream * (bent - inner * slope), axis=0, keepdims=True
        )
        out[at, :] = upstream * (2.0 * slope)
    factor = through_scale / (rows * scale)
    for at in chunks:
        out[at, :] = out[at, :] + latent[at, :].astype(F32) * factor


def latent_grads_kernel(pairs, passed, lq, lo, lu, ld, *refs):
    late, (go, gu, gd, *refs) = refs[:pairs], refs[pairs:]
    come, (oq, oo, ou, od, *gone) = refs[:passed], refs[passed:]
    for source, target in zip(come, gone):
        target[...] = source[...]
    for p in range(pairs):

        @pl.when(lax.rem(pl.program_id(0), pairs) == p)
        def _():
            for i in range(3):
                latent_columns(lq.at[i], late[p].at[0, :, i * 128 : (i + 1) * 128], oq.at[i])

    latent_columns(lo, go, oo)
    latent_columns(ld, gd, od)
    for i in range(0, lu.shape[1], 128):
        at = slice(i, i + 128)
        latent_columns(lu.at[:, at], gu.at[:, at], ou.at[:, at])


def latent_grads(latents, late, early, tall, small):
    pairs = len(late)
    groups, depth, wide = late[0].shape
    steps = groups * pairs
    qkv = pl.BlockSpec((3, depth, depth // steps), lambda i: (0, 0, i))
    flat = [pl.BlockSpec((a.shape[0], a.shape[1] // steps), lambda i: (0, i)) for a in latents[1:]]
    handed = [
        pl.BlockSpec((a.shape[0] // steps,) + a.shape[1:], lambda i: (i, 0, 0)) for a in tall
    ] + [pl.BlockSpec(a.shape, lambda i: (0, 0)) for a in small]
    return pl.pallas_call(
        functools.partial(latent_grads_kernel, pairs, len(handed)),
        grid=(steps,),
        in_specs=[qkv]
        + flat
        + [pl.BlockSpec((1, depth, wide), lambda i: (i // pairs, 0, 0))] * pairs
        + flat
        + handed,
        out_specs=[qkv] + flat + handed,
        out_shape=[jax.ShapeDtypeStruct(a.shape, F32) for a in latents]
        + [jax.ShapeDtypeStruct(a.shape, a.dtype) for a in tall + small],
        compiler_params=pltpu.CompilerParams(vmem_limit_bytes=VMEM_BYTES),
        name="latent_grads",
    )(*latents, *late, *early, *tall, *small)


def shards(
    tokens,
    teacher_tokens,
    segment_ids,
    cotangent,
    latent_qkv,
    latent_out,
    latent_up,
    latent_down,
    student_gain,
    student_bias,
    student_up_bias,
    teacher_qkv,
    teacher_out,
    teacher_up,
    teacher_down,
    teacher_gain,
    teacher_bias,
    teacher_up_bias,
):
    streams, shard_len, depth = tokens.shape
    blocks = lax.axis_size("blk")
    groups = blocks // streams
    seq = shard_len * blocks
    rows = seq // groups
    block = (shard_len, depth)
    gather, swap = Gather(streams, groups, block, BF), Swap(streams, groups, block, BF)
    bin_own, bin_out, bin_up, bin_down, token_blocks, qkv_parts, docs = intake(
        Moves(
            gather,
            Spread(teacher_qkv.shape, BF),
            Gather(streams, groups, (8, shard_len), F32),
        ),
        groups,
        [latent_qkv, latent_out, latent_up, latent_down],
        segment_ids,
        [tokens, teacher_qkv],
        1,
    )
    stream_tokens = token_blocks.reshape(seq, depth)
    (
        queries,
        keys,
        ctx_rows,
        values,
        numerators,
        context,
        inverse,
        active,
        teacher_blocks,
        up_parts,
        out_parts,
    ) = attention(
        stream_tokens,
        bin_own,
        student_bias,
        docs,
        streams,
        groups,
        Moves(gather, Spread(teacher_up.shape, BF), Spread(teacher_out.shape, BF)),
        [teacher_tokens, teacher_up, teacher_out],
        True,
        2,
        "attention_student",
    )
    teacher_stream = teacher_blocks.reshape(seq, depth)
    teacher_queries, teacher_keys, tctx_rows, cot_blocks, down_parts = attention(
        teacher_stream,
        qkv_parts,
        teacher_bias,
        docs,
        streams,
        groups,
        Moves(swap, Spread(teacher_down.shape, BF), others=[gather]),
        [cotangent, teacher_down],
        False,
        3,
        "attention_teacher",
    )
    output, d_one, d_context, g_out, g_up, g_down, small = middle(
        streams,
        groups,
        stream_tokens,
        teacher_stream,
        cot_blocks.reshape(rows, depth),
        ctx_rows,
        tctx_rows,
        [bin_out, bin_up, bin_down],
        [
            out_parts.reshape(-1, depth),
            up_parts.reshape(depth, -1),
            down_parts.reshape(-1, depth),
        ],
        [
            student_gain,
            student_bias,
            student_up_bias.reshape(1, -1),
            teacher_gain,
            teacher_bias,
            teacher_up_bias.reshape(1, -1),
        ],
        4,
    )
    grads = [[g_up], [g_down, g_out]]
    in_kernel = depth % (16 * blocks * lax.axis_size("dp")) == 0
    grad_tokens, early, late, small = attention_back(
        streams,
        groups,
        numerators,
        queries,
        keys,
        values,
        teacher_queries,
        teacher_keys,
        d_context,
        context,
        inverse,
        docs,
        small,
        active,
        bin_own,
        d_one,
        token_blocks,
        grads if in_kernel else [],
        latent_up.shape[1],
        6,
    )
    if not in_kernel:
        early = lax.psum((g_up, g_down, g_out), ("dp", "blk"))
    grad_qkv, grad_out, grad_up, grad_down, output, grad_tokens, gain, bias, shift = latent_grads(
        [latent_qkv, latent_out, latent_up, latent_down],
        late,
        [early[2], early[0], early[1]],
        [output, grad_tokens],
        small,
    )
    return (
        output,
        grad_tokens,
        grad_qkv,
        grad_out,
        grad_up,
        grad_down,
        gain,
        bias,
        shift.reshape(-1),
    )


def solution(mesh):
    return jax.shard_map(
        shards,
        mesh=mesh,
        in_specs=(
            P("dp", "blk", None),
            P("dp", "blk", None),
            P("dp", "blk"),
            P("dp", "blk", None),
            P(),
            P(),
            P(),
            P(),
            P(),
            P(),
            P(),
            P(None, "dp", None),
            P("dp", None),
            P("dp", None),
            P("dp", None),
            P(),
            P(),
            P(),
        ),
        out_specs=(P("dp", "blk", None), P("dp", "blk", None), P(), P(), P(), P(), P(), P(), P()),
        check_vma=False,
    )
```

```python
import functools

import jax
import jax.numpy as jnp
from jax import lax
from jax.experimental import pallas as pl
from jax.experimental.pallas import tpu as pltpu
from jax.sharding import PartitionSpec as P

HEADS = 8
BF = jnp.bfloat16
F32 = jnp.float32
LOG2E = 1.4426950408889634
clip_level = 2.5
masked_score = -1e30
VMEM_BYTES = 56 << 20
MESH = pl.DeviceIdType.MESH
NT = (((1,), (1,)), ((), ()))
TN = (((0,), (0,)), ((), ()))


def squash(tensor):
    return clip_level * jnp.tanh(tensor * (1.0 / clip_level))


def gelu_parts(tensor):
    phi = 0.5 * (1.0 + lax.erf(tensor * 0.7071067811865476))
    return tensor * phi, phi


def binarize(matrix):
    column_scale = jnp.sqrt(jnp.mean(matrix * matrix, axis=-2, keepdims=True) + 1e-06)
    return column_scale * jnp.tanh(2.0 * matrix / column_scale)


def layer_norm(tensor, gain_row, shift_row):
    centre = tensor - jnp.mean(tensor, axis=-1, keepdims=True)
    inverse_std = lax.rsqrt(jnp.mean(centre * centre, axis=-1, keepdims=True) + 1e-05)
    normed = centre * inverse_std
    return (normed * gain_row + shift_row, normed, inverse_std)


def norm_back(upstream, gain_row, normed, inverse_std):
    scaled = upstream * gain_row
    return inverse_std * (
        scaled
        - jnp.mean(scaled, axis=-1, keepdims=True)
        - normed * jnp.mean(scaled * normed, axis=-1, keepdims=True)
    )


def dot(a, b, dims=(((1,), (0,)), ((), ()))):
    return lax.dot_general(a, b, dims, preferred_element_type=F32)


def latent_grad(latent, binary_grad):
    matrix = latent.astype(F32)
    unused, pullback = jax.vjp(binarize, matrix)
    return pullback(binary_grad)[0]


def place(groups):
    here = lax.axis_index("blk")
    return here // groups, lax.rem(here, groups)


def greet(peers):
    barrier = pltpu.get_barrier_semaphore()
    for peer in peers:
        pl.semaphore_signal(barrier, inc=1, device_id=peer, device_id_type=MESH)
    pl.semaphore_wait(barrier, len(peers))


def stream_peers(streams, groups):
    s, r = place(groups)
    return [{"blk": lax.rem(s + d, streams) * groups + r} for d in range(1, streams)]


def core_peers(groups):
    s, r = place(groups)
    return [{"blk": s * groups + lax.rem(r + j, groups)} for j in range(1, groups)]


def dp_peers():
    size = lax.axis_size("dp")
    here = lax.axis_index("dp")
    return [{"dp": lax.rem(here + d, size)} for d in range(1, size)]


def unique(jobs):
    peers, kinds = [], []
    for job in jobs:
        for kind, found in job.peers():
            if kind not in kinds:
                kinds.append(kind)
                peers += found
    return peers


def remote(source, target, send, recv, peer):
    return pltpu.make_async_remote_copy(
        src_ref=source,
        dst_ref=target,
        send_sem=send,
        recv_sem=recv,
        device_id=peer,
        device_id_type=MESH,
    )


def dma(count):
    return pltpu.SemaphoreType.DMA((count,))


class Staged:
    def __init__(self, source, target, stage, sems):
        self.load = pltpu.make_async_copy(source, stage, sems.at[0])
        self.store = pltpu.make_async_copy(stage, target, sems.at[1])

    def first(self):
        self.load.start()

    def last(self):
        self.load.wait()
        self.store.start()
        self.store.wait()


class Gather:
    def __init__(self, streams, groups, block, dtype):
        self.streams, self.groups, self.block, self.dtype = streams, groups, block, dtype

    def scratch(self):
        b, g = self.streams, self.groups
        return [dma(b), dma(b), dma(b * g), dma(b * g), pltpu.VMEM(self.block, self.dtype), dma(2)]

    def out_shape(self):
        return jax.ShapeDtypeStruct((self.streams * self.groups,) + self.block, self.dtype)

    def peers(self):
        return [
            ("stream", stream_peers(self.streams, self.groups)),
            ("core", core_peers(self.groups)),
        ]

    def parts(self, source, target, send, recv, share_send, share_recv, stage, sems):
        b, g = self.streams, self.groups
        s, r = place(g)
        peers, cores = stream_peers(b, g), core_peers(g)
        swaps = [
            remote(
                source.at[lax.rem(s + d, b)],
                target.at[r * b + s],
                send.at[d],
                recv.at[d],
                peers[d - 1],
            )
            for d in range(1, b)
        ]
        shares = [
            [
                remote(
                    source.at[s] if d == 0 else target.at[r * b + lax.rem(s + b - d, b)],
                    target.at[r * b + lax.rem(s + b - d, b)],
                    share_send.at[j * b + d],
                    share_recv.at[j * b + d],
                    cores[j - 1],
                )
                for j in range(1, g)
            ]
            for d in range(b)
        ]
        own = Staged(source.at[s], target.at[r * b + s], stage, sems)
        return swaps, shares, own

    def first(self, *refs):
        swaps, shares, own = self.parts(*refs)
        for copy in swaps:
            copy.start()
        own.first()
        for copy in shares[0]:
            copy.start()

    def middle(self, *refs):
        swaps, shares, own = self.parts(*refs)
        for d in [1, 3, 2] if self.streams == 4 else range(1, self.streams):
            swaps[d - 1].wait_recv()
            for copy in shares[d]:
                copy.start()

    def last(self, *refs):
        swaps, shares, own = self.parts(*refs)
        own.last()
        for row in shares:
            for copy in row:
                copy.wait()
        for copy in swaps:
            copy.wait_send()


class Swap:
    def __init__(self, streams, groups, block, dtype):
        self.streams, self.groups, self.block, self.dtype = streams, groups, block, dtype

    def scratch(self):
        return [dma(self.streams), dma(self.streams), pltpu.VMEM(self.block, self.dtype), dma(2)]

    def out_shape(self):
        return jax.ShapeDtypeStruct((self.streams,) + self.block, self.dtype)

    def peers(self):
        return [("stream", stream_peers(self.streams, self.groups))]

    def parts(self, source, target, send, recv, stage, sems):
        b, g = self.streams, self.groups
        s, r = place(g)
        peers = stream_peers(b, g)
        swaps = [
            remote(source.at[lax.rem(s + d, b)], target.at[s], send.at[d], recv.at[d], peers[d - 1])
            for d in range(1, b)
        ]
        return swaps, Staged(source.at[s], target.at[s], stage, sems)

    def first(self, *refs):
        swaps, own = self.parts(*refs)
        for copy in swaps:
            copy.start()
        own.first()

    def last(self, *refs):
        swaps, own = self.parts(*refs)
        own.last()
        for copy in swaps:
            copy.wait()


class Spread:
    def __init__(self, block, dtype):
        self.block, self.dtype = block, dtype

    def scratch(self):
        size = lax.axis_size("dp")
        return [dma(size), dma(size), pltpu.VMEM(self.block, self.dtype), dma(2)]

    def out_shape(self):
        return jax.ShapeDtypeStruct((lax.axis_size("dp"),) + self.block, self.dtype)

    def peers(self):
        return [("dp", dp_peers())]

    def parts(self, source, target, send, recv, stage, sems):
        here = lax.axis_index("dp")
        copies = [
            remote(source, target.at[here], send.at[d], recv.at[d], peer)
            for d, peer in enumerate(dp_peers(), 1)
        ]
        return copies, Staged(source, target.at[here], stage, sems)

    first = Swap.first
    last = Swap.last


class Tiles:
    def __init__(self, bag, name, groups, pairs, per_owner):
        self.name, self.groups, self.pairs, self.per_owner = name, groups, pairs, per_owner
        count = pairs * per_owner
        bag.add(f"{name}_s", dma(groups * count))
        bag.add(f"{name}_r", dma(groups * count))

    def slot(self, who, pair, at):
        return (who * self.pairs + pair) * self.per_owner + at

    def copy(self, have, source, target, owner, pair, at):
        s, r = place(self.groups)
        return remote(
            source,
            target,
            have[f"{self.name}_s"].at[self.slot(owner, pair, at)],
            have[f"{self.name}_r"].at[self.slot(r, pair, at)],
            {"blk": s * self.groups + owner},
        )

    def own(self, have, source, target, pair, at):
        s, r = place(self.groups)
        return pltpu.make_async_copy(
            source, target, have[f"{self.name}_s"].at[self.slot(r, pair, at)]
        )

    def finish(self, have, source, target):
        s, r = place(self.groups)
        for pair in range(self.pairs):
            for at in range(self.per_owner):
                self.own(have, source, target, pair, at).wait()
                for j in range(1, self.groups):
                    other = lax.rem(r + j, self.groups)
                    remote(
                        source,
                        target,
                        have[f"{self.name}_s"].at[self.slot(other, pair, at)],
                        have[f"{self.name}_r"].at[self.slot(other, pair, at)],
                        {"blk": s * self.groups + other},
                    ).wait()


class Bag:
    def __init__(self):
        self.items = {}

    def add(self, name, item):
        self.items[name] = item

    def bind(self, refs):
        return dict(zip(self.items, refs))


class Reduce:
    def __init__(self, bag, name, streams, groups, shapes, over_cores, two_step):
        self.name, self.streams, self.groups = name, streams, groups
        self.size = lax.axis_size("dp")
        self.over_cores = over_cores
        self.two_step = two_step and self.size == 4 and streams % 2 == 0
        self.count = len(shapes)
        share = self.size * (groups if over_cores else 1)
        self.shapes = [(rows // share, cols) for rows, cols in shapes]
        self.wires = [BF if (c // streams) % 16 == 0 else F32 for c, cols in self.shapes]
        for i, (chunk, cols) in enumerate(self.shapes):
            wire, slim = self.wires[i], chunk // streams
            bag.add(f"{name}half{i}", pltpu.VMEM((self.size, chunk, cols), wire))
            if over_cores:
                bag.add(f"{name}core{i}", pltpu.VMEM((groups - 1, self.size, chunk, cols), wire))
            if self.two_step:
                bag.add(f"{name}first{i}", pltpu.VMEM((4, chunk // 2, cols), wire))
                bag.add(f"{name}second{i}", pltpu.VMEM((2, chunk // 2, cols), wire))
            else:
                bag.add(f"{name}dp{i}", pltpu.VMEM((self.size - 1, chunk, cols), wire))
            bag.add(f"{name}cut{i}", pltpu.VMEM((streams, slim, cols), wire))
            bag.add(f"{name}z{i}", pltpu.VMEM((streams - 1, slim, cols), wire))
            bag.add(f"{name}fin{i}", pltpu.VMEM((slim, cols), wire))
            for kind in self.kinds():
                bag.add(f"{name}{kind}s{i}", dma(self.sem_count(kind)))
                bag.add(f"{name}{kind}r{i}", dma(self.sem_count(kind)))
            bag.add(f"{name}local{i}", dma(2))

    def kinds(self):
        along = ["b1", "b2", "c", "d", "e1", "e2"] if self.two_step else ["b", "c", "d", "e"]
        return (["a"] if self.over_cores else []) + along + ["f"]

    def sem_count(self, kind):
        if kind in ("a", "f"):
            return self.groups
        if kind in ("c", "d"):
            return self.streams
        return max(self.size, 4)

    def out_shapes(self):
        return [
            jax.ShapeDtypeStruct(
                (self.groups, self.size, self.streams, chunk // self.streams, cols), wire
            )
            for (chunk, cols), wire in zip(self.shapes, self.wires)
        ]

    def bind(self, sources, targets, scratch):
        self.sources, self.targets, self.scratch = sources, targets, scratch

    def get(self, what, i):
        return self.scratch[f"{self.name}{what}{i}"]

    def pairs(self, kind, i):
        s, r = place(self.groups)
        here = lax.axis_index("dp")
        b, g, size = self.streams, self.groups, self.size
        x, y = lax.rem(here, 2), here // 2
        beside_x, beside_y = {"dp": 2 * y + 1 - x}, {"dp": 2 * (1 - y) + x}
        if kind == "a":
            for d, peer in enumerate(core_peers(g), 1):
                yield d, self.sources[i].at[lax.rem(r + d, g)], self.get("core", i).at[d - 1], peer
        elif kind == "b":
            half, box = self.get("half", i), self.get("dp", i)
            for d, peer in enumerate(dp_peers(), 1):
                yield d, half.at[lax.rem(here + d, size)], box.at[d - 1], peer
        elif kind == "b1":
            half, box, h = self.get("half", i), self.get("first", i), self.shapes[i][0] // 2
            for n in range(2):
                yield n, half.at[2 * n + 1 - x, pl.ds(0, h)], box.at[n], beside_x
                yield 2 + n, half.at[2 * (1 - y) + n, pl.ds(h, h)], box.at[2 + n], beside_y
        elif kind == "b2":
            half, box, h = self.get("half", i), self.get("second", i), self.shapes[i][0] // 2
            yield 0, half.at[2 * (1 - y) + x, pl.ds(0, h)], box.at[0], beside_y
            yield 1, half.at[2 * y + 1 - x, pl.ds(h, h)], box.at[1], beside_x
        elif kind in "cd":
            peers = list(enumerate(stream_peers(b, g), 1))
            for d, peer in [peers[1], peers[0], peers[2]] if b == 4 else peers:
                if kind == "c":
                    cut = self.get("cut", i)
                    yield d, cut.at[lax.rem(s + d, b)], self.get("z", i).at[d - 1], peer
                else:
                    yield d, self.get("fin", i), self.targets[i].at[r, here, s], peer
        elif kind == "e":
            whole = self.targets[i].at[r, here]
            for d, peer in enumerate(dp_peers(), 1):
                yield d, whole, whole, peer
        elif kind == "e1":
            for n, peer in enumerate((beside_y, beside_x)):
                part = self.targets[i].at[r, here, pl.ds(n * b // 2, b // 2)]
                yield n, part, part, peer
        elif kind == "e2":
            for n in range(2):
                part = self.targets[i].at[r, 2 * n + x, pl.ds(0, b // 2)]
                yield n, part, part, beside_x
                part = self.targets[i].at[r, 2 * y + n, pl.ds(b // 2, b // 2)]
                yield 2 + n, part, part, beside_y
        else:
            whole = self.targets[i].at[r]
            for d, peer in enumerate(core_peers(g), 1):
                yield d, whole, whole, peer

    def copies(self, kind, i):
        send, recv = self.get(kind + "s", i), self.get(kind + "r", i)
        for n, source, target, peer in self.pairs(kind, i):
            yield remote(source, target, send.at[n], recv.at[n], peer)

    def start(self, kind, i):
        for copy in self.copies(kind, i):
            copy.start()

    def arrive(self, kind, i):
        for copy in self.copies(kind, i):
            copy.wait_recv()

    def load(self, i):
        s, r = place(self.groups)
        return pltpu.make_async_copy(
            self.sources[i].at[r], self.get("half", i), self.get("local", i).at[0]
        )

    def keep(self, i):
        s, r = place(self.groups)
        return pltpu.make_async_copy(
            self.get("fin", i),
            self.targets[i].at[r, lax.axis_index("dp"), s],
            self.get("local", i).at[1],
        )

    def stages(self):
        middle = [self.dp_middle] if self.two_step else []
        back = [self.dp_back_middle] if self.two_step else []
        return [self.dp_start, *middle, self.z_start, self.z_back, self.dp_back, *back, self.core_back]

    def core_start(self):
        for i in range(self.count):
            self.start("a", i)
            self.load(i).start()

    def dp_start(self):
        for i in range(self.count):
            if self.over_cores:
                self.load(i).wait()
                self.arrive("a", i)
                half, box, wire = self.get("half", i), self.get("core", i), self.wires[i]
                for p in range(self.size):
                    total = half[p].astype(F32)
                    for j in range(self.groups - 1):
                        total = total + box[j, p].astype(F32)
                    half[p] = total.astype(wire)
            self.start("b1" if self.two_step else "b", i)

    def dp_middle(self):
        here = lax.axis_index("dp")
        x, y = lax.rem(here, 2), here // 2
        for i in range(self.count):
            self.arrive("b1", i)
            half, box, wire = self.get("half", i), self.get("first", i), self.wires[i]
            h = self.shapes[i][0] // 2
            for n in range(2):
                for who, at, part in ((2 * n + x, pl.ds(0, h), n), (2 * y + n, pl.ds(h, h), 2 + n)):
                    total = half[who, at, :].astype(F32) + box[part].astype(F32)
                    half[who, at, :] = total.astype(wire)
            self.start("b2", i)

    def z_start(self):
        here = lax.axis_index("dp")
        for i in range(self.count):
            self.arrive("b2" if self.two_step else "b", i)
            half, cut, wire = self.get("half", i), self.get("cut", i), self.wires[i]
            chunk = self.shapes[i][0]
            slim = chunk // self.streams
            for z in range(self.streams):
                at = slice(z * slim, (z + 1) * slim)
                total = half[here, at, :].astype(F32)
                if self.two_step:
                    which, first = divmod(z * slim, chunk // 2)
                    total = total + self.get("second", i)[which, first : first + slim].astype(F32)
                else:
                    for d in range(self.size - 1):
                        total = total + self.get("dp", i)[d, at, :].astype(F32)
                cut[z] = total.astype(wire)
            self.start("c", i)

    def z_back(self):
        s, r = place(self.groups)
        for i in range(self.count):
            self.arrive("c", i)
            box = self.get("z", i)
            total = self.get("cut", i)[s].astype(F32)
            for d in range(self.streams - 1):
                total = total + box[d].astype(F32)
            self.get("fin", i)[...] = total.astype(self.wires[i])
            self.keep(i).start()
            self.start("d", i)

    def dp_back(self):
        for i in range(self.count):
            self.keep(i).wait()
            self.arrive("d", i)
            self.start("e1" if self.two_step else "e", i)

    def dp_back_middle(self):
        for i in range(self.count):
            self.arrive("e1", i)
            self.start("e2", i)

    def core_back(self):
        for i in range(self.count):
            self.arrive("e2" if self.two_step else "e", i)
            self.start("f", i)

    def end(self):
        for i in range(self.count):
            self.arrive("f", i)
            for kind in self.kinds():
                for copy in self.copies(kind, i):
                    copy.wait_send()


class Moves:
    def __init__(self, *jobs, others=()):
        self.jobs, self.others = list(jobs), list(others)
        self.counts = [len(job.scratch()) for job in jobs]

    def scratch(self):
        return [item for job in self.jobs for item in job.scratch()]

    def out_shapes(self):
        return [job.out_shape() for job in self.jobs]

    def spaces(self):
        return [pl.BlockSpec(memory_space=pl.ANY)] * len(self.jobs)

    def each(self, sources, targets, scratch):
        at = 0
        for job, count, source, target in zip(self.jobs, self.counts, sources, targets):
            yield job, (source, target, *scratch[at : at + count])
            at += count

    def first(self, sources, targets, scratch, count=None):
        greet(unique(self.jobs + self.others))
        for job, refs in list(self.each(sources, targets, scratch))[:count]:
            job.first(*refs)

    def start_last(self, sources, targets, scratch):
        for job, refs in list(self.each(sources, targets, scratch))[-1:]:
            job.first(*refs)

    def middle(self, sources, targets, scratch):
        for job, refs in self.each(sources, targets, scratch):
            if isinstance(job, Gather):
                job.middle(*refs)

    def last(self, sources, targets, scratch):
        for job, refs in self.each(sources, targets, scratch):
            job.last(*refs)


def remote_params(collective_id):
    return pltpu.CompilerParams(
        collective_id=collective_id, has_side_effects=True, vmem_limit_bytes=VMEM_BYTES
    )


def binary_columns(latent):
    matrix = latent.astype(F32)
    scale = jnp.sqrt(jnp.mean(matrix * matrix, axis=0, keepdims=True) + 1e-06)
    return (scale * jnp.tanh(matrix * (2.0 / scale))).astype(BF)


def intake_kernel(moves, groups, *refs):
    count = len(moves.jobs)
    latents, ids_ref, refs = refs[:4], refs[4], refs[5:]
    sources, refs = refs[: count - 1], refs[count - 1 :]
    results, refs = refs[:4], refs[4:]
    targets, refs = refs[:count], refs[count:]
    loaded, made, sems = refs[:4], refs[4:8], refs[8]
    ids_in, ids_box, *scratch = refs[9:]
    sources = (*sources, ids_box)
    moves.first(sources, targets, scratch, count - 1)
    s, r = place(groups)
    width = results[0].shape[3]
    own = pl.ds(pl.multiple_of(r * width, 128), width)
    places = [latents[0].at[:, :, own], *latents[1:]]
    loads = [
        pltpu.make_async_copy(source, target, sems.at[i])
        for i, (source, target) in enumerate(zip(places, loaded))
    ]
    stores = [
        pltpu.make_async_copy(source, target, sems.at[4 + i])
        for i, (source, target) in enumerate(zip(made, [results[0].at[0], *results[1:]]))
    ]
    fetch = pltpu.make_async_copy(ids_ref, ids_in, sems.at[8])
    fetch.start()
    for copy in loads:
        copy.start()
    fetch.wait()
    ids = ids_in[...].astype(F32)
    for i in range(ids.shape[0]):
        ids_box[i] = jnp.broadcast_to(ids[i : i + 1, :], ids_box.shape[1:])
    moves.start_last(sources, targets, scratch)
    loads[0].wait()
    for i in range(3):
        made[0][i] = binary_columns(loaded[0][i])
    stores[0].start()
    for n in range(1, 4):
        loads[n].wait()
        for i in range(0, loaded[n].shape[1], 128):
            made[n][:, i : i + 128] = binary_columns(loaded[n][:, i : i + 128])
        stores[n].start()
    moves.middle(sources, targets, scratch)
    for copy in stores:
        copy.wait()
    moves.last(sources, targets, scratch)


def intake(moves, groups, latents, ids, arrays, collective_id):
    three, depth, unused = latents[0].shape
    own_shape = (three, depth, depth // groups)
    shapes = [(1,) + own_shape] + [a.shape for a in latents[1:]]
    buffers = [pltpu.VMEM(shape, BF) for shape in [own_shape] + shapes[1:]]
    any_space = [pl.BlockSpec(memory_space=pl.ANY)] * 4
    return pl.pallas_call(
        functools.partial(intake_kernel, moves, groups),
        out_shape=[jax.ShapeDtypeStruct(shape, BF) for shape in shapes] + moves.out_shapes(),
        in_specs=any_space
        + moves.spaces(),
        out_specs=any_space + moves.spaces(),
        scratch_shapes=buffers * 2
        + [dma(9), pltpu.VMEM(ids.shape, ids.dtype)]
        + [pltpu.VMEM((ids.shape[0], 8, ids.shape[1]), F32)]
        + moves.scratch(),
        compiler_params=remote_params(collective_id),
        name="intake",
    )(*latents, ids, *arrays)


def lanes_of(shape):
    return lax.broadcasted_iota(jnp.int32, shape, 1)


def forward_kernel(
    moves, keep, streams, groups, tile, bag, tiles, x_ref, w_ref, bias_ref, docs_ref, *rest
):
    count = len(moves.jobs)
    sources, rest = rest[:count], rest[count:]
    q_out, k_out, rows_ref, *rest = rest
    if keep:
        v_out, e_ref, ctx_ref, inv_ref, active_ref, *rest = rest
    targets, rest = rest[:count], rest[count:]
    have = bag.bind(rest)
    scratch = tuple(have[f"moves{i}"] for i in range(len(moves.scratch())))
    k_aug, v_aug, ctx_all, mask, edges = (
        have["k_aug"],
        have["v_aug"],
        have["ctx_all"],
        have["mask"],
        have["edges"],
    )
    active = have["active"] if keep else x_ref
    row_ref = have["row"]
    pair, step = pl.program_id(0), pl.program_id(1)
    pairs, steps = pl.num_programs(0), pl.num_programs(1)
    seq = k_aug.shape[1]
    kept = have["kept"]
    q_ref, k_ref = kept.at[0, pair], kept.at[1, pair]
    outputs = [q_out, k_out, v_out] if keep else [q_out, k_out]

    def writes(p):
        columns = pl.ds(pl.multiple_of(p * 128, 128), 128)
        return [
            pltpu.make_async_copy(kept.at[i, p], target.at[:, columns], have["kept_sems"].at[i, p])
            for i, target in enumerate(outputs)
        ]

    s, r = place(groups)
    sub = min(256, tile)
    width = w_ref.shape[3]
    n_pairs = ctx_all.shape[0]
    offset = pair * 128 if width == n_pairs * 128 else (r * n_pairs + pair) * 128
    offset = pl.multiple_of(offset, 128)
    home = pl.multiple_of((r * n_pairs + pair) * 128, 128)

    @pl.when((pair == 0) & (step == 0))
    def _():
        moves.first(sources, targets, scratch)
        ids = stream_row(docs_ref)
        row_ref[...] = ids
        big_at = long_at(streams, groups, seq)
        big = ids[:, big_at : big_at + 1]
        mask[...] = jnp.where(ids == big, 0.0, masked_score)
        edges[0] = jnp.broadcast_to(ids[:, :sub], (128, sub)).T
        edges[1] = jnp.broadcast_to(ids[:, seq - sub :], (128, sub)).T
        if keep:
            for i in range(0, seq, 256):
                active[i : i + 256, :] = squash(x_ref[i : i + 256, :].astype(F32)).astype(BF)
            pltpu.make_async_copy(active, active_ref, have["active_sem"].at[0]).start()

    @pl.when((pair == pairs - 1) & (step == steps - 2))
    def _():
        moves.middle(sources, targets, scratch)

    @pl.when(step == 0)
    def _():
        columns = pl.ds(offset, 128)

        def project(i, bias):
            matrix = jnp.concatenate(
                [w_ref[d, i, :, columns] for d in range(w_ref.shape[0])], axis=0
            )
            result = dot(active[...], matrix)
            if bias is not None:
                result = result + bias_ref[bias : bias + 1, pl.ds(home, 128)]
            return result.astype(BF)

        low = lanes_of((seq, 128)) < 64
        lane = lanes_of((seq, 128))
        q_ref[...] = (project(0, 0).astype(F32) * 0.125).astype(BF)
        keys = project(1, None)
        k_ref[...] = keys
        keys = keys.astype(F32)
        turned = pltpu.roll(keys, 64, 1)
        k_aug[0] = jnp.where(low, keys, turned).astype(BF)
        k_aug[1] = jnp.where(low, turned, keys).astype(BF)
        values = project(2, 1)
        if keep:
            kept[2, pair] = values
        for copy in writes(pair):
            copy.start()
        values = values.astype(F32)
        v_aug[0] = jnp.where(low, values, jnp.where(lane < 66, 1.0, 0.0)).astype(BF)
        v_aug[1] = jnp.where(low, jnp.where(lane < 2, 1.0, 0.0), values).astype(BF)

    turned = own_rows_last(step, seq, tile, groups)
    start = pl.multiple_of(turned * tile, tile)

    def body(edge_at):
        low = lanes_of((sub, 128)) < 64
        parts = []
        for at in range(0, tile, sub):
            scaled = q_ref[pl.ds(start + at, sub), :].astype(F32) * LOG2E
            upper = scaled.astype(BF).astype(F32)
            lower = scaled - upper
            parts.append(
                (
                    jnp.where(low, upper, pltpu.roll(lower, 64, 1)).astype(BF),
                    jnp.where(low, pltpu.roll(upper, 64, 1), lower).astype(BF),
                )
            )
        chains = [(at, h) for at in range(0, tile, sub) for h in range(2)]

        def scores_of(at, h):
            scores = dot(parts[at // sub][h], k_aug[h], NT)
            if edge_at is not None and at == (0 if edge_at == 0 else tile - sub):
                return jnp.where(edges[edge_at][:, :1] == row_ref[...], scores, masked_score)
            return jnp.concatenate(
                [
                    scores[:, :sub] + mask[:, :sub],
                    scores[:, sub : seq - sub],
                    scores[:, seq - sub :] + mask[:, seq - sub :],
                ],
                axis=1,
            )

        scores = scores_of(*chains[0])
        results = {}
        for n, (at, h) in enumerate(chains):
            if n + 1 < len(chains):
                later = scores_of(*chains[n + 1])
            peak = jnp.max(scores, axis=1, keepdims=True)
            numerators = jnp.exp2(scores - peak).astype(BF)
            if keep:
                e_ref[h, at : at + sub, :] = numerators
            total = dot(numerators, v_aug[h])
            where_sum = 64 if h == 0 else 0
            inverse = 1.0 / total[:, where_sum : where_sum + 1]
            results[h] = (total * inverse, inverse)
            if n + 1 < len(chains):
                scores = later
            if h == 1:
                done = jnp.where(low, results[0][0], results[1][0]).astype(BF)
                ctx_all[pair, pl.ds(start + at, sub), :] = done
                if keep:
                    ctx_ref[at : at + sub, :] = done
                    inv_ref[at : at + sub, :] = jnp.where(low, results[0][1], results[1][1])

    @pl.when(turned == 0)
    def _():
        body(0)

    @pl.when(turned == steps - 1)
    def _():
        body(1)

    @pl.when((turned > 0) & (turned < steps - 1))
    def _():
        body(None)

    owned = seq // groups
    owner = start // owned
    at = lax.rem(turned, owned // tile)
    source = ctx_all.at[pair, pl.ds(start, tile)]
    target = rows_ref.at[r, pair, pl.ds(pl.multiple_of(lax.rem(start, owned), tile), tile)]

    @pl.when(owner == r)
    def _():
        tiles.own(have, source, target, pair, at).start()

    @pl.when(owner != r)
    def _():
        tiles.copy(have, source, target, owner, pair, at).start()

    @pl.when((pair == pairs - 1) & (step == steps - 1))
    def _():
        tiles.finish(have, source, target)
        moves.last(sources, targets, scratch)
        for p in range(n_pairs):
            for copy in writes(p):
                copy.wait()
        if keep:
            pltpu.make_async_copy(active, active_ref, have["active_sem"].at[0]).wait()


def own_rows_last(step, seq, tile, groups):
    s, r = place(groups)
    steps = seq // tile
    return lax.rem(step + (r + 1) * (steps // groups), steps)


def stream_row(docs_ref):
    return jnp.concatenate([docs_ref[i, 0:1, :] for i in range(docs_ref.shape[0])], axis=1)


def long_at(streams, groups, seq):
    shard = seq // (streams * groups)
    return streams * shard if groups > 1 else shard


def attention(x, weights, bias, docs, streams, groups, moves, moved, keep, collective_id, name):
    seq, depth = x.shape
    width = depth // groups
    pairs = width // 128
    tile = 512
    owned = seq // groups
    bag = Bag()
    bag.add("k_aug", pltpu.VMEM((2, seq, 128), BF))
    bag.add("v_aug", pltpu.VMEM((2, seq, 128), BF))
    bag.add("ctx_all", pltpu.VMEM((pairs, seq, 128), BF))
    bag.add("mask", pltpu.VMEM((1, seq), F32))
    bag.add("row", pltpu.VMEM((1, seq), F32))
    bag.add("kept", pltpu.VMEM((3 if keep else 2, pairs, seq, 128), BF))
    bag.add("kept_sems", pltpu.SemaphoreType.DMA((3, pairs)))
    if keep:
        bag.add("active", pltpu.VMEM((seq, depth), BF))
        bag.add("active_sem", dma(1))
    bag.add("edges", pltpu.VMEM((2, 256, 128), F32))
    tiles = Tiles(bag, "tiles", groups, pairs, owned // tile)
    for i, item in enumerate(moves.scratch()):
        bag.add(f"moves{i}", item)

    def constant(shape):
        return pl.BlockSpec(shape, lambda p, i: (0,) * len(shape))

    def turn(i):
        return own_rows_last(i, seq, tile, groups)

    part = pl.BlockSpec((tile, 128), lambda p, i: (turn(i), p))
    any_space = pl.BlockSpec(memory_space=pl.ANY)
    wide = jax.ShapeDtypeStruct((seq, width), BF)
    outs = [any_space, any_space, any_space]
    shapes = [wide, wide, jax.ShapeDtypeStruct((groups, pairs, owned, 128), BF)]
    if keep:
        outs += [
            any_space,
            pl.BlockSpec((2, tile, seq), lambda p, i: (p, turn(i), 0)),
            part,
            part,
            any_space,
        ]
        shapes += [
            wide,
            jax.ShapeDtypeStruct((2 * pairs, seq, seq), BF),
            wide,
            jax.ShapeDtypeStruct((seq, width), F32),
            jax.ShapeDtypeStruct((seq, depth), BF),
        ]
    return pl.pallas_call(
        functools.partial(forward_kernel, moves, keep, streams, groups, tile, bag, tiles),
        grid=(pairs, seq // tile),
        in_specs=[constant(a.shape) for a in (x, weights, bias, docs)]
        + moves.spaces(),
        out_specs=outs + moves.spaces(),
        out_shape=shapes + moves.out_shapes(),
        scratch_shapes=list(bag.items.values()),
        compiler_params=remote_params(collective_id),
        name=name,
    )(x, weights, bias, docs, *moved)


def split(matrix):
    upper = matrix.astype(BF)
    return upper, (matrix - upper.astype(F32)).astype(BF)


def backward_kernel(
    streams,
    groups,
    tile,
    bag,
    early,
    late,
    e_ref,
    q_ref,
    k_ref,
    v_ref,
    tq_ref,
    tk_ref,
    dc_ref,
    ctx_ref,
    inv_ref,
    docs_ref,
    small_ref,
    active_hbm,
    bin_hbm,
    d1_hbm,
    tokens_hbm,
    *rest,
):
    n_early = sum(job.count for job in early)
    sources, rest = rest[:n_early], rest[n_early:]
    grad_ref, *rest = rest
    early_out, rest = rest[:n_early], rest[n_early:]
    late_out, (gain_ref, bias_ref, shift_ref, *rest) = rest[: len(late)], rest[len(late) :]
    have = bag.bind(rest)
    at = 0
    for job in early:
        job.bind(sources[at : at + job.count], early_out[at : at + job.count], have)
        at += job.count
    for job, target in zip(late, late_out):
        job.bind(None, [target], have)

    pair, step = pl.program_id(0), pl.program_id(1)
    pairs, steps = len(late), q_ref.shape[0] // tile
    sub = min(256, tile)
    seq = k_ref.shape[0]
    share = 1.0 / seq
    time = pair * steps + step
    total_time = pairs * steps
    size = lax.axis_size("dp")
    here = lax.axis_index("dp")
    s, r = place(groups)
    rows, depth = d1_hbm.shape
    width = pairs * 128
    v_aug, dk_acc, dv_acc, grams = have["v_aug"], have["dk_acc"], have["dv_acc"], have["grams"]
    dq_all, d_act, active, weights = have["dq_all"], have["d_act"], have["active"], have["weights"]
    d_one, x_rows = have["d_one"], have["x_rows"]
    edges, in_big, pair_box = have["edges"], have["in_big"], have["pair_box"]
    row_ref = have["row"]
    along_z, cores, along_dp = stream_peers(streams, groups), core_peers(groups), dp_peers()

    def loads():
        sems = have["load"]
        return [
            pltpu.make_async_copy(active_hbm, active, sems.at[0]),
            pltpu.make_async_copy(bin_hbm, weights, sems.at[1]),
            pltpu.make_async_copy(d1_hbm, d_one, sems.at[2]),
            pltpu.make_async_copy(tokens_hbm.at[pl.ds(r * streams, streams)], x_rows, sems.at[3]),
        ]

    halves = tile // sub
    plan = []

    def at_time(when, work):
        plan.append((when, work))

    def due(half):
        for when, work in plan:
            if when % halves == half:
                pl.when(time == when // halves)(work)

    def begin():
        greet(along_z + cores + along_dp)
        for job in early:
            job.core_start()
        for copy in loads():
            copy.start()
        ids = stream_row(docs_ref)
        row_ref[...] = ids
        big_at = long_at(streams, groups, seq)
        big = ids[:, big_at : big_at + 1]
        for n, first in enumerate((0, seq - sub)):
            column = jnp.broadcast_to(ids[:, first : first + sub], (128, sub)).T
            edges[n] = column
            in_big[n] = jnp.where(column == big, 1.0, 0.0)

    def big_rows(ref):
        return jnp.concatenate(
            [
                (ref[:sub, :].astype(F32) * in_big[0]).astype(BF),
                ref[sub : seq - sub, :],
                (ref[seq - sub :, :].astype(F32) * in_big[1]).astype(BF),
            ],
            axis=0,
        )

    at_time(0, begin)
    unit = total_time * halves / 16
    left = []
    for n, job in enumerate(early):
        stages, times = job.stages(), EARLY_TIMES[n]
        if not job.two_step:
            times = times[:1] + times[2:5] + times[6:]
        for when, work in zip(times, stages):
            at_time(int(when * unit), work)
        left.append(stages[len(times) :])
    for p, job in enumerate(late[:-1]):
        first = (p + 1) * steps * halves
        for when, work in zip(LATE_TIMES, job.stages()):
            at_time(first + when, work)
        left.append(job.stages()[len(LATE_TIMES) :])

    def go_on(count):
        for unused in range(count):
            for queue in left:
                if queue:
                    queue.pop(0)()

    due(0)

    @pl.when(step == 0)
    def _():
        lane = lanes_of((seq, 128))
        low = lane < 64
        values = v_ref[...].astype(F32)
        v_aug[0] = jnp.where(low, values, jnp.where(lane < 66, 1.0, 0.0)).astype(BF)
        v_aug[1] = jnp.where(low, jnp.where(lane < 2, 1.0, 0.0), values).astype(BF)
        dk_acc[...] = jnp.zeros_like(dk_acc)
        dv_acc[...] = jnp.zeros_like(dv_acc)
        kb, tkb, qb, tqb = (big_rows(ref) for ref in (k_ref, tk_ref, q_ref, tq_ref))
        same_head = (lax.broadcasted_iota(jnp.int32, (128, 128), 0) < 64) == (
            lanes_of((128, 128)) < 64
        )
        for i, (a, b) in enumerate(((kb, kb), (tkb, kb), (qb, qb), (tqb, qb))):
            gram = jnp.where(same_head, dot(a, b, TN) * share, 0.0)
            grams[2 * i], grams[2 * i + 1] = split(gram)

    start = pl.multiple_of(step * tile, tile)
    low = lanes_of((sub, 128)) < 64
    lane = lanes_of((sub, 128))

    def prepare(at):
        here_rows = pl.ds(start + at, sub)
        q8, tq8 = q_ref[here_rows, :], tq_ref[here_rows, :]
        scaled = dc_ref[at : at + sub, :].astype(F32) * inv_ref[at : at + sub, :]
        product = scaled * ctx_ref[at : at + sub, :].astype(F32)
        augmented = []
        for h in range(2):
            mine = low if h == 0 else jnp.logical_not(low)
            delta = -jnp.sum(jnp.where(mine, product, 0.0), axis=1, keepdims=True)
            upper = delta.astype(BF).astype(F32)
            first = 64 if h == 0 else 0
            extra = jnp.where(
                lane == first, upper, jnp.where(lane == first + 1, delta - upper, 0.0)
            )
            augmented.append(jnp.where(mine, scaled, extra).astype(BF))
        q_turned = q8.astype(F32).T.astype(BF)
        dc_turned = scaled.T.astype(BF)
        return here_rows, q8, tq8, augmented, q_turned, dc_turned

    def body(edge, half):
        ready = {half * sub: prepare(half * sub)}
        chains = [(half * sub, h) for h in range(2)]
        edge_at = {None: None, 0: 0, 1: tile - sub}[edge]
        columns = slice(0, sub) if edge == 0 else slice(seq - sub, seq)

        def d_probs_of(at, h):
            return dot(ready[at][3][h], v_aug[h], NT)

        d_probs = d_probs_of(*chains[0])
        d_queries = {}
        for n, (at, h) in enumerate(chains):
            if n + 1 < len(chains):
                later = d_probs_of(*chains[n + 1])
            here_rows, q8, tq8, unused, q_turned, dc_turned = ready[at]
            mine = low if h == 0 else jnp.logical_not(low)
            numerators = e_ref[h, at : at + sub, :]
            d_scores = numerators.astype(F32) * d_probs
            if edge is not None and at == edge_at:
                q_mine = jnp.where(mine, q8, 0.0).astype(BF)
                tq_mine = jnp.where(mine, tq8, 0.0).astype(BF)
                gap = dot(q_mine, k_ref[columns, :], NT) - dot(tq_mine, tk_ref[columns, :], NT)
                same = jnp.where(edges[edge][:, :1] == row_ref[:, columns], share, 0.0)
                gap = gap * (same * (1.0 - in_big[edge][:, :1]))
                if edge == 0:
                    d_scores = jnp.concatenate(
                        [d_scores[:, :sub] + gap, d_scores[:, sub:]], axis=1
                    )
                else:
                    d_scores = jnp.concatenate(
                        [d_scores[:, : seq - sub], d_scores[:, seq - sub :] + gap], axis=1
                    )
            d_scores = d_scores.astype(BF)
            mine = slice(64 * h, 64 * h + 64)
            dv_acc[mine, :] += dot(dc_turned[mine, :], numerators)
            d_queries[h] = dot(d_scores, k_ref[...])
            dk_acc[mine, :] += dot(q_turned[mine, :], d_scores)
            if h == 1:
                d_query = jnp.where(low, d_queries[0], d_queries[1])
                qb, tqb = q8, tq8
                if edge is not None and at == edge_at:
                    qb = (q8.astype(F32) * in_big[edge]).astype(BF)
                    tqb = (tq8.astype(F32) * in_big[edge]).astype(BF)
                d_query += dot(qb, grams[0]) + dot(qb, grams[1])
                d_query -= dot(tqb, grams[2]) + dot(tqb, grams[3])
                dq_all[here_rows, :] = (d_query * 0.125).astype(BF)
            if n + 1 < len(chains):
                d_probs = later

    for half in range(halves):
        if half:
            due(half)
        edge, at_edge = None, None
        if half == 0:
            edge, at_edge = 0, step == 0
        elif half == halves - 1:
            edge, at_edge = 1, step == steps - 1
        if edge is not None:
            pl.when(at_edge)(functools.partial(body, edge, half))
            pl.when(jnp.logical_not(at_edge))(functools.partial(body, None, half))
        else:
            body(None, half)

    def pair_end(p):
        job = late[p]
        kb, tkb = big_rows(k_ref), big_rows(tk_ref)
        d_key = dk_acc[...].T
        d_key += dot(kb, grams[4]) + dot(kb, grams[5]) - dot(tkb, grams[6]) - dot(tkb, grams[7])
        d_value = dv_acc[...].T.astype(BF)
        d_query = dq_all[...]
        d_pair = jnp.concatenate([d_query, d_key.astype(BF), d_value], axis=1)
        if p == 0:
            for copy in loads():
                copy.wait()
        columns = slice(p * 128, (p + 1) * 128)
        bins = jnp.concatenate([weights[0, i, :, columns] for i in range(3)], axis=1)
        chunk = depth // size
        half = job.get("half", 0)
        partial = dot(active[...], d_pair, TN).astype(job.wires[0])
        for d in range(size):
            half[d] = partial[d * chunk : (d + 1) * chunk, :]
        if p == pairs - 1:
            job.dp_start()
        if p < pairs - 1:
            if p == 0:
                d_act[...] = dot(d_pair, bins, NT)
            else:
                d_act[...] += dot(d_pair, bins, NT)
        else:
            pair_box[...] = d_pair
            for j in range(1, groups + 1):
                at = pl.ds(pl.multiple_of(lax.rem(r + j, groups) * rows, rows), rows)
                total = dot(pair_box[at, :], bins, NT)
                if p > 0:
                    total = total + d_act[at, :]
                if j < groups:
                    have["outbox"][j - 1] = total.astype(BF)
                    core_copies()[j - 1].start()
                else:
                    d_act[at, :] = total
        sums = have["sums"]
        sums[0:1, columns] = jnp.sum(d_query.astype(F32), axis=0, keepdims=True)
        sums[1:2, columns] = jnp.sum(d_value.astype(F32), axis=0, keepdims=True)

    def core_copies():
        return [
            remote(
                have["outbox"].at[j - 1],
                have["inbox"].at[j - 1],
                have["core_s"].at[j],
                have["core_r"].at[j],
                cores[j - 1],
            )
            for j in range(1, groups)
        ]

    def small_copies(stage, peers, base):
        return [
            remote(
                have["small"].at[stage],
                have["small_box"].at[base + d],
                have["small_s"].at[base + d],
                have["small_r"].at[base + d],
                peer,
            )
            for d, peer in enumerate(peers)
        ]

    def small_start(stage, peers, base):
        for copy in small_copies(stage, peers, base):
            copy.start()

    def small_sum(stage, peers, base):
        for copy in small_copies(stage, peers, base):
            copy.wait_recv()
        total = have["small"][stage]
        for d in range(len(peers)):
            total = total + have["small_box"][base + d]
        return total

    for p in range(pairs - 1):

        @pl.when((pair == p) & (step == steps - 1))
        def _():
            pair_end(p)

    @pl.when(time == total_time - 1)
    def _():
        pair_end(pairs - 1)
        last = late[-1]
        small = have["small"]
        small[0] = small_ref[...]
        for i in range(2):
            vector = have["sums"][i : i + 1, :]
            small[0, 2 + i : 3 + i, :] = jnp.concatenate(
                [jnp.where(r == j, vector, 0.0) for j in range(groups)], axis=1
            )
        small_start(0, along_dp, 0)
        go_on(TAIL[0])
        last.z_start()
        last.z_back()
        for copy in core_copies():
            copy.wait_recv()
        shard = rows // streams
        back_copies = []
        blocks = have["blocks"]
        order = [2, 1, 3] if streams == 4 else list(range(1, streams))
        for d in order + [0]:
            target = lax.rem(s + d, streams)
            here_rows = pl.ds(pl.multiple_of(target * shard, shard), shard)
            bent = jnp.tanh(x_rows[target].astype(F32) * (1.0 / clip_level))
            total = d_act[pl.ds(pl.multiple_of(r * rows + target * shard, shard), shard), :]
            for j in range(groups - 1):
                total = total + have["inbox"][j, here_rows, :].astype(F32)
            blocks[target] = (d_one[here_rows, :] + total * (1.0 - bent * bent)).astype(BF)
            if d:
                copy = remote(
                    blocks.at[target],
                    grad_ref.at[s],
                    have["grad_s"].at[d],
                    have["grad_r"].at[d],
                    along_z[d - 1],
                )
            else:
                copy = pltpu.make_async_copy(blocks.at[s], grad_ref.at[s], have["grad_s"].at[0])
            copy.start()
            back_copies.append(copy)
        small[1] = small_sum(0, along_dp, 0)
        small_start(1, along_z, size)
        go_on(TAIL[1])
        small[2] = small_sum(1, along_z, size)
        small_start(2, cores, size + streams)
        go_on(TAIL[2])
        last.dp_back()
        summed = small_sum(2, cores, size + streams)
        gain_ref[...] = summed[0:2, :]
        bias_ref[...] = summed[2:8, :]
        for i in range(shift_ref.shape[1] // depth):
            shift_ref[:, i * depth : (i + 1) * depth] = summed[8 + i : 9 + i, :]
        go_on(TAIL[3])
        last.core_back()
        go_on(8)
        for copy in back_copies:
            copy.wait()
        for job in early + late:
            job.end()
        for copy in (
            core_copies()
            + small_copies(0, along_dp, 0)
            + small_copies(1, along_z, size)
            + small_copies(2, cores, size + streams)
        ):
            copy.wait_send()


TWO_STEP = False
TAIL = (1, 1, 0, 0)
EARLY_TIMES = ((2, 0, 7, 9, 12), (4, 0, 12, 14))
LATE_TIMES = (0, 5, 7)


def attention_back(
    streams,
    groups,
    numerators,
    queries,
    keys,
    values,
    teacher_queries,
    teacher_keys,
    d_context,
    context,
    inverse,
    docs,
    small,
    active,
    bin_own,
    d_one,
    tokens,
    early_arrays,
    up_width,
    collective_id,
):
    seq, width = queries.shape
    pairs = width // 128
    tile = 512
    rows, depth = d_one.shape
    size = lax.axis_size("dp")
    shard = rows // streams
    bag = Bag()
    bag.add("v_aug", pltpu.VMEM((2, seq, 128), BF))
    bag.add("dk_acc", pltpu.VMEM((128, seq), F32))
    bag.add("dv_acc", pltpu.VMEM((128, seq), F32))
    bag.add("grams", pltpu.VMEM((8, 128, 128), BF))
    bag.add("dq_all", pltpu.VMEM((seq, 128), BF))
    bag.add("d_act", pltpu.VMEM((seq, depth), F32))
    bag.add("active", pltpu.VMEM((seq, depth), BF))
    bag.add("weights", pltpu.VMEM((1, 3, depth, width), BF))
    bag.add("d_one", pltpu.VMEM((rows, depth), F32))
    bag.add("x_rows", pltpu.VMEM((streams, shard, depth), BF))
    bag.add("load", dma(4))
    bag.add("sums", pltpu.VMEM((8, width), F32))
    bag.add("outbox", pltpu.VMEM((groups - 1, rows, depth), BF))
    bag.add("inbox", pltpu.VMEM((groups - 1, rows, depth), BF))
    bag.add("core_s", dma(groups))
    bag.add("core_r", dma(groups))
    bag.add("blocks", pltpu.VMEM((streams, shard, depth), BF))
    bag.add("grad_s", dma(streams))
    bag.add("grad_r", dma(streams))
    count = size + streams + groups
    bag.add("small", pltpu.VMEM((3,) + small.shape, F32))
    bag.add("small_box", pltpu.VMEM((count,) + small.shape, F32))
    bag.add("small_s", dma(count))
    bag.add("small_r", dma(count))
    bag.add("row", pltpu.VMEM((1, seq), F32))
    bag.add("pair_box", pltpu.VMEM((seq, 3 * 128), BF))
    bag.add("edges", pltpu.VMEM((2, 256, 128), F32))
    bag.add("in_big", pltpu.VMEM((2, 256, 128), F32))
    early, flat = [], []
    for n, arrays in enumerate(early_arrays):
        job = Reduce(bag, f"early{n}", streams, groups, [a.shape for a in arrays], True, TWO_STEP)
        early.append(job)
        flat += [
            a.reshape(groups, size, chunk, cols) for a, (chunk, cols) in zip(arrays, job.shapes)
        ]
    late = [
        Reduce(bag, f"late{p}", streams, groups, [(depth, 3 * 128)], False, False)
        for p in range(pairs)
    ]
    part = pl.BlockSpec((tile, 128), lambda p, i: (i, p))
    any_space = pl.BlockSpec(memory_space=pl.ANY)

    whole = pl.BlockSpec((seq, 128), lambda p, i: (0, p))

    def constant(shape):
        return pl.BlockSpec(shape, lambda p, i: (0,) * len(shape))

    small_shapes = [(2, depth), (6, depth), (1, up_width)]
    early_shapes = [shape for job in early for shape in job.out_shapes()]
    late_shapes = [shape for job in late for shape in job.out_shapes()]
    results = pl.pallas_call(
        functools.partial(backward_kernel, streams, groups, tile, bag, early, late),
        grid=(pairs, seq // tile),
        in_specs=[
            pl.BlockSpec((2, tile, seq), lambda p, i: (p, i, 0)),
            whole,
            whole,
            whole,
            whole,
            whole,
            part,
            part,
            part,
            constant(docs.shape),
            constant(small.shape),
        ]
        + [any_space] * (4 + len(flat)),
        out_specs=[any_space] * (1 + len(early_shapes) + len(late_shapes))
        + [constant(shape) for shape in small_shapes],
        out_shape=[jax.ShapeDtypeStruct((streams, shard, depth), BF)]
        + early_shapes
        + late_shapes
        + [jax.ShapeDtypeStruct(shape, F32) for shape in small_shapes],
        scratch_shapes=list(bag.items.values()),
        compiler_params=remote_params(collective_id),
        name="attention_back",
    )(
        numerators,
        queries,
        keys,
        values,
        teacher_queries,
        teacher_keys,
        d_context,
        context,
        inverse,
        docs,
        small,
        active,
        bin_own,
        d_one,
        tokens,
        *flat,
    )
    grad_tokens, *rest = results
    early_sums = rest[: len(flat)]
    late_sums = rest[len(flat) : -3]
    shapes = [a.shape for arrays in early_arrays for a in arrays]
    return (
        grad_tokens,
        [e.reshape(shape) for e, shape in zip(early_sums, shapes)],
        [l.reshape(groups, depth, 3 * 128) for l in late_sums],
        list(rest[-3:]),
    )


def middle_kernel(
    streams,
    groups,
    bag,
    tiles,
    x_ref,
    tx_ref,
    cot_ref,
    ctx_ref,
    tctx_ref,
    bo_hbm,
    bup_hbm,
    bdown_hbm,
    to_hbm,
    tup_hbm,
    tdown_hbm,
    sg_ref,
    sb_ref,
    sub_ref,
    tg_ref,
    tb_ref,
    tub_ref,
    out_ref,
    d1_ref,
    dctx_ref,
    gout_ref,
    gup_ref,
    gdown_ref,
    small_ref,
    *rest,
):
    have = bag.bind(rest)
    gout_acc, gup_acc, gdown_acc = have["gout"], have["gup"], have["gdown"]
    out_box, d_box = have["out_box"], have["d_box"]
    step = pl.program_id(0)
    far = (to_hbm, bo_hbm, tup_hbm, bup_hbm, tdown_hbm, bdown_hbm)
    to_ref, bo_ref, tup_ref, bup_ref, tdown_ref, bdown_ref = near = [
        have[f"weight{i}"] for i in range(6)
    ]
    loads = [
        pltpu.make_async_copy(source, target, have["weight_sems"].at[i])
        for i, (source, target) in enumerate(zip(far, near))
    ]

    def ready(which):
        @pl.when(step == 0)
        def _():
            for i in which:
                loads[i].wait()

    steps = pl.num_programs(0)
    width = ctx_ref.shape[1] * 128
    tile, depth = cot_ref.shape
    n_steps = out_box.shape[0]
    shard = n_steps * tile // streams
    s, r = place(groups)
    along_z = stream_peers(streams, groups)
    turned = row_tile(step, n_steps, streams, groups)
    start = pl.multiple_of(turned * tile, tile)

    @pl.when(step == 0)
    def _():
        for copy in loads:
            copy.start()
        greet(along_z + core_peers(groups))

    @pl.when(step == 0)
    def _():
        for ref in (gout_acc, gup_acc, gdown_acc, small_ref):
            ref[...] = jnp.zeros_like(ref)

    def row(ref, i):
        return ref[i : i + 1, :]

    pieces = [(j, p) for j in range(groups) for p in range(ctx_ref.shape[1])]
    ff = bup_ref.shape[1]
    wide = min(512, ff)
    chunks = [slice(i, i + wide) for i in range(0, ff, wide)]

    ready((0, 1))
    tctx = jnp.concatenate([tctx_ref[j, p] for j, p in pieces], axis=1)
    t_att = dot(tctx, to_ref[...]) + row(tb_ref, 2)
    context = jnp.concatenate([ctx_ref[j, p] for j, p in pieces], axis=1).astype(F32)
    bent = jnp.tanh(context * (1.0 / clip_level))
    ctx_active = (clip_level * bent).astype(BF)
    ctx_slope = 1.0 - bent * bent
    attended = dot(ctx_active, bo_ref[...]) + row(sb_ref, 2)
    t_hidden = layer_norm(tx_ref[...].astype(F32) + t_att, row(tg_ref, 0), row(tb_ref, 3))[0]
    hidden, normed_one, inverse_one = layer_norm(
        x_ref[...].astype(F32) + attended, row(sg_ref, 0), row(sb_ref, 3)
    )
    bent = jnp.tanh(hidden * (1.0 / clip_level))
    hidden_active = (clip_level * bent).astype(BF)
    hidden_slope = 1.0 - bent * bent
    t_low = t_hidden.astype(BF)

    def up(i):
        return dot(t_low, tup_ref[:, chunks[i]]), dot(hidden_active, bup_ref[:, chunks[i]])

    ready((2, 3, 4, 5))
    ahead = up(0)
    t_branch, branch, actives, slopes = None, None, [], []
    for i, at in enumerate(chunks):
        t_pre, inner_pre = ahead
        if i + 1 < len(chunks):
            ahead = up(i + 1)
        t_inner = gelu_parts(t_pre + tub_ref[:, at])[0]
        inner_pre = inner_pre + sub_ref[:, at]
        inner_act, phi = gelu_parts(inner_pre)
        bent = jnp.tanh(inner_act * (1.0 / clip_level))
        inner_active = (clip_level * bent).astype(BF)
        t_term = dot(t_inner.astype(BF), tdown_ref[at, :])
        term = dot(inner_active, bdown_ref[at, :])
        t_branch = t_term if i == 0 else t_branch + t_term
        branch = term if i == 0 else branch + term
        actives.append(inner_active)
        slopes.append(
            (1.0 - bent * bent)
            * (phi + inner_pre * jnp.exp(-0.5 * inner_pre * inner_pre) * 0.3989422804014327)
        )
    t_out = layer_norm(t_hidden + t_branch + row(tb_ref, 4), row(tg_ref, 1), row(tb_ref, 5))[0]
    branch = branch + row(sb_ref, 4)
    output, normed_two, inverse_two = layer_norm(hidden + branch, row(sg_ref, 1), row(sb_ref, 5))
    out_box[step] = output.astype(BF)
    per_tile = tile // shard
    for n in range(per_tile):
        block = turned * per_tile + n
        source = out_box.at[step, pl.ds(n * shard, shard)]

        @pl.when(block == s)
        def _():
            pltpu.make_async_copy(source, out_ref.at[s], have["out_s"].at[s]).start()

        @pl.when(block != s)
        def _():
            remote(
                source,
                out_ref.at[s],
                have["out_s"].at[block],
                have["out_r"].at[s],
                {"blk": block * groups + r},
            ).start()
    upstream = cot_ref[...].astype(F32) + 0.5 * (output - t_out)
    d_two = norm_back(upstream, row(sg_ref, 1), normed_two, inverse_two)
    d_branch = d_two.astype(BF)

    def down(i):
        return dot(d_branch, bdown_ref[chunks[i], :], NT)

    ahead = down(0)
    through = None
    for i, at in enumerate(chunks):
        d_inner = ahead
        if i + 1 < len(chunks):
            ahead = down(i + 1)
        d_inner = (d_inner * slopes[i]).astype(BF)
        gdown_acc[at, :] += dot(actives[i], d_branch, TN)
        gup_acc[:, at] += dot(hidden_active, d_inner, TN)
        term = dot(d_inner, bup_ref[:, at], NT)
        through = term if i == 0 else through + term
        d_shift = jnp.sum(d_inner.astype(F32), axis=0, keepdims=True)
        for n in range(wide // depth):
            line = 8 + (i * wide) // depth + n
            small_ref[line : line + 1, :] += d_shift[:, n * depth : (n + 1) * depth]
    d_hidden = d_two + through * hidden_slope
    d_one = norm_back(d_hidden, row(sg_ref, 0), normed_one, inverse_one)
    d1_ref[...] = d_one
    d_attended = d_one.astype(BF)
    gout_acc[...] += dot(ctx_active, d_attended, TN)
    d_context = (dot(d_attended, bo_ref[...], NT) * ctx_slope).astype(BF)
    place_rows = pl.ds(pl.multiple_of(r * n_steps * tile + start, tile), tile)
    for j in range(groups):
        d_box[step, j] = d_context[:, j * width : (j + 1) * width]
        piece, target = d_box.at[step, j], dctx_ref.at[place_rows]

        @pl.when(r == j)
        def _():
            tiles.own(have, piece, target, 0, step).start()

        @pl.when(r != j)
        def _():
            tiles.copy(have, piece, target, j, 0, step).start()


    def total(value):
        return jnp.sum(value, axis=0, keepdims=True)

    sums = [
        (0, d_hidden * normed_one),
        (1, upstream * normed_two),
        (4, d_attended.astype(F32)),
        (5, d_hidden),
        (6, d_branch.astype(F32)),
        (7, upstream),
    ]
    for i, value in sums:
        small_ref[i : i + 1, :] += total(value)
    @pl.when(step == steps - 1)
    def _():
        writes = []
        for i, (total_ref, target) in enumerate(
            ((gdown_acc, gdown_ref), (gup_acc, gup_ref), (gout_acc, gout_ref))
        ):
            narrow = have[f"narrow{i}"]
            narrow[...] = total_ref[...].astype(BF)
            copy = pltpu.make_async_copy(narrow, target, have["narrow_sems"].at[i])
            copy.start()
            writes.append(copy)
        tiles.finish(have, d_box.at[0, 0], dctx_ref.at[place_rows])
        source = out_box.at[0, pl.ds(0, shard)]
        pltpu.make_async_copy(source, out_ref.at[s], have["out_s"].at[s]).wait()
        for d, peer in enumerate(along_z, 1):
            block = lax.rem(s + d, streams)
            remote(
                source, out_ref.at[block], have["out_s"].at[block], have["out_r"].at[block], peer
            ).wait()
        for copy in writes:
            copy.wait()


def row_tile(step, steps, streams, groups):
    s, r = place(groups)
    return lax.rem(s // (streams // steps) + 1 + step, steps)


def middle(streams, groups, x, tx, cot, ctx, tctx, weights, teacher_weights, vectors, collective_id):
    rows, depth = cot.shape
    ff = weights[1].shape[1]
    tile = min(256, rows)
    pairs = ctx.shape[1]
    width = pairs * 128
    steps = rows // tile
    shard = rows // streams

    def turn(i):
        return row_tile(i, steps, streams, groups)

    def stream_tile(i):
        return lax.rem(lax.axis_index("blk"), groups) * steps + turn(i)

    tall = pl.BlockSpec((tile, depth), lambda i: (turn(i), 0))
    of_stream = pl.BlockSpec((tile, depth), lambda i: (stream_tile(i), 0))
    split_rows = pl.BlockSpec((groups, pairs, tile, 128), lambda i: (0, 0, turn(i), 0))
    any_space = pl.BlockSpec(memory_space=pl.ANY)

    def full(shape):
        return pl.BlockSpec(shape, lambda i: (0,) * len(shape))

    out_full = [(depth, depth), (depth, ff), (ff, depth), (16, depth)]
    bag = Bag()
    for name, shape in zip(("gout", "gup", "gdown"), out_full):
        bag.add(name, pltpu.VMEM(shape, F32))
    for i in range(3):
        bag.add(f"weight{2 * i}", pltpu.VMEM(teacher_weights[i].shape, BF))
        bag.add(f"weight{2 * i + 1}", pltpu.VMEM(weights[i].shape, BF))
    bag.add("weight_sems", dma(6))
    for i in range(3):
        bag.add(f"narrow{i}", pltpu.VMEM(out_full[2 - i], BF))
    bag.add("narrow_sems", dma(3))
    bag.add("out_box", pltpu.VMEM((steps, tile, depth), BF))
    bag.add("d_box", pltpu.VMEM((steps, groups, tile, width), BF))
    bag.add("out_s", dma(streams))
    bag.add("out_r", dma(streams))
    tiles = Tiles(bag, "tiles", groups, 1, steps)
    return pl.pallas_call(
        functools.partial(middle_kernel, streams, groups, bag, tiles),
        grid=(steps,),
        in_specs=[of_stream, of_stream, tall, split_rows, split_rows]
        + [any_space] * 6
        + [full(a.shape) for a in vectors],
        out_specs=[any_space, tall, any_space] + [any_space] * 3 + [full(out_full[3])],
        out_shape=[
            jax.ShapeDtypeStruct((streams, shard, depth), BF),
            jax.ShapeDtypeStruct((rows, depth), F32),
            jax.ShapeDtypeStruct((rows * groups, width), BF),
        ]
        + [jax.ShapeDtypeStruct(s, BF if i < 3 else F32) for i, s in enumerate(out_full)],
        scratch_shapes=list(bag.items.values()),
        compiler_params=remote_params(collective_id),
        name="middle",
    )(x, tx, cot, ctx, tctx, *weights, *teacher_weights, *vectors)


def latent_columns(latent, grad, out):
    rows = latent.shape[0]
    size = min(256, rows)
    chunks = [slice(i, i + size) for i in range(0, rows, size)]
    squares = jnp.zeros((1, latent.shape[1]), F32)
    for at in chunks:
        matrix = latent[at, :].astype(F32)
        squares = squares + jnp.sum(matrix * matrix, axis=0, keepdims=True)
    scale = jnp.sqrt(squares * (1.0 / rows) + 1e-06)
    twice = 2.0 / scale
    through_scale = jnp.zeros_like(squares)
    for at in chunks:
        matrix, upstream = latent[at, :].astype(F32), grad[at, :].astype(F32)
        inner = matrix * twice
        bent = jnp.tanh(inner)
        slope = 1.0 - bent * bent
        through_scale = through_scale + jnp.sum(
            upstream * (bent - inner * slope), axis=0, keepdims=True
        )
        out[at, :] = upstream * (2.0 * slope)
    factor = through_scale / (rows * scale)
    for at in chunks:
        out[at, :] = out[at, :] + latent[at, :].astype(F32) * factor


def latent_grads_kernel(pairs, passed, lq, lo, lu, ld, *refs):
    late, (go, gu, gd, *refs) = refs[:pairs], refs[pairs:]
    come, (oq, oo, ou, od, *gone) = refs[:passed], refs[passed:]
    for source, target in zip(come, gone):
        target[...] = source[...]
    for p in range(pairs):

        @pl.when(lax.rem(pl.program_id(0), pairs) == p)
        def _():
            for i in range(3):
                latent_columns(lq.at[i], late[p].at[0, :, i * 128 : (i + 1) * 128], oq.at[i])

    latent_columns(lo, go, oo)
    latent_columns(ld, gd, od)
    for i in range(0, lu.shape[1], 128):
        at = slice(i, i + 128)
        latent_columns(lu.at[:, at], gu.at[:, at], ou.at[:, at])


def latent_grads(latents, late, early, tall, small):
    pairs = len(late)
    groups, depth, wide = late[0].shape
    steps = groups * pairs
    qkv = pl.BlockSpec((3, depth, depth // steps), lambda i: (0, 0, i))
    flat = [pl.BlockSpec((a.shape[0], a.shape[1] // steps), lambda i: (0, i)) for a in latents[1:]]
    handed = [
        pl.BlockSpec((a.shape[0] // steps,) + a.shape[1:], lambda i: (i, 0, 0)) for a in tall
    ] + [pl.BlockSpec(a.shape, lambda i: (0, 0)) for a in small]
    return pl.pallas_call(
        functools.partial(latent_grads_kernel, pairs, len(handed)),
        grid=(steps,),
        in_specs=[qkv]
        + flat
        + [pl.BlockSpec((1, depth, wide), lambda i: (i // pairs, 0, 0))] * pairs
        + flat
        + handed,
        out_specs=[qkv] + flat + handed,
        out_shape=[jax.ShapeDtypeStruct(a.shape, F32) for a in latents]
        + [jax.ShapeDtypeStruct(a.shape, a.dtype) for a in tall + small],
        compiler_params=pltpu.CompilerParams(vmem_limit_bytes=VMEM_BYTES),
        name="latent_grads",
    )(*latents, *late, *early, *tall, *small)


def shards(
    tokens,
    teacher_tokens,
    segment_ids,
    cotangent,
    latent_qkv,
    latent_out,
    latent_up,
    latent_down,
    student_gain,
    student_bias,
    student_up_bias,
    teacher_qkv,
    teacher_out,
    teacher_up,
    teacher_down,
    teacher_gain,
    teacher_bias,
    teacher_up_bias,
):
    streams, shard_len, depth = tokens.shape
    blocks = lax.axis_size("blk")
    groups = blocks // streams
    seq = shard_len * blocks
    rows = seq // groups
    block = (shard_len, depth)
    gather, swap = Gather(streams, groups, block, BF), Swap(streams, groups, block, BF)
    bin_own, bin_out, bin_up, bin_down, token_blocks, qkv_parts, docs = intake(
        Moves(
            gather,
            Spread(teacher_qkv.shape, BF),
            Gather(streams, groups, (8, shard_len), F32),
        ),
        groups,
        [latent_qkv, latent_out, latent_up, latent_down],
        segment_ids,
        [tokens, teacher_qkv],
        1,
    )
    stream_tokens = token_blocks.reshape(seq, depth)
    (
        queries,
        keys,
        ctx_rows,
        values,
        numerators,
        context,
        inverse,
        active,
        teacher_blocks,
        up_parts,
        out_parts,
    ) = attention(
        stream_tokens,
        bin_own,
        student_bias,
        docs,
        streams,
        groups,
        Moves(gather, Spread(teacher_up.shape, BF), Spread(teacher_out.shape, BF)),
        [teacher_tokens, teacher_up, teacher_out],
        True,
        2,
        "attention_student",
    )
    teacher_stream = teacher_blocks.reshape(seq, depth)
    teacher_queries, teacher_keys, tctx_rows, cot_blocks, down_parts = attention(
        teacher_stream,
        qkv_parts,
        teacher_bias,
        docs,
        streams,
        groups,
        Moves(swap, Spread(teacher_down.shape, BF), others=[gather]),
        [cotangent, teacher_down],
        False,
        3,
        "attention_teacher",
    )
    output, d_one, d_context, g_out, g_up, g_down, small = middle(
        streams,
        groups,
        stream_tokens,
        teacher_stream,
        cot_blocks.reshape(rows, depth),
        ctx_rows,
        tctx_rows,
        [bin_out, bin_up, bin_down],
        [
            out_parts.reshape(-1, depth),
            up_parts.reshape(depth, -1),
            down_parts.reshape(-1, depth),
        ],
        [
            student_gain,
            student_bias,
            student_up_bias.reshape(1, -1),
            teacher_gain,
            teacher_bias,
            teacher_up_bias.reshape(1, -1),
        ],
        4,
    )
    grads = [[g_up], [g_down, g_out]]
    in_kernel = depth % (16 * blocks * lax.axis_size("dp")) == 0
    grad_tokens, early, late, small = attention_back(
        streams,
        groups,
        numerators,
        queries,
        keys,
        values,
        teacher_queries,
        teacher_keys,
        d_context,
        context,
        inverse,
        docs,
        small,
        active,
        bin_own,
        d_one,
        token_blocks,
        grads if in_kernel else [],
        latent_up.shape[1],
        6,
    )
    if not in_kernel:
        early = lax.psum((g_up, g_down, g_out), ("dp", "blk"))
    grad_qkv, grad_out, grad_up, grad_down, output, grad_tokens, gain, bias, shift = latent_grads(
        [latent_qkv, latent_out, latent_up, latent_down],
        late,
        [early[2], early[0], early[1]],
        [output, grad_tokens],
        small,
    )
    return (
        output,
        grad_tokens,
        grad_qkv,
        grad_out,
        grad_up,
        grad_down,
        gain,
        bias,
        shift.reshape(-1),
    )


def solution(mesh):
    return jax.shard_map(
        shards,
        mesh=mesh,
        in_specs=(
            P("dp", "blk", None),
            P("dp", "blk", None),
            P("dp", "blk"),
            P("dp", "blk", None),
            P(),
            P(),
            P(),
            P(),
            P(),
            P(),
            P(),
            P(None, "dp", None),
            P("dp", None),
            P("dp", None),
            P("dp", None),
            P(),
            P(),
            P(),
        ),
        out_specs=(P("dp", "blk", None), P("dp", "blk", None), P(), P(), P(), P(), P(), P(), P()),
        check_vma=False,
    )
```
